32 devices in a mesh: pipe: 4 (over y, x), dp: 2 (over core), rep: 4 (over z).
Axes of the slice: x: 2, y: 2, z: 4, core: 2. Of those that a mesh axis runs over, the one named last changes fastest.
Arguments:
- images: bfloat16 [64, 196, 1024], P(('dp', 'rep')), may hold values from -80 to 80
- section_weights: bfloat16 [4, 3407872], P('pipe'), may hold values from -3 to 3
- bn_gain: float32 [4, 4, 4096], P('pipe'), may hold values from 0.25 to 1.75
- bn_bias: float32 [4, 4, 4096], P('pipe'), may hold values from -3 to 3
- width: int32 [8, 2], replicated, may hold values from 128 to 512, as said below
- bn_set: int32 [8, 2], replicated, may hold values from 0 to 3
- gate: int32 [8], replicated, may hold values from 0 to 1, as said below
- cotangent: bfloat16 [64, 49, 2048], P(('dp', 'rep')), may hold values from -16 to 16
Outputs:
- output: bfloat16 [64, 49, 2048], P(('dp', 'rep'), None, 'pipe')
- grad_images: float32 [64, 196, 1024], P(('dp', 'rep'), None, 'pipe')
- grad_weights: float32 [4, 3407872], P('pipe')
- grad_gain: float32 [4, 4, 4096], P('pipe')
- grad_bias: float32 [4, 4, 4096], P('pipe')
The draws below stay inside these ranges and needn't reach their ends.
Inputs may be any that keep to these rules, and one draw needn't show every extreme that they name: `width`: both bounds occur in every draw. `gate`: every draw has a micro-batch with 1 and one with 0.
All inputs are finite; a program needn't handle non-finite values.
Results may differ from the reference program's by a relative error of at most 0.035.
Values may be sent and summed in bfloat16 or wider, within the bound.
A program may use at most 256 MiB of HBM per device.

```python
import jax
import jax.numpy as jnp
from jax import lax

C_IN = 1024
C_MID = 512
C_OUT = 2048
SIDE = 14
NSETS = 4
MB = 8
IMG_B = 1
OSIDE = 7
PIX_IN = 196
PIX_OUT = 49
IMAGES = 64
P_SIZE = 3407872
N_DP = 2
N_REP = 4


def log_scale(key, shape, low_end, high_end):
    return jnp.exp(jax.random.uniform(key, shape, jnp.float32, jnp.log(low_end), jnp.log(high_end)))


def draw_images(key, part):
    key = jax.random.fold_in(key, 11)
    key_a, key_b, key_c = jax.random.split(key, 3)
    shape = (IMAGES, PIX_IN, C_IN)
    base_draw = jax.random.truncated_normal(key_a, -4.0, 4.0, shape, jnp.float32)
    image_scale = log_scale(key_b, (IMAGES, 1, 1), 0.3, 3.0)
    position = jnp.arange(IMAGES, dtype=jnp.float32).reshape(IMAGES, 1, 1) / IMAGES
    rising = jnp.exp((position - 0.5) * jnp.log(3.0))
    channel_scale = log_scale(key_c, (1, 1, C_IN), 0.3, 3.0)
    return (base_draw * image_scale * rising * channel_scale).astype(jnp.bfloat16)


def draw_section_weights(key, part):
    key = jax.random.fold_in(key, 12)
    base_draw = jax.random.truncated_normal(key, -3.0, 3.0, (4, P_SIZE), jnp.float32)
    split_at = jnp.array([C_IN * C_MID, C_MID * C_OUT, C_OUT * C_MID, C_MID * C_OUT], jnp.int32).reshape(4, 1)
    first_fan = jnp.array([C_IN, C_MID, C_OUT, C_MID], jnp.float32).reshape(4, 1)
    second_fan = jnp.array([9 * C_MID, C_IN, 9 * C_MID, 1], jnp.float32).reshape(4, 1)
    column = jnp.arange(P_SIZE, dtype=jnp.int32).reshape(1, P_SIZE)
    scaling = jnp.where(column < split_at, lax.rsqrt(first_fan), lax.rsqrt(second_fan))
    return (base_draw * scaling).astype(jnp.bfloat16)


def draw_width(key, part):
    key = jax.random.fold_in(key, 13)
    key_a, key_b = jax.random.split(key)
    values = jax.random.randint(key_a, (MB * 2,), C_MID // 4, C_MID + 1)
    picked = jax.random.permutation(key_b, MB * 2)
    values = values.at[picked[0]].set(C_MID).at[picked[1]].set(C_MID // 4)
    return values.reshape(MB, 2).astype(jnp.int32)


def draw_gate(key, part):
    key = jax.random.fold_in(key, 14)
    key_a, key_b = jax.random.split(key)
    values = jax.random.randint(key_a, (MB,), 0, 2)
    picked = jax.random.permutation(key_b, MB)
    return values.at[picked[0]].set(1).at[picked[1]].set(0).astype(jnp.int32)


def draw_cotangent(key, part):
    key = jax.random.fold_in(key, 15)
    key_a, key_b = jax.random.split(key, 2)
    shape = (IMAGES, PIX_OUT, C_OUT)
    base_draw = jax.random.truncated_normal(key_a, -4.0, 4.0, shape, jnp.float32)
    image_scale = log_scale(key_b, (IMAGES, 1, 1), 0.5, 2.0)
    position = jnp.arange(IMAGES, dtype=jnp.float32).reshape(IMAGES, 1, 1) / IMAGES
    rising = jnp.exp((position - 0.5) * jnp.log(3.0))
    return (base_draw * image_scale * rising).astype(jnp.bfloat16)


def touch_ends(drawn, own_key, low, top_value):
    dims = drawn.shape
    spot = [jax.random.randint(jax.random.fold_in(own_key, axis), (), 0, dims[axis]) for axis in range(len(dims))]
    drawn = drawn.at[tuple(spot)].set(low)
    longest = dims.index(max(dims))
    spot[longest] = (spot[longest] + 1) % dims[longest]
    return drawn.at[tuple(spot)].set(top_value)


def block_levels(rng, extent, cuts, low, top_value):
    factor_of, own = 1.0, jax.random.fold_in(rng, 6)
    for dim, blocks in cuts:
        steps = jnp.exp(jax.random.uniform(jax.random.fold_in(own, dim), (blocks,), jnp.float32, low / len(cuts), top_value / len(cuts)))
        factor_of = factor_of * jnp.repeat(steps, extent[dim] // blocks).reshape([-1 if axis == dim else 1 for axis in range(len(extent))])
    return factor_of


def bell_draw(own_key, shape, scale, limit, cuts=(), kind=jnp.bfloat16):
    values = jax.random.normal(own_key, shape, jnp.float32) * scale
    if len(cuts) > 0:
        values = block_levels(own_key, shape, cuts, -0.22, 0.18) * values
    return jnp.clip(values, min=-limit, max=limit).astype(kind)


def setup_inputs(seed: int = 0) -> dict:
    seeds = jax.random.split(jax.random.key(seed), 9)
    images = draw_images(jax.random.fold_in(seeds[8], 71), 0)
    section_weights = draw_section_weights(jax.random.fold_in(seeds[8], 71), 0)
    bn_gain = jnp.clip(1.0 + 0.15 * jax.random.normal(seeds[2], (4, NSETS, 2 * C_OUT), jnp.float32), 0.25, 1.75)
    bn_bias = bell_draw(seeds[3], (4, NSETS, 2 * C_OUT), 0.5, 3.0, ((0, 4),), jnp.float32)
    width = draw_width(jax.random.fold_in(seeds[8], 71), 0)
    bn_set = touch_ends(jax.random.randint(seeds[5], (MB, 2), 0, NSETS), jax.random.fold_in(seeds[5], 1), 0, NSETS - 1).astype(jnp.int32)
    gate = draw_gate(jax.random.fold_in(seeds[8], 71), 0)
    cotangent = draw_cotangent(jax.random.fold_in(seeds[8], 71), 0)
    return dict(images=images, section_weights=section_weights, bn_gain=bn_gain, bn_bias=bn_bias, width=width, bn_set=bn_set, gate=gate, cotangent=cotangent)


EPSILON = 1e-05
precise = lax.Precision.HIGHEST

@jax.custom_vjp
def low(v):
    return lax.optimization_barrier(v.astype(jnp.bfloat16)).astype(jnp.float32)

@jax.custom_vjp
def low_back(v):
    return v

def low_keep(v):
    return (low(v), None)

def low_pass(kept, grad):
    return (grad,)

def back_keep(v):
    return (v, None)

def back_low(kept, grad):
    return (low(grad),)
low.defvjp(low_keep, low_pass)
low_back.defvjp(back_keep, back_low)

def smooth(inputs):
    return inputs * jax.nn.sigmoid(inputs)

def matmul(left_op, right_op):
    return jnp.dot(left_op, right_op, precision=precise, preferred_element_type=jnp.float32)

def patches(planes, stride):
    images, side_len, channels = (planes.shape[0], planes.shape[1], planes.shape[3])
    out_side = side_len // stride
    padded = jnp.pad(planes, ((0, 0), (1, 1), (1, 1), (0, 0)))
    pieces = []
    for row_off in range(3):
        for col_off in range(3):
            pieces.append(padded[:, row_off:row_off + stride * (out_side - 1) + 1:stride, col_off:col_off + stride * (out_side - 1) + 1:stride, :])
    return jnp.concatenate(pieces, axis=3).reshape(images * out_side * out_side, 9 * channels)

def batch_norm(values, gain_vec, bias_vec):
    center = lax.optimization_barrier(jnp.mean(values, axis=0))
    spread = lax.optimization_barrier(jnp.mean(values * values, axis=0)) - center * center
    return (values - center) * lax.rsqrt(spread + EPSILON) * gain_vec + bias_vec

def group_pass(inputs, weights, gain_all, biases, width_pair, set_pair, gate_flag):
    images = inputs.shape[0]
    channel_ids = jnp.arange(C_MID)
    mask_one = (channel_ids < width_pair[0]).astype(jnp.float32)
    mask_two = (channel_ids < width_pair[1]).astype(jnp.float32)
    gain_zero, bias_zero = (gain_all[0, set_pair[0]], biases[0, set_pair[0]])
    gain_one, bias_one = (gain_all[1, set_pair[0]], biases[1, set_pair[0]])
    gain_two, bias_two = (gain_all[2, set_pair[1]], biases[2, set_pair[1]])
    gain_three, bias_three = (gain_all[3, set_pair[1]], biases[3, set_pair[1]])
    split_zero = C_IN * C_MID
    weight_one = weights[0, :split_zero].reshape(C_IN, C_MID)
    weight_two = weights[0, split_zero:split_zero + 9 * C_MID * C_MID].reshape(9 * C_MID, C_MID)
    weight_three = weights[1, :C_MID * C_OUT].reshape(C_MID, C_OUT)
    weight_short = weights[1, C_MID * C_OUT:C_MID * C_OUT + C_IN * C_OUT].reshape(C_IN, C_OUT)
    weight_four = weights[2, :C_OUT * C_MID].reshape(C_OUT, C_MID)
    weight_five = weights[2, C_OUT * C_MID:C_OUT * C_MID + 9 * C_MID * C_MID].reshape(9 * C_MID, C_MID)
    weight_six = weights[3, :C_MID * C_OUT].reshape(C_MID, C_OUT)
    flat_in = inputs.reshape(images * PIX_IN, C_IN)
    conv_one = low_back(matmul(flat_in, weight_one))
    hid_one = low(smooth(batch_norm(conv_one, gain_zero[:C_MID], bias_zero[:C_MID])) * mask_one)
    conv_two = low_back(matmul(patches(hid_one.reshape(images, SIDE, SIDE, C_MID), 2), weight_two))
    hid_two = low_back(low(smooth(batch_norm(conv_two, gain_zero[C_MID:2 * C_MID], bias_zero[C_MID:2 * C_MID])) * mask_one))
    short_in = inputs.reshape(images, SIDE, SIDE, C_IN)[:, ::2, ::2, :].reshape(images * PIX_OUT, C_IN)
    conv_three = low_back(matmul(hid_two, weight_three))
    conv_short = low_back(matmul(short_in, weight_short))
    block_one = low(smooth(batch_norm(conv_three, gain_one[:C_OUT], bias_one[:C_OUT]) + batch_norm(conv_short, gain_one[C_OUT:], bias_one[C_OUT:])))
    carried = low_back(block_one)
    conv_four = low_back(matmul(carried, weight_four))
    hid_four = low(smooth(batch_norm(conv_four, gain_two[:C_MID], bias_two[:C_MID])) * mask_two)
    conv_five = low_back(matmul(patches(hid_four.reshape(images, OSIDE, OSIDE, C_MID), 1), weight_five))
    hid_five = low_back(low(smooth(batch_norm(conv_five, gain_two[C_MID:2 * C_MID], bias_two[C_MID:2 * C_MID])) * mask_two))
    residual = low_back(carried)
    conv_six = low_back(matmul(hid_five, weight_six))
    merged = smooth(residual + batch_norm(conv_six, gain_three[:C_OUT], bias_three[:C_OUT]))
    output = gate_flag * merged + (1.0 - gate_flag) * residual
    return output.reshape(images, PIX_OUT, C_OUT)

def reference(images, section_weights, bn_gain, bn_bias, width, bn_set, gate, cotangent):
    groups = N_REP * MB
    members = N_DP * IMG_B

    def to_groups(tensor):
        shaped = tensor.astype(jnp.float32).reshape((N_DP, N_REP, MB, IMG_B) + tensor.shape[1:])
        shaped = jnp.moveaxis(shaped, 0, 2)
        return shaped.reshape((groups, members) + tensor.shape[1:])

    def from_groups(tensor):
        shaped = tensor.reshape((N_REP, MB, N_DP, IMG_B) + tensor.shape[2:])
        shaped = jnp.moveaxis(shaped, 2, 0)
        return shaped.reshape((IMAGES,) + tensor.shape[2:])
    micro_ids = jnp.arange(groups) % MB
    widths_g = width[micro_ids]
    sets_g = bn_set[micro_ids]
    gates_g = gate[micro_ids].astype(jnp.float32)
    checked = jax.checkpoint(group_pass)

    def forward(grouped, weights, gain_all, biases):

        def scan_step(state_in, slices):
            result = checked(slices[0], weights, gain_all, biases, slices[1], slices[2], slices[3])
            return (state_in, result)
        unused, outputs = lax.scan(scan_step, jnp.zeros((), jnp.float32), (grouped, widths_g, sets_g, gates_g))
        return outputs
    outputs, pullback = jax.vjp(forward, to_groups(images), section_weights.astype(jnp.float32), bn_gain, bn_bias)
    grad_in, grad_weights, grad_gain, grad_bias = pullback(to_groups(cotangent))
    return (from_groups(outputs).astype(jnp.bfloat16), from_groups(grad_in), grad_weights, grad_gain, grad_bias)
```

```python
import jax
import jax.numpy as jnp
from jax import lax
from jax.experimental import pallas as pl
from jax.experimental.pallas import tpu as pltpu
from jax.sharding import PartitionSpec as P

C_IN = 1024
C_MID = 512
C_OUT = 2048
SIDE = 14
NSETS = 4
MB = 8
IMG_B = 1
OSIDE = 7
PIX_IN = 196
PIX_OUT = 49
IMG_DEV = 8
P_SIZE = 3407872


EPSILON = 1e-05


def for_sending(array):

    def short(part):
        return part.astype(jnp.bfloat16) if part.dtype == jnp.float32 else part

    return jax.tree.map(short, array)


def shifted(value, axis, steps):
    count = lax.axis_size(axis)
    first, last = (max(0, -steps), min(count, count - steps))
    return lax.ppermute(value, axis, [(source, source + steps) for source in range(first, last)])


def smooth(inputs):
    return inputs * jax.nn.sigmoid(inputs)


def smooth_slope(inputs):
    gate_sig = jax.nn.sigmoid(inputs)
    return gate_sig * (1.0 + inputs * (1.0 - gate_sig))


def matmul(left_op, right_op):
    return jnp.dot(left_op, right_op, preferred_element_type=jnp.float32)


def matmul_left_t(left_op, right_op):
    return lax.dot_general(
        left_op, right_op, (((0,), (0,)), ((), ())), preferred_element_type=jnp.float32
    )


def matmul_right_t(left_op, right_op):
    return lax.dot_general(
        left_op, right_op, (((1,), (1,)), ((), ())), preferred_element_type=jnp.float32
    )


def patches(planes, stride):
    images, side_len, channels = (planes.shape[0], planes.shape[1], planes.shape[3])
    out_side = side_len // stride
    padded = jnp.pad(planes, ((0, 0), (1, 1), (1, 1), (0, 0)))
    pieces = []
    for row_off in range(3):
        for col_off in range(3):
            pieces.append(
                padded[
                    :,
                    row_off : row_off + stride * (out_side - 1) + 1 : stride,
                    col_off : col_off + stride * (out_side - 1) + 1 : stride,
                    :,
                ]
            )
    return jnp.concatenate(pieces, axis=3).reshape(images * out_side * out_side, 9 * channels)


def unpatch(columns, images, side_len, stride, channels):
    out_side = side_len // stride
    pieces = columns.reshape(images, out_side, out_side, 9, channels)
    padded = jnp.zeros((images, side_len + 2, side_len + 2, channels), jnp.float32)
    for row_off in range(3):
        for col_off in range(3):
            padded = padded.at[
                :,
                row_off : row_off + stride * (out_side - 1) + 1 : stride,
                col_off : col_off + stride * (out_side - 1) + 1 : stride,
                :,
            ].add(pieces[:, :, :, row_off * 3 + col_off, :])
    return padded[:, 1 : side_len + 1, 1 : side_len + 1, :]


def group_moments(sums_local, squares_local):
    return (
        lax.psum(sums_local.astype(jnp.bfloat16), "dp").astype(jnp.float32),
        lax.psum(squares_local.astype(jnp.bfloat16), "dp").astype(jnp.float32),
    )


def group_grad_sums(bias_local, gain_local):
    return (
        lax.psum(bias_local.astype(jnp.bfloat16), "dp").astype(jnp.float32),
        lax.psum(gain_local.astype(jnp.bfloat16), "dp").astype(jnp.float32),
    )


def stats_of(sum_all, square_all, start, count, row_total):
    center = sum_all[start : start + count] / row_total
    inv_std = lax.rsqrt(square_all[start : start + count] / row_total - center * center + EPSILON)
    return (center, inv_std)


def norm_grad(slope_in, normed, gain_vec, inv_std, sum_bias, sum_gain, row_total):
    return (
        gain_vec * inv_std * (slope_in - sum_bias / row_total - normed * (sum_gain / row_total))
    ).astype(jnp.bfloat16)


def on_device(images, section_weights, bn_gain, bn_bias, width, bn_set, gate, cotangent):
    section_idx = lax.axis_index("pipe")
    pipe_count = lax.axis_size("pipe")
    dp_count = lax.axis_size("dp")
    flat_weights = section_weights[0]
    gain_table = bn_gain[0]
    bias_table = bn_bias[0]
    rows_in = IMG_B * PIX_IN
    rows_out = IMG_B * PIX_OUT
    total_in = float(rows_in * dp_count)
    total_out = float(rows_out * dp_count)
    wide = 2 * C_OUT
    scr_len = IMG_B * max(PIX_IN * C_MID, PIX_OUT * wide)
    image_blocks = images.reshape(MB, IMG_B, PIX_IN, C_IN)
    pad_mid = jnp.zeros((wide - 2 * C_MID,), jnp.float32)
    zero_wide = jnp.zeros((wide,), jnp.float32)
    zero_scr = jnp.zeros((scr_len,), jnp.float32)
    zero_mid = jnp.zeros((rows_out, C_MID), jnp.bfloat16)
    zero_res = jnp.zeros((rows_out, C_OUT), jnp.bfloat16)
    zero_rows = jnp.zeros((rows_out, C_OUT), jnp.float32)
    zero_input = jnp.zeros((IMG_B, PIX_IN, C_IN), jnp.float32)

    def pack(values):
        flat = values.reshape(-1).astype(jnp.float32)
        return jnp.pad(flat, (0, scr_len - flat.shape[0]))

    def unpack(buffer, rows, cols):
        return buffer[: rows * cols].reshape(rows, cols)

    def place(vec, start):
        return jnp.pad(vec, (start, wide - start - vec.shape[0]))

    def add_weight(acc, grad, offset, valid):
        flat = grad.reshape(-1)
        return acc.at[offset : offset + flat.shape[0]].add(jnp.where(valid, flat, 0.0))

    def weights_zero():
        split_at = C_IN * C_MID
        return (
            flat_weights[:split_at].reshape(C_IN, C_MID),
            flat_weights[split_at : split_at + 9 * C_MID * C_MID].reshape(9 * C_MID, C_MID),
        )

    def weights_one():
        split_at = C_MID * C_OUT
        return (
            flat_weights[:split_at].reshape(C_MID, C_OUT),
            flat_weights[split_at : split_at + C_IN * C_OUT].reshape(C_IN, C_OUT),
        )

    def weights_two():
        split_at = C_OUT * C_MID
        return (
            flat_weights[:split_at].reshape(C_OUT, C_MID),
            flat_weights[split_at : split_at + 9 * C_MID * C_MID].reshape(9 * C_MID, C_MID),
        )

    def short_rows(image_block):
        return image_block.reshape(IMG_B, SIDE, SIDE, C_IN)[:, ::2, ::2, :].reshape(rows_out, C_IN)

    def local_stats(values, start):
        return (
            place(jnp.sum(values, axis=0), start),
            place(jnp.sum(values * values, axis=0), start),
        )

    def fwd_a_zero(ops):
        conv_a, conv_b = weights_zero()
        pre_one = matmul(ops[0].reshape(rows_in, C_IN), conv_a)
        sums_local, squares_local = local_stats(pre_one, 0)
        return (pack(pre_one), sums_local, squares_local)

    def fwd_a_one(ops):
        conv_a, conv_b = weights_one()
        pre_both = jnp.concatenate(
            [matmul(ops[1], conv_a), matmul(short_rows(ops[0]), conv_b)], axis=1
        )
        sums_local, squares_local = local_stats(pre_both, 0)
        return (pack(pre_both), sums_local, squares_local)

    def fwd_a_two(ops):
        conv_a, conv_b = weights_two()
        pre_four = matmul(ops[2], conv_a)
        sums_local, squares_local = local_stats(pre_four, 0)
        return (pack(pre_four), sums_local, squares_local)

    def fwd_a_three(ops):
        conv_a = flat_weights[: C_MID * C_OUT].reshape(C_MID, C_OUT)
        pre_six = matmul(ops[1], conv_a)
        sums_local, squares_local = local_stats(pre_six, 0)
        return (pack(pre_six), sums_local, squares_local)

    def fwd_b_zero(args):
        ops, scratch, sum_all, square_all = args
        conv_a, conv_b = weights_zero()
        gain_vec, bias_vec, mask_vec = (ops[3], ops[4], ops[5])
        pre_one = unpack(scratch, rows_in, C_MID)
        center_one, inv_one = stats_of(sum_all, square_all, 0, C_MID, total_in)
        hidden_one = (
            smooth((pre_one - center_one) * inv_one * gain_vec[:C_MID] + bias_vec[:C_MID])
            * mask_vec
        ).astype(jnp.bfloat16)
        pre_two = matmul(patches(hidden_one.reshape(IMG_B, SIDE, SIDE, C_MID), 2), conv_b)
        sums_local, squares_local = local_stats(pre_two, C_MID)
        return (pack(pre_two), sums_local, squares_local)

    def fwd_b_pass(args):
        return (args[1], zero_wide, zero_wide)

    def fwd_b_two(args):
        ops, scratch, sum_all, square_all = args
        conv_a, conv_b = weights_two()
        gain_vec, bias_vec, mask_vec = (ops[3], ops[4], ops[5])
        pre_four = unpack(scratch, rows_out, C_MID)
        center_four, inv_four = stats_of(sum_all, square_all, 0, C_MID, total_out)
        hidden_four = (
            smooth((pre_four - center_four) * inv_four * gain_vec[:C_MID] + bias_vec[:C_MID])
            * mask_vec
        ).astype(jnp.bfloat16)
        pre_five = matmul(patches(hidden_four.reshape(IMG_B, OSIDE, OSIDE, C_MID), 1), conv_b)
        sums_local, squares_local = local_stats(pre_five, C_MID)
        return (pack(pre_five), sums_local, squares_local)

    def fwd_c_double(args, first_total, send_res):
        ops, scratch, sum_all, square_all = args
        gain_vec, bias_vec, mask_vec = (ops[3], ops[4], ops[5])
        pre_two = unpack(scratch, rows_out, C_MID)
        center_one, inv_one = stats_of(sum_all, square_all, 0, C_MID, first_total)
        center_two, inv_two = stats_of(sum_all, square_all, C_MID, C_MID, total_out)
        hidden_two = (
            smooth(
                (pre_two - center_two) * inv_two * gain_vec[C_MID : 2 * C_MID]
                + bias_vec[C_MID : 2 * C_MID]
            )
            * mask_vec
        ).astype(jnp.bfloat16)
        centers = jnp.concatenate([center_one, center_two, pad_mid])
        scales = jnp.concatenate([inv_one, inv_two, pad_mid])
        return (hidden_two, send_res, centers, scales, zero_rows)

    def fwd_c_zero(args):
        return fwd_c_double(args, total_in, zero_res)

    def fwd_c_two(args):
        return fwd_c_double(args, total_out, args[0][2])

    def fwd_c_one(args):
        ops, scratch, sum_all, square_all = args
        gain_vec, bias_vec = (ops[3], ops[4])
        pre_both = unpack(scratch, rows_out, wide)
        centers, scales = stats_of(sum_all, square_all, 0, wide, total_out)
        activ = (pre_both - centers) * scales * gain_vec + bias_vec
        block_out = smooth(activ[:, :C_OUT] + activ[:, C_OUT:]).astype(jnp.bfloat16)
        return (zero_mid, block_out, centers, scales, zero_rows)

    def fwd_c_three(args):
        ops, scratch, sum_all, square_all = args
        gain_vec, bias_vec, gate_val = (ops[3], ops[4], ops[6])
        pre_six = unpack(scratch, rows_out, C_OUT)
        centers, scales = stats_of(sum_all, square_all, 0, wide, total_out)
        residual = ops[2].astype(jnp.float32)
        merged = smooth(
            residual
            + (pre_six - centers[:C_OUT]) * scales[:C_OUT] * gain_vec[:C_OUT]
            + bias_vec[:C_OUT]
        )
        result = gate_val * merged + (1.0 - gate_val) * residual
        return (zero_mid, zero_res, centers, scales, result)

    def bwd_a_double(ops, flat_in, conv_a, conv_b, side_len, stride):
        centers, scales, grad_mid = (ops[3], ops[4], ops[5])
        gain_vec, bias_vec, mask_vec = (ops[8], ops[9], ops[10])
        norm_one = (matmul(flat_in, conv_a) - centers[:C_MID]) * scales[:C_MID]
        hidden_one = (smooth(norm_one * gain_vec[:C_MID] + bias_vec[:C_MID]) * mask_vec).astype(
            jnp.bfloat16
        )
        columns = patches(hidden_one.reshape(IMG_B, side_len, side_len, C_MID), stride)
        norm_two = (matmul(columns, conv_b) - centers[C_MID : 2 * C_MID]) * scales[
            C_MID : 2 * C_MID
        ]
        act_two = norm_two * gain_vec[C_MID : 2 * C_MID] + bias_vec[C_MID : 2 * C_MID]
        slope_two = grad_mid.astype(jnp.float32) * mask_vec * smooth_slope(act_two)
        return (
            pack(slope_two),
            pack(norm_two),
            pack(norm_one),
            place(jnp.sum(slope_two, axis=0), C_MID),
            place(jnp.sum(slope_two * norm_two, axis=0), C_MID),
        )

    def bwd_a_zero(ops):
        conv_a, conv_b = weights_zero()
        return bwd_a_double(ops, ops[0].reshape(rows_in, C_IN), conv_a, conv_b, SIDE, 2)

    def bwd_a_two(ops):
        conv_a, conv_b = weights_two()
        return bwd_a_double(ops, ops[2], conv_a, conv_b, OSIDE, 1)

    def bwd_a_one(ops):
        conv_a, conv_b = weights_one()
        centers, scales, grad_res = (ops[3], ops[4], ops[6])
        gain_vec, bias_vec = (ops[8], ops[9])
        pre_both = jnp.concatenate(
            [matmul(ops[1], conv_a), matmul(short_rows(ops[0]), conv_b)], axis=1
        )
        normed = (pre_both - centers) * scales
        activ = normed * gain_vec + bias_vec
        slope_in = grad_res.astype(jnp.float32) * smooth_slope(activ[:, :C_OUT] + activ[:, C_OUT:])
        both = jnp.concatenate([slope_in, slope_in], axis=1)
        return (
            pack(both),
            pack(normed),
            zero_scr,
            jnp.sum(both, axis=0),
            jnp.sum(both * normed, axis=0),
        )

    def bwd_a_three(ops):
        conv_a = flat_weights[: C_MID * C_OUT].reshape(C_MID, C_OUT)
        centers, scales = (ops[3], ops[4])
        gain_vec, bias_vec, gate_val = (ops[8], ops[9], ops[11])
        normed = (matmul(ops[1], conv_a) - centers[:C_OUT]) * scales[:C_OUT]
        joined = ops[2].astype(jnp.float32) + normed * gain_vec[:C_OUT] + bias_vec[:C_OUT]
        through = ops[7].astype(jnp.float32) * gate_val * smooth_slope(joined)
        return (
            pack(through),
            pack(normed),
            zero_scr,
            place(jnp.sum(through, axis=0), 0),
            place(jnp.sum(through * normed, axis=0), 0),
        )

    def bwd_b_double(args, conv_b, rows_first, side_len, stride, offset):
        ops, first_buf, second_buf, third_buf, sum_bias, sum_gain, acc = args
        scales = ops[4]
        gain_vec, bias_vec, mask_vec, valid = (ops[8], ops[9], ops[10], ops[12])
        slope_two = unpack(first_buf, rows_out, C_MID)
        norm_two = unpack(second_buf, rows_out, C_MID)
        norm_one = unpack(third_buf, rows_first, C_MID)
        grad_two = norm_grad(
            slope_two,
            norm_two,
            gain_vec[C_MID : 2 * C_MID],
            scales[C_MID : 2 * C_MID],
            sum_bias[C_MID : 2 * C_MID],
            sum_gain[C_MID : 2 * C_MID],
            total_out,
        )
        act_one = norm_one * gain_vec[:C_MID] + bias_vec[:C_MID]
        hidden_one = (smooth(act_one) * mask_vec).astype(jnp.bfloat16)
        columns = patches(hidden_one.reshape(IMG_B, side_len, side_len, C_MID), stride)
        acc = add_weight(acc, matmul_left_t(columns, grad_two), offset, valid)
        hid_grad = unpatch(
            matmul_right_t(grad_two, conv_b), IMG_B, side_len, stride, C_MID
        ).reshape(rows_first, C_MID)
        slope_one = hid_grad * mask_vec * smooth_slope(act_one)
        return (
            pack(slope_one),
            second_buf,
            third_buf,
            place(jnp.sum(slope_one, axis=0), 0),
            place(jnp.sum(slope_one * norm_one, axis=0), 0),
            acc,
        )

    def bwd_b_zero(args):
        conv_a, conv_b = weights_zero()
        return bwd_b_double(args, conv_b, rows_in, SIDE, 2, C_IN * C_MID)

    def bwd_b_two(args):
        conv_a, conv_b = weights_two()
        return bwd_b_double(args, conv_b, rows_out, OSIDE, 1, C_OUT * C_MID)

    def bwd_b_pass(args):
        return (args[1], args[2], args[3], zero_wide, zero_wide, args[6])

    def side_none():
        return zero_input

    def bwd_c_zero(args):
        ops, first_buf, second_buf, third_buf, sum_bias, sum_gain, acc = args
        conv_a, conv_b = weights_zero()
        scales, gain_vec, valid = (ops[4], ops[8], ops[12])
        flat_in = ops[0].reshape(rows_in, C_IN)
        slope_one = unpack(first_buf, rows_in, C_MID)
        norm_one = unpack(third_buf, rows_in, C_MID)
        grad_one = norm_grad(
            slope_one,
            norm_one,
            gain_vec[:C_MID],
            scales[:C_MID],
            sum_bias[:C_MID],
            sum_gain[:C_MID],
            total_in,
        )
        acc = add_weight(acc, matmul_left_t(flat_in, grad_one), 0, valid)
        side_out = matmul_right_t(grad_one, conv_a).reshape(IMG_B, PIX_IN, C_IN)
        return (zero_mid, zero_res, acc, side_out)

    def bwd_c_one(args):
        ops, first_buf, second_buf, third_buf, sum_bias, sum_gain, acc = args
        conv_a, conv_b = weights_one()
        scales, gain_vec, valid = (ops[4], ops[8], ops[12])
        short_in = short_rows(ops[0])
        both = unpack(first_buf, rows_out, wide)
        normed = unpack(second_buf, rows_out, wide)
        grad_both = norm_grad(both, normed, gain_vec, scales, sum_bias, sum_gain, total_out)
        acc = add_weight(acc, matmul_left_t(ops[1], grad_both[:, :C_OUT]), 0, valid)
        acc = add_weight(acc, matmul_left_t(short_in, grad_both[:, C_OUT:]), C_MID * C_OUT, valid)
        mid_grad = matmul_right_t(grad_both[:, :C_OUT], conv_a).astype(jnp.bfloat16)
        short_grad = matmul_right_t(grad_both[:, C_OUT:], conv_b).reshape(
            IMG_B, OSIDE, 1, OSIDE, 1, C_IN
        )
        side_out = jnp.pad(short_grad, ((0, 0), (0, 0), (0, 1), (0, 0), (0, 1), (0, 0))).reshape(
            IMG_B, PIX_IN, C_IN
        )
        return (mid_grad, zero_res, acc, side_out)

    def bwd_c_two(args):
        ops, first_buf, second_buf, third_buf, sum_bias, sum_gain, acc = args
        conv_a, conv_b = weights_two()
        scales, grad_res, gain_vec, valid = (ops[4], ops[6], ops[8], ops[12])
        slope_four = unpack(first_buf, rows_out, C_MID)
        norm_four = unpack(third_buf, rows_out, C_MID)
        grad_four = norm_grad(
            slope_four,
            norm_four,
            gain_vec[:C_MID],
            scales[:C_MID],
            sum_bias[:C_MID],
            sum_gain[:C_MID],
            total_out,
        )
        acc = add_weight(acc, matmul_left_t(ops[2], grad_four), 0, valid)
        carried_grad = (grad_res.astype(jnp.float32) + matmul_right_t(grad_four, conv_a)).astype(
            jnp.bfloat16
        )
        return (zero_mid, carried_grad, acc, side_none())

    def bwd_c_three(args):
        ops, first_buf, second_buf, third_buf, sum_bias, sum_gain, acc = args
        conv_a = flat_weights[: C_MID * C_OUT].reshape(C_MID, C_OUT)
        scales, gain_vec, gate_val, valid = (ops[4], ops[8], ops[11], ops[12])
        through = unpack(first_buf, rows_out, C_OUT)
        normed = unpack(second_buf, rows_out, C_OUT)
        res_grad = (through + (1.0 - gate_val) * ops[7].astype(jnp.float32)).astype(jnp.bfloat16)
        grad_six = norm_grad(
            through,
            normed,
            gain_vec[:C_OUT],
            scales[:C_OUT],
            sum_bias[:C_OUT],
            sum_gain[:C_OUT],
            total_out,
        )
        acc = add_weight(acc, matmul_left_t(ops[1], grad_six), 0, valid)
        mid_grad = matmul_right_t(grad_six, conv_a).astype(jnp.bfloat16)
        return (mid_grad, res_grad, acc, side_none())

    def select_params(micro_idx):
        block_id = section_idx // 2
        width_val = width[micro_idx, block_id]
        set_val = bn_set[micro_idx, block_id]
        onehot = (jnp.arange(NSETS) == set_val).astype(jnp.float32)
        gain_vec = jnp.sum(onehot[:, None] * gain_table, axis=0)
        bias_vec = jnp.sum(onehot[:, None] * bias_table, axis=0)
        mask_vec = (jnp.arange(C_MID) < width_val).astype(jnp.float32)
        gate_val = gate[micro_idx].astype(jnp.float32)
        return (gain_vec, bias_vec, mask_vec, gate_val, onehot)

    fwd_first = [fwd_a_zero, fwd_a_one, fwd_a_two, fwd_a_three]
    fwd_second = [fwd_b_zero, fwd_b_pass, fwd_b_two, fwd_b_pass]
    fwd_third = [fwd_c_zero, fwd_c_one, fwd_c_two, fwd_c_three]
    bwd_first = [bwd_a_zero, bwd_a_one, bwd_a_two, bwd_a_three]
    bwd_second = [bwd_b_zero, bwd_b_pass, bwd_b_two, bwd_b_pass]
    bwd_third = [bwd_c_zero, bwd_c_one, bwd_c_two, bwd_c_three]

    def forward_tick(tick_no, state_in):
        recv_mid, recv_res, stash_mid, stash_res, stash_center, stash_scale, out_rows = state_in
        micro_raw = tick_no - section_idx
        is_valid = (micro_raw >= 0) & (micro_raw < MB)
        micro_idx = jnp.clip(micro_raw, 0, MB - 1)
        gain_vec, bias_vec, mask_vec, gate_val, onehot = select_params(micro_idx)
        ops = (image_blocks[micro_idx], recv_mid, recv_res, gain_vec, bias_vec, mask_vec, gate_val)
        scratch, sums_local, squares_local = lax.switch(section_idx, fwd_first, ops)
        sum_first, square_first = group_moments(sums_local, squares_local)
        scratch, sums_local, squares_local = lax.switch(
            section_idx, fwd_second, (ops, scratch, sum_first, square_first)
        )
        sum_second, square_second = group_moments(sums_local, squares_local)
        send_mid, send_res, centers, scales, result = lax.switch(
            section_idx,
            fwd_third,
            (ops, scratch, sum_first + sum_second, square_first + square_second),
        )
        stash_mid = stash_mid.at[micro_idx].set(jnp.where(is_valid, recv_mid, stash_mid[micro_idx]))
        stash_res = stash_res.at[micro_idx].set(jnp.where(is_valid, recv_res, stash_res[micro_idx]))
        stash_center = stash_center.at[micro_idx].set(
            jnp.where(is_valid, centers, stash_center[micro_idx])
        )
        stash_scale = stash_scale.at[micro_idx].set(
            jnp.where(is_valid, scales, stash_scale[micro_idx])
        )
        out_rows = out_rows.at[micro_idx].set(jnp.where(is_valid, result, out_rows[micro_idx]))
        recv_mid, recv_res = (
            shifted(for_sending(send_mid), "pipe", 1).astype(send_mid.dtype),
            shifted(for_sending(send_res), "pipe", 1).astype(send_res.dtype),
        )
        return (recv_mid, recv_res, stash_mid, stash_res, stash_center, stash_scale, out_rows)

    forward_init = (
        zero_mid,
        zero_res,
        jnp.zeros((MB, rows_out, C_MID), jnp.bfloat16),
        jnp.zeros((MB, rows_out, C_OUT), jnp.bfloat16),
        jnp.zeros((MB, wide), jnp.float32),
        jnp.zeros((MB, wide), jnp.float32),
        jnp.zeros((MB, rows_out, C_OUT), jnp.float32),
    )
    forward_state = lax.fori_loop(0, MB + pipe_count - 1, forward_tick, forward_init)
    unused_mid, unused_res, stash_mid, stash_res, stash_center, stash_scale, out_rows = (
        forward_state
    )

    def backward_tick(tick_no, state_in):
        grad_mid, grad_res, weight_acc, gain_acc, bias_acc, input_acc = state_in
        micro_raw = tick_no - (pipe_count - 1 - section_idx)
        is_valid = (micro_raw >= 0) & (micro_raw < MB)
        micro_idx = jnp.clip(micro_raw, 0, MB - 1)
        gain_vec, bias_vec, mask_vec, gate_val, onehot = select_params(micro_idx)
        ops = (
            image_blocks[micro_idx],
            stash_mid[micro_idx],
            stash_res[micro_idx],
            stash_center[micro_idx],
            stash_scale[micro_idx],
            grad_mid,
            grad_res,
            cotangent[micro_idx],
            gain_vec,
            bias_vec,
            mask_vec,
            gate_val,
            is_valid,
        )
        first_buf, second_buf, third_buf, bias_one, gain_one = lax.switch(
            section_idx, bwd_first, ops
        )
        sum_bias_one, sum_gain_one = group_grad_sums(bias_one, gain_one)
        first_buf, second_buf, third_buf, bias_two, gain_two, weight_acc = lax.switch(
            section_idx,
            bwd_second,
            (ops, first_buf, second_buf, third_buf, sum_bias_one, sum_gain_one, weight_acc),
        )
        sum_bias_two, sum_gain_two = group_grad_sums(bias_two, gain_two)
        send_mid, send_res, weight_acc, side_out = lax.switch(
            section_idx,
            bwd_third,
            (
                ops,
                first_buf,
                second_buf,
                third_buf,
                sum_bias_one + sum_bias_two,
                sum_gain_one + sum_gain_two,
                weight_acc,
            ),
        )
        gain_grad = gain_one + gain_two
        bias_grad = bias_one + bias_two
        gain_acc = jnp.where(is_valid, gain_acc + onehot[:, None] * gain_grad[None, :], gain_acc)
        bias_acc = jnp.where(is_valid, bias_acc + onehot[:, None] * bias_grad[None, :], bias_acc)
        input_acc = jax.tree.map(
            lambda stored, fresh: stored.at[micro_idx].set(
                jnp.where(is_valid, fresh, stored[micro_idx])
            ),
            input_acc,
            side_out,
        )
        grad_mid, grad_res = (
            shifted(for_sending(send_mid), "pipe", -1).astype(send_mid.dtype),
            shifted(for_sending(send_res), "pipe", -1).astype(send_res.dtype),
        )
        return (grad_mid, grad_res, weight_acc, gain_acc, bias_acc, input_acc)

    side_init = jnp.zeros((MB, IMG_B, PIX_IN, C_IN), jnp.float32)
    backward_init = (
        zero_mid,
        zero_res,
        jnp.zeros((P_SIZE,), jnp.float32),
        jnp.zeros((NSETS, wide), jnp.float32),
        jnp.zeros((NSETS, wide), jnp.float32),
        side_init,
    )
    backward_state = lax.fori_loop(0, MB + pipe_count - 1, backward_tick, backward_init)
    unused_gmid, unused_gres, weight_acc, gain_acc, bias_acc, input_acc = backward_state
    grad_images, output_sum = (
        lax.psum_scatter(
            input_acc.reshape(IMG_DEV, PIX_IN, C_IN).astype(jnp.bfloat16),
            "pipe",
            scatter_dimension=2,
            tiled=True,
        ).astype(jnp.float32),
        lax.psum_scatter(
            out_rows.astype(jnp.bfloat16), "pipe", scatter_dimension=2, tiled=True
        ).astype(jnp.float32),
    )
    output_part = output_sum.astype(jnp.bfloat16)
    norm_grads = jnp.concatenate([gain_acc.reshape(-1), bias_acc.reshape(-1)])
    weight_sum, norm_sum = lax.psum((weight_acc, norm_grads), ("dp", "rep"))
    grad_gain = norm_sum[: NSETS * wide].reshape(1, NSETS, wide)
    grad_bias = norm_sum[NSETS * wide :].reshape(1, NSETS, wide)
    return (output_part, grad_images, weight_sum.reshape(1, P_SIZE), grad_gain, grad_bias)


PP = PIX_OUT + 1
RW = 8 * PP
RV = 8 * PIX_OUT
BLK = 512
SUB = 65536
F32 = jnp.float32
BF16 = jnp.bfloat16
MESH = pl.DeviceIdType.MESH

C_H2, C_O1, C_H4, C_H5, C_Z6, C_D5, C_D4, C_DH = range(8, 16)
C_SHARE, C_GI, C_GP = 16, 19, 22
C_WIN, C_WPEER, C_WZ, C_WFWD = 25, 30, 35, 40
C_PAR2, C_PAR3, C_DG2, C_DG3 = 45, 46, 47, 48
N_SEM = 49
PIECES = ((0, 512), (2048, 384), (3584, 384), (5120, 384), (6656, 512))


def nn(a, b):
    return jnp.dot(a, b, preferred_element_type=F32)


def nt(a, b):
    return lax.dot_general(a, b, (((1,), (1,)), ((), ())), preferred_element_type=F32)


def tn(a, b):
    return lax.dot_general(a, b, (((0,), (0,)), ((), ())), preferred_element_type=F32)


def rows(start, size):
    return pl.ds(pl.multiple_of(start, 16), size)


def whole_kernel(
    img, wts, gain, bias, meta, cot,
    out, gi, dw, dgb,
    imgb, raw, st, wh, wx, f0, f1, f2, f3, fs, pb, pt, u0, u1, u2, u3, sx, cotb,
    h2, h4, h5, d5, d4, dh, r0, r1, ob, tx, rx, inv, par, parx, dg, dgx, sb, ls, ss, rs,
):
    p, d, r = lax.axis_index("pipe"), lax.axis_index("dp"), lax.axis_index("rep")
    peer = (p, 1 - d, r)
    z_pair = r + 1 - 2 * lax.rem(r, 2)
    quarter = 2 * lax.rem(r, 2) + d

    def remote(src, dst, send, recv, device):
        return pltpu.make_async_remote_copy(
            src_ref=src, dst_ref=dst, send_sem=ss.at[send], recv_sem=rs.at[recv],
            device_id=device, device_id_type=MESH,
        )

    def sync(event, first, count):
        part = pl.ds(first, count)
        copy = remote(tx.at[part], rx.at[part], event, event, peer)
        copy.start()
        copy.wait()

    def both(slot):
        return tx[slot] + rx[slot]

    def moments(slot_sum, slot_square, total, inv_slot):
        center = both(slot_sum) * (1.0 / total)
        scale = lax.rsqrt(both(slot_square) * (1.0 / total) - center * center + EPSILON)
        inv[inv_slot] = scale
        return center, scale

    def silu(v):
        return v * jax.nn.sigmoid(v)

    def slope(v):
        s = jax.nn.sigmoid(v)
        return s * (1.0 + v * (1.0 - s))

    def clear_pad(ref, first):
        tile = ref[rows(first + RW - 16, 16), :].astype(F32)
        keep = lax.broadcasted_iota(jnp.int32, tile.shape, 0) < 8
        ref[rows(first + RW - 16, 16), :] = jnp.where(keep, tile, 0.0).astype(BF16)

    def mask_of(column):
        lane = lax.broadcasted_iota(jnp.int32, (8, BLK), 1).astype(F32)
        return (lane < meta[:, column : column + 1]).astype(F32)

    def five(body, init=0):
        return lax.fori_loop(0, 5, lambda c, carry: body(pl.ds(c * 10, 10), c, carry), init)

    def add_stats(carry, a, b):
        return carry[0] + jnp.sum(a, axis=0), carry[1] + jnp.sum(b, axis=0)

    zero_stats = (jnp.zeros((8, BLK), F32), jnp.zeros((8, BLK), F32))

    def store_z(ref, first, z, slot_sum, slot_square):
        z3 = z.reshape(PP, 8, BLK)
        ref[pl.ds(first, PP)] = z3
        tx[slot_sum] = jnp.sum(z3, axis=0)
        tx[slot_square] = jnp.sum(z3 * z3, axis=0)

    def raw_copy(slot, element):
        return pltpu.make_async_copy(
            wts.at[:, pl.ds(pl.multiple_of(element, SUB), SUB)], raw.at[slot], ls.at[2 + slot]
        )

    def load_weights(count, element_of, put):
        raw_copy(0, element_of(0)).start()

        def body(i, carry):
            slot = lax.rem(i, 2)

            @pl.when(i + 1 < count)
            def _():
                raw_copy(1 - slot, element_of(i + 1)).start()

            raw_copy(slot, element_of(i)).wait()
            st[0:512] = raw[slot].astype(F32).reshape(512, 128)
            put(i)
            return carry

        lax.fori_loop(0, count, body, 0)

    def put_narrow(ref, row_of):
        def put(i):
            for j in range(4):
                ref[rows(row_of(i), 128), j * 128 : (j + 1) * 128] = st[
                    pl.ds(j, 128, stride=4), :
                ].astype(BF16)

        return put

    def put_wide(ref, base, block_rows):
        def put(i):
            for n in range(4):
                for j in range(4):
                    ref[rows(base + n * block_rows + i * 32, 32), j * 128 : (j + 1) * 128] = st[
                        pl.ds(4 * n + j, 32, stride=16), :
                    ].astype(BF16)

        return put

    def img_copy(q, slot):
        return pltpu.make_async_copy(img.at[pl.ds(q * 28, 28)], imgb.at[slot], ls.at[slot])

    def over_images(body, init):
        img_copy(0, 0).start()

        def step(q, carry):
            slot = lax.rem(q, 2)

            @pl.when(q + 1 < 7)
            def _():
                img_copy(q + 1, 1 - slot).start()

            img_copy(q, slot).wait()
            return body(q, slot, carry)

        return lax.fori_loop(0, 7, step, init)

    def dw_copy(slot, chunk):
        return pltpu.make_async_copy(
            sb.at[slot], dw.at[pl.ds(pl.multiple_of(chunk * 2048, 2048), 2048)], ls.at[4 + slot]
        )

    def emit(turn, chunk):
        slot = lax.rem(turn, 2)

        @pl.when(turn >= 2)
        def _():
            dw_copy(slot, chunk).wait()

        sb[slot] = st[...].astype(BF16)
        dw_copy(slot, chunk).start()

    def stage_narrow(block):
        for j in range(4):
            st[pl.ds(j, 512, stride=4), :] = block[:, j * 128 : (j + 1) * 128]

    def stage_wide(n, block):
        for j in range(4):
            st[pl.ds(4 * n + j, 128, stride=16), :] = block[:, j * 128 : (j + 1) * 128]

    def emit_wide(turn, chunk, left, left_rows, left_cols, right):
        for n in range(4):
            stage_wide(n, tn(left[left_rows, left_cols], right[n * RW : (n + 1) * RW, :]))
        emit(turn, chunk)

    def emit_zeros(turn, first):
        st[...] = jnp.zeros_like(st)

        def body(i, carry):
            emit(turn + i, first + i)
            return carry

        lax.fori_loop(0, 13 - first, body, 0)
        dw_copy(0, 0).wait()
        dw_copy(1, 0).wait()

    barrier = pltpu.get_barrier_semaphore()
    for device in (peer, (p, d, z_pair)) + tuple((lax.rem(p + k, 4), d, r) for k in (1, 2, 3)):
        pl.semaphore_signal(barrier, inc=1, device_id=device, device_id_type=MESH)

    block_two = p >= 2
    set_col = jnp.where(block_two, meta[:, 3:4], meta[:, 2:3])
    for k in range(NSETS):
        hot = (set_col == float(k)).astype(F32)
        for n in range(8):
            g = hot * gain[k : k + 1, n * BLK : (n + 1) * BLK]
            b = hot * bias[k : k + 1, n * BLK : (n + 1) * BLK]
            if k == 0:
                par[n] = g
                par[8 + n] = b
            else:
                par[n] += g
                par[8 + n] += b
    dg[...] = jnp.zeros_like(dg)
    pl.semaphore_wait(barrier, 5)

    total_in, total_out = 2.0 * PIX_IN, 2.0 * PIX_OUT

    def build_patches(base):
        def body(tap, carry):
            row, col = base(tap)
            window = pb[pl.ds(row, 7), pl.ds(col, 7)].reshape(RV, BLK)
            pt[tap, 0:RV, :] = window.astype(BF16)
            return carry

        lax.fori_loop(0, 9, body, 0)

    def clear_patch_pad():
        def body(tap, carry):
            pt[tap, RW - 16 : RW, :] = jnp.zeros((16, BLK), BF16)
            return carry

        lax.fori_loop(0, 9, body, 0)

    def strided_base(tap):
        di, dj = tap // 3, lax.rem(tap, 3)
        return lax.rem(di, 2) * 8 + di // 2, lax.rem(dj, 2) * 8 + dj // 2

    def plain_base(tap):
        return tap // 3, lax.rem(tap, 3)

    def conv(ref, first, target):
        target[...] = jnp.zeros_like(target)

        def body(tap, carry):
            z = nn(pt[tap], ref[rows(first + tap * BLK, BLK), :])
            target[...] += z.reshape(PP, 8, BLK)
            return carry

        lax.fori_loop(0, 9, body, 0)

    def conv_back(dz, ref, first, base):
        pb[...] = jnp.zeros_like(pb)

        def body(tap, carry):
            row, col = base(tap)
            part = nt(dz[0:RV, :], ref[rows(first + tap * BLK, BLK), :])
            pb[pl.ds(row, 7), pl.ds(col, 7)] += part.reshape(7, 7, 8, BLK)
            return carry

        lax.fori_loop(0, 9, body, 0)

    def stats_of_map(ref, slot_sum, slot_square):
        def body(c, _, carry):
            z = ref[c]
            return add_stats(carry, z, z * z)

        tx[slot_sum], tx[slot_square] = five(body, zero_stats)

    def act_to(ref, target, center, scale, g, b, mask):
        def body(c, i, carry):
            zhat = (ref[c] - center) * scale
            ref[c] = zhat
            h = silu(zhat * g + b) * mask
            target[rows(i * 80, 80), :] = h.reshape(80, BLK).astype(BF16)
            return carry

        five(body)
        clear_pad(target, 0)

    def upstream(target, grad, zhat_ref, g, b, mask, slot_sum, slot_gain):
        def body(c, i, carry):
            zhat = zhat_ref[c]
            du = grad[rows(i * 80, 80), :].astype(F32).reshape(10, 8, BLK) * mask * slope(zhat * g + b)
            target[c] = du
            return add_stats(carry, du, du * zhat)

        tx[slot_sum], tx[slot_gain] = five(body, zero_stats)

    def norm_back(target, first, du_ref, du_first, zhat_ref, zhat_first, gscale, mean_du, mean_dg):
        def body(c, i, carry):
            du = du_ref[pl.ds(du_first + i * 10, 10)]
            zhat = zhat_ref[pl.ds(zhat_first + i * 10, 10)]
            dz = gscale * (du - mean_du - zhat * mean_dg)
            target[rows(first + i * 80, 80), :] = dz.reshape(80, BLK).astype(BF16)
            return carry

        five(body)
        clear_pad(target, first)

    @pl.when(p == 0)
    def _():
        mask = mask_of(0)
        load_weights(8, lambda i: i * SUB, put_narrow(wh, lambda i: i * 128))

        def first_conv(q, slot, carry):
            rows_q = imgb[slot].astype(F32).reshape(224, 1024).astype(BF16)
            wx[rows(q * 224, 224), :] = rows_q[:, 0:512]
            wx[rows(1568 + q * 224, 224), :] = rows_q[:, 512:1024]
            z = nn(rows_q, wh[0:1024, :]).reshape(28, 8, BLK)
            f0[pl.ds(q * 28, 28)] = z
            return add_stats(carry, z, z * z)

        tx[0], tx[1] = over_images(first_conv, zero_stats)
        exchange = remote(tx.at[pl.ds(0, 2)], rx.at[pl.ds(0, 2)], 0, 0, peer)
        exchange.start()
        pb[...] = jnp.zeros_like(pb)
        clear_patch_pad()
        load_weights(36, lambda i: (8 + i) * SUB, put_narrow(wh, lambda i: 1024 + i * 128))
        exchange.wait()

        center, scale = moments(0, 1, total_in, 0)
        g1, b1, g2, b2 = par[0], par[8], par[1], par[9]

        def hidden(i, carry):
            zhat = (f0[pl.ds(i * 14, 14)] - center) * scale
            f0[pl.ds(i * 14, 14)] = zhat
            h = (silu(zhat * g1 + b1) * mask).astype(BF16).astype(F32).reshape(7, 2, 8, BLK)
            u = i + 1
            row = lax.rem(u, 2) * 8 + u // 2
            pb[row, 8:15] = h[:, 0]
            pb[row, 1:8] = h[:, 1]
            return carry

        lax.fori_loop(0, 14, hidden, 0)
        build_patches(strided_base)
        conv(wh, 1024, fs.at[0])
        stats_of_map(fs.at[0], 2, 3)
        sync(1, 2, 2)
        center, scale = moments(2, 3, total_out, 1)
        act_to(fs.at[0], h2, center, scale, g2, b2, mask)
        send = remote(h2, h2, C_H2, C_H2, (1, d, r))
        send.start()
        send.wait_send()

        remote(dh, dh, C_DH, C_DH, (0, d, r)).wait_recv()
        upstream(fs.at[1], dh, fs.at[0], g2, b2, mask, 4, 5)
        sync(2, 4, 2)
        s_du, s_dg = both(4), both(5)
        dg[1], dg[9] = s_dg, s_du
        norm_back(d5, 0, fs.at[1], 0, fs.at[0], 0, g2 * inv[1], s_du * (1.0 / total_out), s_dg * (1.0 / total_out))
        conv_back(d5, wh, 1024, strided_base)

        def slopes(i, carry):
            u = i + 1
            row = lax.rem(u, 2) * 8 + u // 2
            grad = jnp.stack([pb[row, 8:15], pb[row, 1:8]], axis=1).reshape(14, 8, BLK)
            zhat = f0[pl.ds(i * 14, 14)]
            du = grad * mask * slope(zhat * g1 + b1)
            f1[pl.ds(i * 14, 14)] = du
            return add_stats(carry, du, du * zhat)

        tx[6], tx[7] = lax.fori_loop(0, 14, slopes, zero_stats)
        sync(3, 6, 2)
        s_du, s_dg = both(6), both(7)
        dg[0], dg[8] = s_dg, s_du
        gscale, m_du, m_dg = g1 * inv[0], s_du * (1.0 / total_in), s_dg * (1.0 / total_in)

        def first_back(q, carry):
            part = pl.ds(q * 28, 28)
            dz = gscale * (f1[part] - m_du - f0[part] * m_dg)
            u1[rows(q * 224, 224), :] = dz.reshape(224, BLK).astype(BF16)
            return carry

        lax.fori_loop(0, 7, first_back, 0)

        def share(target, column, k):
            def body(q, carry):
                g = nt(u1[rows(q * 224, 224), :], wh[k * 256 : (k + 1) * 256, :])
                target[rows(q * 224, 224), column : column + 256] = g.astype(BF16)
                return carry

            lax.fori_loop(0, 7, body, 0)

        sends = []
        for k, (target, column) in enumerate(((u0, 0), (u0, 256), (u2, 0)), 1):
            share(target, column, k)
            send = remote(target.at[0:1568, column : column + 256], r0, C_GI + k - 1, C_GI, (k, d, r))
            send.start()
            sends.append(send)
        share(r0, 0, 0)

        def second_weights(tap, carry):
            stage_narrow(tn(pt[tap], d5[...]))
            emit(tap, tap + 2)
            return carry

        lax.fori_loop(0, 9, second_weights, 0)

        def first_weights(k, carry):
            stage_narrow(tn(wx[rows(k * 1568, 1568), :], u1[0:1568, :]))
            emit(9 + k, k)
            return carry

        lax.fori_loop(0, 2, first_weights, 0)
        emit_zeros(11, 11)
        for send in sends:
            send.wait_send()

    @pl.when(p == 1)
    def _():
        mask = mask_of(1)
        gate_col = meta[:, 4:5]
        cot_copy = pltpu.make_async_copy(cot, cotb.at[0:PIX_OUT], ls.at[6])
        cot_copy.start()
        cotb[PIX_OUT] = jnp.zeros((8, C_OUT), BF16)
        clear_patch_pad()
        load_weights(32, lambda i: (16 + i) * SUB, put_wide(wh, 2048, 1024))

        def shorten(a, slot, carry):
            v = imgb[slot, 0:14].astype(F32).reshape(7, 2, 8, 1024)[:, 0]
            f0[pl.ds(a * 7, 7)] = v[:, :, 0:512]
            f0[pl.ds(PP + a * 7, 7)] = v[:, :, 512:1024]
            return carry

        over_images(shorten, 0)
        f0[PIX_OUT] = jnp.zeros((8, BLK), F32)
        f0[PP + PIX_OUT] = jnp.zeros((8, BLK), F32)
        sx[...] = f0[0 : 2 * PP].reshape(2 * RW, BLK).astype(BF16)

        def shortcut(n, carry):
            z = nn(sx[0:RW, :], wh[rows(2048 + n * 1024, 512), :]) + nn(
                sx[RW : 2 * RW, :], wh[rows(2560 + n * 1024, 512), :]
            )
            store_z(f1, n * PP, z, 8 + n, 12 + n)
            return carry

        lax.fori_loop(0, 4, shortcut, 0)
        load_weights(16, lambda i: i * SUB, put_wide(wh, 0, 512))

        sends = []

        def piece(i, q):
            first, size = PIECES[i]
            return wx.at[rows(first + q * size, size)]

        other_z = 2 * (1 - lax.rem(r, 2))

        def pass_own(i):
            mine = piece(i, quarter)
            remote(mine, mine, C_WIN + i, C_WIN + i, (1, d, r)).wait_recv()
            for base, device in ((C_WPEER, peer), (C_WZ, (p, d, z_pair))):
                copy = remote(mine, mine, base + i, base + i, device)
                copy.start()
                sends.append(copy)

        def pass_on(i):
            theirs = piece(i, other_z + d)
            remote(theirs, theirs, C_WZ + i, C_WZ + i, peer).wait_recv()
            copy = remote(theirs, theirs, C_WFWD + i, C_WFWD + i, peer)
            copy.start()
            sends.append(copy)

        def have(i):
            a = piece(i, 2 * lax.rem(r, 2) + 1 - d)
            b = piece(i, other_z + 1 - d)
            remote(a, a, C_WPEER + i, C_WPEER + i, peer).wait_recv()
            remote(b, b, C_WFWD + i, C_WFWD + i, peer).wait_recv()

        pass_own(0)
        remote(h2, h2, C_H2, C_H2, (1, d, r)).wait_recv()

        def third_conv(n, carry):
            store_z(f0, n * PP, nn(h2[...], wh[rows(n * 512, 512), :]), n, 4 + n)
            return carry

        lax.fori_loop(0, 4, third_conv, 0)
        sync(0, 0, 16)

        def join(n, carry):
            c3, s3 = moments(n, 4 + n, total_out, 2 + n)
            cp, sp = moments(8 + n, 12 + n, total_out, 6 + n)
            g3, gp, b = par[n], par[4 + n], par[8 + n] + par[12 + n]

            def body(_, i, carry):
                part = pl.ds(n * PP + i * 10, 10)
                a = (f0[part] - c3) * s3
                b_ = (f1[part] - cp) * sp
                f0[part] = a
                f1[part] = b_
                o = silu(a * g3 + b_ * gp + b)
                u0[rows(n * RW + i * 80, 80), :] = o.reshape(80, BLK).astype(BF16)
                return carry

            five(body)
            clear_pad(u0, n * RW)
            return carry

        lax.fori_loop(0, 4, join, 0)
        copy = remote(u0, u0, C_O1, C_O1, (2, d, r))
        copy.start()
        sends.append(copy)
        pass_on(0)
        have(0)

        zhat4, zhat5 = fs.at[0], fs.at[1]
        z = nn(u0[0:RW, :], wx[0:512, :])
        for n in range(1, 4):
            z += nn(u0[n * RW : (n + 1) * RW, :], wx[n * 512 : (n + 1) * 512, :])
        store_z(zhat4, 0, z, 16, 17)
        sync(1, 16, 2)
        remote(parx.at[0:4], parx.at[0:4], C_PAR2, C_PAR2, (1, d, r)).wait_recv()
        center, scale = moments(16, 17, total_out, 10)
        g4, g5, b4, b5 = parx[0], parx[1], parx[2], parx[3]
        pb[...] = jnp.zeros_like(pb)

        def hidden(a, carry):
            part = pl.ds(a * 7, 7)
            zhat = (zhat4[part] - center) * scale
            zhat4[part] = zhat
            h = silu(zhat * g4 + b4) * mask
            pb[a + 1, 1:8] = h.astype(BF16).astype(F32)
            return carry

        lax.fori_loop(0, 7, hidden, 0)
        h4[0:RV, :] = pb[1:8, 1:8].reshape(RV, BLK).astype(BF16)
        copy = remote(h4, h4, C_H4, C_H4, (2, d, r))
        copy.start()
        sends.append(copy)
        build_patches(plain_base)
        pass_own(1)
        pass_own(2)
        pass_on(1)
        pass_own(3)
        pass_on(2)
        pass_on(3)
        pass_own(4)
        for i in (1, 2, 3):
            have(i)
        conv(wx, 2048, zhat5)
        stats_of_map(zhat5, 18, 19)
        sync(2, 18, 2)
        center, scale = moments(18, 19, total_out, 11)
        act_to(zhat5, h5, center, scale, g5, b5, mask)
        copy = remote(h5, h5, C_H5, C_H5, (3, d, r))
        copy.start()
        sends.append(copy)
        pass_on(4)
        have(4)

        def sixth_conv(n, carry):
            store_z(f2, n * PP, nn(h5[...], wx[rows(6656 + n * 512, 512), :]), 20 + n, 24 + n)
            return carry

        lax.fori_loop(0, 4, sixth_conv, 0)
        sync(3, 20, 8)
        remote(parx.at[4:12], parx.at[4:12], C_PAR3, C_PAR3, (1, d, r)).wait_recv()
        cot_copy.wait()

        def finish(n, carry):
            center, scale = moments(20 + n, 24 + n, total_out, 12 + n)
            g6, b6 = parx[4 + n], parx[8 + n]
            gate_v = jnp.broadcast_to(gate_col, (8, BLK))

            def body(c, i, carry):
                part = pl.ds(n * PP + i * 10, 10)
                part_rows = rows(n * RW + i * 80, 80)
                zhat = (f2[part] - center) * scale
                f2[part] = zhat
                o = u0[part_rows, :].astype(F32).reshape(10, 8, BLK)
                q = o + zhat * g6 + b6
                s = jax.nn.sigmoid(q)
                merged = gate_v * (q * s) + (1.0 - gate_v) * o
                u3[part_rows, :] = merged.reshape(80, BLK).astype(BF16)
                ct = cotb[c, :, pl.ds(pl.multiple_of(n * BLK, BLK), BLK)].astype(F32)
                dq = ct * gate_v * (s * (1.0 + q * (1.0 - s)))
                f3[part] = dq
                dres = dq + (1.0 - gate_v) * ct
                u2[part_rows, :] = dres.reshape(80, BLK).astype(BF16)
                return add_stats(carry, dq, dq * zhat)

            tx[28 + n], tx[32 + n] = five(body, zero_stats)
            return carry

        lax.fori_loop(0, 4, finish, 0)
        out_sends = []
        for slot, k in enumerate((0, 2, 3)):
            copy = remote(u3.at[k * RW : (k + 1) * RW], ob, C_SHARE + slot, C_SHARE, (k, d, r))
            copy.start()
            out_sends.append(copy)
        ob[...] = u3[RW : 2 * RW, :]

        sync(4, 28, 8)

        def sixth_back(n, carry):
            s_du, s_dg = both(28 + n), both(32 + n)
            dgx[4 + n] = s_dg
            dgx[8 + n] = s_du
            norm_back(u1, n * RW, f3, n * PP, f2, n * PP, parx[4 + n] * inv[12 + n], s_du * (1.0 / total_out), s_dg * (1.0 / total_out))
            return carry

        lax.fori_loop(0, 4, sixth_back, 0)
        z6_send = remote(u1, u1, C_Z6, C_Z6, (3, d, r))
        z6_send.start()
        grad = nt(u1[0:RW, :], wx[6656:7168, :])
        for n in range(1, 4):
            grad += nt(u1[n * RW : (n + 1) * RW, :], wx[6656 + n * 512 : 7168 + n * 512, :])
        dh[...] = grad.astype(BF16)

        upstream(f2, dh, zhat5, g5, b5, mask, 36, 37)
        sync(5, 36, 2)
        s_du, s_dg = both(36), both(37)
        dgx[1] = s_dg
        dgx[3] = s_du
        norm_back(d5, 0, f2, 0, zhat5, 0, g5 * inv[11], s_du * (1.0 / total_out), s_dg * (1.0 / total_out))
        copy = remote(d5, d5, C_D5, C_D5, (2, d, r))
        copy.start()
        sends.append(copy)
        conv_back(d5, wx, 2048, plain_base)

        def fourth_slopes(a, carry):
            part = pl.ds(a * 7, 7)
            zhat = zhat4[part]
            du = pb[a + 1, 1:8] * mask * slope(zhat * g4 + b4)
            f2[part] = du
            return add_stats(carry, du, du * zhat)

        tx[38], tx[39] = lax.fori_loop(0, 7, fourth_slopes, zero_stats)
        sync(6, 38, 2)
        s_du, s_dg = both(38), both(39)
        dgx[0] = s_dg
        dgx[2] = s_du
        norm_back(d4, 0, f2, 0, zhat4, 0, g4 * inv[10], s_du * (1.0 / total_out), s_dg * (1.0 / total_out))
        copy = remote(d4, d4, C_D4, C_D4, (2, d, r))
        copy.start()
        sends.append(copy)
        for first, last, sem, chip in ((0, 4, C_DG2, 2), (4, 12, C_DG3, 3)):
            copy = remote(dgx.at[first:last], dgx.at[first:last], sem, sem, (chip, d, r))
            copy.start()
            sends.append(copy)

        def first_block_slopes(n, carry):
            f3[pl.ds(n * PP, PP)] = nt(d4[...], wx[rows(n * 512, 512), :]).reshape(PP, 8, BLK)
            g3, gp, b = par[n], par[4 + n], par[8 + n] + par[12 + n]

            def body(_, i, carry):
                part = pl.ds(n * PP + i * 10, 10)
                do = u2[rows(n * RW + i * 80, 80), :].astype(F32).reshape(10, 8, BLK) + f3[part]
                a, b_ = f0[part], f1[part]
                dp = do.astype(BF16).astype(F32) * slope(a * g3 + b_ * gp + b)
                f3[part] = dp
                s0, s1, s2 = carry
                return s0 + jnp.sum(dp, axis=0), s1 + jnp.sum(dp * a, axis=0), s2 + jnp.sum(dp * b_, axis=0)

            tx[40 + n], tx[44 + n], tx[48 + n] = five(body, zero_stats + zero_stats[:1])
            return carry

        lax.fori_loop(0, 4, first_block_slopes, 0)
        z6_send.wait_send()
        for copy in out_sends:
            copy.wait_send()
        sync(7, 40, 12)

        def third_back(n, carry):
            s_du, s_d3, s_dp = both(40 + n), both(44 + n), both(48 + n)
            dg[n] = s_d3
            dg[4 + n] = s_dp
            dg[8 + n] = s_du
            dg[12 + n] = s_du
            m_du = s_du * (1.0 / total_out)
            norm_back(u1, n * RW, f3, n * PP, f0, n * PP, par[n] * inv[2 + n], m_du, s_d3 * (1.0 / total_out))
            norm_back(u3, n * RW, f3, n * PP, f1, n * PP, par[4 + n] * inv[6 + n], m_du, s_dp * (1.0 / total_out))
            return carry

        lax.fori_loop(0, 4, third_back, 0)
        grad = nt(u1[0:RW, :], wh[0:512, :])
        for n in range(1, 4):
            grad += nt(u1[n * RW : (n + 1) * RW, :], wh[n * 512 : (n + 1) * 512, :])
        dh[...] = grad.astype(BF16)
        copy = remote(dh, dh, C_DH, C_DH, (0, d, r))
        copy.start()
        sends.append(copy)

        def shortcut_share(k):
            g = nt(u3[0:RW, :], wh[2048 + k * 256 : 2304 + k * 256, :])
            for n in range(1, 4):
                g += nt(u3[n * RW : (n + 1) * RW, :], wh[2048 + n * 1024 + k * 256 : 2304 + n * 1024 + k * 256, :])
            return g.astype(BF16)

        for slot, k in enumerate((0, 2, 3)):
            u2[slot * RW : (slot + 1) * RW, 0:256] = shortcut_share(k)
            copy = remote(u2.at[slot * RW : (slot + 1) * RW, 0:256], r1, C_GP + slot, C_GP, (k, d, r))
            copy.start()
            sends.append(copy)
        r1[...] = shortcut_share(1)

        def third_weights(m, carry):
            emit_wide(m, m, h2, slice(None), pl.ds(pl.multiple_of(m * 128, 128), 128), u1)
            return carry

        lax.fori_loop(0, 4, third_weights, 0)

        def shortcut_weights(m, carry):
            emit_wide(4 + m, 4 + m, sx, rows((m // 4) * RW, RW), pl.ds(pl.multiple_of(lax.rem(m, 4) * 128, 128), 128), u3)
            return carry

        lax.fori_loop(0, 8, shortcut_weights, 0)
        emit_zeros(12, 12)
        for copy in sends:
            copy.wait_send()

    @pl.when(p == 2)
    def _():
        for k, slot in ((0, 0), (1, 1), (2, 8), (3, 9)):
            parx[k] = par[slot]
        sends = [remote(parx.at[0:4], parx.at[0:4], C_PAR2, C_PAR2, (1, d, r))]
        sends[0].start()
        load_weights(4, lambda i: (quarter * 4 + i) * SUB, put_narrow(wx, lambda i: quarter * 512 + i * 128))
        for i in range(4):
            first, size = PIECES[i]
            if i > 0:
                load_weights(
                    3,
                    lambda k, i=i: (16 + (i - 1) * 12 + quarter * 3 + k) * SUB,
                    put_narrow(wx, lambda k, first=first: first + quarter * 384 + k * 128),
                )
            part = wx.at[rows(first + quarter * size, size)]
            copy = remote(part, part, C_WIN + i, C_WIN + i, (1, d, r))
            copy.start()
            sends.append(copy)
        pb[...] = jnp.zeros_like(pb)
        clear_patch_pad()
        remote(h4, h4, C_H4, C_H4, (2, d, r)).wait_recv()
        pb[1:8, 1:8] = h4[0:RV, :].astype(F32).reshape(7, 7, 8, BLK)
        build_patches(plain_base)
        remote(d5, d5, C_D5, C_D5, (2, d, r)).wait_recv()

        def fifth_weights(tap, carry):
            stage_narrow(tn(pt[tap], d5[...]))
            emit(tap, tap + 4)
            return carry

        lax.fori_loop(0, 9, fifth_weights, 0)
        remote(u0, u0, C_O1, C_O1, (2, d, r)).wait_recv()
        remote(d4, d4, C_D4, C_D4, (2, d, r)).wait_recv()

        def fourth_weights(n, carry):
            stage_narrow(tn(u0[rows(n * RW, RW), :], d4[...]))
            emit(9 + n, n)
            return carry

        lax.fori_loop(0, 4, fourth_weights, 0)
        dw_copy(0, 0).wait()
        dw_copy(1, 0).wait()
        remote(dgx.at[0:4], dgx.at[0:4], C_DG2, C_DG2, (2, d, r)).wait_recv()
        dg[0], dg[1], dg[8], dg[9] = dgx[0], dgx[1], dgx[2], dgx[3]
        for copy in sends:
            copy.wait_send()

    @pl.when(p == 3)
    def _():
        for k in range(4):
            parx[4 + k] = par[k]
            parx[8 + k] = par[8 + k]
        sends = [remote(parx.at[4:12], parx.at[4:12], C_PAR3, C_PAR3, (1, d, r))]
        sends[0].start()

        def put(i):
            for j in range(4):
                wx[rows(6656 + quarter * 512 + i * 32, 32), j * 128 : (j + 1) * 128] = st[
                    pl.ds(4 * quarter + j, 32, stride=16), :
                ].astype(BF16)

        load_weights(16, lambda i: i * SUB, put)
        part = wx.at[rows(6656 + quarter * 512, 512)]
        copy = remote(part, part, C_WIN + 4, C_WIN + 4, (1, d, r))
        copy.start()
        sends.append(copy)
        remote(h5, h5, C_H5, C_H5, (3, d, r)).wait_recv()
        remote(u1, u1, C_Z6, C_Z6, (3, d, r)).wait_recv()

        def sixth_weights(m, carry):
            emit_wide(m, m, h5, slice(None), pl.ds(pl.multiple_of(m * 128, 128), 128), u1)
            return carry

        lax.fori_loop(0, 4, sixth_weights, 0)
        emit_zeros(4, 4)
        remote(dgx.at[4:12], dgx.at[4:12], C_DG3, C_DG3, (3, d, r)).wait_recv()
        for k in range(4):
            dg[k] = dgx[4 + k]
            dg[8 + k] = dgx[8 + k]
        for copy in sends:
            copy.wait_send()

    @pl.when(p != 1)
    def _():
        remote(ob, ob, C_SHARE, C_SHARE, (p, d, r)).wait_recv()
        remote(r1, r1, C_GP, C_GP, (p, d, r)).wait_recv()

    @pl.when(p != 0)
    def _():
        remote(r0, r0, C_GI, C_GI, (p, d, r)).wait_recv()

    out[...] = ob[0:RV, :].astype(F32).reshape(PIX_OUT, 8, BLK).astype(BF16)
    f0[0:PP, :, 0:256] = r1[...].astype(F32).reshape(PP, 8, 256)

    def place(a, carry):
        m = r0[rows(a * 224, 224), :].astype(F32).reshape(28, 8, 256)
        first = m[0:14].reshape(7, 2, 8, 256)
        even = first[:, 0] + f0[pl.ds(a * 7, 7), :, 0:256]
        f3[pl.ds(a * 28, 14), :, 0:256] = jnp.stack([even, first[:, 1]], axis=1).reshape(14, 8, 256)
        f3[pl.ds(a * 28 + 14, 14), :, 0:256] = m[14:28]
        return carry

    lax.fori_loop(0, 7, place, 0)
    gi_copy = pltpu.make_async_copy(f3.at[0:PIX_IN, :, 0:256], gi, ls.at[7])
    gi_copy.start()
    for k in range(NSETS):
        hot = (set_col == float(k)).astype(F32)
        for n in range(8):
            dgb[k : k + 1, n * BLK : (n + 1) * BLK] = jnp.sum(dg[n] * hot, axis=0, keepdims=True)
            dgb[4 + k : 5 + k, n * BLK : (n + 1) * BLK] = jnp.sum(dg[8 + n] * hot, axis=0, keepdims=True)
    gi_copy.wait()


def one_kernel(images, section_weights, bn_gain, bn_bias, width, bn_set, gate, cotangent):
    meta = jnp.concatenate(
        [width.astype(F32), bn_set.astype(F32), gate.astype(F32)[:, None], jnp.zeros((MB, 123), F32)], axis=1
    )
    any_space = pl.BlockSpec(memory_space=pl.ANY)
    vmem = pl.BlockSpec(memory_space=pltpu.VMEM)
    out, gi, dw, dgb = pl.pallas_call(
        whole_kernel,
        out_shape=(
            jax.ShapeDtypeStruct((PIX_OUT, 8, BLK), BF16),
            jax.ShapeDtypeStruct((PIX_IN, 8, 256), F32),
            jax.ShapeDtypeStruct((P_SIZE // 128, 128), BF16),
            jax.ShapeDtypeStruct((8, 4096), F32),
        ),
        in_specs=[any_space, any_space, vmem, vmem, vmem, any_space],
        out_specs=(vmem, any_space, any_space, vmem),
        scratch_shapes=[
            pltpu.VMEM((2, 28, 8, 1024), BF16),
            pltpu.VMEM((2, 1, SUB), BF16),
            pltpu.VMEM((2048, 128), F32),
            pltpu.VMEM((6144, BLK), BF16),
            pltpu.VMEM((8704, BLK), BF16),
            pltpu.VMEM((4 * PP, 8, BLK), F32),
            pltpu.VMEM((4 * PP, 8, BLK), F32),
            pltpu.VMEM((4 * PP, 8, BLK), F32),
            pltpu.VMEM((4 * PP, 8, BLK), F32),
            pltpu.VMEM((2, PP, 8, BLK), F32),
            pltpu.VMEM((16, 16, 8, BLK), F32),
            pltpu.VMEM((9, RW, BLK), BF16),
            pltpu.VMEM((4 * RW, BLK), BF16),
            pltpu.VMEM((4 * RW, BLK), BF16),
            pltpu.VMEM((4 * RW, BLK), BF16),
            pltpu.VMEM((4 * RW, BLK), BF16),
            pltpu.VMEM((2 * RW, BLK), BF16),
            pltpu.VMEM((PP, 8, C_OUT), BF16),
            pltpu.VMEM((RW, BLK), BF16),
            pltpu.VMEM((RW, BLK), BF16),
            pltpu.VMEM((RW, BLK), BF16),
            pltpu.VMEM((RW, BLK), BF16),
            pltpu.VMEM((RW, BLK), BF16),
            pltpu.VMEM((RW, BLK), BF16),
            pltpu.VMEM((8 * PIX_IN, 256), BF16),
            pltpu.VMEM((RW, 256), BF16),
            pltpu.VMEM((RW, BLK), BF16),
            pltpu.VMEM((52, 8, BLK), F32),
            pltpu.VMEM((52, 8, BLK), F32),
            pltpu.VMEM((16, 8, BLK), F32),
            pltpu.VMEM((16, 8, BLK), F32),
            pltpu.VMEM((12, 8, BLK), F32),
            pltpu.VMEM((16, 8, BLK), F32),
            pltpu.VMEM((12, 8, BLK), F32),
            pltpu.VMEM((2, 2048, 128), BF16),
            pltpu.SemaphoreType.DMA((8,)),
            pltpu.SemaphoreType.DMA((N_SEM,)),
            pltpu.SemaphoreType.DMA((N_SEM,)),
        ],
        compiler_params=pltpu.CompilerParams(
            collective_id=0, has_side_effects=True, vmem_limit_bytes=64 * 1024 * 1024
        ),
    )(
        jnp.transpose(images, (1, 0, 2)),
        section_weights,
        bn_gain[0],
        bn_bias[0],
        meta,
        jnp.transpose(cotangent, (1, 0, 2)),
    )
    dw = lax.psum(dw, ("dp", "rep")).astype(F32).reshape(1, P_SIZE)
    dgb = lax.psum(dgb, "rep")
    return (
        jnp.transpose(out, (1, 0, 2)),
        jnp.transpose(gi, (1, 0, 2)),
        dw,
        dgb[None, :4],
        dgb[None, 4:],
    )


def solution(mesh):
    sizes = dict(mesh.shape)
    fits = sizes["pipe"] == 4 and sizes["dp"] == 2 and sizes["rep"] % 2 == 0
    placed = (
        P(("dp", "rep"), None, None),
        P("pipe", None),
        P("pipe", None, None),
        P("pipe", None, None),
        P(),
        P(),
        P(),
        P(("dp", "rep"), None, None),
    )
    return jax.shard_map(
        one_kernel if fits else on_device,
        mesh=mesh,
        in_specs=placed,
        out_specs=(
            P(("dp", "rep"), None, "pipe"),
            P(("dp", "rep"), None, "pipe"),
            P("pipe", None),
            P("pipe", None, None),
            P("pipe", None, None),
        ),
        check_vma=False,
    )
```

```python
import jax
import jax.numpy as jnp
from jax import lax
from jax.experimental import pallas as pl
from jax.experimental.pallas import tpu as pltpu
from jax.sharding import PartitionSpec as P

C_IN = 1024
C_MID = 512
C_OUT = 2048
SIDE = 14
NSETS = 4
MB = 8
IMG_B = 1
OSIDE = 7
PIX_IN = 196
PIX_OUT = 49
IMG_DEV = 8
P_SIZE = 3407872


EPSILON = 1e-05


def for_sending(array):

    def short(part):
        return part.astype(jnp.bfloat16) if part.dtype == jnp.float32 else part

    return jax.tree.map(short, array)


def shifted(value, axis, steps):
    count = lax.axis_size(axis)
    first, last = (max(0, -steps), min(count, count - steps))
    return lax.ppermute(value, axis, [(source, source + steps) for source in range(first, last)])


def smooth(inputs):
    return inputs * jax.nn.sigmoid(inputs)


def smooth_slope(inputs):
    gate_sig = jax.nn.sigmoid(inputs)
    return gate_sig * (1.0 + inputs * (1.0 - gate_sig))


def matmul(left_op, right_op):
    return jnp.dot(left_op, right_op, preferred_element_type=jnp.float32)


def matmul_left_t(left_op, right_op):
    return lax.dot_general(
        left_op, right_op, (((0,), (0,)), ((), ())), preferred_element_type=jnp.float32
    )


def matmul_right_t(left_op, right_op):
    return lax.dot_general(
        left_op, right_op, (((1,), (1,)), ((), ())), preferred_element_type=jnp.float32
    )


def patches(planes, stride):
    images, side_len, channels = (planes.shape[0], planes.shape[1], planes.shape[3])
    out_side = side_len // stride
    padded = jnp.pad(planes, ((0, 0), (1, 1), (1, 1), (0, 0)))
    pieces = []
    for row_off in range(3):
        for col_off in range(3):
            pieces.append(
                padded[
                    :,
                    row_off : row_off + stride * (out_side - 1) + 1 : stride,
                    col_off : col_off + stride * (out_side - 1) + 1 : stride,
                    :,
                ]
            )
    return jnp.concatenate(pieces, axis=3).reshape(images * out_side * out_side, 9 * channels)


def unpatch(columns, images, side_len, stride, channels):
    out_side = side_len // stride
    pieces = columns.reshape(images, out_side, out_side, 9, channels)
    padded = jnp.zeros((images, side_len + 2, side_len + 2, channels), jnp.float32)
    for row_off in range(3):
        for col_off in range(3):
            padded = padded.at[
                :,
                row_off : row_off + stride * (out_side - 1) + 1 : stride,
                col_off : col_off + stride * (out_side - 1) + 1 : stride,
                :,
            ].add(pieces[:, :, :, row_off * 3 + col_off, :])
    return padded[:, 1 : side_len + 1, 1 : side_len + 1, :]


def group_moments(sums_local, squares_local):
    return (
        lax.psum(sums_local.astype(jnp.bfloat16), "dp").astype(jnp.float32),
        lax.psum(squares_local.astype(jnp.bfloat16), "dp").astype(jnp.float32),
    )


def group_grad_sums(bias_local, gain_local):
    return (
        lax.psum(bias_local.astype(jnp.bfloat16), "dp").astype(jnp.float32),
        lax.psum(gain_local.astype(jnp.bfloat16), "dp").astype(jnp.float32),
    )


def stats_of(sum_all, square_all, start, count, row_total):
    center = sum_all[start : start + count] / row_total
    inv_std = lax.rsqrt(square_all[start : start + count] / row_total - center * center + EPSILON)
    return (center, inv_std)


def norm_grad(slope_in, normed, gain_vec, inv_std, sum_bias, sum_gain, row_total):
    return (
        gain_vec * inv_std * (slope_in - sum_bias / row_total - normed * (sum_gain / row_total))
    ).astype(jnp.bfloat16)


def on_device(images, section_weights, bn_gain, bn_bias, width, bn_set, gate, cotangent):
    section_idx = lax.axis_index("pipe")
    pipe_count = lax.axis_size("pipe")
    dp_count = lax.axis_size("dp")
    flat_weights = section_weights[0]
    gain_table = bn_gain[0]
    bias_table = bn_bias[0]
    rows_in = IMG_B * PIX_IN
    rows_out = IMG_B * PIX_OUT
    total_in = float(rows_in * dp_count)
    total_out = float(rows_out * dp_count)
    wide = 2 * C_OUT
    scr_len = IMG_B * max(PIX_IN * C_MID, PIX_OUT * wide)
    image_blocks = images.reshape(MB, IMG_B, PIX_IN, C_IN)
    pad_mid = jnp.zeros((wide - 2 * C_MID,), jnp.float32)
    zero_wide = jnp.zeros((wide,), jnp.float32)
    zero_scr = jnp.zeros((scr_len,), jnp.float32)
    zero_mid = jnp.zeros((rows_out, C_MID), jnp.bfloat16)
    zero_res = jnp.zeros((rows_out, C_OUT), jnp.bfloat16)
    zero_rows = jnp.zeros((rows_out, C_OUT), jnp.float32)
    zero_input = jnp.zeros((IMG_B, PIX_IN, C_IN), jnp.float32)

    def pack(values):
        flat = values.reshape(-1).astype(jnp.float32)
        return jnp.pad(flat, (0, scr_len - flat.shape[0]))

    def unpack(buffer, rows, cols):
        return buffer[: rows * cols].reshape(rows, cols)

    def place(vec, start):
        return jnp.pad(vec, (start, wide - start - vec.shape[0]))

    def add_weight(acc, grad, offset, valid):
        flat = grad.reshape(-1)
        return acc.at[offset : offset + flat.shape[0]].add(jnp.where(valid, flat, 0.0))

    def weights_zero():
        split_at = C_IN * C_MID
        return (
            flat_weights[:split_at].reshape(C_IN, C_MID),
            flat_weights[split_at : split_at + 9 * C_MID * C_MID].reshape(9 * C_MID, C_MID),
        )

    def weights_one():
        split_at = C_MID * C_OUT
        return (
            flat_weights[:split_at].reshape(C_MID, C_OUT),
            flat_weights[split_at : split_at + C_IN * C_OUT].reshape(C_IN, C_OUT),
        )

    def weights_two():
        split_at = C_OUT * C_MID
        return (
            flat_weights[:split_at].reshape(C_OUT, C_MID),
            flat_weights[split_at : split_at + 9 * C_MID * C_MID].reshape(9 * C_MID, C_MID),
        )

    def short_rows(image_block):
        return image_block.reshape(IMG_B, SIDE, SIDE, C_IN)[:, ::2, ::2, :].reshape(rows_out, C_IN)

    def local_stats(values, start):
        return (
            place(jnp.sum(values, axis=0), start),
            place(jnp.sum(values * values, axis=0), start),
        )

    def fwd_a_zero(ops):
        conv_a, conv_b = weights_zero()
        pre_one = matmul(ops[0].reshape(rows_in, C_IN), conv_a)
        sums_local, squares_local = local_stats(pre_one, 0)
        return (pack(pre_one), sums_local, squares_local)

    def fwd_a_one(ops):
        conv_a, conv_b = weights_one()
        pre_both = jnp.concatenate(
            [matmul(ops[1], conv_a), matmul(short_rows(ops[0]), conv_b)], axis=1
        )
        sums_local, squares_local = local_stats(pre_both, 0)
        return (pack(pre_both), sums_local, squares_local)

    def fwd_a_two(ops):
        conv_a, conv_b = weights_two()
        pre_four = matmul(ops[2], conv_a)
        sums_local, squares_local = local_stats(pre_four, 0)
        return (pack(pre_four), sums_local, squares_local)

    def fwd_a_three(ops):
        conv_a = flat_weights[: C_MID * C_OUT].reshape(C_MID, C_OUT)
        pre_six = matmul(ops[1], conv_a)
        sums_local, squares_local = local_stats(pre_six, 0)
        return (pack(pre_six), sums_local, squares_local)

    def fwd_b_zero(args):
        ops, scratch, sum_all, square_all = args
        conv_a, conv_b = weights_zero()
        gain_vec, bias_vec, mask_vec = (ops[3], ops[4], ops[5])
        pre_one = unpack(scratch, rows_in, C_MID)
        center_one, inv_one = stats_of(sum_all, square_all, 0, C_MID, total_in)
        hidden_one = (
            smooth((pre_one - center_one) * inv_one * gain_vec[:C_MID] + bias_vec[:C_MID])
            * mask_vec
        ).astype(jnp.bfloat16)
        pre_two = matmul(patches(hidden_one.reshape(IMG_B, SIDE, SIDE, C_MID), 2), conv_b)
        sums_local, squares_local = local_stats(pre_two, C_MID)
        return (pack(pre_two), sums_local, squares_local)

    def fwd_b_pass(args):
        return (args[1], zero_wide, zero_wide)

    def fwd_b_two(args):
        ops, scratch, sum_all, square_all = args
        conv_a, conv_b = weights_two()
        gain_vec, bias_vec, mask_vec = (ops[3], ops[4], ops[5])
        pre_four = unpack(scratch, rows_out, C_MID)
        center_four, inv_four = stats_of(sum_all, square_all, 0, C_MID, total_out)
        hidden_four = (
            smooth((pre_four - center_four) * inv_four * gain_vec[:C_MID] + bias_vec[:C_MID])
            * mask_vec
        ).astype(jnp.bfloat16)
        pre_five = matmul(patches(hidden_four.reshape(IMG_B, OSIDE, OSIDE, C_MID), 1), conv_b)
        sums_local, squares_local = local_stats(pre_five, C_MID)
        return (pack(pre_five), sums_local, squares_local)

    def fwd_c_double(args, first_total, send_res):
        ops, scratch, sum_all, square_all = args
        gain_vec, bias_vec, mask_vec = (ops[3], ops[4], ops[5])
        pre_two = unpack(scratch, rows_out, C_MID)
        center_one, inv_one = stats_of(sum_all, square_all, 0, C_MID, first_total)
        center_two, inv_two = stats_of(sum_all, square_all, C_MID, C_MID, total_out)
        hidden_two = (
            smooth(
                (pre_two - center_two) * inv_two * gain_vec[C_MID : 2 * C_MID]
                + bias_vec[C_MID : 2 * C_MID]
            )
            * mask_vec
        ).astype(jnp.bfloat16)
        centers = jnp.concatenate([center_one, center_two, pad_mid])
        scales = jnp.concatenate([inv_one, inv_two, pad_mid])
        return (hidden_two, send_res, centers, scales, zero_rows)

    def fwd_c_zero(args):
        return fwd_c_double(args, total_in, zero_res)

    def fwd_c_two(args):
        return fwd_c_double(args, total_out, args[0][2])

    def fwd_c_one(args):
        ops, scratch, sum_all, square_all = args
        gain_vec, bias_vec = (ops[3], ops[4])
        pre_both = unpack(scratch, rows_out, wide)
        centers, scales = stats_of(sum_all, square_all, 0, wide, total_out)
        activ = (pre_both - centers) * scales * gain_vec + bias_vec
        block_out = smooth(activ[:, :C_OUT] + activ[:, C_OUT:]).astype(jnp.bfloat16)
        return (zero_mid, block_out, centers, scales, zero_rows)

    def fwd_c_three(args):
        ops, scratch, sum_all, square_all = args
        gain_vec, bias_vec, gate_val = (ops[3], ops[4], ops[6])
        pre_six = unpack(scratch, rows_out, C_OUT)
        centers, scales = stats_of(sum_all, square_all, 0, wide, total_out)
        residual = ops[2].astype(jnp.float32)
        merged = smooth(
            residual
            + (pre_six - centers[:C_OUT]) * scales[:C_OUT] * gain_vec[:C_OUT]
            + bias_vec[:C_OUT]
        )
        result = gate_val * merged + (1.0 - gate_val) * residual
        return (zero_mid, zero_res, centers, scales, result)

    def bwd_a_double(ops, flat_in, conv_a, conv_b, side_len, stride):
        centers, scales, grad_mid = (ops[3], ops[4], ops[5])
        gain_vec, bias_vec, mask_vec = (ops[8], ops[9], ops[10])
        norm_one = (matmul(flat_in, conv_a) - centers[:C_MID]) * scales[:C_MID]
        hidden_one = (smooth(norm_one * gain_vec[:C_MID] + bias_vec[:C_MID]) * mask_vec).astype(
            jnp.bfloat16
        )
        columns = patches(hidden_one.reshape(IMG_B, side_len, side_len, C_MID), stride)
        norm_two = (matmul(columns, conv_b) - centers[C_MID : 2 * C_MID]) * scales[
            C_MID : 2 * C_MID
        ]
        act_two = norm_two * gain_vec[C_MID : 2 * C_MID] + bias_vec[C_MID : 2 * C_MID]
        slope_two = grad_mid.astype(jnp.float32) * mask_vec * smooth_slope(act_two)
        return (
            pack(slope_two),
            pack(norm_two),
            pack(norm_one),
            place(jnp.sum(slope_two, axis=0), C_MID),
            place(jnp.sum(slope_two * norm_two, axis=0), C_MID),
        )

    def bwd_a_zero(ops):
        conv_a, conv_b = weights_zero()
        return bwd_a_double(ops, ops[0].reshape(rows_in, C_IN), conv_a, conv_b, SIDE, 2)

    def bwd_a_two(ops):
        conv_a, conv_b = weights_two()
        return bwd_a_double(ops, ops[2], conv_a, conv_b, OSIDE, 1)

    def bwd_a_one(ops):
        conv_a, conv_b = weights_one()
        centers, scales, grad_res = (ops[3], ops[4], ops[6])
        gain_vec, bias_vec = (ops[8], ops[9])
        pre_both = jnp.concatenate(
            [matmul(ops[1], conv_a), matmul(short_rows(ops[0]), conv_b)], axis=1
        )
        normed = (pre_both - centers) * scales
        activ = normed * gain_vec + bias_vec
        slope_in = grad_res.astype(jnp.float32) * smooth_slope(activ[:, :C_OUT] + activ[:, C_OUT:])
        both = jnp.concatenate([slope_in, slope_in], axis=1)
        return (
            pack(both),
            pack(normed),
            zero_scr,
            jnp.sum(both, axis=0),
            jnp.sum(both * normed, axis=0),
        )

    def bwd_a_three(ops):
        conv_a = flat_weights[: C_MID * C_OUT].reshape(C_MID, C_OUT)
        centers, scales = (ops[3], ops[4])
        gain_vec, bias_vec, gate_val = (ops[8], ops[9], ops[11])
        normed = (matmul(ops[1], conv_a) - centers[:C_OUT]) * scales[:C_OUT]
        joined = ops[2].astype(jnp.float32) + normed * gain_vec[:C_OUT] + bias_vec[:C_OUT]
        through = ops[7].astype(jnp.float32) * gate_val * smooth_slope(joined)
        return (
            pack(through),
            pack(normed),
            zero_scr,
            place(jnp.sum(through, axis=0), 0),
            place(jnp.sum(through * normed, axis=0), 0),
        )

    def bwd_b_double(args, conv_b, rows_first, side_len, stride, offset):
        ops, first_buf, second_buf, third_buf, sum_bias, sum_gain, acc = args
        scales = ops[4]
        gain_vec, bias_vec, mask_vec, valid = (ops[8], ops[9], ops[10], ops[12])
        slope_two = unpack(first_buf, rows_out, C_MID)
        norm_two = unpack(second_buf, rows_out, C_MID)
        norm_one = unpack(third_buf, rows_first, C_MID)
        grad_two = norm_grad(
            slope_two,
            norm_two,
            gain_vec[C_MID : 2 * C_MID],
            scales[C_MID : 2 * C_MID],
            sum_bias[C_MID : 2 * C_MID],
            sum_gain[C_MID : 2 * C_MID],
            total_out,
        )
        act_one = norm_one * gain_vec[:C_MID] + bias_vec[:C_MID]
        hidden_one = (smooth(act_one) * mask_vec).astype(jnp.bfloat16)
        columns = patches(hidden_one.reshape(IMG_B, side_len, side_len, C_MID), stride)
        acc = add_weight(acc, matmul_left_t(columns, grad_two), offset, valid)
        hid_grad = unpatch(
            matmul_right_t(grad_two, conv_b), IMG_B, side_len, stride, C_MID
        ).reshape(rows_first, C_MID)
        slope_one = hid_grad * mask_vec * smooth_slope(act_one)
        return (
            pack(slope_one),
            second_buf,
            third_buf,
            place(jnp.sum(slope_one, axis=0), 0),
            place(jnp.sum(slope_one * norm_one, axis=0), 0),
            acc,
        )

    def bwd_b_zero(args):
        conv_a, conv_b = weights_zero()
        return bwd_b_double(args, conv_b, rows_in, SIDE, 2, C_IN * C_MID)

    def bwd_b_two(args):
        conv_a, conv_b = weights_two()
        return bwd_b_double(args, conv_b, rows_out, OSIDE, 1, C_OUT * C_MID)

    def bwd_b_pass(args):
        return (args[1], args[2], args[3], zero_wide, zero_wide, args[6])

    def side_none():
        return zero_input

    def bwd_c_zero(args):
        ops, first_buf, second_buf, third_buf, sum_bias, sum_gain, acc = args
        conv_a, conv_b = weights_zero()
        scales, gain_vec, valid = (ops[4], ops[8], ops[12])
        flat_in = ops[0].reshape(rows_in, C_IN)
        slope_one = unpack(first_buf, rows_in, C_MID)
        norm_one = unpack(third_buf, rows_in, C_MID)
        grad_one = norm_grad(
            slope_one,
            norm_one,
            gain_vec[:C_MID],
            scales[:C_MID],
            sum_bias[:C_MID],
            sum_gain[:C_MID],
            total_in,
        )
        acc = add_weight(acc, matmul_left_t(flat_in, grad_one), 0, valid)
        side_out = matmul_right_t(grad_one, conv_a).reshape(IMG_B, PIX_IN, C_IN)
        return (zero_mid, zero_res, acc, side_out)

    def bwd_c_one(args):
        ops, first_buf, second_buf, third_buf, sum_bias, sum_gain, acc = args
        conv_a, conv_b = weights_one()
        scales, gain_vec, valid = (ops[4], ops[8], ops[12])
        short_in = short_rows(ops[0])
        both = unpack(first_buf, rows_out, wide)
        normed = unpack(second_buf, rows_out, wide)
        grad_both = norm_grad(both, normed, gain_vec, scales, sum_bias, sum_gain, total_out)
        acc = add_weight(acc, matmul_left_t(ops[1], grad_both[:, :C_OUT]), 0, valid)
        acc = add_weight(acc, matmul_left_t(short_in, grad_both[:, C_OUT:]), C_MID * C_OUT, valid)
        mid_grad = matmul_right_t(grad_both[:, :C_OUT], conv_a).astype(jnp.bfloat16)
        short_grad = matmul_right_t(grad_both[:, C_OUT:], conv_b).reshape(
            IMG_B, OSIDE, 1, OSIDE, 1, C_IN
        )
        side_out = jnp.pad(short_grad, ((0, 0), (0, 0), (0, 1), (0, 0), (0, 1), (0, 0))).reshape(
            IMG_B, PIX_IN, C_IN
        )
        return (mid_grad, zero_res, acc, side_out)

    def bwd_c_two(args):
        ops, first_buf, second_buf, third_buf, sum_bias, sum_gain, acc = args
        conv_a, conv_b = weights_two()
        scales, grad_res, gain_vec, valid = (ops[4], ops[6], ops[8], ops[12])
        slope_four = unpack(first_buf, rows_out, C_MID)
        norm_four = unpack(third_buf, rows_out, C_MID)
        grad_four = norm_grad(
            slope_four,
            norm_four,
            gain_vec[:C_MID],
            scales[:C_MID],
            sum_bias[:C_MID],
            sum_gain[:C_MID],
            total_out,
        )
        acc = add_weight(acc, matmul_left_t(ops[2], grad_four), 0, valid)
        carried_grad = (grad_res.astype(jnp.float32) + matmul_right_t(grad_four, conv_a)).astype(
            jnp.bfloat16
        )
        return (zero_mid, carried_grad, acc, side_none())

    def bwd_c_three(args):
        ops, first_buf, second_buf, third_buf, sum_bias, sum_gain, acc = args
        conv_a = flat_weights[: C_MID * C_OUT].reshape(C_MID, C_OUT)
        scales, gain_vec, gate_val, valid = (ops[4], ops[8], ops[11], ops[12])
        through = unpack(first_buf, rows_out, C_OUT)
        normed = unpack(second_buf, rows_out, C_OUT)
        res_grad = (through + (1.0 - gate_val) * ops[7].astype(jnp.float32)).astype(jnp.bfloat16)
        grad_six = norm_grad(
            through,
            normed,
            gain_vec[:C_OUT],
            scales[:C_OUT],
            sum_bias[:C_OUT],
            sum_gain[:C_OUT],
            total_out,
        )
        acc = add_weight(acc, matmul_left_t(ops[1], grad_six), 0, valid)
        mid_grad = matmul_right_t(grad_six, conv_a).astype(jnp.bfloat16)
        return (mid_grad, res_grad, acc, side_none())

    def select_params(micro_idx):
        block_id = section_idx // 2
        width_val = width[micro_idx, block_id]
        set_val = bn_set[micro_idx, block_id]
        onehot = (jnp.arange(NSETS) == set_val).astype(jnp.float32)
        gain_vec = jnp.sum(onehot[:, None] * gain_table, axis=0)
        bias_vec = jnp.sum(onehot[:, None] * bias_table, axis=0)
        mask_vec = (jnp.arange(C_MID) < width_val).astype(jnp.float32)
        gate_val = gate[micro_idx].astype(jnp.float32)
        return (gain_vec, bias_vec, mask_vec, gate_val, onehot)

    fwd_first = [fwd_a_zero, fwd_a_one, fwd_a_two, fwd_a_three]
    fwd_second = [fwd_b_zero, fwd_b_pass, fwd_b_two, fwd_b_pass]
    fwd_third = [fwd_c_zero, fwd_c_one, fwd_c_two, fwd_c_three]
    bwd_first = [bwd_a_zero, bwd_a_one, bwd_a_two, bwd_a_three]
    bwd_second = [bwd_b_zero, bwd_b_pass, bwd_b_two, bwd_b_pass]
    bwd_third = [bwd_c_zero, bwd_c_one, bwd_c_two, bwd_c_three]

    def forward_tick(tick_no, state_in):
        recv_mid, recv_res, stash_mid, stash_res, stash_center, stash_scale, out_rows = state_in
        micro_raw = tick_no - section_idx
        is_valid = (micro_raw >= 0) & (micro_raw < MB)
        micro_idx = jnp.clip(micro_raw, 0, MB - 1)
        gain_vec, bias_vec, mask_vec, gate_val, onehot = select_params(micro_idx)
        ops = (image_blocks[micro_idx], recv_mid, recv_res, gain_vec, bias_vec, mask_vec, gate_val)
        scratch, sums_local, squares_local = lax.switch(section_idx, fwd_first, ops)
        sum_first, square_first = group_moments(sums_local, squares_local)
        scratch, sums_local, squares_local = lax.switch(
            section_idx, fwd_second, (ops, scratch, sum_first, square_first)
        )
        sum_second, square_second = group_moments(sums_local, squares_local)
        send_mid, send_res, centers, scales, result = lax.switch(
            section_idx,
            fwd_third,
            (ops, scratch, sum_first + sum_second, square_first + square_second),
        )
        stash_mid = stash_mid.at[micro_idx].set(jnp.where(is_valid, recv_mid, stash_mid[micro_idx]))
        stash_res = stash_res.at[micro_idx].set(jnp.where(is_valid, recv_res, stash_res[micro_idx]))
        stash_center = stash_center.at[micro_idx].set(
            jnp.where(is_valid, centers, stash_center[micro_idx])
        )
        stash_scale = stash_scale.at[micro_idx].set(
            jnp.where(is_valid, scales, stash_scale[micro_idx])
        )
        out_rows = out_rows.at[micro_idx].set(jnp.where(is_valid, result, out_rows[micro_idx]))
        recv_mid, recv_res = (
            shifted(for_sending(send_mid), "pipe", 1).astype(send_mid.dtype),
            shifted(for_sending(send_res), "pipe", 1).astype(send_res.dtype),
        )
        return (recv_mid, recv_res, stash_mid, stash_res, stash_center, stash_scale, out_rows)

    forward_init = (
        zero_mid,
        zero_res,
        jnp.zeros((MB, rows_out, C_MID), jnp.bfloat16),
        jnp.zeros((MB, rows_out, C_OUT), jnp.bfloat16),
        jnp.zeros((MB, wide), jnp.float32),
        jnp.zeros((MB, wide), jnp.float32),
        jnp.zeros((MB, rows_out, C_OUT), jnp.float32),
    )
    forward_state = lax.fori_loop(0, MB + pipe_count - 1, forward_tick, forward_init)
    unused_mid, unused_res, stash_mid, stash_res, stash_center, stash_scale, out_rows = (
        forward_state
    )

    def backward_tick(tick_no, state_in):
        grad_mid, grad_res, weight_acc, gain_acc, bias_acc, input_acc = state_in
        micro_raw = tick_no - (pipe_count - 1 - section_idx)
        is_valid = (micro_raw >= 0) & (micro_raw < MB)
        micro_idx = jnp.clip(micro_raw, 0, MB - 1)
        gain_vec, bias_vec, mask_vec, gate_val, onehot = select_params(micro_idx)
        ops = (
            image_blocks[micro_idx],
            stash_mid[micro_idx],
            stash_res[micro_idx],
            stash_center[micro_idx],
            stash_scale[micro_idx],
            grad_mid,
            grad_res,
            cotangent[micro_idx],
            gain_vec,
            bias_vec,
            mask_vec,
            gate_val,
            is_valid,
        )
        first_buf, second_buf, third_buf, bias_one, gain_one = lax.switch(
            section_idx, bwd_first, ops
        )
        sum_bias_one, sum_gain_one = group_grad_sums(bias_one, gain_one)
        first_buf, second_buf, third_buf, bias_two, gain_two, weight_acc = lax.switch(
            section_idx,
            bwd_second,
            (ops, first_buf, second_buf, third_buf, sum_bias_one, sum_gain_one, weight_acc),
        )
        sum_bias_two, sum_gain_two = group_grad_sums(bias_two, gain_two)
        send_mid, send_res, weight_acc, side_out = lax.switch(
            section_idx,
            bwd_third,
            (
                ops,
                first_buf,
                second_buf,
                third_buf,
                sum_bias_one + sum_bias_two,
                sum_gain_one + sum_gain_two,
                weight_acc,
            ),
        )
        gain_grad = gain_one + gain_two
        bias_grad = bias_one + bias_two
        gain_acc = jnp.where(is_valid, gain_acc + onehot[:, None] * gain_grad[None, :], gain_acc)
        bias_acc = jnp.where(is_valid, bias_acc + onehot[:, None] * bias_grad[None, :], bias_acc)
        input_acc = jax.tree.map(
            lambda stored, fresh: stored.at[micro_idx].set(
                jnp.where(is_valid, fresh, stored[micro_idx])
            ),
            input_acc,
            side_out,
        )
        grad_mid, grad_res = (
            shifted(for_sending(send_mid), "pipe", -1).astype(send_mid.dtype),
            shifted(for_sending(send_res), "pipe", -1).astype(send_res.dtype),
        )
        return (grad_mid, grad_res, weight_acc, gain_acc, bias_acc, input_acc)

    side_init = jnp.zeros((MB, IMG_B, PIX_IN, C_IN), jnp.float32)
    backward_init = (
        zero_mid,
        zero_res,
        jnp.zeros((P_SIZE,), jnp.float32),
        jnp.zeros((NSETS, wide), jnp.float32),
        jnp.zeros((NSETS, wide), jnp.float32),
        side_init,
    )
    backward_state = lax.fori_loop(0, MB + pipe_count - 1, backward_tick, backward_init)
    unused_gmid, unused_gres, weight_acc, gain_acc, bias_acc, input_acc = backward_state
    grad_images, output_sum = (
        lax.psum_scatter(
            input_acc.reshape(IMG_DEV, PIX_IN, C_IN).astype(jnp.bfloat16),
            "pipe",
            scatter_dimension=2,
            tiled=True,
        ).astype(jnp.float32),
        lax.psum_scatter(
            out_rows.astype(jnp.bfloat16), "pipe", scatter_dimension=2, tiled=True
        ).astype(jnp.float32),
    )
    output_part = output_sum.astype(jnp.bfloat16)
    norm_grads = jnp.concatenate([gain_acc.reshape(-1), bias_acc.reshape(-1)])
    weight_sum, norm_sum = lax.psum((weight_acc, norm_grads), ("dp", "rep"))
    grad_gain = norm_sum[: NSETS * wide].reshape(1, NSETS, wide)
    grad_bias = norm_sum[NSETS * wide :].reshape(1, NSETS, wide)
    return (output_part, grad_images, weight_sum.reshape(1, P_SIZE), grad_gain, grad_bias)


PP = PIX_OUT + 1
RW = 8 * PP
RV = 8 * PIX_OUT
BLK = 512
SUB = 65536
F32 = jnp.float32
BF16 = jnp.bfloat16
MESH = pl.DeviceIdType.MESH

C_H2, C_H4, C_H5, C_Z6, C_D5, C_D4, C_DH = range(8, 15)
C_O1, C_SHARE, C_GI, C_GP = 15, 19, 22, 25
C_PAR2, C_PAR3, C_DG2, C_DG3, C_BN1, C_BN2, C_BN3 = range(28, 35)
N_SEM = 35
N_PIECE = 17
W_OWN, W_PEER, W_Z, W_ON = range(4)
G_CORE, G_IN, G_ACROSS, G_OUT, G_DONE = range(5)
RING = 8


def nn(a, b):
    return jnp.dot(a, b, preferred_element_type=F32)


def nt(a, b):
    return lax.dot_general(a, b, (((1,), (1,)), ((), ())), preferred_element_type=F32)


def tn(a, b):
    return lax.dot_general(a, b, (((0,), (0,)), ((), ())), preferred_element_type=F32)


def rows(start, size):
    return pl.ds(pl.multiple_of(start, 16), size)


def whole_kernel(
    img, wts, gain, bias, meta, cot,
    out, gi, dw, dgb,
    imgb, raw, st, wh, wx, f0, f1, f2, f3, fs, pb, pt, u0, u1, u2, sx, cotb,
    h2, h4, h5, d5, d4, dh, r0, r1, ob, tx, rx, inv, par, parx, dg, dgx, sb, rd, bz, dgs,
    ls, ss, rs, wss, wrs, ass, ars, ready, go,
):
    p, d, r = lax.axis_index("pipe"), lax.axis_index("dp"), lax.axis_index("rep")
    peer = (p, 1 - d, r)
    z_pair = r + 1 - 2 * lax.rem(r, 2)
    quarter = 2 * lax.rem(r, 2) + d

    def remote(src, dst, send, recv, device):
        return pltpu.make_async_remote_copy(
            src_ref=src, dst_ref=dst, send_sem=ss.at[send], recv_sem=rs.at[recv],
            device_id=device, device_id_type=MESH,
        )

    def sync(event, first, count):
        part = pl.ds(first, count)
        copy = remote(tx.at[part], rx.at[part], event, event, peer)
        copy.start()
        copy.wait()

    def both(slot):
        return tx[slot] + rx[slot]

    def moments(slot_sum, slot_square, total, inv_slot):
        center = both(slot_sum) * (1.0 / total)
        scale = lax.rsqrt(both(slot_square) * (1.0 / total) - center * center + EPSILON)
        inv[inv_slot] = scale
        return center, scale

    def silu(v):
        return v * jax.nn.sigmoid(v)

    def slope(v):
        s = jax.nn.sigmoid(v)
        return s * (1.0 + v * (1.0 - s))

    def clear_pad(ref, first):
        tile = ref[rows(first + RW - 16, 16), :].astype(F32)
        keep = lax.broadcasted_iota(jnp.int32, tile.shape, 0) < 8
        ref[rows(first + RW - 16, 16), :] = jnp.where(keep, tile, 0.0).astype(BF16)

    def mask_of(column):
        lane = lax.broadcasted_iota(jnp.int32, (8, BLK), 1).astype(F32)
        return (lane < meta[:, column : column + 1]).astype(F32)

    def five(body, init=0):
        return lax.fori_loop(0, 5, lambda c, carry: body(pl.ds(c * 10, 10), c, carry), init)

    def add_stats(carry, a, b):
        return carry[0] + jnp.sum(a, axis=0), carry[1] + jnp.sum(b, axis=0)

    zero_stats = (jnp.zeros((8, BLK), F32), jnp.zeros((8, BLK), F32))

    def store_z(ref, first, z, slot_sum, slot_square):
        z3 = z.reshape(PP, 8, BLK)
        ref[pl.ds(first, PP)] = z3
        tx[slot_sum] = jnp.sum(z3, axis=0)
        tx[slot_square] = jnp.sum(z3 * z3, axis=0)

    def raw_copy(turn, element_of):
        slot = lax.rem(turn, RING)
        return pltpu.make_async_copy(
            wts.at[:, pl.ds(pl.multiple_of(element_of(turn) * SUB, SUB), SUB)], raw.at[slot], ls.at[8 + slot]
        )

    def open_weights(element_of, total):
        for turn in range(min(RING - 1, total)):
            raw_copy(turn, element_of).start()

    def load_weights(element_of, total, first, count, put):
        def body(k, carry):
            turn = first + k

            @pl.when(turn + RING - 1 < total)
            def _():
                raw_copy(turn + RING - 1, element_of).start()

            raw_copy(turn, element_of).wait()
            st[0:512] = raw[lax.rem(turn, RING)].astype(F32).reshape(512, 128)
            put(turn)
            return carry

        lax.fori_loop(0, count, body, 0)

    def put_narrow(ref, row_of):
        def put(i):
            for j in range(4):
                ref[rows(row_of(i), 128), j * 128 : (j + 1) * 128] = st[
                    pl.ds(j, 128, stride=4), :
                ].astype(BF16)

        return put

    def put_wide(ref, base, block_rows, first):
        def put(i):
            for n in range(4):
                for j in range(4):
                    ref[rows(base + n * block_rows + (i - first) * 32, 32), j * 128 : (j + 1) * 128] = st[
                        pl.ds(4 * n + j, 32, stride=16), :
                    ].astype(BF16)

        return put

    def put_chunk(t, n, block):
        wh[rows(t * 512 + n * 64, 64), :] = block[0:64].astype(BF16)
        wh[rows(t * 512 + 256 + n * 64, 64), :] = block[64:128].astype(BF16)

    def plain(turn):
        return turn

    def every_fourth(turn):
        return 4 * turn + quarter

    def four_rows(turn):
        return 4 * quarter + turn

    def img_copy(q, slot):
        return pltpu.make_async_copy(img.at[pl.ds(q * 28, 28)], imgb.at[slot], ls.at[slot])

    def open_images():
        for q in range(3):
            img_copy(q, q).start()

    def over_images(body, init):
        def step(q, carry):
            slot = lax.rem(q, 4)

            @pl.when(q + 3 < 7)
            def _():
                img_copy(q + 3, lax.rem(q + 3, 4)).start()

            img_copy(q, slot).wait()
            return body(q, slot, carry)

        return lax.fori_loop(0, 7, step, init)

    outer = (r == 0) | (r == 3)
    inner = jnp.logical_not(outer)
    z_dev, across = (p, d, z_pair), (p, d, 3 - r)

    def grad_copy(kind, t, src, dst, device):
        return pltpu.make_async_remote_copy(
            src_ref=src, dst_ref=dst, send_sem=ass.at[kind, t], recv_sem=ars.at[kind, t],
            device_id=device, device_id_type=MESH,
        )

    def chunk_rows(chunk, half):
        return dw.at[pl.ds(pl.multiple_of(chunk * 2048 + half * 1024, 1024), 1024)]

    def zero_rest(first):
        sb[0] = jnp.zeros((1024, 128), BF16)

        def body(i, carry):
            for half in range(2):
                copy = pltpu.make_async_copy(sb.at[0], chunk_rows(first + i, half), ls.at[4])
                copy.start()
                copy.wait()
            return carry

        lax.fori_loop(0, 13 - first, body, 0)

    def bn_sums():
        for k in range(NSETS):
            hot = (set_col == float(k)).astype(F32)
            for n in range(8):
                cols = slice(n * BLK, (n + 1) * BLK)
                dgs[k : k + 1, cols] = jnp.sum(dg[n] * hot, axis=0, keepdims=True)
                dgs[4 + k : 5 + k, cols] = jnp.sum(dg[8 + n] * hot, axis=0, keepdims=True)

    def bn_in():
        return remote(dgs, bz.at[0], C_BN1, C_BN1, z_dev)

    def bn_across():
        return remote(dgs, bz.at[1], C_BN2, C_BN2, across)

    def bn_out():
        return remote(dgb, bz.at[0], C_BN3, C_BN3, z_dev)

    def say_ready():
        pl.semaphore_signal(ready.at[0], inc=1, device_id=z_dev, device_id_type=MESH)

        @pl.when(inner)
        def _():
            pl.semaphore_signal(ready.at[1], inc=1, device_id=across, device_id_type=MESH)

    def sum_gradients(count, compute, at_row, chunk_of, wide, z1, extra):
        z2 = z1 + count * 256

        def half(t, which):
            return wh.at[rows(at_row(t) + which * 256, 256)]

        def from_z(t):
            return wx.at[rows(z1 + t * 256, 256)]

        def from_across(t):
            return wx.at[rows(z2 + t * 256, 256)]

        def to_core(t):
            return grad_copy(G_CORE, t, half(t, 1 - d), rd.at[rows(t * 256, 256)], peer)

        def inwards(t):
            return grad_copy(G_IN, t, half(t, d), from_z(t), z_dev)

        def exchange(t):
            return grad_copy(G_ACROSS, t, half(t, d), from_across(t), across)

        def outwards(t):
            return grad_copy(G_OUT, t, half(t, d), from_z(t), z_dev)

        def done_core(t):
            part = chunk_rows(chunk_of(t), d)
            return grad_copy(G_DONE, t, sb.at[lax.rem(t, 4)], part, peer)

        def done_here(t):
            return pltpu.make_async_copy(sb.at[lax.rem(t, 4)], chunk_rows(chunk_of(t), d), ls.at[4 + lax.rem(t, 4)])

        def add(t, other):
            total = half(t, d)[...].astype(F32) + other[...].astype(F32)
            half(t, d)[...] = total.astype(BF16)

        def finish(t, ref):
            @pl.when(t >= 4)
            def _():
                done_here(t - 4).wait()
                done_core(t - 4).wait_send()

            value = ref[...].astype(F32)
            for j in range(4):
                cols = slice(j * 128, (j + 1) * 128)
                if wide:
                    for n in range(4):
                        st[pl.ds(4 * n + j, 64, stride=16), :] = value[n * 64 : (n + 1) * 64, cols]
                else:
                    st[pl.ds(j, 256, stride=4), :] = value[:, cols]
            sb[lax.rem(t, 4)] = st[...].astype(BF16)
            done_here(t).start()
            done_core(t).start()

        def step(it, carry):
            for when, work in extra.items():
                pl.when(it == when)(work)

            @pl.when(it < count)
            def _():
                compute(it)
                to_core(it).start()

            t1 = it - 1

            @pl.when((t1 >= 0) & (t1 < count))
            def _():
                to_core(t1).wait_recv()
                add(t1, rd.at[rows(t1 * 256, 256)])

                @pl.when(outer & (t1 == 0))
                def _():
                    pl.semaphore_wait(ready.at[0], 1)

                @pl.when(outer)
                def _():
                    inwards(t1).start()

            t2 = it - 2

            @pl.when(inner & (t2 >= 0) & (t2 < count))
            def _():
                @pl.when(t2 == 0)
                def _():
                    pl.semaphore_wait(ready.at[1], 1)

                inwards(t2).wait_recv()
                add(t2, from_z(t2))
                exchange(t2).start()

            t3 = it - 3

            @pl.when(inner & (t3 >= 0) & (t3 < count))
            def _():
                @pl.when(t3 == 0)
                def _():
                    pl.semaphore_wait(ready.at[0], 1)

                exchange(t3).wait()
                add(t3, from_across(t3))
                outwards(t3).start()
                finish(t3, half(t3, d))

            t5 = it - 5

            @pl.when(outer & (t5 >= 0) & (t5 < count))
            def _():
                outwards(t5).wait_recv()
                finish(t5, from_z(t5))

            @pl.when(it == count - 3)
            def _():
                bn_sums()

                @pl.when(outer)
                def _():
                    bn_in().start()

            @pl.when(inner & (it == count))
            def _():
                bn_in().wait_recv()
                dgs[...] += bz[0]
                bn_across().start()

            @pl.when(inner & (it == count + 3))
            def _():
                bn_across().wait()
                dgb[...] = dgs[...] + bz[1]
                bn_out().start()

            return carry

        lax.fori_loop(0, count + 5, step, 0)

        @pl.when(outer)
        def _():
            bn_in().wait_send()
            bn_out().wait_recv()
            dgb[...] = bz[0]

        @pl.when(inner)
        def _():
            bn_out().wait_send()

        def drain(t, carry):
            to_core(t).wait_send()

            @pl.when(outer)
            def _():
                inwards(t).wait_send()

            @pl.when(inner)
            def _():
                outwards(t).wait_send()

            @pl.when(t >= count - 4)
            def _():
                done_here(t).wait()
                done_core(t).wait_send()

            theirs = chunk_rows(chunk_of(t), 1 - d)
            grad_copy(G_DONE, t, sb.at[0], theirs, peer).wait_recv()
            return carry

        lax.fori_loop(0, count, drain, 0)

    @pl.when(p == 0)
    def _():
        open_weights(plain, 44)
        open_images()

    @pl.when(p == 1)
    def _():
        open_weights(plain, 48)
        open_images()
        pltpu.make_async_copy(cot, cotb.at[0:PIX_OUT], ls.at[16]).start()

    @pl.when(p == 2)
    def _():
        open_weights(every_fourth, 13)

    @pl.when(p == 3)
    def _():
        open_weights(four_rows, 4)

    barrier = pltpu.get_barrier_semaphore()
    for device in (peer, (p, d, z_pair), (p, d, 3 - r)) + tuple((lax.rem(p + k, 4), d, r) for k in (1, 2, 3)):
        pl.semaphore_signal(barrier, inc=1, device_id=device, device_id_type=MESH)

    block_two = p >= 2
    set_col = jnp.where(block_two, meta[:, 3:4], meta[:, 2:3])
    for k in range(NSETS):
        hot = (set_col == float(k)).astype(F32)
        for n in range(8):
            g = hot * gain[k : k + 1, n * BLK : (n + 1) * BLK]
            b = hot * bias[k : k + 1, n * BLK : (n + 1) * BLK]
            if k == 0:
                par[n] = g
                par[8 + n] = b
            else:
                par[n] += g
                par[8 + n] += b
    dg[...] = jnp.zeros_like(dg)
    pl.semaphore_wait(barrier, 6)

    total_in, total_out = 2.0 * PIX_IN, 2.0 * PIX_OUT

    def build_patches(base):
        def body(tap, carry):
            row, col = base(tap)
            window = pb[pl.ds(row, 7), pl.ds(col, 7)].reshape(RV, BLK)
            pt[tap, 0:RV, :] = window.astype(BF16)
            return carry

        lax.fori_loop(0, 9, body, 0)

    def clear_patch_pad():
        def body(tap, carry):
            pt[tap, RW - 16 : RW, :] = jnp.zeros((16, BLK), BF16)
            return carry

        lax.fori_loop(0, 9, body, 0)

    def strided_base(tap):
        di, dj = tap // 3, lax.rem(tap, 3)
        return lax.rem(di, 2) * 8 + di // 2, lax.rem(dj, 2) * 8 + dj // 2

    def plain_base(tap):
        return tap // 3, lax.rem(tap, 3)

    def conv(ref, first, target):
        target[...] = jnp.zeros_like(target)

        def body(tap, carry):
            z = nn(pt[tap], ref[rows(first + tap * BLK, BLK), :])
            target[...] += z.reshape(PP, 8, BLK)
            return carry

        lax.fori_loop(0, 9, body, 0)

    def conv_back(dz, ref, first, base):
        pb[...] = jnp.zeros_like(pb)

        def body(tap, carry):
            row, col = base(tap)
            part = nt(dz[0:RV, :], ref[rows(first + tap * BLK, BLK), :])
            pb[pl.ds(row, 7), pl.ds(col, 7)] += part.reshape(7, 7, 8, BLK)
            return carry

        lax.fori_loop(0, 9, body, 0)

    def stats_of_map(ref, slot_sum, slot_square):
        def body(c, _, carry):
            z = ref[c]
            return add_stats(carry, z, z * z)

        tx[slot_sum], tx[slot_square] = five(body, zero_stats)

    def act_to(ref, target, center, scale, g, b, mask):
        def body(c, i, carry):
            zhat = (ref[c] - center) * scale
            ref[c] = zhat
            h = silu(zhat * g + b) * mask
            target[rows(i * 80, 80), :] = h.reshape(80, BLK).astype(BF16)
            return carry

        five(body)
        clear_pad(target, 0)

    def upstream(target, grad, zhat_ref, g, b, mask, slot_sum, slot_gain):
        def body(c, i, carry):
            zhat = zhat_ref[c]
            du = grad[rows(i * 80, 80), :].astype(F32).reshape(10, 8, BLK) * mask * slope(zhat * g + b)
            target[c] = du
            return add_stats(carry, du, du * zhat)

        tx[slot_sum], tx[slot_gain] = five(body, zero_stats)

    def norm_back(target, first, du_ref, du_first, zhat_ref, zhat_first, gscale, mean_du, mean_dg):
        def body(c, i, carry):
            du = du_ref[pl.ds(du_first + i * 10, 10)]
            zhat = zhat_ref[pl.ds(zhat_first + i * 10, 10)]
            dz = gscale * (du - mean_du - zhat * mean_dg)
            target[rows(first + i * 80, 80), :] = dz.reshape(80, BLK).astype(BF16)
            return carry

        five(body)
        clear_pad(target, first)

    @pl.when(p == 0)
    def _():
        mask = mask_of(0)
        say_ready()
        put_w = put_narrow(wh, lambda i: i * 128)
        load_weights(plain, 44, 0, 8, put_w)

        def first_conv(q, slot, carry):
            rows_q = imgb[slot].astype(F32).reshape(224, 1024).astype(BF16)
            wx[rows(q * 224, 224), :] = rows_q[:, 0:512]
            wx[rows(1568 + q * 224, 224), :] = rows_q[:, 512:1024]
            z = nn(rows_q, wh[0:1024, :]).reshape(28, 8, BLK)
            f0[pl.ds(q * 28, 28)] = z
            load_weights(plain, 44, 8 + 5 * q, 5, put_w)
            return add_stats(carry, z, z * z)

        tx[0], tx[1] = over_images(first_conv, zero_stats)
        exchange = remote(tx.at[pl.ds(0, 2)], rx.at[pl.ds(0, 2)], 0, 0, peer)
        exchange.start()
        pb[...] = jnp.zeros_like(pb)
        clear_patch_pad()
        load_weights(plain, 44, 43, 1, put_w)
        exchange.wait()

        center, scale = moments(0, 1, total_in, 0)
        g1, b1, g2, b2 = par[0], par[8], par[1], par[9]

        def hidden(i, carry):
            zhat = (f0[pl.ds(i * 14, 14)] - center) * scale
            f0[pl.ds(i * 14, 14)] = zhat
            h = (silu(zhat * g1 + b1) * mask).astype(BF16).astype(F32).reshape(7, 2, 8, BLK)
            u = i + 1
            row = lax.rem(u, 2) * 8 + u // 2
            pb[row, 8:15] = h[:, 0]
            pb[row, 1:8] = h[:, 1]
            return carry

        lax.fori_loop(0, 14, hidden, 0)
        build_patches(strided_base)
        conv(wh, 1024, fs.at[0])
        stats_of_map(fs.at[0], 2, 3)
        sync(1, 2, 2)
        center, scale = moments(2, 3, total_out, 1)
        act_to(fs.at[0], h2, center, scale, g2, b2, mask)
        send = remote(h2, h2, C_H2, C_H2, (1, d, r))
        send.start()
        zero_rest(11)
        send.wait_send()

        remote(dh, dh, C_DH, C_DH, (0, d, r)).wait_recv()
        upstream(fs.at[1], dh, fs.at[0], g2, b2, mask, 4, 5)
        sync(2, 4, 2)
        s_du, s_dg = both(4), both(5)
        dg[1], dg[9] = s_dg, s_du
        norm_back(d5, 0, fs.at[1], 0, fs.at[0], 0, g2 * inv[1], s_du * (1.0 / total_out), s_dg * (1.0 / total_out))
        def back_conv():
            conv_back(d5, wh, 1024, strided_base)

        def slopes(i, carry):
            u = i + 1
            row = lax.rem(u, 2) * 8 + u // 2
            grad = jnp.stack([pb[row, 8:15], pb[row, 1:8]], axis=1).reshape(14, 8, BLK)
            zhat = f0[pl.ds(i * 14, 14)]
            du = grad * mask * slope(zhat * g1 + b1)
            f1[pl.ds(i * 14, 14)] = du
            return add_stats(carry, du, du * zhat)

        def first_slopes():
            tx[6], tx[7] = lax.fori_loop(0, 14, slopes, zero_stats)
            sync(3, 6, 2)
            dg[0], dg[8] = both(7), both(6)

        def first_back():
            s_du, s_dg = both(6), both(7)
            gscale, m_du, m_dg = g1 * inv[0], s_du * (1.0 / total_in), s_dg * (1.0 / total_in)

            def body(q, carry):
                part = pl.ds(q * 28, 28)
                dz = gscale * (f1[part] - m_du - f0[part] * m_dg)
                u1[rows(q * 224, 224), :] = dz.reshape(224, BLK).astype(BF16)
                return carry

            lax.fori_loop(0, 7, body, 0)

        def share(target, column, k):
            def body(q, carry):
                g = nt(u1[rows(q * 224, 224), :], wh[k * 256 : (k + 1) * 256, :])
                target[rows(q * 224, 224), column : column + 256] = g.astype(BF16)
                return carry

            lax.fori_loop(0, 7, body, 0)

        places = {1: (u0, 0), 2: (u0, 256), 3: (u2, 0)}

        def share_copy(k):
            target, column = places[k]
            return remote(target.at[0:1568, column : column + 256], r0, C_GI + k - 1, C_GI, (k, d, r))

        def share_out(k):
            share(*places[k], k)
            share_copy(k).start()

        def back_and_share():
            first_back()
            share_out(3)

        def compute(t):
            @pl.when(t < 9)
            def _():
                wh[rows(at_row(t), 512), :] = tn(pt[t], d5[...]).astype(BF16)

            @pl.when(t >= 9)
            def _():
                block = tn(wx[rows((t - 9) * 1568, 1568), :], u1[0:1568, :])
                wh[rows(at_row(t), 512), :] = block.astype(BF16)

        def at_row(t):
            return jnp.where(t < 2, 5632 + t * 512, t * 512)

        sum_gradients(
            11, compute, at_row, lambda t: lax.rem(t + 2, 11), False, 3136,
            {
                2: back_conv,
                3: first_slopes,
                4: back_and_share,
                5: lambda: share_out(1),
                6: lambda: share_out(2),
                7: lambda: share(r0, 0, 0),
            },
        )
        for k in (1, 2, 3):
            share_copy(k).wait_send()

    @pl.when(p == 1)
    def _():
        mask = mask_of(1)
        gate_col = meta[:, 4:5]
        cotb[PIX_OUT] = jnp.zeros((8, C_OUT), BF16)
        clear_patch_pad()
        load_weights(plain, 48, 0, 16, put_wide(wh, 0, 512, 0))
        load_weights(plain, 48, 16, 32, put_wide(wh, 2048, 1024, 16))

        def shorten(a, slot, carry):
            v = imgb[slot, 0:14].astype(F32).reshape(7, 2, 8, 1024)[:, 0]
            f0[pl.ds(a * 7, 7)] = v[:, :, 0:512]
            f0[pl.ds(PP + a * 7, 7)] = v[:, :, 512:1024]
            return carry

        over_images(shorten, 0)
        f0[PIX_OUT] = jnp.zeros((8, BLK), F32)
        f0[PP + PIX_OUT] = jnp.zeros((8, BLK), F32)
        sx[...] = f0[0 : 2 * PP].reshape(2 * RW, BLK).astype(BF16)

        def shortcut(n, carry):
            z = nn(sx[0:RW, :], wh[rows(2048 + n * 1024, 512), :]) + nn(
                sx[RW : 2 * RW, :], wh[rows(2560 + n * 1024, 512), :]
            )
            store_z(f1, n * PP, z, 8 + n, 12 + n)
            return carry

        lax.fori_loop(0, 4, shortcut, 0)

        other_z = 2 * (1 - lax.rem(r, 2))
        this_z = 2 * lax.rem(r, 2)

        def piece(i, q):
            return wx.at[rows(i * 512 + q * 128, 128)]

        def piece_copy(kind, i, q, device):
            part = piece(i, q)
            return pltpu.make_async_remote_copy(
                src_ref=part, dst_ref=part, send_sem=wss.at[kind, i], recv_sem=wrs.at[kind, i],
                device_id=device, device_id_type=MESH,
            )

        def pass_own(i):
            piece_copy(W_OWN, i, quarter, (1, d, r)).wait_recv()
            piece_copy(W_PEER, i, quarter, peer).start()
            piece_copy(W_Z, i, quarter, z_dev).start()

        def pass_on(i):
            piece_copy(W_Z, i, other_z + d, peer).wait_recv()
            piece_copy(W_ON, i, other_z + d, peer).start()

        def have(i):
            piece_copy(W_PEER, i, this_z + 1 - d, peer).wait_recv()
            piece_copy(W_ON, i, other_z + 1 - d, peer).wait_recv()

        def each(work, first, last):
            def body(i, carry):
                work(i)
                return carry

            lax.fori_loop(first, last, body, 0)

        zero_rest(12)
        each(pass_own, 0, 7)
        each(pass_on, 0, 4)
        remote(h2, h2, C_H2, C_H2, (1, d, r)).wait_recv()

        def third_conv(n, carry):
            store_z(f0, n * PP, nn(h2[...], wh[rows(n * 512, 512), :]), n, 4 + n)
            return carry

        lax.fori_loop(0, 4, third_conv, 0)
        sync(0, 0, 16)
        pass_own(7)
        pass_on(4)

        def join(n, carry):
            c3, s3 = moments(n, 4 + n, total_out, 2 + n)
            cp, sp = moments(8 + n, 12 + n, total_out, 6 + n)
            g3, gp, b = par[n], par[4 + n], par[8 + n] + par[12 + n]

            def body(_, i, carry):
                part = pl.ds(n * PP + i * 10, 10)
                a = (f0[part] - c3) * s3
                b_ = (f1[part] - cp) * sp
                f0[part] = a
                f1[part] = b_
                o = silu(a * g3 + b_ * gp + b)
                u0[rows(n * RW + i * 80, 80), :] = o.reshape(80, BLK).astype(BF16)
                return carry

            five(body)
            clear_pad(u0, n * RW)
            return carry

        lax.fori_loop(0, 4, join, 0)
        pass_own(8)
        pass_on(5)
        each(have, 0, 4)
        zhat4, zhat5 = fs.at[0], fs.at[1]
        z = nn(u0[0:RW, :], wx[0:512, :])
        for n in range(1, 4):
            z += nn(u0[n * RW : (n + 1) * RW, :], wx[n * 512 : (n + 1) * 512, :])
        store_z(zhat4, 0, z, 16, 17)
        sync(1, 16, 2)
        remote(parx.at[0:4], parx.at[0:4], C_PAR2, C_PAR2, (1, d, r)).wait_recv()
        center, scale = moments(16, 17, total_out, 10)
        g4, g5, b4, b5 = parx[0], parx[1], parx[2], parx[3]
        pb[...] = jnp.zeros_like(pb)

        def hidden(a, carry):
            part = pl.ds(a * 7, 7)
            zhat = (zhat4[part] - center) * scale
            zhat4[part] = zhat
            h = silu(zhat * g4 + b4) * mask
            pb[a + 1, 1:8] = h.astype(BF16).astype(F32)
            return carry

        lax.fori_loop(0, 7, hidden, 0)
        h4[0:RV, :] = pb[1:8, 1:8].reshape(RV, BLK).astype(BF16)
        h4_send = remote(h4, h4, C_H4, C_H4, (2, d, r))
        h4_send.start()

        def o1_copy(n):
            part = u0.at[n * RW : (n + 1) * RW]
            return remote(part, part, C_O1 + n, C_O1 + n, (2, d, r))

        o1_copy(0).start()
        o1_copy(1).start()
        build_patches(plain_base)
        each(pass_own, 9, 11)
        pl.semaphore_signal(go, inc=1, device_id=(3, d, r), device_id_type=MESH)
        pass_on(6)
        pass_own(11)
        pass_on(7)
        pass_own(12)
        pass_on(8)
        zhat5[...] = jnp.zeros_like(zhat5)

        def fifth_conv(t, carry):
            @pl.when(t >= 5)
            def _():
                pass_on(4 + t)

            have(4 + t)
            z = nn(pt[t], wx[rows(2048 + t * 512, 512), :])
            zhat5[...] += z.reshape(PP, 8, BLK)
            return carry

        lax.fori_loop(0, 9, fifth_conv, 0)
        each(pass_own, 13, 17)
        stats_of_map(zhat5, 18, 19)
        sync(2, 18, 2)
        center, scale = moments(18, 19, total_out, 11)
        act_to(zhat5, h5, center, scale, g5, b5, mask)
        h5_send = remote(h5, h5, C_H5, C_H5, (3, d, r))
        h5_send.start()
        each(pass_on, 13, 17)

        def sixth_conv(n, carry):
            have(13 + n)
            store_z(f2, n * PP, nn(h5[...], wx[rows(6656 + n * 512, 512), :]), 20 + n, 24 + n)
            return carry

        lax.fori_loop(0, 4, sixth_conv, 0)
        sync(3, 20, 8)
        remote(parx.at[4:12], parx.at[4:12], C_PAR3, C_PAR3, (1, d, r)).wait_recv()
        pltpu.make_async_copy(cot, cotb.at[0:PIX_OUT], ls.at[16]).wait()

        def finish(n, carry):
            center, scale = moments(20 + n, 24 + n, total_out, 12 + n)
            g6, b6 = parx[4 + n], parx[8 + n]
            gate_v = jnp.broadcast_to(gate_col, (8, BLK))

            def body(c, i, carry):
                part = pl.ds(n * PP + i * 10, 10)
                part_rows = rows(n * RW + i * 80, 80)
                zhat = (f2[part] - center) * scale
                f2[part] = zhat
                o = u0[part_rows, :].astype(F32).reshape(10, 8, BLK)
                q = o + zhat * g6 + b6
                s = jax.nn.sigmoid(q)
                merged = gate_v * (q * s) + (1.0 - gate_v) * o
                pt[n, rows(i * 80, 80), :] = merged.reshape(80, BLK).astype(BF16)
                ct = cotb[c, :, pl.ds(pl.multiple_of(n * BLK, BLK), BLK)].astype(F32)
                dq = ct * gate_v * (s * (1.0 + q * (1.0 - s)))
                f3[part] = dq
                dres = dq + (1.0 - gate_v) * ct
                u2[part_rows, :] = dres.reshape(80, BLK).astype(BF16)
                return add_stats(carry, dq, dq * zhat)

            tx[28 + n], tx[32 + n] = five(body, zero_stats)
            return carry

        lax.fori_loop(0, 4, finish, 0)
        ob[...] = pt[1]

        sync(4, 28, 8)

        def sixth_back(n, carry):
            s_du, s_dg = both(28 + n), both(32 + n)
            dgx[4 + n] = s_dg
            dgx[8 + n] = s_du
            norm_back(u1, n * RW, f3, n * PP, f2, n * PP, parx[4 + n] * inv[12 + n], s_du * (1.0 / total_out), s_dg * (1.0 / total_out))
            return carry

        lax.fori_loop(0, 4, sixth_back, 0)
        z6_send = remote(u1, u1, C_Z6, C_Z6, (3, d, r))
        z6_send.start()
        grad = nt(u1[0:RW, :], wx[6656:7168, :])
        for n in range(1, 4):
            grad += nt(u1[n * RW : (n + 1) * RW, :], wx[6656 + n * 512 : 7168 + n * 512, :])
        dh[...] = grad.astype(BF16)

        upstream(f2, dh, zhat5, g5, b5, mask, 36, 37)
        sync(5, 36, 2)
        s_du, s_dg = both(36), both(37)
        dgx[1] = s_dg
        dgx[3] = s_du
        norm_back(d5, 0, f2, 0, zhat5, 0, g5 * inv[11], s_du * (1.0 / total_out), s_dg * (1.0 / total_out))
        d5_send = remote(d5, d5, C_D5, C_D5, (2, d, r))
        d5_send.start()
        conv_back(d5, wx, 2048, plain_base)

        def fourth_slopes(a, carry):
            part = pl.ds(a * 7, 7)
            zhat = zhat4[part]
            du = pb[a + 1, 1:8] * mask * slope(zhat * g4 + b4)
            f2[part] = du
            return add_stats(carry, du, du * zhat)

        tx[38], tx[39] = lax.fori_loop(0, 7, fourth_slopes, zero_stats)
        sync(6, 38, 2)
        s_du, s_dg = both(38), both(39)
        dgx[0] = s_dg
        dgx[2] = s_du
        norm_back(d4, 0, f2, 0, zhat4, 0, g4 * inv[10], s_du * (1.0 / total_out), s_dg * (1.0 / total_out))

        def first_block_slopes(n, carry):
            f3[pl.ds(n * PP, PP)] = nt(d4[...], wx[rows(n * 512, 512), :]).reshape(PP, 8, BLK)
            g3, gp, b = par[n], par[4 + n], par[8 + n] + par[12 + n]

            def body(_, i, carry):
                part = pl.ds(n * PP + i * 10, 10)
                do = u2[rows(n * RW + i * 80, 80), :].astype(F32).reshape(10, 8, BLK) + f3[part]
                a, b_ = f0[part], f1[part]
                dp = do.astype(BF16).astype(F32) * slope(a * g3 + b_ * gp + b)
                f3[part] = dp
                s0, s1, s2 = carry
                return s0 + jnp.sum(dp, axis=0), s1 + jnp.sum(dp * a, axis=0), s2 + jnp.sum(dp * b_, axis=0)

            tx[40 + n], tx[44 + n], tx[48 + n] = five(body, zero_stats + zero_stats[:1])
            return carry

        lax.fori_loop(0, 4, first_block_slopes, 0)
        sync(7, 40, 12)

        def third_back(n, carry):
            s_du, s_d3, s_dp = both(40 + n), both(44 + n), both(48 + n)
            dg[n] = s_d3
            dg[4 + n] = s_dp
            dg[8 + n] = s_du
            dg[12 + n] = s_du
            m_du = s_du * (1.0 / total_out)
            norm_back(pt.at[4 + n], 0, f3, n * PP, f0, n * PP, par[n] * inv[2 + n], m_du, s_d3 * (1.0 / total_out))
            norm_back(u2, n * RW, f3, n * PP, f1, n * PP, par[4 + n] * inv[6 + n], m_du, s_dp * (1.0 / total_out))
            return carry

        lax.fori_loop(0, 4, third_back, 0)
        grad = nt(pt[4], wh[0:512, :])
        for n in range(1, 4):
            grad += nt(pt[4 + n], wh[n * 512 : (n + 1) * 512, :])
        dh[...] = grad.astype(BF16)
        dh_send = remote(dh, dh, C_DH, C_DH, (0, d, r))
        dh_send.start()

        d4_send = remote(d4, d4, C_D4, C_D4, (2, d, r))
        d4_send.start()
        def drain_pieces(i, carry):
            piece_copy(W_PEER, i, quarter, peer).wait_send()
            piece_copy(W_Z, i, quarter, z_dev).wait_send()
            piece_copy(W_ON, i, other_z + d, peer).wait_send()
            return carry

        lax.fori_loop(0, N_PIECE, drain_pieces, 0)
        say_ready()
        o1_copy(2).start()
        o1_copy(3).start()
        sends = [d4_send, dh_send, d5_send, h5_send, z6_send] + [o1_copy(n) for n in range(4)]
        for first, last, sem, chip in ((0, 4, C_DG2, 2), (4, 12, C_DG3, 3)):
            copy = remote(dgx.at[first:last], dgx.at[first:last], sem, sem, (chip, d, r))
            copy.start()
            sends.append(copy)
        for slot, k in enumerate((0, 2, 3)):
            copy = remote(pt.at[k], ob, C_SHARE + slot, C_SHARE, (k, d, r))
            copy.start()
            sends.append(copy)

        def shortcut_share(k):
            g = nt(u2[0:RW, :], wh[2048 + k * 256 : 2304 + k * 256, :])
            for n in range(1, 4):
                g += nt(u2[n * RW : (n + 1) * RW, :], wh[2048 + n * 1024 + k * 256 : 2304 + n * 1024 + k * 256, :])
            return g.astype(BF16)

        places = ((h4.at[:, 0:256], 0), (h4.at[:, 256:512], 2), (pt.at[8, :, 0:256], 3))

        def share_copy(slot):
            place, k = places[slot]
            return remote(place, r1, C_GP + slot, C_GP, (k, d, r))

        def shortcut_shares():
            h4_send.wait_send()
            for slot, (place, k) in enumerate(places):
                place[...] = shortcut_share(k)
                share_copy(slot).start()
            r1[...] = shortcut_share(1)

        def compute(t):
            @pl.when(t < 4)
            def _():
                left = h2[:, pl.ds(pl.multiple_of(t * 128, 128), 128)]
                for n in range(4):
                    put_chunk(t, n, tn(left, pt[4 + n]))

            @pl.when(t >= 4)
            def _():
                m = t - 4
                left = sx[rows((m // 4) * RW, RW), pl.ds(pl.multiple_of(lax.rem(m, 4) * 128, 128), 128)]
                for n in range(4):
                    put_chunk(t, n, tn(left, u2[n * RW : (n + 1) * RW, :]))

        sum_gradients(12, compute, lambda t: t * 512, lambda t: t, True, 0, {1: shortcut_shares})
        for copy in sends:
            copy.wait_send()
        for slot in range(3):
            share_copy(slot).wait_send()


    @pl.when(p == 2)
    def _():
        for k, slot in ((0, 0), (1, 1), (2, 8), (3, 9)):
            parx[k] = par[slot]
        par_send = remote(parx.at[0:4], parx.at[0:4], C_PAR2, C_PAR2, (1, d, r))
        par_send.start()

        def piece_copy(i):
            part = wx.at[rows(i * 512 + quarter * 128, 128)]
            return pltpu.make_async_remote_copy(
                src_ref=part, dst_ref=part, send_sem=wss.at[W_OWN, i], recv_sem=wrs.at[W_OWN, i],
                device_id=(1, d, r), device_id_type=MESH,
            )

        put_w = put_narrow(wx, lambda i: i * 512 + quarter * 128)

        def put(i):
            put_w(i)
            piece_copy(i).start()

        load_weights(every_fourth, 13, 0, 13, put)
        pb[...] = jnp.zeros_like(pb)
        clear_patch_pad()

        def drain(i, carry):
            piece_copy(i).wait_send()
            return carry

        lax.fori_loop(0, 13, drain, 0)
        say_ready()
        remote(h4, h4, C_H4, C_H4, (2, d, r)).wait_recv()
        pb[1:8, 1:8] = h4[0:RV, :].astype(F32).reshape(7, 7, 8, BLK)
        build_patches(plain_base)
        remote(d5, d5, C_D5, C_D5, (2, d, r)).wait_recv()

        def compute(t):
            @pl.when(t < 9)
            def _():
                wh[rows(t * 512, 512), :] = tn(pt[t], d5[...]).astype(BF16)

            @pl.when(t == 9)
            def _():
                remote(d4, d4, C_D4, C_D4, (2, d, r)).wait_recv()
                for n in range(4):
                    part = u0.at[n * RW : (n + 1) * RW]
                    remote(part, part, C_O1 + n, C_O1 + n, (2, d, r)).wait_recv()

            @pl.when(t >= 9)
            def _():
                wh[rows(t * 512, 512), :] = tn(u0[rows((t - 9) * RW, RW), :], d4[...]).astype(BF16)

        def norm_grads():
            remote(dgx.at[0:4], dgx.at[0:4], C_DG2, C_DG2, (2, d, r)).wait_recv()
            dg[0], dg[1], dg[8], dg[9] = dgx[0], dgx[1], dgx[2], dgx[3]

        sum_gradients(
            13, compute, lambda t: t * 512, lambda t: lax.rem(t + 4, 13), False, 0, {10: norm_grads}
        )
        par_send.wait_send()

    @pl.when(p == 3)
    def _():
        for k in range(4):
            parx[4 + k] = par[k]
            parx[8 + k] = par[8 + k]
        par_send = remote(parx.at[4:12], parx.at[4:12], C_PAR3, C_PAR3, (1, d, r))
        par_send.start()
        say_ready()

        def put(i):
            for n in range(4):
                for j in range(4):
                    wx[rows(6656 + n * 512 + quarter * 128 + i * 32, 32), j * 128 : (j + 1) * 128] = st[
                        pl.ds(4 * n + j, 32, stride=16), :
                    ].astype(BF16)

        load_weights(four_rows, 4, 0, 4, put)
        zero_rest(4)
        pl.semaphore_wait(go, 1)

        def piece_copy(n):
            part = wx.at[rows(6656 + n * 512 + quarter * 128, 128)]
            return pltpu.make_async_remote_copy(
                src_ref=part, dst_ref=part, send_sem=wss.at[W_OWN, 13 + n], recv_sem=wrs.at[W_OWN, 13 + n],
                device_id=(1, d, r), device_id_type=MESH,
            )

        for n in range(4):
            piece_copy(n).start()
        remote(h5, h5, C_H5, C_H5, (3, d, r)).wait_recv()
        remote(u1, u1, C_Z6, C_Z6, (3, d, r)).wait_recv()

        def compute(t):
            left = h5[:, pl.ds(pl.multiple_of(t * 128, 128), 128)]
            for n in range(4):
                put_chunk(t, n, tn(left, u1[n * RW : (n + 1) * RW, :]))

        def norm_grads():
            remote(dgx.at[4:12], dgx.at[4:12], C_DG3, C_DG3, (3, d, r)).wait_recv()
            for k in range(4):
                dg[k] = dgx[4 + k]
                dg[8 + k] = dgx[8 + k]

        sum_gradients(4, compute, lambda t: t * 512, lambda t: t, True, 0, {1: norm_grads})
        for n in range(4):
            piece_copy(n).wait_send()
        par_send.wait_send()

    @pl.when(p != 1)
    def _():
        remote(ob, ob, C_SHARE, C_SHARE, (p, d, r)).wait_recv()
        remote(r1, r1, C_GP, C_GP, (p, d, r)).wait_recv()

    @pl.when(p != 0)
    def _():
        remote(r0, r0, C_GI, C_GI, (p, d, r)).wait_recv()

    out[...] = ob[0:RV, :].astype(F32).reshape(PIX_OUT, 8, BLK).astype(BF16)
    f0[0:PP, :, 0:256] = r1[...].astype(F32).reshape(PP, 8, 256)

    def place(a, carry):
        m = r0[rows(a * 224, 224), :].astype(F32).reshape(28, 8, 256)
        first = m[0:14].reshape(7, 2, 8, 256)
        even = first[:, 0] + f0[pl.ds(a * 7, 7), :, 0:256]
        f3[pl.ds(a * 28, 14), :, 0:256] = jnp.stack([even, first[:, 1]], axis=1).reshape(14, 8, 256)
        f3[pl.ds(a * 28 + 14, 14), :, 0:256] = m[14:28]
        return carry

    lax.fori_loop(0, 7, place, 0)
    gi_copy = pltpu.make_async_copy(f3.at[0:PIX_IN, :, 0:256], gi, ls.at[17])
    gi_copy.start()
    gi_copy.wait()


def one_kernel(images, section_weights, bn_gain, bn_bias, width, bn_set, gate, cotangent):
    meta = jnp.concatenate(
        [width.astype(F32), bn_set.astype(F32), gate.astype(F32)[:, None], jnp.zeros((MB, 123), F32)], axis=1
    )
    any_space = pl.BlockSpec(memory_space=pl.ANY)
    vmem = pl.BlockSpec(memory_space=pltpu.VMEM)
    out, gi, dw, dgb = pl.pallas_call(
        whole_kernel,
        out_shape=(
            jax.ShapeDtypeStruct((PIX_OUT, 8, BLK), BF16),
            jax.ShapeDtypeStruct((PIX_IN, 8, 256), F32),
            jax.ShapeDtypeStruct((P_SIZE // 128, 128), BF16),
            jax.ShapeDtypeStruct((8, 4096), F32),
        ),
        in_specs=[any_space, any_space, vmem, vmem, vmem, any_space],
        out_specs=(vmem, any_space, any_space, vmem),
        scratch_shapes=[
            pltpu.VMEM((4, 28, 8, 1024), BF16),
            pltpu.VMEM((RING, 1, SUB), BF16),
            pltpu.VMEM((1024, 128), F32),
            pltpu.VMEM((6656, BLK), BF16),
            pltpu.VMEM((8768, BLK), BF16),
            pltpu.VMEM((4 * PP, 8, BLK), F32),
            pltpu.VMEM((4 * PP, 8, BLK), F32),
            pltpu.VMEM((4 * PP, 8, BLK), F32),
            pltpu.VMEM((4 * PP, 8, BLK), F32),
            pltpu.VMEM((2, PP, 8, BLK), F32),
            pltpu.VMEM((16, 16, 8, BLK), F32),
            pltpu.VMEM((9, RW, BLK), BF16),
            pltpu.VMEM((4 * RW, BLK), BF16),
            pltpu.VMEM((4 * RW, BLK), BF16),
            pltpu.VMEM((4 * RW, BLK), BF16),
            pltpu.VMEM((2 * RW, BLK), BF16),
            pltpu.VMEM((PP, 8, C_OUT), BF16),
            pltpu.VMEM((RW, BLK), BF16),
            pltpu.VMEM((RW, BLK), BF16),
            pltpu.VMEM((RW, BLK), BF16),
            pltpu.VMEM((RW, BLK), BF16),
            pltpu.VMEM((RW, BLK), BF16),
            pltpu.VMEM((RW, BLK), BF16),
            pltpu.VMEM((8 * PIX_IN, 256), BF16),
            pltpu.VMEM((RW, 256), BF16),
            pltpu.VMEM((RW, BLK), BF16),
            pltpu.VMEM((52, 8, BLK), F32),
            pltpu.VMEM((52, 8, BLK), F32),
            pltpu.VMEM((16, 8, BLK), F32),
            pltpu.VMEM((16, 8, BLK), F32),
            pltpu.VMEM((12, 8, BLK), F32),
            pltpu.VMEM((16, 8, BLK), F32),
            pltpu.VMEM((12, 8, BLK), F32),
            pltpu.VMEM((4, 1024, 128), BF16),
            pltpu.VMEM((3328, BLK), BF16),
            pltpu.VMEM((2, 8, 4096), F32),
            pltpu.VMEM((8, 4096), F32),
            pltpu.SemaphoreType.DMA((18,)),
            pltpu.SemaphoreType.DMA((N_SEM,)),
            pltpu.SemaphoreType.DMA((N_SEM,)),
            pltpu.SemaphoreType.DMA((4, N_PIECE)),
            pltpu.SemaphoreType.DMA((4, N_PIECE)),
            pltpu.SemaphoreType.DMA((5, 13)),
            pltpu.SemaphoreType.DMA((5, 13)),
            pltpu.SemaphoreType.REGULAR((2,)),
            pltpu.SemaphoreType.REGULAR,
        ],
        compiler_params=pltpu.CompilerParams(
            collective_id=0, has_side_effects=True, vmem_limit_bytes=64 * 1024 * 1024
        ),
    )(
        jnp.transpose(images, (1, 0, 2)),
        section_weights,
        bn_gain[0],
        bn_bias[0],
        meta,
        jnp.transpose(cotangent, (1, 0, 2)),
    )
    dw = dw.astype(F32).reshape(1, P_SIZE)
    return (
        jnp.transpose(out, (1, 0, 2)),
        jnp.transpose(gi, (1, 0, 2)),
        dw,
        dgb[None, :4],
        dgb[None, 4:],
    )


def solution(mesh):
    sizes = dict(mesh.shape)
    fits = sizes["pipe"] == 4 and sizes["dp"] == 2 and sizes["rep"] == 4
    placed = (
        P(("dp", "rep"), None, None),
        P("pipe", None),
        P("pipe", None, None),
        P("pipe", None, None),
        P(),
        P(),
        P(),
        P(("dp", "rep"), None, None),
    )
    return jax.shard_map(
        one_kernel if fits else on_device,
        mesh=mesh,
        in_specs=placed,
        out_specs=(
            P(("dp", "rep"), None, "pipe"),
            P(("dp", "rep"), None, "pipe"),
            P("pipe", None),
            P("pipe", None, None),
            P("pipe", None, None),
        ),
        check_vma=False,
    )
```

```python
import jax
import jax.numpy as jnp
from jax import lax
from jax.experimental import pallas as pl
from jax.experimental.pallas import tpu as pltpu
from jax.sharding import PartitionSpec as P

C_IN = 1024
C_MID = 512
C_OUT = 2048
SIDE = 14
NSETS = 4
MB = 8
IMG_B = 1
OSIDE = 7
PIX_IN = 196
PIX_OUT = 49
IMG_DEV = 8
P_SIZE = 3407872


EPSILON = 1e-05


def for_sending(array):

    def short(part):
        return part.astype(jnp.bfloat16) if part.dtype == jnp.float32 else part

    return jax.tree.map(short, array)


def shifted(value, axis, steps):
    count = lax.axis_size(axis)
    first, last = (max(0, -steps), min(count, count - steps))
    return lax.ppermute(value, axis, [(source, source + steps) for source in range(first, last)])


def smooth(inputs):
    return inputs * jax.nn.sigmoid(inputs)


def smooth_slope(inputs):
    gate_sig = jax.nn.sigmoid(inputs)
    return gate_sig * (1.0 + inputs * (1.0 - gate_sig))


def matmul(left_op, right_op):
    return jnp.dot(left_op, right_op, preferred_element_type=jnp.float32)


def matmul_left_t(left_op, right_op):
    return lax.dot_general(
        left_op, right_op, (((0,), (0,)), ((), ())), preferred_element_type=jnp.float32
    )


def matmul_right_t(left_op, right_op):
    return lax.dot_general(
        left_op, right_op, (((1,), (1,)), ((), ())), preferred_element_type=jnp.float32
    )


def patches(planes, stride):
    images, side_len, channels = (planes.shape[0], planes.shape[1], planes.shape[3])
    out_side = side_len // stride
    padded = jnp.pad(planes, ((0, 0), (1, 1), (1, 1), (0, 0)))
    pieces = []
    for row_off in range(3):
        for col_off in range(3):
            pieces.append(
                padded[
                    :,
                    row_off : row_off + stride * (out_side - 1) + 1 : stride,
                    col_off : col_off + stride * (out_side - 1) + 1 : stride,
                    :,
                ]
            )
    return jnp.concatenate(pieces, axis=3).reshape(images * out_side * out_side, 9 * channels)


def unpatch(columns, images, side_len, stride, channels):
    out_side = side_len // stride
    pieces = columns.reshape(images, out_side, out_side, 9, channels)
    padded = jnp.zeros((images, side_len + 2, side_len + 2, channels), jnp.float32)
    for row_off in range(3):
        for col_off in range(3):
            padded = padded.at[
                :,
                row_off : row_off + stride * (out_side - 1) + 1 : stride,
                col_off : col_off + stride * (out_side - 1) + 1 : stride,
                :,
            ].add(pieces[:, :, :, row_off * 3 + col_off, :])
    return padded[:, 1 : side_len + 1, 1 : side_len + 1, :]


def group_moments(sums_local, squares_local):
    return (
        lax.psum(sums_local.astype(jnp.bfloat16), "dp").astype(jnp.float32),
        lax.psum(squares_local.astype(jnp.bfloat16), "dp").astype(jnp.float32),
    )


def group_grad_sums(bias_local, gain_local):
    return (
        lax.psum(bias_local.astype(jnp.bfloat16), "dp").astype(jnp.float32),
        lax.psum(gain_local.astype(jnp.bfloat16), "dp").astype(jnp.float32),
    )


def stats_of(sum_all, square_all, start, count, row_total):
    center = sum_all[start : start + count] / row_total
    inv_std = lax.rsqrt(square_all[start : start + count] / row_total - center * center + EPSILON)
    return (center, inv_std)


def norm_grad(slope_in, normed, gain_vec, inv_std, sum_bias, sum_gain, row_total):
    return (
        gain_vec * inv_std * (slope_in - sum_bias / row_total - normed * (sum_gain / row_total))
    ).astype(jnp.bfloat16)


def on_device(images, section_weights, bn_gain, bn_bias, width, bn_set, gate, cotangent):
    section_idx = lax.axis_index("pipe")
    pipe_count = lax.axis_size("pipe")
    dp_count = lax.axis_size("dp")
    flat_weights = section_weights[0]
    gain_table = bn_gain[0]
    bias_table = bn_bias[0]
    rows_in = IMG_B * PIX_IN
    rows_out = IMG_B * PIX_OUT
    total_in = float(rows_in * dp_count)
    total_out = float(rows_out * dp_count)
    wide = 2 * C_OUT
    scr_len = IMG_B * max(PIX_IN * C_MID, PIX_OUT * wide)
    image_blocks = images.reshape(MB, IMG_B, PIX_IN, C_IN)
    pad_mid = jnp.zeros((wide - 2 * C_MID,), jnp.float32)
    zero_wide = jnp.zeros((wide,), jnp.float32)
    zero_scr = jnp.zeros((scr_len,), jnp.float32)
    zero_mid = jnp.zeros((rows_out, C_MID), jnp.bfloat16)
    zero_res = jnp.zeros((rows_out, C_OUT), jnp.bfloat16)
    zero_rows = jnp.zeros((rows_out, C_OUT), jnp.float32)
    zero_input = jnp.zeros((IMG_B, PIX_IN, C_IN), jnp.float32)

    def pack(values):
        flat = values.reshape(-1).astype(jnp.float32)
        return jnp.pad(flat, (0, scr_len - flat.shape[0]))

    def unpack(buffer, rows, cols):
        return buffer[: rows * cols].reshape(rows, cols)

    def place(vec, start):
        return jnp.pad(vec, (start, wide - start - vec.shape[0]))

    def add_weight(acc, grad, offset, valid):
        flat = grad.reshape(-1)
        return acc.at[offset : offset + flat.shape[0]].add(jnp.where(valid, flat, 0.0))

    def weights_zero():
        split_at = C_IN * C_MID
        return (
            flat_weights[:split_at].reshape(C_IN, C_MID),
            flat_weights[split_at : split_at + 9 * C_MID * C_MID].reshape(9 * C_MID, C_MID),
        )

    def weights_one():
        split_at = C_MID * C_OUT
        return (
            flat_weights[:split_at].reshape(C_MID, C_OUT),
            flat_weights[split_at : split_at + C_IN * C_OUT].reshape(C_IN, C_OUT),
        )

    def weights_two():
        split_at = C_OUT * C_MID
        return (
            flat_weights[:split_at].reshape(C_OUT, C_MID),
            flat_weights[split_at : split_at + 9 * C_MID * C_MID].reshape(9 * C_MID, C_MID),
        )

    def short_rows(image_block):
        return image_block.reshape(IMG_B, SIDE, SIDE, C_IN)[:, ::2, ::2, :].reshape(rows_out, C_IN)

    def local_stats(values, start):
        return (
            place(jnp.sum(values, axis=0), start),
            place(jnp.sum(values * values, axis=0), start),
        )

    def fwd_a_zero(ops):
        conv_a, conv_b = weights_zero()
        pre_one = matmul(ops[0].reshape(rows_in, C_IN), conv_a)
        sums_local, squares_local = local_stats(pre_one, 0)
        return (pack(pre_one), sums_local, squares_local)

    def fwd_a_one(ops):
        conv_a, conv_b = weights_one()
        pre_both = jnp.concatenate(
            [matmul(ops[1], conv_a), matmul(short_rows(ops[0]), conv_b)], axis=1
        )
        sums_local, squares_local = local_stats(pre_both, 0)
        return (pack(pre_both), sums_local, squares_local)

    def fwd_a_two(ops):
        conv_a, conv_b = weights_two()
        pre_four = matmul(ops[2], conv_a)
        sums_local, squares_local = local_stats(pre_four, 0)
        return (pack(pre_four), sums_local, squares_local)

    def fwd_a_three(ops):
        conv_a = flat_weights[: C_MID * C_OUT].reshape(C_MID, C_OUT)
        pre_six = matmul(ops[1], conv_a)
        sums_local, squares_local = local_stats(pre_six, 0)
        return (pack(pre_six), sums_local, squares_local)

    def fwd_b_zero(args):
        ops, scratch, sum_all, square_all = args
        conv_a, conv_b = weights_zero()
        gain_vec, bias_vec, mask_vec = (ops[3], ops[4], ops[5])
        pre_one = unpack(scratch, rows_in, C_MID)
        center_one, inv_one = stats_of(sum_all, square_all, 0, C_MID, total_in)
        hidden_one = (
            smooth((pre_one - center_one) * inv_one * gain_vec[:C_MID] + bias_vec[:C_MID])
            * mask_vec
        ).astype(jnp.bfloat16)
        pre_two = matmul(patches(hidden_one.reshape(IMG_B, SIDE, SIDE, C_MID), 2), conv_b)
        sums_local, squares_local = local_stats(pre_two, C_MID)
        return (pack(pre_two), sums_local, squares_local)

    def fwd_b_pass(args):
        return (args[1], zero_wide, zero_wide)

    def fwd_b_two(args):
        ops, scratch, sum_all, square_all = args
        conv_a, conv_b = weights_two()
        gain_vec, bias_vec, mask_vec = (ops[3], ops[4], ops[5])
        pre_four = unpack(scratch, rows_out, C_MID)
        center_four, inv_four = stats_of(sum_all, square_all, 0, C_MID, total_out)
        hidden_four = (
            smooth((pre_four - center_four) * inv_four * gain_vec[:C_MID] + bias_vec[:C_MID])
            * mask_vec
        ).astype(jnp.bfloat16)
        pre_five = matmul(patches(hidden_four.reshape(IMG_B, OSIDE, OSIDE, C_MID), 1), conv_b)
        sums_local, squares_local = local_stats(pre_five, C_MID)
        return (pack(pre_five), sums_local, squares_local)

    def fwd_c_double(args, first_total, send_res):
        ops, scratch, sum_all, square_all = args
        gain_vec, bias_vec, mask_vec = (ops[3], ops[4], ops[5])
        pre_two = unpack(scratch, rows_out, C_MID)
        center_one, inv_one = stats_of(sum_all, square_all, 0, C_MID, first_total)
        center_two, inv_two = stats_of(sum_all, square_all, C_MID, C_MID, total_out)
        hidden_two = (
            smooth(
                (pre_two - center_two) * inv_two * gain_vec[C_MID : 2 * C_MID]
                + bias_vec[C_MID : 2 * C_MID]
            )
            * mask_vec
        ).astype(jnp.bfloat16)
        centers = jnp.concatenate([center_one, center_two, pad_mid])
        scales = jnp.concatenate([inv_one, inv_two, pad_mid])
        return (hidden_two, send_res, centers, scales, zero_rows)

    def fwd_c_zero(args):
        return fwd_c_double(args, total_in, zero_res)

    def fwd_c_two(args):
        return fwd_c_double(args, total_out, args[0][2])

    def fwd_c_one(args):
        ops, scratch, sum_all, square_all = args
        gain_vec, bias_vec = (ops[3], ops[4])
        pre_both = unpack(scratch, rows_out, wide)
        centers, scales = stats_of(sum_all, square_all, 0, wide, total_out)
        activ = (pre_both - centers) * scales * gain_vec + bias_vec
        block_out = smooth(activ[:, :C_OUT] + activ[:, C_OUT:]).astype(jnp.bfloat16)
        return (zero_mid, block_out, centers, scales, zero_rows)

    def fwd_c_three(args):
        ops, scratch, sum_all, square_all = args
        gain_vec, bias_vec, gate_val = (ops[3], ops[4], ops[6])
        pre_six = unpack(scratch, rows_out, C_OUT)
        centers, scales = stats_of(sum_all, square_all, 0, wide, total_out)
        residual = ops[2].astype(jnp.float32)
        merged = smooth(
            residual
            + (pre_six - centers[:C_OUT]) * scales[:C_OUT] * gain_vec[:C_OUT]
            + bias_vec[:C_OUT]
        )
        result = gate_val * merged + (1.0 - gate_val) * residual
        return (zero_mid, zero_res, centers, scales, result)

    def bwd_a_double(ops, flat_in, conv_a, conv_b, side_len, stride):
        centers, scales, grad_mid = (ops[3], ops[4], ops[5])
        gain_vec, bias_vec, mask_vec = (ops[8], ops[9], ops[10])
        norm_one = (matmul(flat_in, conv_a) - centers[:C_MID]) * scales[:C_MID]
        hidden_one = (smooth(norm_one * gain_vec[:C_MID] + bias_vec[:C_MID]) * mask_vec).astype(
            jnp.bfloat16
        )
        columns = patches(hidden_one.reshape(IMG_B, side_len, side_len, C_MID), stride)
        norm_two = (matmul(columns, conv_b) - centers[C_MID : 2 * C_MID]) * scales[
            C_MID : 2 * C_MID
        ]
        act_two = norm_two * gain_vec[C_MID : 2 * C_MID] + bias_vec[C_MID : 2 * C_MID]
        slope_two = grad_mid.astype(jnp.float32) * mask_vec * smooth_slope(act_two)
        return (
            pack(slope_two),
            pack(norm_two),
            pack(norm_one),
            place(jnp.sum(slope_two, axis=0), C_MID),
            place(jnp.sum(slope_two * norm_two, axis=0), C_MID),
        )

    def bwd_a_zero(ops):
        conv_a, conv_b = weights_zero()
        return bwd_a_double(ops, ops[0].reshape(rows_in, C_IN), conv_a, conv_b, SIDE, 2)

    def bwd_a_two(ops):
        conv_a, conv_b = weights_two()
        return bwd_a_double(ops, ops[2], conv_a, conv_b, OSIDE, 1)

    def bwd_a_one(ops):
        conv_a, conv_b = weights_one()
        centers, scales, grad_res = (ops[3], ops[4], ops[6])
        gain_vec, bias_vec = (ops[8], ops[9])
        pre_both = jnp.concatenate(
            [matmul(ops[1], conv_a), matmul(short_rows(ops[0]), conv_b)], axis=1
        )
        normed = (pre_both - centers) * scales
        activ = normed * gain_vec + bias_vec
        slope_in = grad_res.astype(jnp.float32) * smooth_slope(activ[:, :C_OUT] + activ[:, C_OUT:])
        both = jnp.concatenate([slope_in, slope_in], axis=1)
        return (
            pack(both),
            pack(normed),
            zero_scr,
            jnp.sum(both, axis=0),
            jnp.sum(both * normed, axis=0),
        )

    def bwd_a_three(ops):
        conv_a = flat_weights[: C_MID * C_OUT].reshape(C_MID, C_OUT)
        centers, scales = (ops[3], ops[4])
        gain_vec, bias_vec, gate_val = (ops[8], ops[9], ops[11])
        normed = (matmul(ops[1], conv_a) - centers[:C_OUT]) * scales[:C_OUT]
        joined = ops[2].astype(jnp.float32) + normed * gain_vec[:C_OUT] + bias_vec[:C_OUT]
        through = ops[7].astype(jnp.float32) * gate_val * smooth_slope(joined)
        return (
            pack(through),
            pack(normed),
            zero_scr,
            place(jnp.sum(through, axis=0), 0),
            place(jnp.sum(through * normed, axis=0), 0),
        )

    def bwd_b_double(args, conv_b, rows_first, side_len, stride, offset):
        ops, first_buf, second_buf, third_buf, sum_bias, sum_gain, acc = args
        scales = ops[4]
        gain_vec, bias_vec, mask_vec, valid = (ops[8], ops[9], ops[10], ops[12])
        slope_two = unpack(first_buf, rows_out, C_MID)
        norm_two = unpack(second_buf, rows_out, C_MID)
        norm_one = unpack(third_buf, rows_first, C_MID)
        grad_two = norm_grad(
            slope_two,
            norm_two,
            gain_vec[C_MID : 2 * C_MID],
            scales[C_MID : 2 * C_MID],
            sum_bias[C_MID : 2 * C_MID],
            sum_gain[C_MID : 2 * C_MID],
            total_out,
        )
        act_one = norm_one * gain_vec[:C_MID] + bias_vec[:C_MID]
        hidden_one = (smooth(act_one) * mask_vec).astype(jnp.bfloat16)
        columns = patches(hidden_one.reshape(IMG_B, side_len, side_len, C_MID), stride)
        acc = add_weight(acc, matmul_left_t(columns, grad_two), offset, valid)
        hid_grad = unpatch(
            matmul_right_t(grad_two, conv_b), IMG_B, side_len, stride, C_MID
        ).reshape(rows_first, C_MID)
        slope_one = hid_grad * mask_vec * smooth_slope(act_one)
        return (
            pack(slope_one),
            second_buf,
            third_buf,
            place(jnp.sum(slope_one, axis=0), 0),
            place(jnp.sum(slope_one * norm_one, axis=0), 0),
            acc,
        )

    def bwd_b_zero(args):
        conv_a, conv_b = weights_zero()
        return bwd_b_double(args, conv_b, rows_in, SIDE, 2, C_IN * C_MID)

    def bwd_b_two(args):
        conv_a, conv_b = weights_two()
        return bwd_b_double(args, conv_b, rows_out, OSIDE, 1, C_OUT * C_MID)

    def bwd_b_pass(args):
        return (args[1], args[2], args[3], zero_wide, zero_wide, args[6])

    def side_none():
        return zero_input

    def bwd_c_zero(args):
        ops, first_buf, second_buf, third_buf, sum_bias, sum_gain, acc = args
        conv_a, conv_b = weights_zero()
        scales, gain_vec, valid = (ops[4], ops[8], ops[12])
        flat_in = ops[0].reshape(rows_in, C_IN)
        slope_one = unpack(first_buf, rows_in, C_MID)
        norm_one = unpack(third_buf, rows_in, C_MID)
        grad_one = norm_grad(
            slope_one,
            norm_one,
            gain_vec[:C_MID],
            scales[:C_MID],
            sum_bias[:C_MID],
            sum_gain[:C_MID],
            total_in,
        )
        acc = add_weight(acc, matmul_left_t(flat_in, grad_one), 0, valid)
        side_out = matmul_right_t(grad_one, conv_a).reshape(IMG_B, PIX_IN, C_IN)
        return (zero_mid, zero_res, acc, side_out)

    def bwd_c_one(args):
        ops, first_buf, second_buf, third_buf, sum_bias, sum_gain, acc = args
        conv_a, conv_b = weights_one()
        scales, gain_vec, valid = (ops[4], ops[8], ops[12])
        short_in = short_rows(ops[0])
        both = unpack(first_buf, rows_out, wide)
        normed = unpack(second_buf, rows_out, wide)
        grad_both = norm_grad(both, normed, gain_vec, scales, sum_bias, sum_gain, total_out)
        acc = add_weight(acc, matmul_left_t(ops[1], grad_both[:, :C_OUT]), 0, valid)
        acc = add_weight(acc, matmul_left_t(short_in, grad_both[:, C_OUT:]), C_MID * C_OUT, valid)
        mid_grad = matmul_right_t(grad_both[:, :C_OUT], conv_a).astype(jnp.bfloat16)
        short_grad = matmul_right_t(grad_both[:, C_OUT:], conv_b).reshape(
            IMG_B, OSIDE, 1, OSIDE, 1, C_IN
        )
        side_out = jnp.pad(short_grad, ((0, 0), (0, 0), (0, 1), (0, 0), (0, 1), (0, 0))).reshape(
            IMG_B, PIX_IN, C_IN
        )
        return (mid_grad, zero_res, acc, side_out)

    def bwd_c_two(args):
        ops, first_buf, second_buf, third_buf, sum_bias, sum_gain, acc = args
        conv_a, conv_b = weights_two()
        scales, grad_res, gain_vec, valid = (ops[4], ops[6], ops[8], ops[12])
        slope_four = unpack(first_buf, rows_out, C_MID)
        norm_four = unpack(third_buf, rows_out, C_MID)
        grad_four = norm_grad(
            slope_four,
            norm_four,
            gain_vec[:C_MID],
            scales[:C_MID],
            sum_bias[:C_MID],
            sum_gain[:C_MID],
            total_out,
        )
        acc = add_weight(acc, matmul_left_t(ops[2], grad_four), 0, valid)
        carried_grad = (grad_res.astype(jnp.float32) + matmul_right_t(grad_four, conv_a)).astype(
            jnp.bfloat16
        )
        return (zero_mid, carried_grad, acc, side_none())

    def bwd_c_three(args):
        ops, first_buf, second_buf, third_buf, sum_bias, sum_gain, acc = args
        conv_a = flat_weights[: C_MID * C_OUT].reshape(C_MID, C_OUT)
        scales, gain_vec, gate_val, valid = (ops[4], ops[8], ops[11], ops[12])
        through = unpack(first_buf, rows_out, C_OUT)
        normed = unpack(second_buf, rows_out, C_OUT)
        res_grad = (through + (1.0 - gate_val) * ops[7].astype(jnp.float32)).astype(jnp.bfloat16)
        grad_six = norm_grad(
            through,
            normed,
            gain_vec[:C_OUT],
            scales[:C_OUT],
            sum_bias[:C_OUT],
            sum_gain[:C_OUT],
            total_out,
        )
        acc = add_weight(acc, matmul_left_t(ops[1], grad_six), 0, valid)
        mid_grad = matmul_right_t(grad_six, conv_a).astype(jnp.bfloat16)
        return (mid_grad, res_grad, acc, side_none())

    def select_params(micro_idx):
        block_id = section_idx // 2
        width_val = width[micro_idx, block_id]
        set_val = bn_set[micro_idx, block_id]
        onehot = (jnp.arange(NSETS) == set_val).astype(jnp.float32)
        gain_vec = jnp.sum(onehot[:, None] * gain_table, axis=0)
        bias_vec = jnp.sum(onehot[:, None] * bias_table, axis=0)
        mask_vec = (jnp.arange(C_MID) < width_val).astype(jnp.float32)
        gate_val = gate[micro_idx].astype(jnp.float32)
        return (gain_vec, bias_vec, mask_vec, gate_val, onehot)

    fwd_first = [fwd_a_zero, fwd_a_one, fwd_a_two, fwd_a_three]
    fwd_second = [fwd_b_zero, fwd_b_pass, fwd_b_two, fwd_b_pass]
    fwd_third = [fwd_c_zero, fwd_c_one, fwd_c_two, fwd_c_three]
    bwd_first = [bwd_a_zero, bwd_a_one, bwd_a_two, bwd_a_three]
    bwd_second = [bwd_b_zero, bwd_b_pass, bwd_b_two, bwd_b_pass]
    bwd_third = [bwd_c_zero, bwd_c_one, bwd_c_two, bwd_c_three]

    def forward_tick(tick_no, state_in):
        recv_mid, recv_res, stash_mid, stash_res, stash_center, stash_scale, out_rows = state_in
        micro_raw = tick_no - section_idx
        is_valid = (micro_raw >= 0) & (micro_raw < MB)
        micro_idx = jnp.clip(micro_raw, 0, MB - 1)
        gain_vec, bias_vec, mask_vec, gate_val, onehot = select_params(micro_idx)
        ops = (image_blocks[micro_idx], recv_mid, recv_res, gain_vec, bias_vec, mask_vec, gate_val)
        scratch, sums_local, squares_local = lax.switch(section_idx, fwd_first, ops)
        sum_first, square_first = group_moments(sums_local, squares_local)
        scratch, sums_local, squares_local = lax.switch(
            section_idx, fwd_second, (ops, scratch, sum_first, square_first)
        )
        sum_second, square_second = group_moments(sums_local, squares_local)
        send_mid, send_res, centers, scales, result = lax.switch(
            section_idx,
            fwd_third,
            (ops, scratch, sum_first + sum_second, square_first + square_second),
        )
        stash_mid = stash_mid.at[micro_idx].set(jnp.where(is_valid, recv_mid, stash_mid[micro_idx]))
        stash_res = stash_res.at[micro_idx].set(jnp.where(is_valid, recv_res, stash_res[micro_idx]))
        stash_center = stash_center.at[micro_idx].set(
            jnp.where(is_valid, centers, stash_center[micro_idx])
        )
        stash_scale = stash_scale.at[micro_idx].set(
            jnp.where(is_valid, scales, stash_scale[micro_idx])
        )
        out_rows = out_rows.at[micro_idx].set(jnp.where(is_valid, result, out_rows[micro_idx]))
        recv_mid, recv_res = (
            shifted(for_sending(send_mid), "pipe", 1).astype(send_mid.dtype),
            shifted(for_sending(send_res), "pipe", 1).astype(send_res.dtype),
        )
        return (recv_mid, recv_res, stash_mid, stash_res, stash_center, stash_scale, out_rows)

    forward_init = (
        zero_mid,
        zero_res,
        jnp.zeros((MB, rows_out, C_MID), jnp.bfloat16),
        jnp.zeros((MB, rows_out, C_OUT), jnp.bfloat16),
        jnp.zeros((MB, wide), jnp.float32),
        jnp.zeros((MB, wide), jnp.float32),
        jnp.zeros((MB, rows_out, C_OUT), jnp.float32),
    )
    forward_state = lax.fori_loop(0, MB + pipe_count - 1, forward_tick, forward_init)
    unused_mid, unused_res, stash_mid, stash_res, stash_center, stash_scale, out_rows = (
        forward_state
    )

    def backward_tick(tick_no, state_in):
        grad_mid, grad_res, weight_acc, gain_acc, bias_acc, input_acc = state_in
        micro_raw = tick_no - (pipe_count - 1 - section_idx)
        is_valid = (micro_raw >= 0) & (micro_raw < MB)
        micro_idx = jnp.clip(micro_raw, 0, MB - 1)
        gain_vec, bias_vec, mask_vec, gate_val, onehot = select_params(micro_idx)
        ops = (
            image_blocks[micro_idx],
            stash_mid[micro_idx],
            stash_res[micro_idx],
            stash_center[micro_idx],
            stash_scale[micro_idx],
            grad_mid,
            grad_res,
            cotangent[micro_idx],
            gain_vec,
            bias_vec,
            mask_vec,
            gate_val,
            is_valid,
        )
        first_buf, second_buf, third_buf, bias_one, gain_one = lax.switch(
            section_idx, bwd_first, ops
        )
        sum_bias_one, sum_gain_one = group_grad_sums(bias_one, gain_one)
        first_buf, second_buf, third_buf, bias_two, gain_two, weight_acc = lax.switch(
            section_idx,
            bwd_second,
            (ops, first_buf, second_buf, third_buf, sum_bias_one, sum_gain_one, weight_acc),
        )
        sum_bias_two, sum_gain_two = group_grad_sums(bias_two, gain_two)
        send_mid, send_res, weight_acc, side_out = lax.switch(
            section_idx,
            bwd_third,
            (
                ops,
                first_buf,
                second_buf,
                third_buf,
                sum_bias_one + sum_bias_two,
                sum_gain_one + sum_gain_two,
                weight_acc,
            ),
        )
        gain_grad = gain_one + gain_two
        bias_grad = bias_one + bias_two
        gain_acc = jnp.where(is_valid, gain_acc + onehot[:, None] * gain_grad[None, :], gain_acc)
        bias_acc = jnp.where(is_valid, bias_acc + onehot[:, None] * bias_grad[None, :], bias_acc)
        input_acc = jax.tree.map(
            lambda stored, fresh: stored.at[micro_idx].set(
                jnp.where(is_valid, fresh, stored[micro_idx])
            ),
            input_acc,
            side_out,
        )
        grad_mid, grad_res = (
            shifted(for_sending(send_mid), "pipe", -1).astype(send_mid.dtype),
            shifted(for_sending(send_res), "pipe", -1).astype(send_res.dtype),
        )
        return (grad_mid, grad_res, weight_acc, gain_acc, bias_acc, input_acc)

    side_init = jnp.zeros((MB, IMG_B, PIX_IN, C_IN), jnp.float32)
    backward_init = (
        zero_mid,
        zero_res,
        jnp.zeros((P_SIZE,), jnp.float32),
        jnp.zeros((NSETS, wide), jnp.float32),
        jnp.zeros((NSETS, wide), jnp.float32),
        side_init,
    )
    backward_state = lax.fori_loop(0, MB + pipe_count - 1, backward_tick, backward_init)
    unused_gmid, unused_gres, weight_acc, gain_acc, bias_acc, input_acc = backward_state
    grad_images, output_sum = (
        lax.psum_scatter(
            input_acc.reshape(IMG_DEV, PIX_IN, C_IN).astype(jnp.bfloat16),
            "pipe",
            scatter_dimension=2,
            tiled=True,
        ).astype(jnp.float32),
        lax.psum_scatter(
            out_rows.astype(jnp.bfloat16), "pipe", scatter_dimension=2, tiled=True
        ).astype(jnp.float32),
    )
    output_part = output_sum.astype(jnp.bfloat16)
    norm_grads = jnp.concatenate([gain_acc.reshape(-1), bias_acc.reshape(-1)])
    weight_sum, norm_sum = lax.psum((weight_acc, norm_grads), ("dp", "rep"))
    grad_gain = norm_sum[: NSETS * wide].reshape(1, NSETS, wide)
    grad_bias = norm_sum[NSETS * wide :].reshape(1, NSETS, wide)
    return (output_part, grad_images, weight_sum.reshape(1, P_SIZE), grad_gain, grad_bias)


PP = PIX_OUT + 1
RW = 8 * PP
RV = 8 * PIX_OUT
BLK = 512
SUB = 65536
F32 = jnp.float32
BF16 = jnp.bfloat16
MESH = pl.DeviceIdType.MESH

E_WIDE, E_WIDE_NEXT = 2, 6
C_H2, C_H4, C_D5, C_D4, C_DH = range(10, 15)
C_O1, C_SHARE, C_GI, C_GP = 15, 19, 22, 25
C_PAR2, C_PAR3, C_DG2, C_DG3, C_BN1, C_BN2, C_BN3 = range(28, 35)
N_SEM = 35
N_PIECE = 17
W_OWN, W_PEER, W_Z, W_ON, W_VIA = range(5)
VIA, HALF = 8, 11
W_BASE = (0, 17, 34, 45, 56 - VIA)
S_CORE, S_IN, S_OUT, S_HAND, S_BACK, S_DONE, S_ACROSS, N_SUM_SEND = 0, 1, 2, 3, 4, 5, 9, 17
R_CORE, R_IN, R_ACROSS, R_OUT, R_GIVE = (0, 8), (8, 12), (20, 8), (28, 12), (40, 4)
R_DONE, R_BACK, R_HAND, N_SUM_RECV = 44, 45, 46, 64
RING = 8
SUBS = 2
SUB_ROWS = 256 // SUBS
Z1_ZERO = 3136
ACROSS_LAG, OUT_LAG = 3 * SUBS // 2 + 1, 4 * SUBS
LAST_TURN = OUT_LAG - 2


def nn(a, b):
    return jnp.dot(a, b, preferred_element_type=F32)


def nt(a, b):
    return lax.dot_general(a, b, (((1,), (1,)), ((), ())), preferred_element_type=F32)


def tn(a, b):
    return lax.dot_general(a, b, (((0,), (0,)), ((), ())), preferred_element_type=F32)


def sigmoid(v):
    return 0.5 + 0.5 * jnp.tanh(0.5 * v)


def rows(start, size):
    return pl.ds(pl.multiple_of(start, 16), size)


def whole_kernel(
    img, wts, gain, bias, width, sets, gates, cot,
    out, gi, dw, dgb,
    imgb, raw, st, wh, wx, f0, f1, f2, f3, fs, pb, pt, u0, u1, u2, sx, cotb,
    h2, h4, h5, d5, d4, dh, r0, r1, ob, tx, rx, inv, par, parx, dg, dgx, sb, rd, bz, dgs,
    ls, ss, rs, wss, wrs, ass, ars, ready, go,
):
    p, d, r = lax.axis_index("pipe"), lax.axis_index("dp"), lax.axis_index("rep")
    peer = (p, 1 - d, r)
    z_pair = r + 1 - 2 * lax.rem(r, 2)
    quarter = 2 * lax.rem(r, 2) + d

    def remote(src, dst, send, recv, device):
        return pltpu.make_async_remote_copy(
            src_ref=src, dst_ref=dst, send_sem=ss.at[send], recv_sem=rs.at[recv],
            device_id=device, device_id_type=MESH,
        )

    def sync(event, first, count):
        part = pl.ds(first, count)
        copy = remote(tx.at[part], rx.at[part], event, event, peer)
        copy.start()
        copy.wait()

    def exchange_of(event, first, count):
        part = pl.ds(first, count)
        return remote(tx.at[part], rx.at[part], event, event, peer)

    def both(slot):
        return tx[slot] + rx[slot]

    def moments(slot_sum, slot_square, total, inv_slot):
        center = both(slot_sum) * (1.0 / total)
        scale = lax.rsqrt(both(slot_square) * (1.0 / total) - center * center + EPSILON)
        inv[inv_slot] = scale
        return center, scale

    def silu(v):
        return v * sigmoid(v)

    def slope(v):
        s = sigmoid(v)
        return s * (1.0 + v * (1.0 - s))

    def clear_pad(ref, first):
        tile = ref[rows(first + RW - 16, 16), :].astype(F32)
        keep = lax.broadcasted_iota(jnp.int32, tile.shape, 0) < 8
        ref[rows(first + RW - 16, 16), :] = jnp.where(keep, tile, 0.0).astype(BF16)

    def per_row(value_of):
        row = lax.broadcasted_iota(jnp.int32, (8, BLK), 0)
        out = jnp.zeros((8, BLK), jnp.int32)
        for m in range(MB):
            out = jnp.where(row == m, value_of(m), out)
        return out

    def mask_of(block):
        lane = lax.broadcasted_iota(jnp.int32, (8, BLK), 1)
        return (lane < per_row(lambda m: width[block, m])).astype(F32)

    def five(body, init=0):
        return lax.fori_loop(0, 5, lambda c, carry: body(pl.ds(c * 10, 10), c, carry), init)

    def add_stats(carry, a, b):
        return carry[0] + jnp.sum(a, axis=0), carry[1] + jnp.sum(b, axis=0)

    zero_stats = (jnp.zeros((8, BLK), F32), jnp.zeros((8, BLK), F32))

    def store_z(ref, first, z, slot_sum, slot_square):
        z3 = z.reshape(PP, 8, BLK)
        ref[pl.ds(first, PP)] = z3
        tx[slot_sum] = jnp.sum(z3, axis=0)
        tx[slot_square] = jnp.sum(z3 * z3, axis=0)

    def raw_copy(turn, element_of):
        slot = lax.rem(turn, RING)
        return pltpu.make_async_copy(
            wts.at[:, pl.ds(pl.multiple_of(element_of(turn) * SUB, SUB), SUB)], raw.at[slot], ls.at[8 + slot]
        )

    def open_weights(element_of, total):
        for turn in range(min(RING - 1, total)):
            raw_copy(turn, element_of).start()

    def load_weights(element_of, total, first, count, put):
        def body(k, carry):
            turn = first + k

            @pl.when(turn + RING - 1 < total)
            def _():
                raw_copy(turn + RING - 1, element_of).start()

            raw_copy(turn, element_of).wait()
            st[0:512] = raw[lax.rem(turn, RING)].astype(F32).reshape(512, 128)
            put(turn)
            return carry

        lax.fori_loop(0, count, body, 0)

    def put_narrow(ref, row_of):
        def put(i):
            for j in range(4):
                ref[rows(row_of(i), 128), j * 128 : (j + 1) * 128] = st[
                    pl.ds(j, 128, stride=4), :
                ].astype(BF16)

        return put

    def put_wide(ref, base, block_rows, first):
        def put(i):
            for n in range(4):
                for j in range(4):
                    ref[rows(base + n * block_rows + (i - first) * 32, 32), j * 128 : (j + 1) * 128] = st[
                        pl.ds(4 * n + j, 32, stride=16), :
                    ].astype(BF16)

        return put

    def put_chunk(t, n, block):
        size = SUB_ROWS // 4
        for part in range(2 * SUBS):
            wh[rows(t * 512 + part * SUB_ROWS + n * size, size), :] = block[part * size : (part + 1) * size].astype(BF16)

    def plain(turn):
        return turn

    def own_parts(turn):
        late = turn - HALF
        return jnp.where(late < 0, 4 * turn + quarter, 4 * HALF + (late // 2) * 4 + 2 * d + lax.rem(late, 2))

    def half_rows(turn):
        return 8 * d + turn

    def piece_copy(kind, i, q, device):
        part = wx.at[rows(i * 512 + q * 128, 128)]
        return pltpu.make_async_remote_copy(
            src_ref=part, dst_ref=part, send_sem=wss.at[kind], recv_sem=wrs.at[W_BASE[kind] + i],
            device_id=device, device_id_type=MESH,
        )

    def half_copy(kind, i, which, device):
        part = wx.at[rows(i * 512 + which * 256, 256)]
        order = min(i, 13) if kind == W_VIA else i
        return pltpu.make_async_remote_copy(
            src_ref=part, dst_ref=part, send_sem=wss.at[kind], recv_sem=wrs.at[W_BASE[kind] + order],
            device_id=device, device_id_type=MESH,
        )

    def all_sent(semaphore, ref):
        pltpu.make_async_remote_copy(
            src_ref=ref, dst_ref=ref, send_sem=semaphore, recv_sem=rs.at[0], device_id=peer, device_id_type=MESH
        ).wait_send()

    def all_here(semaphore, ref):
        pltpu.make_async_remote_copy(
            src_ref=ref, dst_ref=ref, send_sem=ss.at[0], recv_sem=semaphore, device_id=peer, device_id_type=MESH
        ).wait_recv()

    def o1_copy(n, chip):
        part = u0.at[n * RW : (n + 1) * RW]
        return remote(part, part, C_O1 + n, C_O1 + n, (chip, d, r))

    def each(work, first, last):
        def body(i, carry):
            work(i)
            return carry

        lax.fori_loop(first, last, body, 0)

    def img_copy(q, slot):
        return pltpu.make_async_copy(img.at[pl.ds(q * 28, 28)], imgb.at[slot], ls.at[slot])

    def open_images():
        for q in range(3):
            img_copy(q, q).start()

    def over_images(body, init):
        def step(q, carry):
            slot = lax.rem(q, 4)

            @pl.when(q + 3 < 7)
            def _():
                img_copy(q + 3, lax.rem(q + 3, 4)).start()

            img_copy(q, slot).wait()
            return body(q, slot, carry)

        return lax.fori_loop(0, 7, step, init)

    outer = (r == 0) | (r == 3)
    inner = jnp.logical_not(outer)
    z_dev, across = (p, d, z_pair), (p, d, 3 - r)

    def grad_copy(send, recv, src, dst, device):
        return pltpu.make_async_remote_copy(
            src_ref=src, dst_ref=dst, send_sem=ass.at[send], recv_sem=ars.at[recv],
            device_id=device, device_id_type=MESH,
        )

    def in_turn(ring, u):
        return ring[0] + lax.rem(u, ring[1])

    def zero_rest(first, source):
        source[...] = jnp.zeros(source.shape, BF16)

        def body(i, carry):
            copy = pltpu.make_async_copy(source, dw.at[pl.ds((first + i) * 4, 4)], ls.at[18])
            copy.start()
            copy.wait()
            return carry

        lax.fori_loop(0, 13 - first, body, 0)

    def bn_sums():
        for k in range(NSETS):
            hot = (set_of == k).astype(F32)
            for n in range(8):
                cols = slice(n * BLK, (n + 1) * BLK)
                dgs[k : k + 1, cols] = jnp.sum(dg[n] * hot, axis=0, keepdims=True)
                dgs[4 + k : 5 + k, cols] = jnp.sum(dg[8 + n] * hot, axis=0, keepdims=True)

    def bn_in():
        return remote(dgs, bz.at[0], C_BN1, C_BN1, z_dev)

    def bn_across():
        return remote(dgs, bz.at[1], C_BN2, C_BN2, across)

    def bn_out():
        return remote(dgb, bz.at[0], C_BN3, C_BN3, z_dev)

    def say_ready():
        pl.semaphore_signal(ready.at[0], inc=1, device_id=z_dev, device_id_type=MESH)

        @pl.when(inner)
        def _():
            pl.semaphore_signal(ready.at[1], inc=1, device_id=across, device_id_type=MESH)

    def sum_gradients(
        count, compute, at_row, chunk_of, wide, z1, extra,
        lend=(), passed=(), helper=0, helper_turn=None, handed_in=None, lent_by=None, computed=None, packed_here=None,
    ):
        turns = SUBS * count
        last_lent = SUBS * (count + len(lend))
        last_given = last_lent + SUBS * len(passed)
        computed = (0, count) if computed is None else computed
        packed_here = (0, count) if packed_here is None else packed_here
        first_own, own_turns = packed_here[0] * SUBS, packed_here[1] * SUBS
        z2 = z1 + last_given * SUB_ROWS

        def when_own(u, work):
            if handed_in is None:
                work()
            else:
                pl.when(jnp.logical_not(handed_in(u // SUBS)))(work)

        def when_handed(u, work):
            if handed_in is not None:
                pl.when(handed_in(u // SUBS))(work)

        def when_kept(u, work):
            if lent_by is None:
                work()
            else:
                pl.when(jnp.logical_not(lent_by[0](u // SUBS)))(work)

        def when_lent(u, work):
            if lent_by is not None:
                pl.when(lent_by[0](u // SUBS))(work)

        def half(u, which):
            return wh.at[rows(at_row(u // SUBS) + which * 256 + lax.rem(u, SUBS) * SUB_ROWS, SUB_ROWS)]

        def from_z(u):
            return wx.at[rows(z1 + u * SUB_ROWS, SUB_ROWS)]

        def from_across(u):
            return wx.at[rows(z2 + u * SUB_ROWS, SUB_ROWS)]

        def from_core(u):
            return rd.at[rows(u * SUB_ROWS, SUB_ROWS)]

        def to_core(u):
            recv = jnp.where(u < turns, in_turn(R_CORE, u), in_turn(R_GIVE, u))
            return grad_copy(S_CORE, recv, half(u, 1 - d), from_core(u), peer)

        def inwards(u):
            return grad_copy(S_IN, in_turn(R_IN, u), half(u, d), from_z(u), z_dev)

        def exchange(u):
            return grad_copy(S_ACROSS + lax.rem(u, 8), in_turn(R_ACROSS, u), half(u, d), from_across(u), across)

        def outwards(u):
            return grad_copy(S_OUT, in_turn(R_OUT, u), half(u, d), from_z(u), z_dev)

        def packed(u, which):
            return dw.at[chunk_of(u // SUBS) * 4 + which * 2 + lax.rem(u, SUBS)]

        def done_core(u, turn):
            slot = lax.rem(turn, 4)
            return grad_copy(S_DONE + slot, R_DONE, sb.at[slot], packed(u, d), peer)

        def done_here(u, turn):
            slot = lax.rem(turn, 4)
            return pltpu.make_async_copy(sb.at[slot], packed(u, d), ls.at[4 + slot])

        def add(u, other):
            sums = half(u, d)[...].astype(F32) + other[...].astype(F32)
            half(u, d)[...] = sums.astype(BF16)

        def pack(u, turn, ref):
            @pl.when(turn >= 4)
            def _():
                done_here(u, turn).wait()
                done_core(u, turn).wait_send()

            value = ref[...].astype(F32)
            for j in range(4):
                cols = slice(j * 128, (j + 1) * 128)
                if wide:
                    for n in range(4):
                        part = SUB_ROWS // 4
                        st[pl.ds(4 * n + j, part, stride=16), :] = value[n * part : (n + 1) * part, cols]
                else:
                    st[pl.ds(j, SUB_ROWS, stride=4), :] = value[:, cols]
            sb[lax.rem(turn, 4)] = st[...].astype(BF16)
            done_here(u, turn).start()
            done_core(u, turn).start()

        def hand(u):
            theirs = helper_turn(u // SUBS) * SUBS + lax.rem(u, SUBS)
            place = wh.at[rows(theirs * SUB_ROWS + (theirs // SUBS + d) * 256, SUB_ROWS)]
            return grad_copy(S_HAND, R_HAND + theirs, half(u, d), place, (helper, d, r))

        def handed(u):
            return grad_copy(S_HAND, R_HAND + u, half(u, d), half(u, d), (p, d, r))

        def give_back(u, ref):
            t = u // SUBS
            theirs = lent_by[2](t) * SUBS + lax.rem(u, SUBS)
            place = wx.at[rows(jnp.where(lent_by[1](t) == 0, Z1_ZERO, 0) + theirs * SUB_ROWS, SUB_ROWS)]
            return grad_copy(S_BACK, R_BACK, ref, place, (lent_by[1](t), d, r))

        def finish(u, ref):
            when_kept(u, lambda: pack(u, u - first_own, ref))
            when_lent(u, lambda: give_back(u, ref).start())

        def give(t):
            compute(t)
            for k in range(SUBS):
                to_core(t * SUBS + k).start()
            for k in range(SUBS):
                u = t * SUBS + k
                to_core(u).wait_recv()
                add(u, from_core(u))
                hand(u).start()

        def step(it, carry):
            for when, work in extra.items():
                pl.when(it == when)(work)
            for k, when in enumerate(lend + passed):
                pl.when(it == when)(lambda k=k: give(jnp.int32(count + k)))

            def start():
                @pl.when(lax.rem(it, SUBS) == 0)
                def _():
                    compute(it // SUBS)

                to_core(it).start()

            @pl.when(it < turns)
            def _():
                when_own(it, start)

            u1 = it - 1

            @pl.when((u1 >= 0) & (u1 < turns))
            def _():
                def join_cores():
                    to_core(u1).wait_recv()
                    add(u1, from_core(u1))

                when_own(u1, join_cores)
                when_handed(u1, lambda: handed(u1).wait_recv())

                @pl.when(outer & (u1 == 0))
                def _():
                    pl.semaphore_wait(ready.at[0], 1)

                @pl.when(outer)
                def _():
                    inwards(u1).start()

            u2 = it - 2

            @pl.when(inner & (u2 >= 0) & (u2 < turns))
            def _():
                @pl.when(u2 == 0)
                def _():
                    pl.semaphore_wait(ready.at[1], 1)

                inwards(u2).wait_recv()
                add(u2, from_z(u2))
                exchange(u2).start()

            u4 = it - ACROSS_LAG

            @pl.when(inner & (u4 >= 0) & (u4 < turns))
            def _():
                @pl.when(u4 == 0)
                def _():
                    pl.semaphore_wait(ready.at[0], 1)

                exchange(u4).wait()
                add(u4, from_across(u4))
                outwards(u4).start()
                finish(u4, half(u4, d))

            u8 = it - OUT_LAG

            @pl.when(outer & (u8 >= 0) & (u8 < turns))
            def _():
                outwards(u8).wait_recv()
                finish(u8, from_z(u8))

            @pl.when(it == turns - 2 * SUBS)
            def _():
                bn_sums()

                @pl.when(outer)
                def _():
                    bn_in().start()

            @pl.when(inner & (it == turns))
            def _():
                bn_in().wait_recv()
                dgs[...] += bz[0]
                bn_across().start()

            @pl.when(inner & (it == turns + 2 * SUBS))
            def _():
                bn_across().wait()
                dgb[...] = dgs[...] + bz[1]
                bn_out().start()

            return carry

        lax.fori_loop(0, turns + OUT_LAG, step, 0)

        @pl.when(outer)
        def _():
            bn_in().wait_send()
            bn_out().wait_recv()
            dgb[...] = bz[0]

        @pl.when(inner)
        def _():
            bn_out().wait_send()

        def unit_rows(units):
            return wh.at[0 : units * SUB_ROWS]

        if lend:
            all_here(ars.at[R_BACK], unit_rows(last_lent - turns))

            def take(u, carry):
                pack(u, own_turns + u - turns, from_z(u))
                return carry

            lax.fori_loop(turns, last_lent, take, 0)

        @pl.when(outer)
        def _():
            all_sent(ass.at[S_IN], unit_rows(turns))

        @pl.when(inner)
        def _():
            all_sent(ass.at[S_OUT], unit_rows(turns))

        made = computed[1] * SUBS + last_given - turns
        if made:
            all_sent(ass.at[S_CORE], unit_rows(made))
        if last_given > turns:
            all_sent(ass.at[S_HAND], unit_rows(last_given - turns))
        if lent_by is not None:
            all_sent(ass.at[S_BACK], unit_rows(lent_by[3] * SUBS))
        all_here(ars.at[R_DONE], dw.at[pl.ds(0, own_turns + last_lent - turns)])
        for slot in range(4):
            done_here(first_own, jnp.int32(slot)).wait()
            done_core(first_own, jnp.int32(slot)).wait_send()

    @pl.when(p == 0)
    def _():
        open_weights(plain, 44)
        open_images()

    @pl.when(p == 1)
    def _():
        open_weights(plain, 48)
        open_images()
        pltpu.make_async_copy(cot, cotb.at[0:PIX_OUT], ls.at[16]).start()

    @pl.when(p == 2)
    def _():
        open_weights(own_parts, 15)

    @pl.when(p == 3)
    def _():
        open_weights(half_rows, 8)

    barrier = pltpu.get_barrier_semaphore()
    for device in (peer, (p, d, z_pair), (p, d, 3 - r)) + tuple((lax.rem(p + k, 4), d, r) for k in (1, 2, 3)):
        pl.semaphore_signal(barrier, inc=1, device_id=device, device_id_type=MESH)

    block_two = p >= 2
    set_of = per_row(lambda m: jnp.where(block_two, sets[1, m], sets[0, m]))
    for k in range(NSETS):
        hot = (set_of == k).astype(F32)
        for n in range(8):
            g = hot * gain[k : k + 1, n * BLK : (n + 1) * BLK]
            b = hot * bias[k : k + 1, n * BLK : (n + 1) * BLK]
            if k == 0:
                par[n] = g
                par[8 + n] = b
            else:
                par[n] += g
                par[8 + n] += b
    dg[...] = jnp.zeros_like(dg)
    pl.semaphore_wait(barrier, 6)

    total_in, total_out = 2.0 * PIX_IN, 2.0 * PIX_OUT

    def build_patches(base):
        def body(tap, carry):
            row, col = base(tap)
            window = pb[pl.ds(row, 7), pl.ds(col, 7)].reshape(RV, BLK)
            pt[tap, 0:RV, :] = window.astype(BF16)
            return carry

        lax.fori_loop(0, 9, body, 0)

    def clear_patch_pad():
        def body(tap, carry):
            pt[tap, RW - 16 : RW, :] = jnp.zeros((16, BLK), BF16)
            return carry

        lax.fori_loop(0, 9, body, 0)

    def strided_base(tap):
        di, dj = tap // 3, lax.rem(tap, 3)
        return lax.rem(di, 2) * 8 + di // 2, lax.rem(dj, 2) * 8 + dj // 2

    def plain_base(tap):
        return tap // 3, lax.rem(tap, 3)

    def conv(ref, first, target):
        target[...] = jnp.zeros_like(target)

        def body(tap, carry):
            z = nn(pt[tap], ref[rows(first + tap * BLK, BLK), :])
            target[...] += z.reshape(PP, 8, BLK)
            return carry

        lax.fori_loop(0, 9, body, 0)

    def conv_back(dz, ref, first, base):
        pb[...] = jnp.zeros_like(pb)

        def body(tap, carry):
            row, col = base(tap)
            part = nt(dz[0:RV, :], ref[rows(first + tap * BLK, BLK), :])
            pb[pl.ds(row, 7), pl.ds(col, 7)] += part.reshape(7, 7, 8, BLK)
            return carry

        lax.fori_loop(0, 9, body, 0)

    def stats_of_map(ref, slot_sum, slot_square):
        def body(c, _, carry):
            z = ref[c]
            return add_stats(carry, z, z * z)

        tx[slot_sum], tx[slot_square] = five(body, zero_stats)

    def act_to(ref, target, center, scale, g, b, mask):
        def body(c, i, carry):
            zhat = (ref[c] - center) * scale
            ref[c] = zhat
            h = silu(zhat * g + b) * mask
            target[rows(i * 80, 80), :] = h.reshape(80, BLK).astype(BF16)
            return carry

        five(body)
        clear_pad(target, 0)

    def upstream(target, grad, zhat_ref, g, b, mask, slot_sum, slot_gain):
        def body(c, i, carry):
            zhat = zhat_ref[c]
            du = grad[rows(i * 80, 80), :].astype(F32).reshape(10, 8, BLK) * mask * slope(zhat * g + b)
            target[c] = du
            return add_stats(carry, du, du * zhat)

        tx[slot_sum], tx[slot_gain] = five(body, zero_stats)

    def norm_back(target, first, du_ref, du_first, zhat_ref, zhat_first, gscale, mean_du, mean_dg):
        def body(c, i, carry):
            du = du_ref[pl.ds(du_first + i * 10, 10)]
            zhat = zhat_ref[pl.ds(zhat_first + i * 10, 10)]
            dz = gscale * (du - mean_du - zhat * mean_dg)
            target[rows(first + i * 80, 80), :] = dz.reshape(80, BLK).astype(BF16)
            return carry

        five(body)
        clear_pad(target, first)

    def gi_copy():
        return pltpu.make_async_copy(f3.at[0:PIX_IN, :, 0:256], gi, ls.at[17])

    def final_part():
        @pl.when(p != 1)
        def _():
            remote(ob, ob, C_SHARE, C_SHARE, (p, d, r)).wait_recv()
            remote(r1, r1, C_GP, C_GP, (p, d, r)).wait_recv()

        @pl.when(p != 0)
        def _():
            remote(r0, r0, C_GI, C_GI, (p, d, r)).wait_recv()

        out[...] = ob[0:RV, :].astype(F32).reshape(PIX_OUT, 8, BLK).astype(BF16)
        f0[0:PP, :, 0:256] = r1[...].astype(F32).reshape(PP, 8, 256)

        def place(a, carry):
            m = r0[rows(a * 224, 224), :].astype(F32).reshape(28, 8, 256)
            first = m[0:14].reshape(7, 2, 8, 256)
            even = first[:, 0] + f0[pl.ds(a * 7, 7), :, 0:256]
            f3[pl.ds(a * 28, 14), :, 0:256] = jnp.stack([even, first[:, 1]], axis=1).reshape(14, 8, 256)
            f3[pl.ds(a * 28 + 14, 14), :, 0:256] = m[14:28]
            return carry

        lax.fori_loop(0, 7, place, 0)
        gi_copy().start()

    @pl.when(p == 0)
    def _():
        mask = mask_of(0)

        def relay(i):
            piece_copy(W_VIA, i, quarter, (0, d, r)).wait_recv()
            piece_copy(W_OWN, i, quarter, (1, d, r)).start()

        def relay_half(i):
            half_copy(W_VIA, i, d, (0, d, r)).wait_recv()
            half_copy(W_OWN, i, d, (1, d, r)).start()

        put_w = put_narrow(wh, lambda i: i * 128)
        load_weights(plain, 44, 0, 8, put_w)

        def first_conv(q, slot, carry):
            rows_q = imgb[slot].astype(F32).reshape(224, 1024).astype(BF16)
            wx[rows(q * 224, 224), :] = rows_q[:, 0:512]
            wx[rows(1568 + q * 224, 224), :] = rows_q[:, 512:1024]
            z = nn(rows_q, wh[0:1024, :]).reshape(28, 8, BLK)
            f0[pl.ds(q * 28, 28)] = z
            load_weights(plain, 44, 8 + 5 * q, 5, put_w)
            return add_stats(carry, z, z * z)

        tx[0], tx[1] = over_images(first_conv, zero_stats)
        relay(VIA)
        exchange = remote(tx.at[pl.ds(0, 2)], rx.at[pl.ds(0, 2)], 0, 0, peer)
        exchange.start()
        pb[...] = jnp.zeros_like(pb)
        clear_patch_pad()
        load_weights(plain, 44, 43, 1, put_w)
        exchange.wait()

        center, scale = moments(0, 1, total_in, 0)
        g1, b1, g2, b2 = par[0], par[8], par[1], par[9]

        def hidden(i, carry):
            zhat = (f0[pl.ds(i * 14, 14)] - center) * scale
            f0[pl.ds(i * 14, 14)] = zhat
            h = (silu(zhat * g1 + b1) * mask).astype(BF16).astype(F32).reshape(7, 2, 8, BLK)
            u = i + 1
            row = lax.rem(u, 2) * 8 + u // 2
            pb[row, 8:15] = h[:, 0]
            pb[row, 1:8] = h[:, 1]
            return carry

        lax.fori_loop(0, 14, hidden, 0)
        relay(VIA + 1)
        build_patches(strided_base)
        conv(wh, 1024, fs.at[0])
        relay(VIA + 2)
        stats_of_map(fs.at[0], 2, 3)
        sync(1, 2, 2)
        center, scale = moments(2, 3, total_out, 1)
        act_to(fs.at[0], h2, center, scale, g2, b2, mask)
        send = remote(h2, h2, C_H2, C_H2, (1, d, r))
        send.start()
        for i in (HALF, HALF + 1, 16):
            relay_half(i)
        zero_rest(11, sb)
        send.wait_send()
        all_sent(wss.at[W_OWN], wx.at[0 : 3 * 128 + 3 * 256])
        say_ready()

        remote(dh, dh, C_DH, C_DH, (0, d, r)).wait_recv()
        upstream(fs.at[1], dh, fs.at[0], g2, b2, mask, 4, 5)
        sync(0, 4, 2)
        s_du, s_dg = both(4), both(5)
        dg[1], dg[9] = s_dg, s_du
        norm_back(d5, 0, fs.at[1], 0, fs.at[0], 0, g2 * inv[1], s_du * (1.0 / total_out), s_dg * (1.0 / total_out))
        def back_conv():
            conv_back(d5, wh, 1024, strided_base)

        def slopes(i, carry):
            u = i + 1
            row = lax.rem(u, 2) * 8 + u // 2
            grad = jnp.stack([pb[row, 8:15], pb[row, 1:8]], axis=1).reshape(14, 8, BLK)
            zhat = f0[pl.ds(i * 14, 14)]
            du = grad * mask * slope(zhat * g1 + b1)
            f1[pl.ds(i * 14, 14)] = du
            return add_stats(carry, du, du * zhat)

        def first_slopes():
            tx[6], tx[7] = lax.fori_loop(0, 14, slopes, zero_stats)
            sync(1, 6, 2)
            dg[0], dg[8] = both(7), both(6)

        def first_back():
            s_du, s_dg = both(6), both(7)
            gscale, m_du, m_dg = g1 * inv[0], s_du * (1.0 / total_in), s_dg * (1.0 / total_in)

            def body(q, carry):
                part = pl.ds(q * 28, 28)
                dz = gscale * (f1[part] - m_du - f0[part] * m_dg)
                u1[rows(q * 224, 224), :] = dz.reshape(224, BLK).astype(BF16)
                return carry

            lax.fori_loop(0, 7, body, 0)

        def share(target, column, k):
            def body(q, carry):
                g = nt(u1[rows(q * 224, 224), :], wh[k * 256 : (k + 1) * 256, :])
                target[rows(q * 224, 224), column : column + 256] = g.astype(BF16)
                return carry

            lax.fori_loop(0, 7, body, 0)

        places = {1: (u0, 0), 2: (u0, 256), 3: (u2, 0)}

        def share_copy(k):
            target, column = places[k]
            return remote(target.at[0:1568, column : column + 256], r0, C_GI + k - 1, C_GI, (k, d, r))

        def share_out(k):
            share(*places[k], k)
            share_copy(k).start()

        def back_and_share():
            first_back()
            share_out(3)

        def compute(t):
            taps = (t < 7) | (t >= 9)

            @pl.when(taps)
            def _():
                tap = jnp.where(t < 7, t, t - 2)
                wh[rows(at_row(t), 512), :] = tn(pt[tap], d5[...]).astype(BF16)

            @pl.when(jnp.logical_not(taps))
            def _():
                block = tn(wx[rows((t - 7) * 1568, 1568), :], u1[0:1568, :])
                wh[rows(at_row(t), 512), :] = block.astype(BF16)

        def at_row(t):
            return jnp.where(t < 2, 5632 + t * 512, jnp.where(t < 9, t * 512, 2048 + t * 512))

        sum_gradients(
            9, compute, at_row, lambda t: jnp.where(t < 7, t + 2, jnp.where(t < 9, t - 7, t)), False, Z1_ZERO,
            {
                2 * SUBS: back_conv,
                3 * SUBS: first_slopes,
                4 * SUBS: back_and_share,
                5 * SUBS: lambda: share_out(1),
                6 * SUBS: lambda: share_out(2),
                7 * SUBS: lambda: share(r0, 0, 0),
                LAST_TURN + 9 * SUBS: final_part,
            },
            lend=(2, 3), helper=2, helper_turn=lambda t: t - 5,
        )
        for k in (1, 2, 3):
            share_copy(k).wait_send()

    @pl.when(p == 1)
    def _():
        mask = mask_of(1)
        gate_v = per_row(lambda m: gates[m]).astype(F32)
        cotb[PIX_OUT] = jnp.zeros((8, C_OUT), BF16)
        clear_patch_pad()
        load_weights(plain, 48, 0, 16, put_wide(wh, 0, 512, 0))
        load_weights(plain, 48, 16, 32, put_wide(wh, 2048, 1024, 16))

        def shorten(a, slot, carry):
            v = imgb[slot, 0:14].astype(F32).reshape(7, 2, 8, 1024)[:, 0]
            f0[pl.ds(a * 7, 7)] = v[:, :, 0:512]
            f0[pl.ds(PP + a * 7, 7)] = v[:, :, 512:1024]
            return carry

        other_z = 2 * (1 - lax.rem(r, 2))
        this_z = 2 * lax.rem(r, 2)

        def pass_own(i):
            piece_copy(W_OWN, i, quarter, (1, d, r)).wait_recv()
            piece_copy(W_PEER, i, quarter, peer).start()
            piece_copy(W_Z, i, quarter, z_dev).start()

        def pass_on(i):
            piece_copy(W_Z, i, other_z + d, peer).wait_recv()
            piece_copy(W_ON, i, other_z + d, peer).start()

        def have(i):
            piece_copy(W_PEER, i, this_z + 1 - d, peer).wait_recv()
            piece_copy(W_ON, i, other_z + 1 - d, peer).wait_recv()

        def pass_half(i):
            half_copy(W_OWN, i, d, (1, d, r)).wait_recv()
            half_copy(W_PEER, i, d, peer).start()

        def have_half(i):
            half_copy(W_PEER, i, 1 - d, peer).wait_recv()

        pass_own(0)
        over_images(shorten, 0)
        f0[PIX_OUT] = jnp.zeros((8, BLK), F32)
        f0[PP + PIX_OUT] = jnp.zeros((8, BLK), F32)
        sx[...] = f0[0 : 2 * PP].reshape(2 * RW, BLK).astype(BF16)

        def shortcut(n, carry):
            z = nn(sx[0:RW, :], wh[rows(2048 + n * 1024, 512), :]) + nn(
                sx[RW : 2 * RW, :], wh[rows(2560 + n * 1024, 512), :]
            )
            store_z(f1, n * PP, z, 4 * n + 2, 4 * n + 3)
            return carry

        pass_own(1)
        lax.fori_loop(0, 4, shortcut, 0)

        pass_own(2)
        pass_own(VIA)
        pass_on(0)
        pass_own(3)
        pass_on(1)
        pass_own(VIA + 1)
        pass_own(4)
        pl.semaphore_signal(go, inc=1, device_id=(3, d, r), device_id_type=MESH)
        pass_on(2)
        pass_own(VIA + 2)
        pass_own(5)
        pass_on(VIA)
        pass_own(6)
        pass_on(3)
        pass_own(7)
        pass_on(VIA + 1)
        remote(h2, h2, C_H2, C_H2, (1, d, r)).wait_recv()

        def third_conv(n, carry):
            store_z(f0, n * PP, nn(h2[...], wh[rows(n * 512, 512), :]), 4 * n, 4 * n + 1)
            exchange_of(E_WIDE + n, 4 * n, 4).start()
            return carry

        lax.fori_loop(0, 4, third_conv, 0)
        pass_on(4)

        def join(n, carry):
            exchange_of(E_WIDE + n, 4 * n, 4).wait()
            c3, s3 = moments(4 * n, 4 * n + 1, total_out, 2 + n)
            cp, sp = moments(4 * n + 2, 4 * n + 3, total_out, 6 + n)
            g3, gp, b = par[n], par[4 + n], par[8 + n] + par[12 + n]

            def body(_, i, carry):
                part = pl.ds(n * PP + i * 10, 10)
                a = (f0[part] - c3) * s3
                b_ = (f1[part] - cp) * sp
                f0[part] = a
                f1[part] = b_
                o = silu(a * g3 + b_ * gp + b)
                u0[rows(n * RW + i * 80, 80), :] = o.reshape(80, BLK).astype(BF16)
                return carry

            five(body)
            clear_pad(u0, n * RW)
            return carry

        lax.fori_loop(0, 4, join, 0)
        for n in (1, 2, 3):
            o1_copy(n, 3).start()
        pass_half(13)
        pass_on(VIA + 2)
        pass_half(HALF)
        each(have, 0, 4)
        zhat4, zhat5 = fs.at[0], fs.at[1]
        z = nn(u0[0:RW, :], wx[0:512, :])
        for n in range(1, 4):
            z += nn(u0[n * RW : (n + 1) * RW, :], wx[n * 512 : (n + 1) * 512, :])
        store_z(zhat4, 0, z, 16, 17)
        sync(0, 16, 2)
        remote(parx.at[0:4], parx.at[0:4], C_PAR2, C_PAR2, (1, d, r)).wait_recv()
        center, scale = moments(16, 17, total_out, 10)
        g4, g5, b4, b5 = parx[0], parx[1], parx[2], parx[3]
        pb[...] = jnp.zeros_like(pb)

        def hidden(a, carry):
            part = pl.ds(a * 7, 7)
            zhat = (zhat4[part] - center) * scale
            zhat4[part] = zhat
            h = silu(zhat * g4 + b4) * mask
            pb[a + 1, 1:8] = h.astype(BF16).astype(F32)
            return carry

        lax.fori_loop(0, 7, hidden, 0)
        h4[0:RV, :] = pb[1:8, 1:8].reshape(RV, BLK).astype(BF16)
        h4_send = remote(h4, h4, C_H4, C_H4, (2, d, r))
        h4_send.start()

        o1_copy(0, 2).start()
        pass_on(5)
        build_patches(plain_base)
        pass_half(14)
        pass_on(6)
        pass_half(HALF + 1)
        pass_on(7)
        zhat5[...] = jnp.zeros_like(zhat5)

        def fifth_conv(t, carry):
            @pl.when(t < HALF - 4)
            def _():
                have(4 + t)

            @pl.when(t >= HALF - 4)
            def _():
                have_half(4 + t)

            z = nn(pt[t], wx[rows(2048 + t * 512, 512), :])
            zhat5[...] += z.reshape(PP, 8, BLK)
            return carry

        lax.fori_loop(0, 9, fifth_conv, 0)
        pass_half(15)
        stats_of_map(zhat5, 18, 19)
        sync(1, 18, 2)
        center, scale = moments(18, 19, total_out, 11)
        act_to(zhat5, h5, center, scale, g5, b5, mask)

        pass_half(16)

        def sixth_conv(n, carry):
            have_half(13 + n)
            store_z(f2, n * PP, nn(h5[...], wx[rows(6656 + n * 512, 512), :]), 20 + 2 * n, 21 + 2 * n)
            exchange_of(E_WIDE_NEXT + n, 20 + 2 * n, 2).start()
            return carry

        lax.fori_loop(0, 4, sixth_conv, 0)
        remote(parx.at[4:12], parx.at[4:12], C_PAR3, C_PAR3, (1, d, r)).wait_recv()
        pltpu.make_async_copy(cot, cotb.at[0:PIX_OUT], ls.at[16]).wait()

        def finish(n, carry):
            exchange_of(E_WIDE_NEXT + n, 20 + 2 * n, 2).wait()
            center, scale = moments(20 + 2 * n, 21 + 2 * n, total_out, 12 + n)
            g6, b6 = parx[4 + n], parx[8 + n]

            def body(c, i, carry):
                part = pl.ds(n * PP + i * 10, 10)
                part_rows = rows(n * RW + i * 80, 80)
                zhat = (f2[part] - center) * scale
                f2[part] = zhat
                o = u0[part_rows, :].astype(F32).reshape(10, 8, BLK)
                q = o + zhat * g6 + b6
                s = sigmoid(q)
                merged = gate_v * (q * s) + (1.0 - gate_v) * o
                pt[n, rows(i * 80, 80), :] = merged.reshape(80, BLK).astype(BF16)
                ct = cotb[c, :, pl.ds(pl.multiple_of(n * BLK, BLK), BLK)].astype(F32)
                dq = ct * gate_v * (s * (1.0 + q * (1.0 - s)))
                f3[part] = dq
                dres = dq + (1.0 - gate_v) * ct
                u2[part_rows, :] = dres.reshape(80, BLK).astype(BF16)
                return add_stats(carry, dq, dq * zhat)

            tx[28 + 2 * n], tx[29 + 2 * n] = five(body, zero_stats)
            exchange_of(E_WIDE + n, 28 + 2 * n, 2).start()
            return carry

        lax.fori_loop(0, 4, finish, 0)
        ob[...] = pt[1]


        def sixth_back(n, carry):
            exchange_of(E_WIDE + n, 28 + 2 * n, 2).wait()
            s_du, s_dg = both(28 + 2 * n), both(29 + 2 * n)
            dgx[4 + n] = s_dg
            dgx[8 + n] = s_du
            norm_back(u1, n * RW, f3, n * PP, f2, n * PP, parx[4 + n] * inv[12 + n], s_du * (1.0 / total_out), s_dg * (1.0 / total_out))
            return carry

        lax.fori_loop(0, 4, sixth_back, 0)
        grad = nt(u1[0:RW, :], wx[6656:7168, :])
        for n in range(1, 4):
            grad += nt(u1[n * RW : (n + 1) * RW, :], wx[6656 + n * 512 : 7168 + n * 512, :])
        dh[...] = grad.astype(BF16)

        upstream(f2, dh, zhat5, g5, b5, mask, 36, 37)
        sync(0, 36, 2)
        s_du, s_dg = both(36), both(37)
        dgx[1] = s_dg
        dgx[3] = s_du
        norm_back(d5, 0, f2, 0, zhat5, 0, g5 * inv[11], s_du * (1.0 / total_out), s_dg * (1.0 / total_out))
        d5_send = remote(d5, d5, C_D5, C_D5, (2, d, r))
        d5_send.start()
        conv_back(d5, wx, 2048, plain_base)

        def fourth_slopes(a, carry):
            part = pl.ds(a * 7, 7)
            zhat = zhat4[part]
            du = pb[a + 1, 1:8] * mask * slope(zhat * g4 + b4)
            f2[part] = du
            return add_stats(carry, du, du * zhat)

        tx[38], tx[39] = lax.fori_loop(0, 7, fourth_slopes, zero_stats)
        sync(1, 38, 2)
        s_du, s_dg = both(38), both(39)
        dgx[0] = s_dg
        dgx[2] = s_du
        norm_back(d4, 0, f2, 0, zhat4, 0, g4 * inv[10], s_du * (1.0 / total_out), s_dg * (1.0 / total_out))

        def first_block_slopes(n, carry):
            f3[pl.ds(n * PP, PP)] = nt(d4[...], wx[rows(n * 512, 512), :]).reshape(PP, 8, BLK)
            g3, gp, b = par[n], par[4 + n], par[8 + n] + par[12 + n]

            def body(_, i, carry):
                part = pl.ds(n * PP + i * 10, 10)
                do = u2[rows(n * RW + i * 80, 80), :].astype(F32).reshape(10, 8, BLK) + f3[part]
                a, b_ = f0[part], f1[part]
                dp = do.astype(BF16).astype(F32) * slope(a * g3 + b_ * gp + b)
                f3[part] = dp
                s0, s1, s2 = carry
                return s0 + jnp.sum(dp, axis=0), s1 + jnp.sum(dp * a, axis=0), s2 + jnp.sum(dp * b_, axis=0)

            first = 40 + 3 * n
            tx[first], tx[first + 1], tx[first + 2] = five(body, zero_stats + zero_stats[:1])
            exchange_of(E_WIDE_NEXT + n, first, 3).start()
            return carry

        lax.fori_loop(0, 4, first_block_slopes, 0)

        def third_back(n, carry):
            first = 40 + 3 * n
            exchange_of(E_WIDE_NEXT + n, first, 3).wait()
            s_du, s_d3, s_dp = both(first), both(first + 1), both(first + 2)
            dg[n] = s_d3
            dg[4 + n] = s_dp
            dg[8 + n] = s_du
            dg[12 + n] = s_du
            m_du = s_du * (1.0 / total_out)
            norm_back(pt.at[4 + n], 0, f3, n * PP, f0, n * PP, par[n] * inv[2 + n], m_du, s_d3 * (1.0 / total_out))
            norm_back(u2, n * RW, f3, n * PP, f1, n * PP, par[4 + n] * inv[6 + n], m_du, s_dp * (1.0 / total_out))
            return carry

        lax.fori_loop(0, 4, third_back, 0)
        grad = nt(pt[4], wh[0:512, :])
        for n in range(1, 4):
            grad += nt(pt[4 + n], wh[n * 512 : (n + 1) * 512, :])
        dh[...] = grad.astype(BF16)
        dh_send = remote(dh, dh, C_DH, C_DH, (0, d, r))
        dh_send.start()

        all_sent(wss.at[W_PEER], wx.at[0 : HALF * 128 + 6 * 256])
        all_sent(wss.at[W_Z], wx.at[0 : HALF * 128])
        all_sent(wss.at[W_ON], wx.at[0 : HALF * 128])
        say_ready()

        late = [remote(d4, d4, C_D4, C_D4, (2, d, r))]
        for first, last, sem, chip in ((0, 4, C_DG2, 2), (4, 12, C_DG3, 3)):
            late.append(remote(dgx.at[first:last], dgx.at[first:last], sem, sem, (chip, d, r)))
        later = [
            remote(pt.at[k], ob, C_SHARE + slot, C_SHARE, (k, d, r)) for slot, k in enumerate((0, 2, 3))
        ]

        def late_sends():
            dh_send.wait_send()
            for copy in late:
                copy.start()

        def shortcut_share(k):
            g = nt(u2[0:RW, :], wh[2048 + k * 256 : 2304 + k * 256, :])
            for n in range(1, 4):
                g += nt(u2[n * RW : (n + 1) * RW, :], wh[2048 + n * 1024 + k * 256 : 2304 + n * 1024 + k * 256, :])
            return g.astype(BF16)

        places = ((h4.at[:, 0:256], 0), (h4.at[:, 256:512], 2), (pt.at[8, :, 0:256], 3))

        def share_copy(slot):
            place, k = places[slot]
            return remote(place, r1, C_GP + slot, C_GP, (k, d, r))

        def shortcut_shares(slot):
            place, k = places[slot]
            if slot == 0:
                h4_send.wait_send()
            place[...] = shortcut_share(k)

        def shortcut_own():
            r1[...] = shortcut_share(1)

        def late_shares():
            for copy in later:
                copy.start()
            for slot in range(3):
                share_copy(slot).start()

        def compute(t):
            @pl.when(t < 4)
            def _():
                left = h2[:, pl.ds(pl.multiple_of(t * 128, 128), 128)]
                for n in range(4):
                    put_chunk(t, n, tn(left, pt[4 + n]))

            @pl.when((t >= 4) & (t < 12))
            def _():
                m = t - 4
                left = sx[rows((m // 4) * RW, RW), pl.ds(pl.multiple_of(lax.rem(m, 4) * 128, 128), 128)]
                for n in range(4):
                    put_chunk(t, n, tn(left, u2[n * RW : (n + 1) * RW, :]))

            @pl.when(t >= 12)
            def _():
                left = h5[:, pl.ds(pl.multiple_of((t - 12) * 128, 128), 128)]
                for n in range(4):
                    put_chunk(t, n, tn(left, u1[n * RW : (n + 1) * RW, :]))

        zero_rest(12, sb)
        sum_gradients(
            12, compute, lambda t: t * 512, lambda t: t, True, 0,
            {
                2: lambda: shortcut_shares(0),
                4: lambda: shortcut_shares(1),
                6: lambda: shortcut_shares(2),
                7: late_sends,
                8: shortcut_own,
                10: late_shares,
                LAST_TURN + 12 * SUBS: final_part,
            },
            passed=(3, 5, 7, 9), helper=3, helper_turn=lambda t: t - 7,
        )
        for copy in [d5_send, o1_copy(0, 2)] + [o1_copy(n, 3) for n in (1, 2, 3)] + late + later:
            copy.wait_send()
        for slot in range(3):
            share_copy(slot).wait_send()


    @pl.when(p == 2)
    def _():
        for k, slot in ((0, 0), (1, 1), (2, 8), (3, 9)):
            parx[k] = par[slot]
        par_send = remote(parx.at[0:4], parx.at[0:4], C_PAR2, C_PAR2, (1, d, r))
        par_send.start()

        put_w = put_narrow(wx, lambda i: own_parts(i) * 128)

        def put(i):
            put_w(i)

            @pl.when(i < VIA)
            def _():
                piece_copy(W_OWN, i, quarter, (1, d, r)).start()

            @pl.when((i >= VIA) & (i < HALF))
            def _():
                piece_copy(W_VIA, i, quarter, (0, d, r)).start()

            for k in range(HALF, 13):
                @pl.when(i == HALF + 2 * (k - HALF) + 1)
                def _(k=k):
                    half_copy(W_VIA, k, d, (0, d, r)).start()

        load_weights(own_parts, 15, 0, 15, put)
        pb[...] = jnp.zeros_like(pb)
        clear_patch_pad()

        all_sent(wss.at[W_OWN], wx.at[0 : VIA * 128])
        all_sent(wss.at[W_VIA], wx.at[0 : 3 * 128 + 2 * 256])
        say_ready()
        remote(h4, h4, C_H4, C_H4, (2, d, r)).wait_recv()
        pb[1:8, 1:8] = h4[0:RV, :].astype(F32).reshape(7, 7, 8, BLK)
        build_patches(plain_base)
        remote(d5, d5, C_D5, C_D5, (2, d, r)).wait_recv()

        def compute(t):
            taps = (t < 4) | (t >= 10)

            @pl.when(taps)
            def _():
                tap = jnp.where(t < 4, t + 5, t - 10)
                wh[rows(t * 512, 512), :] = tn(pt[tap], d5[...]).astype(BF16)

            @pl.when(t == 6)
            def _():
                remote(d4, d4, C_D4, C_D4, (2, d, r)).wait_recv()
                for n in range(4):
                    o1_copy(n, 2).wait_recv()

            @pl.when(jnp.logical_not(taps))
            def _():
                wh[rows(t * 512, 512), :] = tn(u0[rows((t - 6) * RW, RW), :], d4[...]).astype(BF16)

        def norm_grads():
            remote(dgx.at[0:4], dgx.at[0:4], C_DG2, C_DG2, (2, d, r)).wait_recv()
            dg[0], dg[1], dg[8], dg[9] = dgx[0], dgx[1], dgx[2], dgx[3]

        sum_gradients(
            10, compute, lambda t: t * 512, lambda t: jnp.where(t < 4, t + 9, t - 6), False, 0,
            {7 * SUBS: norm_grads, LAST_TURN + 10 * SUBS: final_part},
            lend=(2, 3, 4, 5, 6), helper=3, helper_turn=lambda t: t - 10,
            handed_in=lambda t: (t >= 4) & (t < 6),
            lent_by=(lambda t: (t >= 4) & (t < 6), lambda t: 0, lambda t: t + 5, 2),
            computed=(0, 8), packed_here=(0, 8),
        )
        par_send.wait_send()

    @pl.when(p == 3)
    def _():
        for k in range(4):
            parx[4 + k] = par[k]
            parx[8 + k] = par[8 + k]
        par_send = remote(parx.at[4:12], parx.at[4:12], C_PAR3, C_PAR3, (1, d, r))
        par_send.start()
        say_ready()

        def put(i):
            for n in range(4):
                for j in range(4):
                    wx[rows(6656 + n * 512 + d * 256 + i * 32, 32), j * 128 : (j + 1) * 128] = st[
                        pl.ds(4 * n + j, 32, stride=16), :
                    ].astype(BF16)

        load_weights(half_rows, 8, 0, 8, put)
        zero_rest(4, sb)
        pl.semaphore_wait(go, 1)

        half_copy(W_VIA, 16, d, (0, d, r)).start()
        for i in (13, 14, 15):
            half_copy(W_OWN, i, d, (1, d, r)).start()
        for n in (1, 2, 3):
            o1_copy(n, 3).wait_recv()
            o1_copy(n, 2).start()
        def norm_grads():
            remote(dgx.at[4:12], dgx.at[4:12], C_DG3, C_DG3, (3, d, r)).wait_recv()
            for k in range(4):
                dg[k] = dgx[4 + k]
                dg[8 + k] = dgx[8 + k]

        sum_gradients(
            9, lambda t: None, lambda t: t * 512, lambda t: t - 5, True, 0,
            {6 * SUBS: norm_grads, LAST_TURN + 9 * SUBS: final_part},
            handed_in=lambda t: t >= 0,
            lent_by=(lambda t: t < 5, lambda t: 2, lambda t: t + 10, 5),
            computed=(0, 0), packed_here=(5, 4),
        )
        for n in (1, 2, 3):
            o1_copy(n, 2).wait_send()
        all_sent(wss.at[W_VIA], wx.at[0:256])
        all_sent(wss.at[W_OWN], wx.at[0 : 3 * 256])
        par_send.wait_send()

    gi_copy().wait()


def widen_kernel(out_in, gi_in, dw_in, dgb_in, out, gi, dw, gain, bias, v_out, v_gi, v_dw, v_wide, v_dgb, sin, sout):
    count = v_dw.shape[0] // 2048

    def part(i):
        return pl.ds(i * 2048, 2048)

    loads = [pltpu.make_async_copy(dw_in.at[part(i)], v_dw.at[part(i)], sin.at[i]) for i in range(count)]
    others = (
        (dgb_in, v_dgb, ((v_dgb.at[0:4], gain), (v_dgb.at[4:8], bias))),
        (out_in, v_out, ((v_out, out),)),
        (gi_in, v_gi, ((v_gi, gi),)),
    )
    more = [pltpu.make_async_copy(a, b, sin.at[count + k]) for k, (a, b, _) in enumerate(others)]
    for copy in loads + more:
        copy.start()
    stores = []
    for i in range(count):
        loads[i].wait()
        v_wide[part(i)] = v_dw[part(i)].astype(F32)
        stores.append(pltpu.make_async_copy(v_wide.at[part(i)], dw.at[part(i)], sout.at[i]))
        stores[-1].start()
    for k, (_, _, ends) in enumerate(others):
        more[k].wait()
        for a, b in ends:
            stores.append(pltpu.make_async_copy(a, b, sout.at[len(stores)]))
            stores[-1].start()
    for copy in stores:
        copy.wait()


def widen(out, gi, dw, dgb):
    count = P_SIZE // 128 // 2048
    any_space = pl.BlockSpec(memory_space=pl.ANY)
    return pl.pallas_call(
        widen_kernel,
        out_shape=(
            jax.ShapeDtypeStruct(out.shape, out.dtype),
            jax.ShapeDtypeStruct(gi.shape, gi.dtype),
            jax.ShapeDtypeStruct(dw.shape, F32),
            jax.ShapeDtypeStruct((4, 4096), F32),
            jax.ShapeDtypeStruct((4, 4096), F32),
        ),
        in_specs=[any_space] * 4,
        out_specs=(any_space,) * 5,
        scratch_shapes=[
            pltpu.VMEM(out.shape, out.dtype),
            pltpu.VMEM(gi.shape, gi.dtype),
            pltpu.VMEM(dw.shape, BF16),
            pltpu.VMEM(dw.shape, F32),
            pltpu.VMEM(dgb.shape, F32),
            pltpu.SemaphoreType.DMA((count + 3,)),
            pltpu.SemaphoreType.DMA((count + 4,)),
        ],
        compiler_params=pltpu.CompilerParams(vmem_limit_bytes=64 * 1024 * 1024),
    )(out, gi, dw, dgb)


def one_kernel(images, section_weights, bn_gain, bn_bias, width, bn_set, gate, cotangent):
    any_space = pl.BlockSpec(memory_space=pl.ANY)
    vmem = pl.BlockSpec(memory_space=pltpu.VMEM)
    smem = pl.BlockSpec(memory_space=pltpu.SMEM)
    out, gi, dw, dgb = pl.pallas_call(
        whole_kernel,
        out_shape=(
            jax.ShapeDtypeStruct((PIX_OUT, 8, BLK), BF16),
            jax.ShapeDtypeStruct((PIX_IN, 8, 256), F32),
            jax.ShapeDtypeStruct((P_SIZE // SUB, 512, 128), BF16),
            jax.ShapeDtypeStruct((8, 4096), F32),
        ),
        in_specs=[any_space, any_space, vmem, vmem, smem, smem, smem, any_space],
        out_specs=(vmem, any_space, any_space, vmem),
        scratch_shapes=[
            pltpu.VMEM((4, 28, 8, 1024), BF16),
            pltpu.VMEM((RING, 1, SUB), BF16),
            pltpu.VMEM((512, 128), F32),
            pltpu.VMEM((8192, BLK), BF16),
            pltpu.VMEM((8768, BLK), BF16),
            pltpu.VMEM((4 * PP, 8, BLK), F32),
            pltpu.VMEM((4 * PP, 8, BLK), F32),
            pltpu.VMEM((4 * PP, 8, BLK), F32),
            pltpu.VMEM((4 * PP, 8, BLK), F32),
            pltpu.VMEM((2, PP, 8, BLK), F32),
            pltpu.VMEM((16, 16, 8, BLK), F32),
            pltpu.VMEM((9, RW, BLK), BF16),
            pltpu.VMEM((4 * RW, BLK), BF16),
            pltpu.VMEM((4 * RW, BLK), BF16),
            pltpu.VMEM((4 * RW, BLK), BF16),
            pltpu.VMEM((2 * RW, BLK), BF16),
            pltpu.VMEM((PP, 8, C_OUT), BF16),
            pltpu.VMEM((RW, BLK), BF16),
            pltpu.VMEM((RW, BLK), BF16),
            pltpu.VMEM((RW, BLK), BF16),
            pltpu.VMEM((RW, BLK), BF16),
            pltpu.VMEM((RW, BLK), BF16),
            pltpu.VMEM((RW, BLK), BF16),
            pltpu.VMEM((8 * PIX_IN, 256), BF16),
            pltpu.VMEM((RW, 256), BF16),
            pltpu.VMEM((RW, BLK), BF16),
            pltpu.VMEM((52, 8, BLK), F32),
            pltpu.VMEM((52, 8, BLK), F32),
            pltpu.VMEM((16, 8, BLK), F32),
            pltpu.VMEM((16, 8, BLK), F32),
            pltpu.VMEM((12, 8, BLK), F32),
            pltpu.VMEM((16, 8, BLK), F32),
            pltpu.VMEM((12, 8, BLK), F32),
            pltpu.VMEM((4, 512, 128), BF16),
            pltpu.VMEM((4096, BLK), BF16),
            pltpu.VMEM((2, 8, 4096), F32),
            pltpu.VMEM((8, 4096), F32),
            pltpu.SemaphoreType.DMA((19,)),
            pltpu.SemaphoreType.DMA((N_SEM,)),
            pltpu.SemaphoreType.DMA((N_SEM,)),
            pltpu.SemaphoreType.DMA((5,)),
            pltpu.SemaphoreType.DMA((62,)),
            pltpu.SemaphoreType.DMA((N_SUM_SEND,)),
            pltpu.SemaphoreType.DMA((N_SUM_RECV,)),
            pltpu.SemaphoreType.REGULAR((2,)),
            pltpu.SemaphoreType.REGULAR,
        ],
        compiler_params=pltpu.CompilerParams(
            collective_id=0, has_side_effects=True, vmem_limit_bytes=64 * 1024 * 1024
        ),
    )(
        jnp.transpose(images, (1, 0, 2)),
        section_weights,
        bn_gain[0],
        bn_bias[0],
        width.T,
        bn_set.T,
        gate,
        jnp.transpose(cotangent, (1, 0, 2)),
    )
    out, gi, dw, gain_sum, bias_sum = widen(out, gi, dw.reshape(P_SIZE // 128, 128), dgb)
    return (
        jnp.transpose(out, (1, 0, 2)),
        jnp.transpose(gi, (1, 0, 2)),
        dw.reshape(1, P_SIZE),
        gain_sum[None],
        bias_sum[None],
    )


def solution(mesh):
    sizes = dict(mesh.shape)
    fits = sizes["pipe"] == 4 and sizes["dp"] == 2 and sizes["rep"] == 4
    placed = (
        P(("dp", "rep"), None, None),
        P("pipe", None),
        P("pipe", None, None),
        P("pipe", None, None),
        P(),
        P(),
        P(),
        P(("dp", "rep"), None, None),
    )
    return jax.shard_map(
        one_kernel if fits else on_device,
        mesh=mesh,
        in_specs=placed,
        out_specs=(
            P(("dp", "rep"), None, "pipe"),
            P(("dp", "rep"), None, "pipe"),
            P("pipe", None),
            P("pipe", None, None),
            P("pipe", None, None),
        ),
        check_vma=False,
    )
```

```python
import jax
import jax.numpy as jnp
from jax import lax
from jax.experimental import pallas as pl
from jax.experimental.pallas import tpu as pltpu
from jax.sharding import PartitionSpec as P

C_IN = 1024
C_MID = 512
C_OUT = 2048
SIDE = 14
NSETS = 4
MB = 8
IMG_B = 1
OSIDE = 7
PIX_IN = 196
PIX_OUT = 49
IMG_DEV = 8
P_SIZE = 3407872


EPSILON = 1e-05


def for_sending(array):

    def short(part):
        return part.astype(jnp.bfloat16) if part.dtype == jnp.float32 else part

    return jax.tree.map(short, array)


def shifted(value, axis, steps):
    count = lax.axis_size(axis)
    first, last = (max(0, -steps), min(count, count - steps))
    return lax.ppermute(value, axis, [(source, source + steps) for source in range(first, last)])


def smooth(inputs):
    return inputs * jax.nn.sigmoid(inputs)


def smooth_slope(inputs):
    gate_sig = jax.nn.sigmoid(inputs)
    return gate_sig * (1.0 + inputs * (1.0 - gate_sig))


def matmul(left_op, right_op):
    return jnp.dot(left_op, right_op, preferred_element_type=jnp.float32)


def matmul_left_t(left_op, right_op):
    return lax.dot_general(
        left_op, right_op, (((0,), (0,)), ((), ())), preferred_element_type=jnp.float32
    )


def matmul_right_t(left_op, right_op):
    return lax.dot_general(
        left_op, right_op, (((1,), (1,)), ((), ())), preferred_element_type=jnp.float32
    )


def patches(planes, stride):
    images, side_len, channels = (planes.shape[0], planes.shape[1], planes.shape[3])
    out_side = side_len // stride
    padded = jnp.pad(planes, ((0, 0), (1, 1), (1, 1), (0, 0)))
    pieces = []
    for row_off in range(3):
        for col_off in range(3):
            pieces.append(
                padded[
                    :,
                    row_off : row_off + stride * (out_side - 1) + 1 : stride,
                    col_off : col_off + stride * (out_side - 1) + 1 : stride,
                    :,
                ]
            )
    return jnp.concatenate(pieces, axis=3).reshape(images * out_side * out_side, 9 * channels)


def unpatch(columns, images, side_len, stride, channels):
    out_side = side_len // stride
    pieces = columns.reshape(images, out_side, out_side, 9, channels)
    padded = jnp.zeros((images, side_len + 2, side_len + 2, channels), jnp.float32)
    for row_off in range(3):
        for col_off in range(3):
            padded = padded.at[
                :,
                row_off : row_off + stride * (out_side - 1) + 1 : stride,
                col_off : col_off + stride * (out_side - 1) + 1 : stride,
                :,
            ].add(pieces[:, :, :, row_off * 3 + col_off, :])
    return padded[:, 1 : side_len + 1, 1 : side_len + 1, :]


def group_moments(sums_local, squares_local):
    return (
        lax.psum(sums_local.astype(jnp.bfloat16), "dp").astype(jnp.float32),
        lax.psum(squares_local.astype(jnp.bfloat16), "dp").astype(jnp.float32),
    )


def group_grad_sums(bias_local, gain_local):
    return (
        lax.psum(bias_local.astype(jnp.bfloat16), "dp").astype(jnp.float32),
        lax.psum(gain_local.astype(jnp.bfloat16), "dp").astype(jnp.float32),
    )


def stats_of(sum_all, square_all, start, count, row_total):
    center = sum_all[start : start + count] / row_total
    inv_std = lax.rsqrt(square_all[start : start + count] / row_total - center * center + EPSILON)
    return (center, inv_std)


def norm_grad(slope_in, normed, gain_vec, inv_std, sum_bias, sum_gain, row_total):
    return (
        gain_vec * inv_std * (slope_in - sum_bias / row_total - normed * (sum_gain / row_total))
    ).astype(jnp.bfloat16)


def on_device(images, section_weights, bn_gain, bn_bias, width, bn_set, gate, cotangent):
    section_idx = lax.axis_index("pipe")
    pipe_count = lax.axis_size("pipe")
    dp_count = lax.axis_size("dp")
    flat_weights = section_weights[0]
    gain_table = bn_gain[0]
    bias_table = bn_bias[0]
    rows_in = IMG_B * PIX_IN
    rows_out = IMG_B * PIX_OUT
    total_in = float(rows_in * dp_count)
    total_out = float(rows_out * dp_count)
    wide = 2 * C_OUT
    scr_len = IMG_B * max(PIX_IN * C_MID, PIX_OUT * wide)
    image_blocks = images.reshape(MB, IMG_B, PIX_IN, C_IN)
    pad_mid = jnp.zeros((wide - 2 * C_MID,), jnp.float32)
    zero_wide = jnp.zeros((wide,), jnp.float32)
    zero_scr = jnp.zeros((scr_len,), jnp.float32)
    zero_mid = jnp.zeros((rows_out, C_MID), jnp.bfloat16)
    zero_res = jnp.zeros((rows_out, C_OUT), jnp.bfloat16)
    zero_rows = jnp.zeros((rows_out, C_OUT), jnp.float32)
    zero_input = jnp.zeros((IMG_B, PIX_IN, C_IN), jnp.float32)

    def pack(values):
        flat = values.reshape(-1).astype(jnp.float32)
        return jnp.pad(flat, (0, scr_len - flat.shape[0]))

    def unpack(buffer, rows, cols):
        return buffer[: rows * cols].reshape(rows, cols)

    def place(vec, start):
        return jnp.pad(vec, (start, wide - start - vec.shape[0]))

    def add_weight(acc, grad, offset, valid):
        flat = grad.reshape(-1)
        return acc.at[offset : offset + flat.shape[0]].add(jnp.where(valid, flat, 0.0))

    def weights_zero():
        split_at = C_IN * C_MID
        return (
            flat_weights[:split_at].reshape(C_IN, C_MID),
            flat_weights[split_at : split_at + 9 * C_MID * C_MID].reshape(9 * C_MID, C_MID),
        )

    def weights_one():
        split_at = C_MID * C_OUT
        return (
            flat_weights[:split_at].reshape(C_MID, C_OUT),
            flat_weights[split_at : split_at + C_IN * C_OUT].reshape(C_IN, C_OUT),
        )

    def weights_two():
        split_at = C_OUT * C_MID
        return (
            flat_weights[:split_at].reshape(C_OUT, C_MID),
            flat_weights[split_at : split_at + 9 * C_MID * C_MID].reshape(9 * C_MID, C_MID),
        )

    def short_rows(image_block):
        return image_block.reshape(IMG_B, SIDE, SIDE, C_IN)[:, ::2, ::2, :].reshape(rows_out, C_IN)

    def local_stats(values, start):
        return (
            place(jnp.sum(values, axis=0), start),
            place(jnp.sum(values * values, axis=0), start),
        )

    def fwd_a_zero(ops):
        conv_a, conv_b = weights_zero()
        pre_one = matmul(ops[0].reshape(rows_in, C_IN), conv_a)
        sums_local, squares_local = local_stats(pre_one, 0)
        return (pack(pre_one), sums_local, squares_local)

    def fwd_a_one(ops):
        conv_a, conv_b = weights_one()
        pre_both = jnp.concatenate(
            [matmul(ops[1], conv_a), matmul(short_rows(ops[0]), conv_b)], axis=1
        )
        sums_local, squares_local = local_stats(pre_both, 0)
        return (pack(pre_both), sums_local, squares_local)

    def fwd_a_two(ops):
        conv_a, conv_b = weights_two()
        pre_four = matmul(ops[2], conv_a)
        sums_local, squares_local = local_stats(pre_four, 0)
        return (pack(pre_four), sums_local, squares_local)

    def fwd_a_three(ops):
        conv_a = flat_weights[: C_MID * C_OUT].reshape(C_MID, C_OUT)
        pre_six = matmul(ops[1], conv_a)
        sums_local, squares_local = local_stats(pre_six, 0)
        return (pack(pre_six), sums_local, squares_local)

    def fwd_b_zero(args):
        ops, scratch, sum_all, square_all = args
        conv_a, conv_b = weights_zero()
        gain_vec, bias_vec, mask_vec = (ops[3], ops[4], ops[5])
        pre_one = unpack(scratch, rows_in, C_MID)
        center_one, inv_one = stats_of(sum_all, square_all, 0, C_MID, total_in)
        hidden_one = (
            smooth((pre_one - center_one) * inv_one * gain_vec[:C_MID] + bias_vec[:C_MID])
            * mask_vec
        ).astype(jnp.bfloat16)
        pre_two = matmul(patches(hidden_one.reshape(IMG_B, SIDE, SIDE, C_MID), 2), conv_b)
        sums_local, squares_local = local_stats(pre_two, C_MID)
        return (pack(pre_two), sums_local, squares_local)

    def fwd_b_pass(args):
        return (args[1], zero_wide, zero_wide)

    def fwd_b_two(args):
        ops, scratch, sum_all, square_all = args
        conv_a, conv_b = weights_two()
        gain_vec, bias_vec, mask_vec = (ops[3], ops[4], ops[5])
        pre_four = unpack(scratch, rows_out, C_MID)
        center_four, inv_four = stats_of(sum_all, square_all, 0, C_MID, total_out)
        hidden_four = (
            smooth((pre_four - center_four) * inv_four * gain_vec[:C_MID] + bias_vec[:C_MID])
            * mask_vec
        ).astype(jnp.bfloat16)
        pre_five = matmul(patches(hidden_four.reshape(IMG_B, OSIDE, OSIDE, C_MID), 1), conv_b)
        sums_local, squares_local = local_stats(pre_five, C_MID)
        return (pack(pre_five), sums_local, squares_local)

    def fwd_c_double(args, first_total, send_res):
        ops, scratch, sum_all, square_all = args
        gain_vec, bias_vec, mask_vec = (ops[3], ops[4], ops[5])
        pre_two = unpack(scratch, rows_out, C_MID)
        center_one, inv_one = stats_of(sum_all, square_all, 0, C_MID, first_total)
        center_two, inv_two = stats_of(sum_all, square_all, C_MID, C_MID, total_out)
        hidden_two = (
            smooth(
                (pre_two - center_two) * inv_two * gain_vec[C_MID : 2 * C_MID]
                + bias_vec[C_MID : 2 * C_MID]
            )
            * mask_vec
        ).astype(jnp.bfloat16)
        centers = jnp.concatenate([center_one, center_two, pad_mid])
        scales = jnp.concatenate([inv_one, inv_two, pad_mid])
        return (hidden_two, send_res, centers, scales, zero_rows)

    def fwd_c_zero(args):
        return fwd_c_double(args, total_in, zero_res)

    def fwd_c_two(args):
        return fwd_c_double(args, total_out, args[0][2])

    def fwd_c_one(args):
        ops, scratch, sum_all, square_all = args
        gain_vec, bias_vec = (ops[3], ops[4])
        pre_both = unpack(scratch, rows_out, wide)
        centers, scales = stats_of(sum_all, square_all, 0, wide, total_out)
        activ = (pre_both - centers) * scales * gain_vec + bias_vec
        block_out = smooth(activ[:, :C_OUT] + activ[:, C_OUT:]).astype(jnp.bfloat16)
        return (zero_mid, block_out, centers, scales, zero_rows)

    def fwd_c_three(args):
        ops, scratch, sum_all, square_all = args
        gain_vec, bias_vec, gate_val = (ops[3], ops[4], ops[6])
        pre_six = unpack(scratch, rows_out, C_OUT)
        centers, scales = stats_of(sum_all, square_all, 0, wide, total_out)
        residual = ops[2].astype(jnp.float32)
        merged = smooth(
            residual
            + (pre_six - centers[:C_OUT]) * scales[:C_OUT] * gain_vec[:C_OUT]
            + bias_vec[:C_OUT]
        )
        result = gate_val * merged + (1.0 - gate_val) * residual
        return (zero_mid, zero_res, centers, scales, result)

    def bwd_a_double(ops, flat_in, conv_a, conv_b, side_len, stride):
        centers, scales, grad_mid = (ops[3], ops[4], ops[5])
        gain_vec, bias_vec, mask_vec = (ops[8], ops[9], ops[10])
        norm_one = (matmul(flat_in, conv_a) - centers[:C_MID]) * scales[:C_MID]
        hidden_one = (smooth(norm_one * gain_vec[:C_MID] + bias_vec[:C_MID]) * mask_vec).astype(
            jnp.bfloat16
        )
        columns = patches(hidden_one.reshape(IMG_B, side_len, side_len, C_MID), stride)
        norm_two = (matmul(columns, conv_b) - centers[C_MID : 2 * C_MID]) * scales[
            C_MID : 2 * C_MID
        ]
        act_two = norm_two * gain_vec[C_MID : 2 * C_MID] + bias_vec[C_MID : 2 * C_MID]
        slope_two = grad_mid.astype(jnp.float32) * mask_vec * smooth_slope(act_two)
        return (
            pack(slope_two),
            pack(norm_two),
            pack(norm_one),
            place(jnp.sum(slope_two, axis=0), C_MID),
            place(jnp.sum(slope_two * norm_two, axis=0), C_MID),
        )

    def bwd_a_zero(ops):
        conv_a, conv_b = weights_zero()
        return bwd_a_double(ops, ops[0].reshape(rows_in, C_IN), conv_a, conv_b, SIDE, 2)

    def bwd_a_two(ops):
        conv_a, conv_b = weights_two()
        return bwd_a_double(ops, ops[2], conv_a, conv_b, OSIDE, 1)

    def bwd_a_one(ops):
        conv_a, conv_b = weights_one()
        centers, scales, grad_res = (ops[3], ops[4], ops[6])
        gain_vec, bias_vec = (ops[8], ops[9])
        pre_both = jnp.concatenate(
            [matmul(ops[1], conv_a), matmul(short_rows(ops[0]), conv_b)], axis=1
        )
        normed = (pre_both - centers) * scales
        activ = normed * gain_vec + bias_vec
        slope_in = grad_res.astype(jnp.float32) * smooth_slope(activ[:, :C_OUT] + activ[:, C_OUT:])
        both = jnp.concatenate([slope_in, slope_in], axis=1)
        return (
            pack(both),
            pack(normed),
            zero_scr,
            jnp.sum(both, axis=0),
            jnp.sum(both * normed, axis=0),
        )

    def bwd_a_three(ops):
        conv_a = flat_weights[: C_MID * C_OUT].reshape(C_MID, C_OUT)
        centers, scales = (ops[3], ops[4])
        gain_vec, bias_vec, gate_val = (ops[8], ops[9], ops[11])
        normed = (matmul(ops[1], conv_a) - centers[:C_OUT]) * scales[:C_OUT]
        joined = ops[2].astype(jnp.float32) + normed * gain_vec[:C_OUT] + bias_vec[:C_OUT]
        through = ops[7].astype(jnp.float32) * gate_val * smooth_slope(joined)
        return (
            pack(through),
            pack(normed),
            zero_scr,
            place(jnp.sum(through, axis=0), 0),
            place(jnp.sum(through * normed, axis=0), 0),
        )

    def bwd_b_double(args, conv_b, rows_first, side_len, stride, offset):
        ops, first_buf, second_buf, third_buf, sum_bias, sum_gain, acc = args
        scales = ops[4]
        gain_vec, bias_vec, mask_vec, valid = (ops[8], ops[9], ops[10], ops[12])
        slope_two = unpack(first_buf, rows_out, C_MID)
        norm_two = unpack(second_buf, rows_out, C_MID)
        norm_one = unpack(third_buf, rows_first, C_MID)
        grad_two = norm_grad(
            slope_two,
            norm_two,
            gain_vec[C_MID : 2 * C_MID],
            scales[C_MID : 2 * C_MID],
            sum_bias[C_MID : 2 * C_MID],
            sum_gain[C_MID : 2 * C_MID],
            total_out,
        )
        act_one = norm_one * gain_vec[:C_MID] + bias_vec[:C_MID]
        hidden_one = (smooth(act_one) * mask_vec).astype(jnp.bfloat16)
        columns = patches(hidden_one.reshape(IMG_B, side_len, side_len, C_MID), stride)
        acc = add_weight(acc, matmul_left_t(columns, grad_two), offset, valid)
        hid_grad = unpatch(
            matmul_right_t(grad_two, conv_b), IMG_B, side_len, stride, C_MID
        ).reshape(rows_first, C_MID)
        slope_one = hid_grad * mask_vec * smooth_slope(act_one)
        return (
            pack(slope_one),
            second_buf,
            third_buf,
            place(jnp.sum(slope_one, axis=0), 0),
            place(jnp.sum(slope_one * norm_one, axis=0), 0),
            acc,
        )

    def bwd_b_zero(args):
        conv_a, conv_b = weights_zero()
        return bwd_b_double(args, conv_b, rows_in, SIDE, 2, C_IN * C_MID)

    def bwd_b_two(args):
        conv_a, conv_b = weights_two()
        return bwd_b_double(args, conv_b, rows_out, OSIDE, 1, C_OUT * C_MID)

    def bwd_b_pass(args):
        return (args[1], args[2], args[3], zero_wide, zero_wide, args[6])

    def side_none():
        return zero_input

    def bwd_c_zero(args):
        ops, first_buf, second_buf, third_buf, sum_bias, sum_gain, acc = args
        conv_a, conv_b = weights_zero()
        scales, gain_vec, valid = (ops[4], ops[8], ops[12])
        flat_in = ops[0].reshape(rows_in, C_IN)
        slope_one = unpack(first_buf, rows_in, C_MID)
        norm_one = unpack(third_buf, rows_in, C_MID)
        grad_one = norm_grad(
            slope_one,
            norm_one,
            gain_vec[:C_MID],
            scales[:C_MID],
            sum_bias[:C_MID],
            sum_gain[:C_MID],
            total_in,
        )
        acc = add_weight(acc, matmul_left_t(flat_in, grad_one), 0, valid)
        side_out = matmul_right_t(grad_one, conv_a).reshape(IMG_B, PIX_IN, C_IN)
        return (zero_mid, zero_res, acc, side_out)

    def bwd_c_one(args):
        ops, first_buf, second_buf, third_buf, sum_bias, sum_gain, acc = args
        conv_a, conv_b = weights_one()
        scales, gain_vec, valid = (ops[4], ops[8], ops[12])
        short_in = short_rows(ops[0])
        both = unpack(first_buf, rows_out, wide)
        normed = unpack(second_buf, rows_out, wide)
        grad_both = norm_grad(both, normed, gain_vec, scales, sum_bias, sum_gain, total_out)
        acc = add_weight(acc, matmul_left_t(ops[1], grad_both[:, :C_OUT]), 0, valid)
        acc = add_weight(acc, matmul_left_t(short_in, grad_both[:, C_OUT:]), C_MID * C_OUT, valid)
        mid_grad = matmul_right_t(grad_both[:, :C_OUT], conv_a).astype(jnp.bfloat16)
        short_grad = matmul_right_t(grad_both[:, C_OUT:], conv_b).reshape(
            IMG_B, OSIDE, 1, OSIDE, 1, C_IN
        )
        side_out = jnp.pad(short_grad, ((0, 0), (0, 0), (0, 1), (0, 0), (0, 1), (0, 0))).reshape(
            IMG_B, PIX_IN, C_IN
        )
        return (mid_grad, zero_res, acc, side_out)

    def bwd_c_two(args):
        ops, first_buf, second_buf, third_buf, sum_bias, sum_gain, acc = args
        conv_a, conv_b = weights_two()
        scales, grad_res, gain_vec, valid = (ops[4], ops[6], ops[8], ops[12])
        slope_four = unpack(first_buf, rows_out, C_MID)
        norm_four = unpack(third_buf, rows_out, C_MID)
        grad_four = norm_grad(
            slope_four,
            norm_four,
            gain_vec[:C_MID],
            scales[:C_MID],
            sum_bias[:C_MID],
            sum_gain[:C_MID],
            total_out,
        )
        acc = add_weight(acc, matmul_left_t(ops[2], grad_four), 0, valid)
        carried_grad = (grad_res.astype(jnp.float32) + matmul_right_t(grad_four, conv_a)).astype(
            jnp.bfloat16
        )
        return (zero_mid, carried_grad, acc, side_none())

    def bwd_c_three(args):
        ops, first_buf, second_buf, third_buf, sum_bias, sum_gain, acc = args
        conv_a = flat_weights[: C_MID * C_OUT].reshape(C_MID, C_OUT)
        scales, gain_vec, gate_val, valid = (ops[4], ops[8], ops[11], ops[12])
        through = unpack(first_buf, rows_out, C_OUT)
        normed = unpack(second_buf, rows_out, C_OUT)
        res_grad = (through + (1.0 - gate_val) * ops[7].astype(jnp.float32)).astype(jnp.bfloat16)
        grad_six = norm_grad(
            through,
            normed,
            gain_vec[:C_OUT],
            scales[:C_OUT],
            sum_bias[:C_OUT],
            sum_gain[:C_OUT],
            total_out,
        )
        acc = add_weight(acc, matmul_left_t(ops[1], grad_six), 0, valid)
        mid_grad = matmul_right_t(grad_six, conv_a).astype(jnp.bfloat16)
        return (mid_grad, res_grad, acc, side_none())

    def select_params(micro_idx):
        block_id = section_idx // 2
        width_val = width[micro_idx, block_id]
        set_val = bn_set[micro_idx, block_id]
        onehot = (jnp.arange(NSETS) == set_val).astype(jnp.float32)
        gain_vec = jnp.sum(onehot[:, None] * gain_table, axis=0)
        bias_vec = jnp.sum(onehot[:, None] * bias_table, axis=0)
        mask_vec = (jnp.arange(C_MID) < width_val).astype(jnp.float32)
        gate_val = gate[micro_idx].astype(jnp.float32)
        return (gain_vec, bias_vec, mask_vec, gate_val, onehot)

    fwd_first = [fwd_a_zero, fwd_a_one, fwd_a_two, fwd_a_three]
    fwd_second = [fwd_b_zero, fwd_b_pass, fwd_b_two, fwd_b_pass]
    fwd_third = [fwd_c_zero, fwd_c_one, fwd_c_two, fwd_c_three]
    bwd_first = [bwd_a_zero, bwd_a_one, bwd_a_two, bwd_a_three]
    bwd_second = [bwd_b_zero, bwd_b_pass, bwd_b_two, bwd_b_pass]
    bwd_third = [bwd_c_zero, bwd_c_one, bwd_c_two, bwd_c_three]

    def forward_tick(tick_no, state_in):
        recv_mid, recv_res, stash_mid, stash_res, stash_center, stash_scale, out_rows = state_in
        micro_raw = tick_no - section_idx
        is_valid = (micro_raw >= 0) & (micro_raw < MB)
        micro_idx = jnp.clip(micro_raw, 0, MB - 1)
        gain_vec, bias_vec, mask_vec, gate_val, onehot = select_params(micro_idx)
        ops = (image_blocks[micro_idx], recv_mid, recv_res, gain_vec, bias_vec, mask_vec, gate_val)
        scratch, sums_local, squares_local = lax.switch(section_idx, fwd_first, ops)
        sum_first, square_first = group_moments(sums_local, squares_local)
        scratch, sums_local, squares_local = lax.switch(
            section_idx, fwd_second, (ops, scratch, sum_first, square_first)
        )
        sum_second, square_second = group_moments(sums_local, squares_local)
        send_mid, send_res, centers, scales, result = lax.switch(
            section_idx,
            fwd_third,
            (ops, scratch, sum_first + sum_second, square_first + square_second),
        )
        stash_mid = stash_mid.at[micro_idx].set(jnp.where(is_valid, recv_mid, stash_mid[micro_idx]))
        stash_res = stash_res.at[micro_idx].set(jnp.where(is_valid, recv_res, stash_res[micro_idx]))
        stash_center = stash_center.at[micro_idx].set(
            jnp.where(is_valid, centers, stash_center[micro_idx])
        )
        stash_scale = stash_scale.at[micro_idx].set(
            jnp.where(is_valid, scales, stash_scale[micro_idx])
        )
        out_rows = out_rows.at[micro_idx].set(jnp.where(is_valid, result, out_rows[micro_idx]))
        recv_mid, recv_res = (
            shifted(for_sending(send_mid), "pipe", 1).astype(send_mid.dtype),
            shifted(for_sending(send_res), "pipe", 1).astype(send_res.dtype),
        )
        return (recv_mid, recv_res, stash_mid, stash_res, stash_center, stash_scale, out_rows)

    forward_init = (
        zero_mid,
        zero_res,
        jnp.zeros((MB, rows_out, C_MID), jnp.bfloat16),
        jnp.zeros((MB, rows_out, C_OUT), jnp.bfloat16),
        jnp.zeros((MB, wide), jnp.float32),
        jnp.zeros((MB, wide), jnp.float32),
        jnp.zeros((MB, rows_out, C_OUT), jnp.float32),
    )
    forward_state = lax.fori_loop(0, MB + pipe_count - 1, forward_tick, forward_init)
    unused_mid, unused_res, stash_mid, stash_res, stash_center, stash_scale, out_rows = (
        forward_state
    )

    def backward_tick(tick_no, state_in):
        grad_mid, grad_res, weight_acc, gain_acc, bias_acc, input_acc = state_in
        micro_raw = tick_no - (pipe_count - 1 - section_idx)
        is_valid = (micro_raw >= 0) & (micro_raw < MB)
        micro_idx = jnp.clip(micro_raw, 0, MB - 1)
        gain_vec, bias_vec, mask_vec, gate_val, onehot = select_params(micro_idx)
        ops = (
            image_blocks[micro_idx],
            stash_mid[micro_idx],
            stash_res[micro_idx],
            stash_center[micro_idx],
            stash_scale[micro_idx],
            grad_mid,
            grad_res,
            cotangent[micro_idx],
            gain_vec,
            bias_vec,
            mask_vec,
            gate_val,
            is_valid,
        )
        first_buf, second_buf, third_buf, bias_one, gain_one = lax.switch(
            section_idx, bwd_first, ops
        )
        sum_bias_one, sum_gain_one = group_grad_sums(bias_one, gain_one)
        first_buf, second_buf, third_buf, bias_two, gain_two, weight_acc = lax.switch(
            section_idx,
            bwd_second,
            (ops, first_buf, second_buf, third_buf, sum_bias_one, sum_gain_one, weight_acc),
        )
        sum_bias_two, sum_gain_two = group_grad_sums(bias_two, gain_two)
        send_mid, send_res, weight_acc, side_out = lax.switch(
            section_idx,
            bwd_third,
            (
                ops,
                first_buf,
                second_buf,
                third_buf,
                sum_bias_one + sum_bias_two,
                sum_gain_one + sum_gain_two,
                weight_acc,
            ),
        )
        gain_grad = gain_one + gain_two
        bias_grad = bias_one + bias_two
        gain_acc = jnp.where(is_valid, gain_acc + onehot[:, None] * gain_grad[None, :], gain_acc)
        bias_acc = jnp.where(is_valid, bias_acc + onehot[:, None] * bias_grad[None, :], bias_acc)
        input_acc = jax.tree.map(
            lambda stored, fresh: stored.at[micro_idx].set(
                jnp.where(is_valid, fresh, stored[micro_idx])
            ),
            input_acc,
            side_out,
        )
        grad_mid, grad_res = (
            shifted(for_sending(send_mid), "pipe", -1).astype(send_mid.dtype),
            shifted(for_sending(send_res), "pipe", -1).astype(send_res.dtype),
        )
        return (grad_mid, grad_res, weight_acc, gain_acc, bias_acc, input_acc)

    side_init = jnp.zeros((MB, IMG_B, PIX_IN, C_IN), jnp.float32)
    backward_init = (
        zero_mid,
        zero_res,
        jnp.zeros((P_SIZE,), jnp.float32),
        jnp.zeros((NSETS, wide), jnp.float32),
        jnp.zeros((NSETS, wide), jnp.float32),
        side_init,
    )
    backward_state = lax.fori_loop(0, MB + pipe_count - 1, backward_tick, backward_init)
    unused_gmid, unused_gres, weight_acc, gain_acc, bias_acc, input_acc = backward_state
    grad_images, output_sum = (
        lax.psum_scatter(
            input_acc.reshape(IMG_DEV, PIX_IN, C_IN).astype(jnp.bfloat16),
            "pipe",
            scatter_dimension=2,
            tiled=True,
        ).astype(jnp.float32),
        lax.psum_scatter(
            out_rows.astype(jnp.bfloat16), "pipe", scatter_dimension=2, tiled=True
        ).astype(jnp.float32),
    )
    output_part = output_sum.astype(jnp.bfloat16)
    norm_grads = jnp.concatenate([gain_acc.reshape(-1), bias_acc.reshape(-1)])
    weight_sum, norm_sum = lax.psum((weight_acc, norm_grads), ("dp", "rep"))
    grad_gain = norm_sum[: NSETS * wide].reshape(1, NSETS, wide)
    grad_bias = norm_sum[NSETS * wide :].reshape(1, NSETS, wide)
    return (output_part, grad_images, weight_sum.reshape(1, P_SIZE), grad_gain, grad_bias)


PP = PIX_OUT + 1
RW = 8 * PP
RV = 8 * PIX_OUT
BLK = 512
SUB = 65536
F32 = jnp.float32
BF16 = jnp.bfloat16
MESH = pl.DeviceIdType.MESH

E_WIDE, E_WIDE_NEXT = 2, 6
C_H2, C_H4, C_D5, C_D4, C_DH = range(10, 15)
C_O1, C_SHARE, C_GI, C_GP = 15, 19, 22, 25
C_PAR2, C_PAR3, C_DG2, C_DG3, C_BN1, C_BN2, C_BN3, C_BN4 = range(28, 36)
N_SEM = 36
N_PIECE = 17
W_OWN, W_PEER, W_Z, W_ON, W_VIA = range(5)
VIA, HALF = 8, 11
W_BASE = (0, 17, 34, 45, 56 - VIA)
S_CORE, S_IN, S_OUT, S_HAND, S_BACK, S_DONE, S_ACROSS, N_SUM_SEND = 0, 1, 2, 3, 4, 5, 9, 17
R_CORE, R_IN, R_ACROSS, R_OUT, R_GIVE = (0, 8), (8, 12), (20, 8), (28, 12), (40, 4)
R_DONE, R_BACK, R_HAND, N_SUM_RECV = 44, 45, 46, 66
RING = 8
SUBS = 2
SUB_ROWS = 256 // SUBS
Z1_ZERO = 3136
ACROSS_LAG, OUT_LAG = 3 * SUBS // 2 + 1, 4 * SUBS
LAST_TURN = OUT_LAG - 2


def nn(a, b):
    return jnp.dot(a, b, preferred_element_type=F32)


def nt(a, b):
    return lax.dot_general(a, b, (((1,), (1,)), ((), ())), preferred_element_type=F32)


def tn(a, b):
    return lax.dot_general(a, b, (((0,), (0,)), ((), ())), preferred_element_type=F32)


def sigmoid(v):
    return 0.5 + 0.5 * jnp.tanh(0.5 * v)


def rows(start, size):
    return pl.ds(start if isinstance(start, int) else pl.multiple_of(start, 16), size)


def whole_kernel(
    img, wts, gain, bias, width, sets, gates, cot,
    out, gi, dw, dgb_out,
    imgb, raw, st, wh, wx, f0, f1, f2, f3, fs, pb, pt, u0, u1, u2, sx, cotb,
    h2, h4, h5, d5, d4, dh, r0, r1, ob, tx, rx, inv, par, parx, dg, dgx, sb, rd, bz, dgs, dgb, v_out,
    ls, ss, rs, wss, wrs, ass, ars, ready, go,
):
    p, d, r = lax.axis_index("pipe"), lax.axis_index("dp"), lax.axis_index("rep")
    peer = (p, 1 - d, r)
    z_pair = r + 1 - 2 * lax.rem(r, 2)
    quarter = 2 * lax.rem(r, 2) + d

    def remote(src, dst, send, recv, device):
        return pltpu.make_async_remote_copy(
            src_ref=src, dst_ref=dst, send_sem=ss.at[send], recv_sem=rs.at[recv],
            device_id=device, device_id_type=MESH,
        )

    def sync(event, first, count):
        part = pl.ds(first, count)
        copy = remote(tx.at[part], rx.at[part], event, event, peer)
        copy.start()
        copy.wait()

    def exchange_of(event, first, count):
        part = pl.ds(first, count)
        return remote(tx.at[part], rx.at[part], event, event, peer)

    def both(slot):
        return tx[slot] + rx[slot]

    def moments(slot_sum, slot_square, total, inv_slot):
        center = both(slot_sum) * (1.0 / total)
        scale = lax.rsqrt(both(slot_square) * (1.0 / total) - center * center + EPSILON)
        inv[inv_slot] = scale
        return center, scale

    def silu(v):
        return v * sigmoid(v)

    def slope(v):
        s = sigmoid(v)
        return s + v * s * (1.0 - s)

    def clear_pad(ref, first):
        tile = ref[rows(first + RW - 16, 16), :].astype(F32)
        keep = lax.broadcasted_iota(jnp.int32, tile.shape, 0) < 8
        ref[rows(first + RW - 16, 16), :] = jnp.where(keep, tile, 0.0).astype(BF16)

    def per_row(value_of):
        row = lax.broadcasted_iota(jnp.int32, (8, BLK), 0)
        out = jnp.zeros((8, BLK), jnp.int32)
        for m in range(MB):
            out = jnp.where(row == m, value_of(m), out)
        return out

    def mask_of(block):
        lane = lax.broadcasted_iota(jnp.int32, (8, BLK), 1)
        return (lane < per_row(lambda m: width[block, m])).astype(F32)

    def five(body, init=0, unrolled=False):
        if unrolled:
            for c in range(5):
                init = body(pl.ds(c * 10, 10), c, init)
            return init
        return lax.fori_loop(0, 5, lambda c, carry: body(pl.ds(c * 10, 10), c, carry), init)

    def add_stats(carry, a, b):
        return carry[0] + jnp.sum(a, axis=0), carry[1] + jnp.sum(b, axis=0)

    zero_stats = (jnp.zeros((8, BLK), F32), jnp.zeros((8, BLK), F32))

    def store_z(ref, first, z, slot_sum, slot_square):
        z3 = z.reshape(PP, 8, BLK)
        ref[pl.ds(first, PP)] = z3
        tx[slot_sum] = jnp.sum(z3, axis=0)
        tx[slot_square] = jnp.sum(z3 * z3, axis=0)

    def raw_copy(turn, element_of):
        slot = lax.rem(turn, RING)
        return pltpu.make_async_copy(
            wts.at[:, pl.ds(pl.multiple_of(element_of(turn) * SUB, SUB), SUB)], raw.at[slot], ls.at[8 + slot]
        )

    def open_weights(element_of, total):
        for turn in range(min(RING - 1, total)):
            raw_copy(turn, element_of).start()

    def load_weights(element_of, total, first, count, put):
        def body(k, carry):
            turn = first + k

            @pl.when(turn + RING - 1 < total)
            def _():
                raw_copy(turn + RING - 1, element_of).start()

            raw_copy(turn, element_of).wait()
            st[0:512] = raw[lax.rem(turn, RING)].astype(F32).reshape(512, 128)
            put(turn)
            return carry

        lax.fori_loop(0, count, body, 0)

    def put_narrow(ref, row_of):
        def put(i):
            for j in range(4):
                ref[rows(row_of(i), 128), j * 128 : (j + 1) * 128] = st[
                    pl.ds(j, 128, stride=4), :
                ].astype(BF16)

        return put

    def put_wide(ref, base, block_rows, first):
        def put(i):
            for n in range(4):
                for j in range(4):
                    ref[rows(base + n * block_rows + (i - first) * 32, 32), j * 128 : (j + 1) * 128] = st[
                        pl.ds(4 * n + j, 32, stride=16), :
                    ].astype(BF16)

        return put

    def put_chunk(row, n, block):
        size = SUB_ROWS // 4
        for part in range(2 * SUBS):
            wh[rows(row + part * SUB_ROWS + n * size, size), :] = block[part * size : (part + 1) * size].astype(BF16)

    def plain(turn):
        return turn

    def own_parts(turn):
        late = turn - HALF
        return jnp.where(late < 0, 4 * turn + quarter, 4 * HALF + (late // 2) * 4 + 2 * d + lax.rem(late, 2))

    def half_rows(turn):
        return 8 * d + turn

    def piece_copy(kind, i, q, device):
        part = wx.at[rows(i * 512 + q * 128, 128)]
        return pltpu.make_async_remote_copy(
            src_ref=part, dst_ref=part, send_sem=wss.at[kind], recv_sem=wrs.at[W_BASE[kind] + i],
            device_id=device, device_id_type=MESH,
        )

    def half_copy(kind, i, which, device):
        part = wx.at[rows(i * 512 + which * 256, 256)]
        order = min(i, 13) if kind == W_VIA else i
        return pltpu.make_async_remote_copy(
            src_ref=part, dst_ref=part, send_sem=wss.at[kind], recv_sem=wrs.at[W_BASE[kind] + order],
            device_id=device, device_id_type=MESH,
        )

    def all_sent(semaphore, ref):
        pltpu.make_async_remote_copy(
            src_ref=ref, dst_ref=ref, send_sem=semaphore, recv_sem=rs.at[0], device_id=peer, device_id_type=MESH
        ).wait_send()

    def all_here(semaphore, ref):
        pltpu.make_async_remote_copy(
            src_ref=ref, dst_ref=ref, send_sem=ss.at[0], recv_sem=semaphore, device_id=peer, device_id_type=MESH
        ).wait_recv()

    def o1_copy(n, chip):
        part = u0.at[n * RW : (n + 1) * RW]
        return remote(part, part, C_O1 + n, C_O1 + n, (chip, d, r))

    def each(work, first, last):
        def body(i, carry):
            work(i)
            return carry

        lax.fori_loop(first, last, body, 0)

    def img_copy(q, slot):
        return pltpu.make_async_copy(img.at[pl.ds(q * 28, 28)], imgb.at[slot], ls.at[slot])

    def open_images():
        for q in range(3):
            img_copy(q, q).start()

    def over_images(body, init):
        def step(q, carry):
            slot = lax.rem(q, 4)

            @pl.when(q + 3 < 7)
            def _():
                img_copy(q + 3, lax.rem(q + 3, 4)).start()

            img_copy(q, slot).wait()
            return body(q, slot, carry)

        return lax.fori_loop(0, 7, step, init)

    outer = (r == 0) | (r == 3)
    inner = jnp.logical_not(outer)
    z_dev, across = (p, d, z_pair), (p, d, 3 - r)

    def grad_copy(send, recv, src, dst, device):
        return pltpu.make_async_remote_copy(
            src_ref=src, dst_ref=dst, send_sem=ass.at[send], recv_sem=ars.at[recv],
            device_id=device, device_id_type=MESH,
        )

    def in_turn(ring, u):
        return ring[0] + lax.rem(u, ring[1])

    def zero_rest(first, source):
        source[...] = jnp.zeros(source.shape, BF16)

        def body(i, carry):
            copy = pltpu.make_async_copy(source, dw.at[pl.ds((first + i) * 4, 4)], ls.at[18])
            copy.start()
            copy.wait()
            return carry

        lax.fori_loop(0, 13 - first, body, 0)

    def bn_sums():
        for k in range(NSETS):
            hot = (set_of == k).astype(F32)
            for n in range(8):
                cols = slice(n * BLK, (n + 1) * BLK)
                dgs[k : k + 1, cols] = jnp.sum(dg[n] * hot, axis=0, keepdims=True)
                dgs[4 + k : 5 + k, cols] = jnp.sum(dg[8 + n] * hot, axis=0, keepdims=True)

    norm_half = pl.ds(pl.multiple_of(d * 2048, 2048), 2048)

    def bn_in():
        return remote(dgs.at[:, norm_half], bz.at[0, :, norm_half], C_BN1, C_BN1, z_dev)

    def bn_across():
        return remote(dgs.at[:, norm_half], bz.at[1, :, norm_half], C_BN2, C_BN2, across)

    def bn_out():
        return remote(dgb.at[:, norm_half], bz.at[0, :, norm_half], C_BN3, C_BN3, z_dev)

    def bn_core():
        return remote(dgb.at[:, norm_half], dgb.at[:, norm_half], C_BN4, C_BN4, peer)

    def say_ready():
        pl.semaphore_signal(ready.at[0], inc=1, device_id=z_dev, device_id_type=MESH)

        @pl.when(inner)
        def _():
            pl.semaphore_signal(ready.at[1], inc=1, device_id=across, device_id_type=MESH)

    def sum_gradients(
        count, compute, at_row, chunk_of, wide, z1, extra,
        lend=(), passed=(), helper=0, helper_turn=None, handed_in=None, lent_by=None, computed=None, packed_here=None,
        norms_at=0,
    ):
        turns = SUBS * count
        last_lent = SUBS * (count + len(lend))
        last_given = last_lent + SUBS * len(passed)
        computed = (0, count) if computed is None else computed
        packed_here = (0, count) if packed_here is None else packed_here
        first_own, own_turns = packed_here[0] * SUBS, packed_here[1] * SUBS
        z2 = z1 + last_given * SUB_ROWS

        def when_own(u, work):
            if handed_in is None:
                work()
            else:
                pl.when(jnp.logical_not(handed_in(u // SUBS)))(work)

        def when_handed(u, work):
            if handed_in is not None:
                pl.when(handed_in(u // SUBS))(work)

        def when_kept(u, work):
            if lent_by is None:
                work()
            else:
                pl.when(jnp.logical_not(lent_by[0](u // SUBS)))(work)

        def when_lent(u, work):
            if lent_by is not None:
                pl.when(lent_by[0](u // SUBS))(work)

        def half(u, which):
            return wh.at[rows(at_row(u // SUBS) + which * 256 + lax.rem(u, SUBS) * SUB_ROWS, SUB_ROWS)]

        def from_z(u):
            return wx.at[rows(z1 + u * SUB_ROWS, SUB_ROWS)]

        def from_across(u):
            return wx.at[rows(z2 + u * SUB_ROWS, SUB_ROWS)]

        def from_core(u):
            return rd.at[rows(u * SUB_ROWS, SUB_ROWS)]

        def to_core(u):
            recv = jnp.where(u < turns, in_turn(R_CORE, u), in_turn(R_GIVE, u))
            return grad_copy(S_CORE, recv, half(u, 1 - d), from_core(u), peer)

        def inwards(u):
            return grad_copy(S_IN, in_turn(R_IN, u), half(u, d), from_z(u), z_dev)

        def exchange(u):
            return grad_copy(S_ACROSS + lax.rem(u, 8), in_turn(R_ACROSS, u), half(u, d), from_across(u), across)

        def outwards(u):
            return grad_copy(S_OUT, in_turn(R_OUT, u), half(u, d), from_z(u), z_dev)

        def packed(u, which):
            return dw.at[chunk_of(u // SUBS) * 4 + which * 2 + lax.rem(u, SUBS)]

        def done_core(u, turn):
            slot = lax.rem(turn, 4)
            return grad_copy(S_DONE + slot, R_DONE, sb.at[slot], packed(u, d), peer)

        def done_here(u, turn):
            slot = lax.rem(turn, 4)
            return pltpu.make_async_copy(sb.at[slot], packed(u, d), ls.at[4 + slot])

        def add(u, other):
            sums = half(u, d)[...].astype(F32) + other[...].astype(F32)
            half(u, d)[...] = sums.astype(BF16)

        def pack(u, turn, ref):
            @pl.when(turn >= 4)
            def _():
                done_here(u, turn).wait()
                done_core(u, turn).wait_send()

            value = ref[...].astype(F32)
            for j in range(4):
                cols = slice(j * 128, (j + 1) * 128)
                if wide:
                    for n in range(4):
                        part = SUB_ROWS // 4
                        st[pl.ds(4 * n + j, part, stride=16), :] = value[n * part : (n + 1) * part, cols]
                else:
                    st[pl.ds(j, SUB_ROWS, stride=4), :] = value[:, cols]
            sb[lax.rem(turn, 4)] = st[...].astype(BF16)
            done_here(u, turn).start()
            done_core(u, turn).start()

        def hand(u):
            theirs = helper_turn(u // SUBS) * SUBS + lax.rem(u, SUBS)
            place = wh.at[rows(theirs * SUB_ROWS + (theirs // SUBS + d) * 256, SUB_ROWS)]
            return grad_copy(S_HAND, R_HAND + theirs, half(u, d), place, (helper, d, r))

        def handed(u):
            return grad_copy(S_HAND, R_HAND + u, half(u, d), half(u, d), (p, d, r))

        def give_back(u, ref):
            t = u // SUBS
            theirs = lent_by[2](t) * SUBS + lax.rem(u, SUBS)
            place = wx.at[rows(jnp.where(lent_by[1](t) == 0, Z1_ZERO, 0) + theirs * SUB_ROWS, SUB_ROWS)]
            return grad_copy(S_BACK, R_BACK, ref, place, (lent_by[1](t), d, r))

        def finish(u, ref):
            when_kept(u, lambda: pack(u, u - first_own, ref))
            when_lent(u, lambda: give_back(u, ref).start())

        def give(t):
            compute(t)
            for k in range(SUBS):
                to_core(t * SUBS + k).start()
            for k in range(SUBS):
                u = t * SUBS + k
                to_core(u).wait_recv()
                add(u, from_core(u))
                hand(u).start()

        def unit_rows(units):
            return wh.at[0 : units * SUB_ROWS]

        take_at = turns + OUT_LAG - (last_lent - turns)

        def step(it, carry):
            for when, work in extra.items():
                pl.when(it == when)(work)
            for k, when in enumerate(lend + passed):
                pl.when(it == when)(lambda k=k: give(jnp.int32(count + k)))

            def start():
                @pl.when(lax.rem(it, SUBS) == 0)
                def _():
                    compute(it // SUBS)

                to_core(it).start()

            @pl.when(it < turns)
            def _():
                when_own(it, start)

            u1 = it - 1

            @pl.when((u1 >= 0) & (u1 < turns))
            def _():
                def join_cores():
                    to_core(u1).wait_recv()
                    add(u1, from_core(u1))

                when_own(u1, join_cores)
                when_handed(u1, lambda: handed(u1).wait_recv())

                @pl.when(outer & (u1 == 0))
                def _():
                    pl.semaphore_wait(ready.at[0], 1)

                @pl.when(outer)
                def _():
                    inwards(u1).start()

            u2 = it - 2

            @pl.when(inner & (u2 >= 0) & (u2 < turns))
            def _():
                @pl.when(u2 == 0)
                def _():
                    pl.semaphore_wait(ready.at[1], 1)

                inwards(u2).wait_recv()
                add(u2, from_z(u2))
                exchange(u2).start()

            u4 = it - ACROSS_LAG

            @pl.when(inner & (u4 >= 0) & (u4 < turns))
            def _():
                @pl.when(u4 == 0)
                def _():
                    pl.semaphore_wait(ready.at[0], 1)

                exchange(u4).wait()
                add(u4, from_across(u4))
                outwards(u4).start()
                finish(u4, half(u4, d))

            u8 = it - OUT_LAG

            @pl.when(outer & (u8 >= 0) & (u8 < turns))
            def _():
                outwards(u8).wait_recv()
                finish(u8, from_z(u8))

            @pl.when(it == norms_at)
            def _():
                bn_sums()

                @pl.when(outer)
                def _():
                    bn_in().start()

            @pl.when(inner & (it == norms_at + 4))
            def _():
                bn_in().wait_recv()
                dgs[:, norm_half] += bz[0, :, norm_half]
                bn_across().start()

            @pl.when(inner & (it == norms_at + 8))
            def _():
                bn_across().wait()
                dgb[:, norm_half] = dgs[:, norm_half] + bz[1, :, norm_half]
                bn_out().start()
                bn_core().start()

            @pl.when(outer & (it == norms_at + 14))
            def _():
                bn_out().wait_recv()
                dgb[:, norm_half] = bz[0, :, norm_half]
                bn_core().start()

            if lend:
                u_back = turns + it - take_at

                @pl.when(it == take_at)
                def _():
                    all_here(ars.at[R_BACK], unit_rows(last_lent - turns))

                @pl.when((u_back >= turns) & (u_back < last_lent))
                def _():
                    pack(u_back, own_turns + u_back - turns, from_z(u_back))

            return carry

        lax.fori_loop(0, turns + OUT_LAG, step, 0)

        bn_core().wait()

        @pl.when(outer)
        def _():
            bn_in().wait_send()

        @pl.when(inner)
        def _():
            bn_out().wait_send()

        @pl.when(outer)
        def _():
            all_sent(ass.at[S_IN], unit_rows(turns))

        @pl.when(inner)
        def _():
            all_sent(ass.at[S_OUT], unit_rows(turns))

        made = computed[1] * SUBS + last_given - turns
        if made:
            all_sent(ass.at[S_CORE], unit_rows(made))
        if last_given > turns:
            all_sent(ass.at[S_HAND], unit_rows(last_given - turns))
        if lent_by is not None:
            all_sent(ass.at[S_BACK], unit_rows(lent_by[3] * SUBS))
        all_here(ars.at[R_DONE], dw.at[pl.ds(0, own_turns + last_lent - turns)])
        for slot in range(4):
            done_here(first_own, jnp.int32(slot)).wait()
            done_core(first_own, jnp.int32(slot)).wait_send()

    @pl.when(p == 0)
    def _():
        open_weights(plain, 44)
        open_images()

    @pl.when(p == 1)
    def _():
        open_weights(plain, 48)
        open_images()
        pltpu.make_async_copy(cot, cotb.at[0:PIX_OUT], ls.at[16]).start()

    @pl.when(p == 2)
    def _():
        open_weights(own_parts, 15)

    @pl.when(p == 3)
    def _():
        open_weights(half_rows, 8)

    barrier = pltpu.get_barrier_semaphore()
    for device in (peer, (p, d, z_pair), (p, d, 3 - r)) + tuple((lax.rem(p + k, 4), d, r) for k in (1, 2, 3)):
        pl.semaphore_signal(barrier, inc=1, device_id=device, device_id_type=MESH)

    block_two = p >= 2
    set_of = per_row(lambda m: jnp.where(block_two, sets[1, m], sets[0, m]))
    for k in range(NSETS):
        hot = (set_of == k).astype(F32)
        for n in range(8):
            g = hot * gain[k : k + 1, n * BLK : (n + 1) * BLK]
            b = hot * bias[k : k + 1, n * BLK : (n + 1) * BLK]
            if k == 0:
                par[n] = g
                par[8 + n] = b
            else:
                par[n] += g
                par[8 + n] += b
    dg[...] = jnp.zeros_like(dg)
    pl.semaphore_wait(barrier, 6)

    total_in, total_out = 2.0 * PIX_IN, 2.0 * PIX_OUT

    def build_patches(base):
        def body(tap, carry):
            row, col = base(tap)
            window = pb[pl.ds(row, 7), pl.ds(col, 7)].reshape(RV, BLK)
            pt[tap, 0:RV, :] = window.astype(BF16)
            return carry

        lax.fori_loop(0, 9, body, 0)

    def clear_patch_pad():
        def body(tap, carry):
            pt[tap, RW - 16 : RW, :] = jnp.zeros((16, BLK), BF16)
            return carry

        lax.fori_loop(0, 9, body, 0)

    def strided_base(tap):
        di, dj = tap // 3, lax.rem(tap, 3)
        return lax.rem(di, 2) * 8 + di // 2, lax.rem(dj, 2) * 8 + dj // 2

    def plain_base(tap):
        return tap // 3, lax.rem(tap, 3)

    def conv(ref, first, target):
        target[...] = jnp.zeros_like(target)

        def body(tap, carry):
            z = nn(pt[tap], ref[rows(first + tap * BLK, BLK), :])
            target[...] += z.reshape(PP, 8, BLK)
            return carry

        lax.fori_loop(0, 9, body, 0)

    def conv_back(dz, ref, first, base, side):
        pb[0:side, 0:side] = jnp.zeros((side, side, 8, BLK), F32)

        def body(tap, carry):
            row, col = base(tap)
            part = nt(dz[0:RV, :], ref[rows(first + tap * BLK, BLK), :])
            pb[pl.ds(row, 7), pl.ds(col, 7)] += part.reshape(7, 7, 8, BLK)
            return carry

        lax.fori_loop(0, 9, body, 0)

    def stats_of_map(ref, slot_sum, slot_square):
        def body(c, _, carry):
            z = ref[c]
            return add_stats(carry, z, z * z)

        tx[slot_sum], tx[slot_square] = five(body, zero_stats)

    def act_to(ref, target, center, scale, g, b, mask):
        def body(c, i, carry):
            zhat = (ref[c] - center) * scale
            ref[c] = zhat
            h = silu(zhat * g + b) * mask
            target[rows(i * 80, 80), :] = h.reshape(80, BLK).astype(BF16)
            return carry

        five(body)
        clear_pad(target, 0)

    def upstream(target, grad, zhat_ref, g, b, mask, slot_sum, slot_gain):
        def body(c, i, carry):
            zhat = zhat_ref[c]
            du = grad[rows(i * 80, 80), :].astype(F32).reshape(10, 8, BLK) * mask * slope(zhat * g + b)
            target[c] = du
            return add_stats(carry, du, du * zhat)

        tx[slot_sum], tx[slot_gain] = five(body, zero_stats)

    def norm_back(target, first, du_ref, du_first, zhat_ref, zhat_first, gscale, mean_du, mean_dg, unrolled=False):
        def body(c, i, carry):
            du = du_ref[pl.ds(du_first + i * 10, 10)]
            zhat = zhat_ref[pl.ds(zhat_first + i * 10, 10)]
            dz = gscale * (du - mean_du - zhat * mean_dg)
            target[rows(first + i * 80, 80), :] = dz.reshape(80, BLK).astype(BF16)
            return carry

        five(body, unrolled=unrolled)
        clear_pad(target, first)

    def gi_copy():
        return pltpu.make_async_copy(f3.at[0:PIX_IN, :, 0:256], gi, ls.at[17])

    def out_copy():
        return pltpu.make_async_copy(v_out, out, ls.at[0])

    def dgb_copy():
        return pltpu.make_async_copy(dgb, dgb_out, ls.at[1])

    def final_part():
        @pl.when(p != 1)
        def _():
            remote(ob, ob, C_SHARE, C_SHARE, (p, d, r)).wait_recv()
            remote(r1, r1, C_GP, C_GP, (p, d, r)).wait_recv()

        @pl.when(p != 0)
        def _():
            remote(r0, r0, C_GI, C_GI, (p, d, r)).wait_recv()

        v_out[...] = ob[0:RV, :].astype(F32).reshape(PIX_OUT, 8, BLK).astype(BF16)
        out_copy().start()
        f0[0:PP, :, 0:256] = r1[...].astype(F32).reshape(PP, 8, 256)

        def place(a, carry):
            m = r0[rows(a * 224, 224), :].astype(F32).reshape(28, 8, 256)
            first = m[0:14].reshape(7, 2, 8, 256)
            even = first[:, 0] + f0[pl.ds(a * 7, 7), :, 0:256]
            f3[pl.ds(a * 28, 14), :, 0:256] = jnp.stack([even, first[:, 1]], axis=1).reshape(14, 8, 256)
            f3[pl.ds(a * 28 + 14, 14), :, 0:256] = m[14:28]
            return carry

        lax.fori_loop(0, 7, place, 0)
        gi_copy().start()

    @pl.when(p == 0)
    def _():
        mask = mask_of(0)

        def relay(i):
            piece_copy(W_VIA, i, quarter, (0, d, r)).wait_recv()
            piece_copy(W_OWN, i, quarter, (1, d, r)).start()

        def relay_half(i):
            half_copy(W_VIA, i, d, (0, d, r)).wait_recv()
            half_copy(W_OWN, i, d, (1, d, r)).start()

        put_w = put_narrow(wh, lambda i: i * 128)
        load_weights(plain, 44, 0, 8, put_w)

        def first_conv(q, slot, carry):
            rows_q = imgb[slot].astype(F32).reshape(224, 1024).astype(BF16)
            wx[rows(q * 224, 224), :] = rows_q[:, 0:512]
            wx[rows(1568 + q * 224, 224), :] = rows_q[:, 512:1024]
            z = nn(rows_q, wh[0:1024, :]).reshape(28, 8, BLK)
            f0[pl.ds(q * 28, 28)] = z
            load_weights(plain, 44, 8 + 5 * q, 5, put_w)
            return add_stats(carry, z, z * z)

        tx[0], tx[1] = over_images(first_conv, zero_stats)
        relay(VIA)
        exchange = remote(tx.at[pl.ds(0, 2)], rx.at[pl.ds(0, 2)], 0, 0, peer)
        exchange.start()
        pb[...] = jnp.zeros_like(pb)
        clear_patch_pad()
        load_weights(plain, 44, 43, 1, put_w)
        exchange.wait()

        center, scale = moments(0, 1, total_in, 0)
        g1, b1, g2, b2 = par[0], par[8], par[1], par[9]

        def hidden(i, carry):
            zhat = (f0[pl.ds(i * 14, 14)] - center) * scale
            f0[pl.ds(i * 14, 14)] = zhat
            h = (silu(zhat * g1 + b1) * mask).astype(BF16).astype(F32).reshape(7, 2, 8, BLK)
            u = i + 1
            row = lax.rem(u, 2) * 8 + u // 2
            pb[row, 8:15] = h[:, 0]
            pb[row, 1:8] = h[:, 1]
            return carry

        lax.fori_loop(0, 14, hidden, 0)
        relay(VIA + 1)
        build_patches(strided_base)
        conv(wh, 1024, fs.at[0])
        relay(VIA + 2)
        stats_of_map(fs.at[0], 2, 3)
        sync(1, 2, 2)
        center, scale = moments(2, 3, total_out, 1)
        act_to(fs.at[0], h2, center, scale, g2, b2, mask)
        send = remote(h2, h2, C_H2, C_H2, (1, d, r))
        send.start()
        for i in (HALF, HALF + 1, 16):
            relay_half(i)
        zero_rest(11, sb)
        send.wait_send()
        all_sent(wss.at[W_OWN], wx.at[0 : 3 * 128 + 3 * 256])
        say_ready()

        remote(dh, dh, C_DH, C_DH, (0, d, r)).wait_recv()
        upstream(fs.at[1], dh, fs.at[0], g2, b2, mask, 4, 5)
        sync(0, 4, 2)
        s_du, s_dg = both(4), both(5)
        dg[1], dg[9] = s_dg, s_du
        norm_back(d5, 0, fs.at[1], 0, fs.at[0], 0, g2 * inv[1], s_du * (1.0 / total_out), s_dg * (1.0 / total_out))
        def back_conv():
            conv_back(d5, wh, 1024, strided_base, 16)

        def slopes(i, carry):
            u = i + 1
            row = lax.rem(u, 2) * 8 + u // 2
            grad = jnp.stack([pb[row, 8:15], pb[row, 1:8]], axis=1).reshape(14, 8, BLK)
            zhat = f0[pl.ds(i * 14, 14)]
            du = grad * mask * slope(zhat * g1 + b1)
            f1[pl.ds(i * 14, 14)] = du
            return add_stats(carry, du, du * zhat)

        def first_slopes():
            tx[6], tx[7] = lax.fori_loop(0, 14, slopes, zero_stats)
            sync(1, 6, 2)
            dg[0], dg[8] = both(7), both(6)

        def first_back():
            s_du, s_dg = both(6), both(7)
            gscale, m_du, m_dg = g1 * inv[0], s_du * (1.0 / total_in), s_dg * (1.0 / total_in)

            def body(q, carry):
                part = pl.ds(q * 28, 28)
                dz = gscale * (f1[part] - m_du - f0[part] * m_dg)
                u1[rows(q * 224, 224), :] = dz.reshape(224, BLK).astype(BF16)
                return carry

            lax.fori_loop(0, 7, body, 0)

        def share(target, column, k):
            def body(q, carry):
                g = nt(u1[rows(q * 224, 224), :], wh[k * 256 : (k + 1) * 256, :])
                target[rows(q * 224, 224), column : column + 256] = g.astype(BF16)
                return carry

            lax.fori_loop(0, 7, body, 0)

        places = {1: (u0, 0), 2: (u0, 256), 3: (u2, 0)}

        def share_copy(k):
            target, column = places[k]
            return remote(target.at[0:1568, column : column + 256], r0, C_GI + k - 1, C_GI, (k, d, r))

        def share_out(k):
            share(*places[k], k)
            share_copy(k).start()

        def back_and_share():
            first_back()
            share_out(1)

        def compute(t):
            taps = (t < 7) | (t >= 9)

            @pl.when(taps)
            def _():
                tap = jnp.where(t < 7, t, t - 2)
                wh[rows(at_row(t), 512), :] = tn(pt[tap], d5[...]).astype(BF16)

            @pl.when(jnp.logical_not(taps))
            def _():
                block = tn(wx[rows((t - 7) * 1568, 1568), :], u1[0:1568, :])
                wh[rows(at_row(t), 512), :] = block.astype(BF16)

        def at_row(t):
            return jnp.where(t < 2, 5632 + t * 512, jnp.where(t < 9, t * 512, 2048 + t * 512))

        sum_gradients(
            9, compute, at_row, lambda t: jnp.where(t < 7, t + 2, jnp.where(t < 9, t - 7, t)), False, Z1_ZERO,
            {
                2 * SUBS: back_conv,
                3 * SUBS: first_slopes,
                4 * SUBS: back_and_share,
                5 * SUBS: lambda: share_out(2),
                6 * SUBS: lambda: share_out(3),
                7 * SUBS: lambda: share(r0, 0, 0),
                LAST_TURN + 9 * SUBS: final_part,
            },
            lend=(2, 3), helper=2, helper_turn=lambda t: t - 4, norms_at=4 * SUBS,
        )
        for k in (1, 2, 3):
            share_copy(k).wait_send()

    @pl.when(p == 1)
    def _():
        mask = mask_of(1)
        gate_v = per_row(lambda m: gates[m]).astype(F32)
        cotb[PIX_OUT] = jnp.zeros((8, C_OUT), BF16)
        clear_patch_pad()
        load_weights(plain, 48, 0, 16, put_wide(wh, 0, 512, 0))
        load_weights(plain, 48, 16, 32, put_wide(wh, 2048, 1024, 16))

        def shorten(a, slot, carry):
            v = imgb[slot, 0:14].astype(F32).reshape(7, 2, 8, 1024)[:, 0]
            f0[pl.ds(a * 7, 7)] = v[:, :, 0:512]
            f0[pl.ds(PP + a * 7, 7)] = v[:, :, 512:1024]
            return carry

        other_z = 2 * (1 - lax.rem(r, 2))
        this_z = 2 * lax.rem(r, 2)

        def pass_own(i):
            piece_copy(W_OWN, i, quarter, (1, d, r)).wait_recv()
            piece_copy(W_PEER, i, quarter, peer).start()
            piece_copy(W_Z, i, quarter, z_dev).start()

        def pass_on(i):
            piece_copy(W_Z, i, other_z + d, peer).wait_recv()
            piece_copy(W_ON, i, other_z + d, peer).start()

        def have(i):
            piece_copy(W_PEER, i, this_z + 1 - d, peer).wait_recv()
            piece_copy(W_ON, i, other_z + 1 - d, peer).wait_recv()

        def pass_half(i):
            half_copy(W_OWN, i, d, (1, d, r)).wait_recv()
            half_copy(W_PEER, i, d, peer).start()

        def have_half(i):
            half_copy(W_PEER, i, 1 - d, peer).wait_recv()

        pass_own(0)
        over_images(shorten, 0)
        f0[PIX_OUT] = jnp.zeros((8, BLK), F32)
        f0[PP + PIX_OUT] = jnp.zeros((8, BLK), F32)
        sx[...] = f0[0 : 2 * PP].reshape(2 * RW, BLK).astype(BF16)

        def shortcut(n, carry):
            z = nn(sx[0:RW, :], wh[rows(2048 + n * 1024, 512), :]) + nn(
                sx[RW : 2 * RW, :], wh[rows(2560 + n * 1024, 512), :]
            )
            store_z(f1, n * PP, z, 4 * n + 2, 4 * n + 3)
            return carry

        pass_own(1)
        lax.fori_loop(0, 4, shortcut, 0)

        pass_own(2)
        pass_own(VIA)
        pass_on(0)
        pass_own(3)
        pass_on(1)
        pass_own(VIA + 1)
        pass_own(4)
        pl.semaphore_signal(go, inc=1, device_id=(3, d, r), device_id_type=MESH)
        pass_on(2)
        pass_own(VIA + 2)
        pass_own(5)
        pass_on(VIA)
        pass_own(6)
        pass_on(3)
        pass_own(7)
        pass_on(VIA + 1)
        remote(h2, h2, C_H2, C_H2, (1, d, r)).wait_recv()

        def third_conv(n, carry):
            store_z(f0, n * PP, nn(h2[...], wh[rows(n * 512, 512), :]), 4 * n, 4 * n + 1)
            exchange_of(E_WIDE + n, 4 * n, 4).start()
            return carry

        lax.fori_loop(0, 4, third_conv, 0)
        pass_on(4)

        def join(n, carry):
            exchange_of(E_WIDE + n, 4 * n, 4).wait()
            c3, s3 = moments(4 * n, 4 * n + 1, total_out, 2 + n)
            cp, sp = moments(4 * n + 2, 4 * n + 3, total_out, 6 + n)
            g3, gp, b = par[n], par[4 + n], par[8 + n] + par[12 + n]

            def body(_, i, carry):
                part = pl.ds(n * PP + i * 10, 10)
                a = (f0[part] - c3) * s3
                b_ = (f1[part] - cp) * sp
                f0[part] = a
                f1[part] = b_
                o = silu(a * g3 + b_ * gp + b)
                u0[rows(n * RW + i * 80, 80), :] = o.reshape(80, BLK).astype(BF16)
                return carry

            five(body)
            clear_pad(u0, n * RW)
            return carry

        lax.fori_loop(0, 4, join, 0)
        for n in (1, 2, 3):
            o1_copy(n, 3).start()
        pass_half(13)
        pass_on(VIA + 2)
        pass_half(HALF)
        each(have, 0, 4)
        zhat4, zhat5 = fs.at[0], fs.at[1]
        z = nn(u0[0:RW, :], wx[0:512, :])
        for n in range(1, 4):
            z += nn(u0[n * RW : (n + 1) * RW, :], wx[n * 512 : (n + 1) * 512, :])
        store_z(zhat4, 0, z, 16, 17)
        sync(0, 16, 2)
        remote(parx.at[0:4], parx.at[0:4], C_PAR2, C_PAR2, (1, d, r)).wait_recv()
        center, scale = moments(16, 17, total_out, 10)
        g4, g5, b4, b5 = parx[0], parx[1], parx[2], parx[3]
        pb[0:9, 0:9] = jnp.zeros((9, 9, 8, BLK), F32)

        def hidden(a, carry):
            part = pl.ds(a * 7, 7)
            zhat = (zhat4[part] - center) * scale
            zhat4[part] = zhat
            h = silu(zhat * g4 + b4) * mask
            pb[a + 1, 1:8] = h.astype(BF16).astype(F32)
            return carry

        lax.fori_loop(0, 7, hidden, 0)
        h4[0:RV, :] = pb[1:8, 1:8].reshape(RV, BLK).astype(BF16)
        h4_send = remote(h4, h4, C_H4, C_H4, (2, d, r))
        h4_send.start()

        o1_copy(0, 2).start()
        pass_on(5)
        build_patches(plain_base)

        def fifth_conv(taps):
            left = jnp.concatenate([pt[t] for t in taps], axis=1)
            right = jnp.concatenate([wx[2048 + t * 512 : 2560 + t * 512, :] for t in taps], axis=0)
            return nn(left, right).reshape(PP, 8, BLK)

        for i in (4, 5, VIA):
            have(i)
        zhat5[...] = fifth_conv((0, 1, 4))
        pass_half(14)
        pass_on(6)
        for i in (6, VIA + 1, VIA + 2):
            have(i)
        zhat5[...] += fifth_conv((2, 5, 6))
        pass_half(HALF + 1)
        pass_on(7)
        have(7)
        have_half(HALF)
        have_half(HALF + 1)
        zhat5[...] += fifth_conv((3, 7, 8))
        pass_half(15)
        stats_of_map(zhat5, 18, 19)
        sync(1, 18, 2)
        center, scale = moments(18, 19, total_out, 11)
        act_to(zhat5, h5, center, scale, g5, b5, mask)

        pass_half(16)

        def sixth_conv(n):
            have_half(13 + n)
            store_z(f2, n * PP, nn(h5[...], wx[6656 + n * 512 : 7168 + n * 512, :]), 20 + 2 * n, 21 + 2 * n)

        def exchange_z6(n):
            return exchange_of(E_WIDE_NEXT + n, 20 + 2 * n, 2)

        def exchange_d6(n):
            return exchange_of(E_WIDE + n, 28 + 2 * n, 2)

        def finish(n):
            center, scale = moments(20 + 2 * n, 21 + 2 * n, total_out, 12 + n)
            g6, b6 = parx[4 + n], parx[8 + n]

            def body(c, i, carry):
                part = pl.ds(n * PP + i * 10, 10)
                part_rows = rows(n * RW + i * 80, 80)
                zhat = (f2[part] - center) * scale
                f2[part] = zhat
                o = u0[part_rows, :].astype(F32).reshape(10, 8, BLK)
                q = o + zhat * g6 + b6
                s = sigmoid(q)
                act = q * s
                pt[n, rows(i * 80, 80), :] = (o + gate_v * (act - o)).reshape(80, BLK).astype(BF16)
                ct = cotb[c, :, n * BLK : (n + 1) * BLK].astype(F32)
                through = ct * gate_v
                dq = through * (s + act * (1.0 - s))
                f3[part] = dq
                u2[part_rows, :] = (dq + (ct - through)).reshape(80, BLK).astype(BF16)
                return add_stats(carry, dq, dq * zhat)

            tx[28 + 2 * n], tx[29 + 2 * n] = five(body, zero_stats, unrolled=True)

        for n in (0, 1):
            sixth_conv(n)
            exchange_z6(n).start()
        remote(parx.at[4:12], parx.at[4:12], C_PAR3, C_PAR3, (1, d, r)).wait_recv()
        pltpu.make_async_copy(cot, cotb.at[0:PIX_OUT], ls.at[16]).wait()
        for n in range(4):
            if n < 2:
                have_half(15 + n)
            exchange_z6(n).wait()
            if n < 2:
                store_z(
                    f2, (n + 2) * PP, nn(h5[...], wx[7680 + n * 512 : 8192 + n * 512, :]), 24 + 2 * n, 25 + 2 * n
                )
            finish(n)
            if n < 2:
                exchange_z6(n + 2).start()
            exchange_d6(n).start()
        ob[...] = pt[1]


        def sixth_back(n):
            s_du, s_dg = both(28 + 2 * n), both(29 + 2 * n)
            dgx[4 + n] = s_dg
            dgx[8 + n] = s_du
            norm_back(
                u1, n * RW, f3, n * PP, f2, n * PP, parx[4 + n] * inv[12 + n],
                s_du * (1.0 / total_out), s_dg * (1.0 / total_out), unrolled=True,
            )

        for n in range(4):
            exchange_d6(n).wait()
        grad = jnp.zeros((RW, BLK), F32)
        for n in range(5):
            if n < 4:
                sixth_back(n)
            if n > 0:
                grad += nt(u1[(n - 1) * RW : n * RW, :], wx[6144 + n * 512 : 6656 + n * 512, :])
        dh[...] = grad.astype(BF16)

        upstream(f2, dh, zhat5, g5, b5, mask, 36, 37)
        sync(0, 36, 2)
        s_du, s_dg = both(36), both(37)
        dgx[1] = s_dg
        dgx[3] = s_du
        norm_back(d5, 0, f2, 0, zhat5, 0, g5 * inv[11], s_du * (1.0 / total_out), s_dg * (1.0 / total_out))
        d5_send = remote(d5, d5, C_D5, C_D5, (2, d, r))
        d5_send.start()
        pb[0:9, 0:9] = jnp.zeros((9, 9, 8, BLK), F32)
        for tap in range(9):
            row, col = tap // 3, tap % 3
            part = nt(d5[0:RV, :], wx[2048 + tap * 512 : 2560 + tap * 512, :])
            pb[row : row + 7, col : col + 7] += part.reshape(7, 7, 8, BLK)

        def fourth_slopes(a, carry):
            part = pl.ds(a * 7, 7)
            zhat = zhat4[part]
            du = pb[a + 1, 1:8] * mask * slope(zhat * g4 + b4)
            f2[part] = du
            return add_stats(carry, du, du * zhat)

        tx[38], tx[39] = lax.fori_loop(0, 7, fourth_slopes, zero_stats)
        sync(1, 38, 2)
        s_du, s_dg = both(38), both(39)
        dgx[0] = s_dg
        dgx[2] = s_du
        norm_back(d4, 0, f2, 0, zhat4, 0, g4 * inv[10], s_du * (1.0 / total_out), s_dg * (1.0 / total_out))

        def carried_back(n):
            z = nt(d4[...], wx[n * 512 : (n + 1) * 512, :])
            f2[(n % 2) * PP : (n % 2 + 1) * PP] = z.reshape(PP, 8, BLK)

        def exchange_d1(n):
            return exchange_of(E_WIDE_NEXT + n, 40 + 3 * n, 3)

        def first_block_slopes(n):
            g3, gp, b = par[n], par[4 + n], par[8 + n] + par[12 + n]

            def body(_, i, carry):
                part = pl.ds(n * PP + i * 10, 10)
                do = u2[n * RW + i * 80 : n * RW + (i + 1) * 80, :].astype(F32).reshape(10, 8, BLK)
                do += f2[pl.ds((n % 2) * PP + i * 10, 10)]
                a, b_ = f0[part], f1[part]
                dp = do.astype(BF16).astype(F32) * slope(a * g3 + b_ * gp + b)
                f3[part] = dp
                s0, s1, s2 = carry
                return s0 + jnp.sum(dp, axis=0), s1 + jnp.sum(dp * a, axis=0), s2 + jnp.sum(dp * b_, axis=0)

            first = 40 + 3 * n
            tx[first], tx[first + 1], tx[first + 2] = five(body, zero_stats + zero_stats[:1], unrolled=True)

        carried_back(0)
        for n in range(4):
            if n < 3:
                carried_back(n + 1)
            first_block_slopes(n)
            exchange_d1(n).start()

        def third_back(n):
            first = 40 + 3 * n
            m_du, m_dg = both(first) * (1.0 / total_out), both(first + 1) * (1.0 / total_out)
            norm_back(
                pt.at[4 + n], 0, f3, n * PP, f0, n * PP, par[n] * inv[2 + n], m_du, m_dg, unrolled=True
            )

        for n in range(4):
            exchange_d1(n).wait()
        grad = jnp.zeros((RW, BLK), F32)
        for n in range(5):
            if n < 4:
                third_back(n)
            if n > 0:
                grad += nt(pt[3 + n], wh[(n - 1) * 512 : n * 512, :])
        dh[...] = grad.astype(BF16)
        dh_send = remote(dh, dh, C_DH, C_DH, (0, d, r))
        dh_send.start()

        def shortcut_back(n, carry):
            first = 40 + 3 * n
            s_du, s_d3, s_dp = both(first), both(first + 1), both(first + 2)
            dg[n] = s_d3
            dg[4 + n] = s_dp
            dg[8 + n] = s_du
            dg[12 + n] = s_du
            m_du, m_dg = s_du * (1.0 / total_out), s_dp * (1.0 / total_out)
            norm_back(u2, n * RW, f3, n * PP, f1, n * PP, par[4 + n] * inv[6 + n], m_du, m_dg)
            return carry

        lax.fori_loop(0, 4, shortcut_back, 0)
        all_sent(wss.at[W_PEER], wx.at[0 : HALF * 128 + 6 * 256])
        all_sent(wss.at[W_Z], wx.at[0 : HALF * 128])
        all_sent(wss.at[W_ON], wx.at[0 : HALF * 128])
        say_ready()

        late = [remote(d4, d4, C_D4, C_D4, (2, d, r))]
        for first, last, sem, chip in ((0, 4, C_DG2, 2), (4, 12, C_DG3, 3)):
            late.append(remote(dgx.at[first:last], dgx.at[first:last], sem, sem, (chip, d, r)))
        later = [
            remote(pt.at[k], ob, C_SHARE + slot, C_SHARE, (k, d, r)) for slot, k in enumerate((0, 2, 3))
        ]

        def late_sends():
            dh_send.wait_send()
            for copy in late:
                copy.start()

        def shortcut_share(k):
            g = nt(u2[0:RW, :], wh[2048 + k * 256 : 2304 + k * 256, :])
            for n in range(1, 4):
                g += nt(u2[n * RW : (n + 1) * RW, :], wh[2048 + n * 1024 + k * 256 : 2304 + n * 1024 + k * 256, :])
            return g.astype(BF16)

        places = ((h4.at[:, 0:256], 0), (h4.at[:, 256:512], 2), (pt.at[8, :, 0:256], 3))

        def share_copy(slot):
            place, k = places[slot]
            return remote(place, r1, C_GP + slot, C_GP, (k, d, r))

        def shortcut_shares(slot):
            place, k = places[slot]
            if slot == 0:
                h4_send.wait_send()
            place[...] = shortcut_share(k)

        def shortcut_own():
            r1[...] = shortcut_share(1)

        def late_shares():
            for copy in later:
                copy.start()
            for slot in range(3):
                share_copy(slot).start()

        def at_row(t):
            return jnp.where(t < 10, t * 512, jnp.where(t < 15, t * 512 + 1024, 5632))

        def compute(t):
            @pl.when(t < 4)
            def _():
                left = h2[:, pl.ds(pl.multiple_of(t * 128, 128), 128)]
                for n in range(4):
                    put_chunk(at_row(t), n, tn(left, pt[4 + n]))

            @pl.when((t >= 4) & (t < 12))
            def _():
                m = t - 4
                left = sx[rows((m // 4) * RW, RW), pl.ds(pl.multiple_of(lax.rem(m, 4) * 128, 128), 128)]
                for n in range(4):
                    put_chunk(at_row(t), n, tn(left, u2[n * RW : (n + 1) * RW, :]))

            @pl.when(t >= 12)
            def _():
                left = h5[:, pl.ds(pl.multiple_of((t - 12) * 128, 128), 128)]
                for n in range(4):
                    put_chunk(at_row(t), n, tn(left, u1[n * RW : (n + 1) * RW, :]))

        zero_rest(12, sb)
        sum_gradients(
            10, compute, at_row, lambda t: t, True, 0,
            {
                2: lambda: shortcut_shares(0),
                4: lambda: shortcut_shares(1),
                5: late_sends,
                6: lambda: shortcut_shares(2),
                8: shortcut_own,
                14: late_shares,
                LAST_TURN + 10 * SUBS: final_part,
            },
            lend=(3, 5), passed=(7, 9, 11, 13), helper=3, helper_turn=lambda t: t - 6, norms_at=2,
        )
        for copy in [d5_send, o1_copy(0, 2)] + [o1_copy(n, 3) for n in (1, 2, 3)] + late + later:
            copy.wait_send()
        for slot in range(3):
            share_copy(slot).wait_send()


    @pl.when(p == 2)
    def _():
        for k, slot in ((0, 0), (1, 1), (2, 8), (3, 9)):
            parx[k] = par[slot]
        par_send = remote(parx.at[0:4], parx.at[0:4], C_PAR2, C_PAR2, (1, d, r))
        par_send.start()

        put_w = put_narrow(wx, lambda i: own_parts(i) * 128)

        def put(i):
            put_w(i)

            @pl.when(i < VIA)
            def _():
                piece_copy(W_OWN, i, quarter, (1, d, r)).start()

            @pl.when((i >= VIA) & (i < HALF))
            def _():
                piece_copy(W_VIA, i, quarter, (0, d, r)).start()

            for k in range(HALF, 13):
                @pl.when(i == HALF + 2 * (k - HALF) + 1)
                def _(k=k):
                    half_copy(W_VIA, k, d, (0, d, r)).start()

        load_weights(own_parts, 15, 0, 15, put)
        pb[...] = jnp.zeros_like(pb)
        clear_patch_pad()

        all_sent(wss.at[W_OWN], wx.at[0 : VIA * 128])
        all_sent(wss.at[W_VIA], wx.at[0 : 3 * 128 + 2 * 256])
        say_ready()
        remote(h4, h4, C_H4, C_H4, (2, d, r)).wait_recv()
        pb[1:8, 1:8] = h4[0:RV, :].astype(F32).reshape(7, 7, 8, BLK)
        build_patches(plain_base)
        remote(d5, d5, C_D5, C_D5, (2, d, r)).wait_recv()

        def compute(t):
            taps = (t < 5) | (t >= 11)

            @pl.when(taps)
            def _():
                tap = jnp.where(t < 5, t + 4, t - 11)
                wh[rows(t * 512, 512), :] = tn(pt[tap], d5[...]).astype(BF16)

            @pl.when(t == 7)
            def _():
                remote(d4, d4, C_D4, C_D4, (2, d, r)).wait_recv()
                for n in range(4):
                    o1_copy(n, 2).wait_recv()

            @pl.when(jnp.logical_not(taps))
            def _():
                wh[rows(t * 512, 512), :] = tn(u0[rows((t - 7) * RW, RW), :], d4[...]).astype(BF16)

        def norm_grads():
            remote(dgx.at[0:4], dgx.at[0:4], C_DG2, C_DG2, (2, d, r)).wait_recv()
            dg[0], dg[1], dg[8], dg[9] = dgx[0], dgx[1], dgx[2], dgx[3]

        sum_gradients(
            11, compute, lambda t: t * 512, lambda t: jnp.where(t < 5, t + 8, t - 7), False, 0,
            {6 * SUBS: norm_grads, LAST_TURN + 11 * SUBS: final_part},
            lend=(2, 3, 4, 6), helper=3, helper_turn=lambda t: t - 11,
            handed_in=lambda t: (t >= 5) & (t < 7),
            lent_by=(lambda t: (t >= 5) & (t < 7), lambda t: 0, lambda t: t + 4, 2),
            computed=(0, 9), packed_here=(0, 9), norms_at=6 * SUBS,
        )
        par_send.wait_send()

    @pl.when(p == 3)
    def _():
        for k in range(4):
            parx[4 + k] = par[k]
            parx[8 + k] = par[8 + k]
        par_send = remote(parx.at[4:12], parx.at[4:12], C_PAR3, C_PAR3, (1, d, r))
        par_send.start()
        say_ready()

        def put(i):
            for n in range(4):
                for j in range(4):
                    wx[rows(6656 + n * 512 + d * 256 + i * 32, 32), j * 128 : (j + 1) * 128] = st[
                        pl.ds(4 * n + j, 32, stride=16), :
                    ].astype(BF16)

        load_weights(half_rows, 8, 0, 8, put)
        zero_rest(4, sb)
        pl.semaphore_wait(go, 1)

        half_copy(W_VIA, 16, d, (0, d, r)).start()
        for i in (13, 14, 15):
            half_copy(W_OWN, i, d, (1, d, r)).start()
        for n in (1, 2, 3):
            o1_copy(n, 3).wait_recv()
            o1_copy(n, 2).start()
        def norm_grads():
            remote(dgx.at[4:12], dgx.at[4:12], C_DG3, C_DG3, (3, d, r)).wait_recv()
            for k in range(4):
                dg[k] = dgx[4 + k]
                dg[8 + k] = dgx[8 + k]

        sum_gradients(
            10, lambda t: None, lambda t: t * 512, lambda t: t - 6, True, 0,
            {5 * SUBS: norm_grads, LAST_TURN + 10 * SUBS: final_part},
            handed_in=lambda t: t >= 0,
            lent_by=(lambda t: t < 6, lambda t: jnp.where(t < 4, 2, 1), lambda t: jnp.where(t < 4, t + 11, t + 6), 6),
            computed=(0, 0), packed_here=(6, 4), norms_at=5 * SUBS,
        )
        for n in (1, 2, 3):
            o1_copy(n, 2).wait_send()
        all_sent(wss.at[W_VIA], wx.at[0:256])
        all_sent(wss.at[W_OWN], wx.at[0 : 3 * 256])
        par_send.wait_send()

    dgb_copy().start()
    gi_copy().wait()
    out_copy().wait()
    dgb_copy().wait()


def widen_kernel(out_in, gi_in, dw_in, dgb_in, out, gi, dw, gain, bias, v_out, v_gi, v_dw, v_wide, v_dgb, sin, sout):
    count = v_dw.shape[0] // 2048

    def part(i):
        return pl.ds(i * 2048, 2048)

    loads = [pltpu.make_async_copy(dw_in.at[part(i)], v_dw.at[part(i)], sin.at[i]) for i in range(count)]
    others = (
        (dgb_in, v_dgb, ((v_dgb.at[0:4], gain), (v_dgb.at[4:8], bias))),
        (out_in, v_out, ((v_out, out),)),
        (gi_in, v_gi, ((v_gi, gi),)),
    )
    more = [pltpu.make_async_copy(a, b, sin.at[count + k]) for k, (a, b, _) in enumerate(others)]
    for copy in loads + more:
        copy.start()
    stores = []
    for i in range(count):
        loads[i].wait()
        v_wide[part(i)] = v_dw[part(i)].astype(F32)
        stores.append(pltpu.make_async_copy(v_wide.at[part(i)], dw.at[part(i)], sout.at[i]))
        stores[-1].start()
    for k, (_, _, ends) in enumerate(others):
        more[k].wait()
        for a, b in ends:
            stores.append(pltpu.make_async_copy(a, b, sout.at[len(stores)]))
            stores[-1].start()
    for copy in stores:
        copy.wait()


def widen(out, gi, dw, dgb):
    count = P_SIZE // 128 // 2048
    any_space = pl.BlockSpec(memory_space=pl.ANY)
    return pl.pallas_call(
        widen_kernel,
        out_shape=(
            jax.ShapeDtypeStruct(out.shape, out.dtype),
            jax.ShapeDtypeStruct(gi.shape, gi.dtype),
            jax.ShapeDtypeStruct(dw.shape, F32),
            jax.ShapeDtypeStruct((4, 4096), F32),
            jax.ShapeDtypeStruct((4, 4096), F32),
        ),
        in_specs=[any_space] * 4,
        out_specs=(any_space,) * 5,
        scratch_shapes=[
            pltpu.VMEM(out.shape, out.dtype),
            pltpu.VMEM(gi.shape, gi.dtype),
            pltpu.VMEM(dw.shape, BF16),
            pltpu.VMEM(dw.shape, F32),
            pltpu.VMEM(dgb.shape, F32),
            pltpu.SemaphoreType.DMA((count + 3,)),
            pltpu.SemaphoreType.DMA((count + 4,)),
        ],
        compiler_params=pltpu.CompilerParams(vmem_limit_bytes=64 * 1024 * 1024),
    )(out, gi, dw, dgb)


def one_kernel(images, section_weights, bn_gain, bn_bias, width, bn_set, gate, cotangent):
    any_space = pl.BlockSpec(memory_space=pl.ANY)
    vmem = pl.BlockSpec(memory_space=pltpu.VMEM)
    smem = pl.BlockSpec(memory_space=pltpu.SMEM)
    out, gi, dw, dgb = pl.pallas_call(
        whole_kernel,
        out_shape=(
            jax.ShapeDtypeStruct((PIX_OUT, 8, BLK), BF16),
            jax.ShapeDtypeStruct((PIX_IN, 8, 256), F32),
            jax.ShapeDtypeStruct((P_SIZE // SUB, 512, 128), BF16),
            jax.ShapeDtypeStruct((8, 4096), F32),
        ),
        in_specs=[any_space, any_space, vmem, vmem, smem, smem, smem, any_space],
        out_specs=(any_space,) * 4,
        scratch_shapes=[
            pltpu.VMEM((4, 28, 8, 1024), BF16),
            pltpu.VMEM((RING, 1, SUB), BF16),
            pltpu.VMEM((512, 128), F32),
            pltpu.VMEM((8704, BLK), BF16),
            pltpu.VMEM((8768, BLK), BF16),
            pltpu.VMEM((4 * PP, 8, BLK), F32),
            pltpu.VMEM((4 * PP, 8, BLK), F32),
            pltpu.VMEM((4 * PP, 8, BLK), F32),
            pltpu.VMEM((4 * PP, 8, BLK), F32),
            pltpu.VMEM((2, PP, 8, BLK), F32),
            pltpu.VMEM((16, 16, 8, BLK), F32),
            pltpu.VMEM((9, RW, BLK), BF16),
            pltpu.VMEM((4 * RW, BLK), BF16),
            pltpu.VMEM((4 * RW, BLK), BF16),
            pltpu.VMEM((4 * RW, BLK), BF16),
            pltpu.VMEM((2 * RW, BLK), BF16),
            pltpu.VMEM((PP, 8, C_OUT), BF16),
            pltpu.VMEM((RW, BLK), BF16),
            pltpu.VMEM((RW, BLK), BF16),
            pltpu.VMEM((RW, BLK), BF16),
            pltpu.VMEM((RW, BLK), BF16),
            pltpu.VMEM((RW, BLK), BF16),
            pltpu.VMEM((RW, BLK), BF16),
            pltpu.VMEM((8 * PIX_IN, 256), BF16),
            pltpu.VMEM((RW, 256), BF16),
            pltpu.VMEM((RW, BLK), BF16),
            pltpu.VMEM((52, 8, BLK), F32),
            pltpu.VMEM((52, 8, BLK), F32),
            pltpu.VMEM((16, 8, BLK), F32),
            pltpu.VMEM((16, 8, BLK), F32),
            pltpu.VMEM((12, 8, BLK), F32),
            pltpu.VMEM((16, 8, BLK), F32),
            pltpu.VMEM((12, 8, BLK), F32),
            pltpu.VMEM((4, 512, 128), BF16),
            pltpu.VMEM((4096, BLK), BF16),
            pltpu.VMEM((2, 8, 4096), F32),
            pltpu.VMEM((8, 4096), F32),
            pltpu.VMEM((8, 4096), F32),
            pltpu.VMEM((PIX_OUT, 8, BLK), BF16),
            pltpu.SemaphoreType.DMA((19,)),
            pltpu.SemaphoreType.DMA((N_SEM,)),
            pltpu.SemaphoreType.DMA((N_SEM,)),
            pltpu.SemaphoreType.DMA((5,)),
            pltpu.SemaphoreType.DMA((62,)),
            pltpu.SemaphoreType.DMA((N_SUM_SEND,)),
            pltpu.SemaphoreType.DMA((N_SUM_RECV,)),
            pltpu.SemaphoreType.REGULAR((2,)),
            pltpu.SemaphoreType.REGULAR,
        ],
        compiler_params=pltpu.CompilerParams(
            collective_id=0, has_side_effects=True, vmem_limit_bytes=64 * 1024 * 1024
        ),
    )(
        jnp.transpose(images, (1, 0, 2)),
        section_weights,
        bn_gain[0],
        bn_bias[0],
        width.T,
        bn_set.T,
        gate,
        jnp.transpose(cotangent, (1, 0, 2)),
    )
    out, gi, dw, gain_sum, bias_sum = widen(out, gi, dw.reshape(P_SIZE // 128, 128), dgb)
    return (
        jnp.transpose(out, (1, 0, 2)),
        jnp.transpose(gi, (1, 0, 2)),
        dw.reshape(1, P_SIZE),
        gain_sum[None],
        bias_sum[None],
    )


def solution(mesh):
    sizes = dict(mesh.shape)
    fits = sizes["pipe"] == 4 and sizes["dp"] == 2 and sizes["rep"] == 4
    placed = (
        P(("dp", "rep"), None, None),
        P("pipe", None),
        P("pipe", None, None),
        P("pipe", None, None),
        P(),
        P(),
        P(),
        P(("dp", "rep"), None, None),
    )
    return jax.shard_map(
        one_kernel if fits else on_device,
        mesh=mesh,
        in_specs=placed,
        out_specs=(
            P(("dp", "rep"), None, "pipe"),
            P(("dp", "rep"), None, "pipe"),
            P("pipe", None),
            P("pipe", None, None),
            P("pipe", None, None),
        ),
        check_vma=False,
    )
```

```python
import jax
import jax.numpy as jnp
from jax import lax
from jax.experimental import pallas as pl
from jax.experimental.pallas import tpu as pltpu
from jax.sharding import PartitionSpec as P

C_IN = 1024
C_MID = 512
C_OUT = 2048
SIDE = 14
NSETS = 4
MB = 8
IMG_B = 1
OSIDE = 7
PIX_IN = 196
PIX_OUT = 49
IMG_DEV = 8
P_SIZE = 3407872


EPSILON = 1e-05


def for_sending(array):

    def short(part):
        return part.astype(jnp.bfloat16) if part.dtype == jnp.float32 else part

    return jax.tree.map(short, array)


def shifted(value, axis, steps):
    count = lax.axis_size(axis)
    first, last = (max(0, -steps), min(count, count - steps))
    return lax.ppermute(value, axis, [(source, source + steps) for source in range(first, last)])


def smooth(inputs):
    return inputs * jax.nn.sigmoid(inputs)


def smooth_slope(inputs):
    gate_sig = jax.nn.sigmoid(inputs)
    return gate_sig * (1.0 + inputs * (1.0 - gate_sig))


def matmul(left_op, right_op):
    return jnp.dot(left_op, right_op, preferred_element_type=jnp.float32)


def matmul_left_t(left_op, right_op):
    return lax.dot_general(
        left_op, right_op, (((0,), (0,)), ((), ())), preferred_element_type=jnp.float32
    )


def matmul_right_t(left_op, right_op):
    return lax.dot_general(
        left_op, right_op, (((1,), (1,)), ((), ())), preferred_element_type=jnp.float32
    )


def patches(planes, stride):
    images, side_len, channels = (planes.shape[0], planes.shape[1], planes.shape[3])
    out_side = side_len // stride
    padded = jnp.pad(planes, ((0, 0), (1, 1), (1, 1), (0, 0)))
    pieces = []
    for row_off in range(3):
        for col_off in range(3):
            pieces.append(
                padded[
                    :,
                    row_off : row_off + stride * (out_side - 1) + 1 : stride,
                    col_off : col_off + stride * (out_side - 1) + 1 : stride,
                    :,
                ]
            )
    return jnp.concatenate(pieces, axis=3).reshape(images * out_side * out_side, 9 * channels)


def unpatch(columns, images, side_len, stride, channels):
    out_side = side_len // stride
    pieces = columns.reshape(images, out_side, out_side, 9, channels)
    padded = jnp.zeros((images, side_len + 2, side_len + 2, channels), jnp.float32)
    for row_off in range(3):
        for col_off in range(3):
            padded = padded.at[
                :,
                row_off : row_off + stride * (out_side - 1) + 1 : stride,
                col_off : col_off + stride * (out_side - 1) + 1 : stride,
                :,
            ].add(pieces[:, :, :, row_off * 3 + col_off, :])
    return padded[:, 1 : side_len + 1, 1 : side_len + 1, :]


def group_moments(sums_local, squares_local):
    return (
        lax.psum(sums_local.astype(jnp.bfloat16), "dp").astype(jnp.float32),
        lax.psum(squares_local.astype(jnp.bfloat16), "dp").astype(jnp.float32),
    )


def group_grad_sums(bias_local, gain_local):
    return (
        lax.psum(bias_local.astype(jnp.bfloat16), "dp").astype(jnp.float32),
        lax.psum(gain_local.astype(jnp.bfloat16), "dp").astype(jnp.float32),
    )


def stats_of(sum_all, square_all, start, count, row_total):
    center = sum_all[start : start + count] / row_total
    inv_std = lax.rsqrt(square_all[start : start + count] / row_total - center * center + EPSILON)
    return (center, inv_std)


def norm_grad(slope_in, normed, gain_vec, inv_std, sum_bias, sum_gain, row_total):
    return (
        gain_vec * inv_std * (slope_in - sum_bias / row_total - normed * (sum_gain / row_total))
    ).astype(jnp.bfloat16)


def on_device(images, section_weights, bn_gain, bn_bias, width, bn_set, gate, cotangent):
    section_idx = lax.axis_index("pipe")
    pipe_count = lax.axis_size("pipe")
    dp_count = lax.axis_size("dp")
    flat_weights = section_weights[0]
    gain_table = bn_gain[0]
    bias_table = bn_bias[0]
    rows_in = IMG_B * PIX_IN
    rows_out = IMG_B * PIX_OUT
    total_in = float(rows_in * dp_count)
    total_out = float(rows_out * dp_count)
    wide = 2 * C_OUT
    scr_len = IMG_B * max(PIX_IN * C_MID, PIX_OUT * wide)
    image_blocks = images.reshape(MB, IMG_B, PIX_IN, C_IN)
    pad_mid = jnp.zeros((wide - 2 * C_MID,), jnp.float32)
    zero_wide = jnp.zeros((wide,), jnp.float32)
    zero_scr = jnp.zeros((scr_len,), jnp.float32)
    zero_mid = jnp.zeros((rows_out, C_MID), jnp.bfloat16)
    zero_res = jnp.zeros((rows_out, C_OUT), jnp.bfloat16)
    zero_rows = jnp.zeros((rows_out, C_OUT), jnp.float32)
    zero_input = jnp.zeros((IMG_B, PIX_IN, C_IN), jnp.float32)

    def pack(values):
        flat = values.reshape(-1).astype(jnp.float32)
        return jnp.pad(flat, (0, scr_len - flat.shape[0]))

    def unpack(buffer, rows, cols):
        return buffer[: rows * cols].reshape(rows, cols)

    def place(vec, start):
        return jnp.pad(vec, (start, wide - start - vec.shape[0]))

    def add_weight(acc, grad, offset, valid):
        flat = grad.reshape(-1)
        return acc.at[offset : offset + flat.shape[0]].add(jnp.where(valid, flat, 0.0))

    def weights_zero():
        split_at = C_IN * C_MID
        return (
            flat_weights[:split_at].reshape(C_IN, C_MID),
            flat_weights[split_at : split_at + 9 * C_MID * C_MID].reshape(9 * C_MID, C_MID),
        )

    def weights_one():
        split_at = C_MID * C_OUT
        return (
            flat_weights[:split_at].reshape(C_MID, C_OUT),
            flat_weights[split_at : split_at + C_IN * C_OUT].reshape(C_IN, C_OUT),
        )

    def weights_two():
        split_at = C_OUT * C_MID
        return (
            flat_weights[:split_at].reshape(C_OUT, C_MID),
            flat_weights[split_at : split_at + 9 * C_MID * C_MID].reshape(9 * C_MID, C_MID),
        )

    def short_rows(image_block):
        return image_block.reshape(IMG_B, SIDE, SIDE, C_IN)[:, ::2, ::2, :].reshape(rows_out, C_IN)

    def local_stats(values, start):
        return (
            place(jnp.sum(values, axis=0), start),
            place(jnp.sum(values * values, axis=0), start),
        )

    def fwd_a_zero(ops):
        conv_a, conv_b = weights_zero()
        pre_one = matmul(ops[0].reshape(rows_in, C_IN), conv_a)
        sums_local, squares_local = local_stats(pre_one, 0)
        return (pack(pre_one), sums_local, squares_local)

    def fwd_a_one(ops):
        conv_a, conv_b = weights_one()
        pre_both = jnp.concatenate(
            [matmul(ops[1], conv_a), matmul(short_rows(ops[0]), conv_b)], axis=1
        )
        sums_local, squares_local = local_stats(pre_both, 0)
        return (pack(pre_both), sums_local, squares_local)

    def fwd_a_two(ops):
        conv_a, conv_b = weights_two()
        pre_four = matmul(ops[2], conv_a)
        sums_local, squares_local = local_stats(pre_four, 0)
        return (pack(pre_four), sums_local, squares_local)

    def fwd_a_three(ops):
        conv_a = flat_weights[: C_MID * C_OUT].reshape(C_MID, C_OUT)
        pre_six = matmul(ops[1], conv_a)
        sums_local, squares_local = local_stats(pre_six, 0)
        return (pack(pre_six), sums_local, squares_local)

    def fwd_b_zero(args):
        ops, scratch, sum_all, square_all = args
        conv_a, conv_b = weights_zero()
        gain_vec, bias_vec, mask_vec = (ops[3], ops[4], ops[5])
        pre_one = unpack(scratch, rows_in, C_MID)
        center_one, inv_one = stats_of(sum_all, square_all, 0, C_MID, total_in)
        hidden_one = (
            smooth((pre_one - center_one) * inv_one * gain_vec[:C_MID] + bias_vec[:C_MID])
            * mask_vec
        ).astype(jnp.bfloat16)
        pre_two = matmul(patches(hidden_one.reshape(IMG_B, SIDE, SIDE, C_MID), 2), conv_b)
        sums_local, squares_local = local_stats(pre_two, C_MID)
        return (pack(pre_two), sums_local, squares_local)

    def fwd_b_pass(args):
        return (args[1], zero_wide, zero_wide)

    def fwd_b_two(args):
        ops, scratch, sum_all, square_all = args
        conv_a, conv_b = weights_two()
        gain_vec, bias_vec, mask_vec = (ops[3], ops[4], ops[5])
        pre_four = unpack(scratch, rows_out, C_MID)
        center_four, inv_four = stats_of(sum_all, square_all, 0, C_MID, total_out)
        hidden_four = (
            smooth((pre_four - center_four) * inv_four * gain_vec[:C_MID] + bias_vec[:C_MID])
            * mask_vec
        ).astype(jnp.bfloat16)
        pre_five = matmul(patches(hidden_four.reshape(IMG_B, OSIDE, OSIDE, C_MID), 1), conv_b)
        sums_local, squares_local = local_stats(pre_five, C_MID)
        return (pack(pre_five), sums_local, squares_local)

    def fwd_c_double(args, first_total, send_res):
        ops, scratch, sum_all, square_all = args
        gain_vec, bias_vec, mask_vec = (ops[3], ops[4], ops[5])
        pre_two = unpack(scratch, rows_out, C_MID)
        center_one, inv_one = stats_of(sum_all, square_all, 0, C_MID, first_total)
        center_two, inv_two = stats_of(sum_all, square_all, C_MID, C_MID, total_out)
        hidden_two = (
            smooth(
                (pre_two - center_two) * inv_two * gain_vec[C_MID : 2 * C_MID]
                + bias_vec[C_MID : 2 * C_MID]
            )
            * mask_vec
        ).astype(jnp.bfloat16)
        centers = jnp.concatenate([center_one, center_two, pad_mid])
        scales = jnp.concatenate([inv_one, inv_two, pad_mid])
        return (hidden_two, send_res, centers, scales, zero_rows)

    def fwd_c_zero(args):
        return fwd_c_double(args, total_in, zero_res)

    def fwd_c_two(args):
        return fwd_c_double(args, total_out, args[0][2])

    def fwd_c_one(args):
        ops, scratch, sum_all, square_all = args
        gain_vec, bias_vec = (ops[3], ops[4])
        pre_both = unpack(scratch, rows_out, wide)
        centers, scales = stats_of(sum_all, square_all, 0, wide, total_out)
        activ = (pre_both - centers) * scales * gain_vec + bias_vec
        block_out = smooth(activ[:, :C_OUT] + activ[:, C_OUT:]).astype(jnp.bfloat16)
        return (zero_mid, block_out, centers, scales, zero_rows)

    def fwd_c_three(args):
        ops, scratch, sum_all, square_all = args
        gain_vec, bias_vec, gate_val = (ops[3], ops[4], ops[6])
        pre_six = unpack(scratch, rows_out, C_OUT)
        centers, scales = stats_of(sum_all, square_all, 0, wide, total_out)
        residual = ops[2].astype(jnp.float32)
        merged = smooth(
            residual
            + (pre_six - centers[:C_OUT]) * scales[:C_OUT] * gain_vec[:C_OUT]
            + bias_vec[:C_OUT]
        )
        result = gate_val * merged + (1.0 - gate_val) * residual
        return (zero_mid, zero_res, centers, scales, result)

    def bwd_a_double(ops, flat_in, conv_a, conv_b, side_len, stride):
        centers, scales, grad_mid = (ops[3], ops[4], ops[5])
        gain_vec, bias_vec, mask_vec = (ops[8], ops[9], ops[10])
        norm_one = (matmul(flat_in, conv_a) - centers[:C_MID]) * scales[:C_MID]
        hidden_one = (smooth(norm_one * gain_vec[:C_MID] + bias_vec[:C_MID]) * mask_vec).astype(
            jnp.bfloat16
        )
        columns = patches(hidden_one.reshape(IMG_B, side_len, side_len, C_MID), stride)
        norm_two = (matmul(columns, conv_b) - centers[C_MID : 2 * C_MID]) * scales[
            C_MID : 2 * C_MID
        ]
        act_two = norm_two * gain_vec[C_MID : 2 * C_MID] + bias_vec[C_MID : 2 * C_MID]
        slope_two = grad_mid.astype(jnp.float32) * mask_vec * smooth_slope(act_two)
        return (
            pack(slope_two),
            pack(norm_two),
            pack(norm_one),
            place(jnp.sum(slope_two, axis=0), C_MID),
            place(jnp.sum(slope_two * norm_two, axis=0), C_MID),
        )

    def bwd_a_zero(ops):
        conv_a, conv_b = weights_zero()
        return bwd_a_double(ops, ops[0].reshape(rows_in, C_IN), conv_a, conv_b, SIDE, 2)

    def bwd_a_two(ops):
        conv_a, conv_b = weights_two()
        return bwd_a_double(ops, ops[2], conv_a, conv_b, OSIDE, 1)

    def bwd_a_one(ops):
        conv_a, conv_b = weights_one()
        centers, scales, grad_res = (ops[3], ops[4], ops[6])
        gain_vec, bias_vec = (ops[8], ops[9])
        pre_both = jnp.concatenate(
            [matmul(ops[1], conv_a), matmul(short_rows(ops[0]), conv_b)], axis=1
        )
        normed = (pre_both - centers) * scales
        activ = normed * gain_vec + bias_vec
        slope_in = grad_res.astype(jnp.float32) * smooth_slope(activ[:, :C_OUT] + activ[:, C_OUT:])
        both = jnp.concatenate([slope_in, slope_in], axis=1)
        return (
            pack(both),
            pack(normed),
            zero_scr,
            jnp.sum(both, axis=0),
            jnp.sum(both * normed, axis=0),
        )

    def bwd_a_three(ops):
        conv_a = flat_weights[: C_MID * C_OUT].reshape(C_MID, C_OUT)
        centers, scales = (ops[3], ops[4])
        gain_vec, bias_vec, gate_val = (ops[8], ops[9], ops[11])
        normed = (matmul(ops[1], conv_a) - centers[:C_OUT]) * scales[:C_OUT]
        joined = ops[2].astype(jnp.float32) + normed * gain_vec[:C_OUT] + bias_vec[:C_OUT]
        through = ops[7].astype(jnp.float32) * gate_val * smooth_slope(joined)
        return (
            pack(through),
            pack(normed),
            zero_scr,
            place(jnp.sum(through, axis=0), 0),
            place(jnp.sum(through * normed, axis=0), 0),
        )

    def bwd_b_double(args, conv_b, rows_first, side_len, stride, offset):
        ops, first_buf, second_buf, third_buf, sum_bias, sum_gain, acc = args
        scales = ops[4]
        gain_vec, bias_vec, mask_vec, valid = (ops[8], ops[9], ops[10], ops[12])
        slope_two = unpack(first_buf, rows_out, C_MID)
        norm_two = unpack(second_buf, rows_out, C_MID)
        norm_one = unpack(third_buf, rows_first, C_MID)
        grad_two = norm_grad(
            slope_two,
            norm_two,
            gain_vec[C_MID : 2 * C_MID],
            scales[C_MID : 2 * C_MID],
            sum_bias[C_MID : 2 * C_MID],
            sum_gain[C_MID : 2 * C_MID],
            total_out,
        )
        act_one = norm_one * gain_vec[:C_MID] + bias_vec[:C_MID]
        hidden_one = (smooth(act_one) * mask_vec).astype(jnp.bfloat16)
        columns = patches(hidden_one.reshape(IMG_B, side_len, side_len, C_MID), stride)
        acc = add_weight(acc, matmul_left_t(columns, grad_two), offset, valid)
        hid_grad = unpatch(
            matmul_right_t(grad_two, conv_b), IMG_B, side_len, stride, C_MID
        ).reshape(rows_first, C_MID)
        slope_one = hid_grad * mask_vec * smooth_slope(act_one)
        return (
            pack(slope_one),
            second_buf,
            third_buf,
            place(jnp.sum(slope_one, axis=0), 0),
            place(jnp.sum(slope_one * norm_one, axis=0), 0),
            acc,
        )

    def bwd_b_zero(args):
        conv_a, conv_b = weights_zero()
        return bwd_b_double(args, conv_b, rows_in, SIDE, 2, C_IN * C_MID)

    def bwd_b_two(args):
        conv_a, conv_b = weights_two()
        return bwd_b_double(args, conv_b, rows_out, OSIDE, 1, C_OUT * C_MID)

    def bwd_b_pass(args):
        return (args[1], args[2], args[3], zero_wide, zero_wide, args[6])

    def side_none():
        return zero_input

    def bwd_c_zero(args):
        ops, first_buf, second_buf, third_buf, sum_bias, sum_gain, acc = args
        conv_a, conv_b = weights_zero()
        scales, gain_vec, valid = (ops[4], ops[8], ops[12])
        flat_in = ops[0].reshape(rows_in, C_IN)
        slope_one = unpack(first_buf, rows_in, C_MID)
        norm_one = unpack(third_buf, rows_in, C_MID)
        grad_one = norm_grad(
            slope_one,
            norm_one,
            gain_vec[:C_MID],
            scales[:C_MID],
            sum_bias[:C_MID],
            sum_gain[:C_MID],
            total_in,
        )
        acc = add_weight(acc, matmul_left_t(flat_in, grad_one), 0, valid)
        side_out = matmul_right_t(grad_one, conv_a).reshape(IMG_B, PIX_IN, C_IN)
        return (zero_mid, zero_res, acc, side_out)

    def bwd_c_one(args):
        ops, first_buf, second_buf, third_buf, sum_bias, sum_gain, acc = args
        conv_a, conv_b = weights_one()
        scales, gain_vec, valid = (ops[4], ops[8], ops[12])
        short_in = short_rows(ops[0])
        both = unpack(first_buf, rows_out, wide)
        normed = unpack(second_buf, rows_out, wide)
        grad_both = norm_grad(both, normed, gain_vec, scales, sum_bias, sum_gain, total_out)
        acc = add_weight(acc, matmul_left_t(ops[1], grad_both[:, :C_OUT]), 0, valid)
        acc = add_weight(acc, matmul_left_t(short_in, grad_both[:, C_OUT:]), C_MID * C_OUT, valid)
        mid_grad = matmul_right_t(grad_both[:, :C_OUT], conv_a).astype(jnp.bfloat16)
        short_grad = matmul_right_t(grad_both[:, C_OUT:], conv_b).reshape(
            IMG_B, OSIDE, 1, OSIDE, 1, C_IN
        )
        side_out = jnp.pad(short_grad, ((0, 0), (0, 0), (0, 1), (0, 0), (0, 1), (0, 0))).reshape(
            IMG_B, PIX_IN, C_IN
        )
        return (mid_grad, zero_res, acc, side_out)

    def bwd_c_two(args):
        ops, first_buf, second_buf, third_buf, sum_bias, sum_gain, acc = args
        conv_a, conv_b = weights_two()
        scales, grad_res, gain_vec, valid = (ops[4], ops[6], ops[8], ops[12])
        slope_four = unpack(first_buf, rows_out, C_MID)
        norm_four = unpack(third_buf, rows_out, C_MID)
        grad_four = norm_grad(
            slope_four,
            norm_four,
            gain_vec[:C_MID],
            scales[:C_MID],
            sum_bias[:C_MID],
            sum_gain[:C_MID],
            total_out,
        )
        acc = add_weight(acc, matmul_left_t(ops[2], grad_four), 0, valid)
        carried_grad = (grad_res.astype(jnp.float32) + matmul_right_t(grad_four, conv_a)).astype(
            jnp.bfloat16
        )
        return (zero_mid, carried_grad, acc, side_none())

    def bwd_c_three(args):
        ops, first_buf, second_buf, third_buf, sum_bias, sum_gain, acc = args
        conv_a = flat_weights[: C_MID * C_OUT].reshape(C_MID, C_OUT)
        scales, gain_vec, gate_val, valid = (ops[4], ops[8], ops[11], ops[12])
        through = unpack(first_buf, rows_out, C_OUT)
        normed = unpack(second_buf, rows_out, C_OUT)
        res_grad = (through + (1.0 - gate_val) * ops[7].astype(jnp.float32)).astype(jnp.bfloat16)
        grad_six = norm_grad(
            through,
            normed,
            gain_vec[:C_OUT],
            scales[:C_OUT],
            sum_bias[:C_OUT],
            sum_gain[:C_OUT],
            total_out,
        )
        acc = add_weight(acc, matmul_left_t(ops[1], grad_six), 0, valid)
        mid_grad = matmul_right_t(grad_six, conv_a).astype(jnp.bfloat16)
        return (mid_grad, res_grad, acc, side_none())

    def select_params(micro_idx):
        block_id = section_idx // 2
        width_val = width[micro_idx, block_id]
        set_val = bn_set[micro_idx, block_id]
        onehot = (jnp.arange(NSETS) == set_val).astype(jnp.float32)
        gain_vec = jnp.sum(onehot[:, None] * gain_table, axis=0)
        bias_vec = jnp.sum(onehot[:, None] * bias_table, axis=0)
        mask_vec = (jnp.arange(C_MID) < width_val).astype(jnp.float32)
        gate_val = gate[micro_idx].astype(jnp.float32)
        return (gain_vec, bias_vec, mask_vec, gate_val, onehot)

    fwd_first = [fwd_a_zero, fwd_a_one, fwd_a_two, fwd_a_three]
    fwd_second = [fwd_b_zero, fwd_b_pass, fwd_b_two, fwd_b_pass]
    fwd_third = [fwd_c_zero, fwd_c_one, fwd_c_two, fwd_c_three]
    bwd_first = [bwd_a_zero, bwd_a_one, bwd_a_two, bwd_a_three]
    bwd_second = [bwd_b_zero, bwd_b_pass, bwd_b_two, bwd_b_pass]
    bwd_third = [bwd_c_zero, bwd_c_one, bwd_c_two, bwd_c_three]

    def forward_tick(tick_no, state_in):
        recv_mid, recv_res, stash_mid, stash_res, stash_center, stash_scale, out_rows = state_in
        micro_raw = tick_no - section_idx
        is_valid = (micro_raw >= 0) & (micro_raw < MB)
        micro_idx = jnp.clip(micro_raw, 0, MB - 1)
        gain_vec, bias_vec, mask_vec, gate_val, onehot = select_params(micro_idx)
        ops = (image_blocks[micro_idx], recv_mid, recv_res, gain_vec, bias_vec, mask_vec, gate_val)
        scratch, sums_local, squares_local = lax.switch(section_idx, fwd_first, ops)
        sum_first, square_first = group_moments(sums_local, squares_local)
        scratch, sums_local, squares_local = lax.switch(
            section_idx, fwd_second, (ops, scratch, sum_first, square_first)
        )
        sum_second, square_second = group_moments(sums_local, squares_local)
        send_mid, send_res, centers, scales, result = lax.switch(
            section_idx,
            fwd_third,
            (ops, scratch, sum_first + sum_second, square_first + square_second),
        )
        stash_mid = stash_mid.at[micro_idx].set(jnp.where(is_valid, recv_mid, stash_mid[micro_idx]))
        stash_res = stash_res.at[micro_idx].set(jnp.where(is_valid, recv_res, stash_res[micro_idx]))
        stash_center = stash_center.at[micro_idx].set(
            jnp.where(is_valid, centers, stash_center[micro_idx])
        )
        stash_scale = stash_scale.at[micro_idx].set(
            jnp.where(is_valid, scales, stash_scale[micro_idx])
        )
        out_rows = out_rows.at[micro_idx].set(jnp.where(is_valid, result, out_rows[micro_idx]))
        recv_mid, recv_res = (
            shifted(for_sending(send_mid), "pipe", 1).astype(send_mid.dtype),
            shifted(for_sending(send_res), "pipe", 1).astype(send_res.dtype),
        )
        return (recv_mid, recv_res, stash_mid, stash_res, stash_center, stash_scale, out_rows)

    forward_init = (
        zero_mid,
        zero_res,
        jnp.zeros((MB, rows_out, C_MID), jnp.bfloat16),
        jnp.zeros((MB, rows_out, C_OUT), jnp.bfloat16),
        jnp.zeros((MB, wide), jnp.float32),
        jnp.zeros((MB, wide), jnp.float32),
        jnp.zeros((MB, rows_out, C_OUT), jnp.float32),
    )
    forward_state = lax.fori_loop(0, MB + pipe_count - 1, forward_tick, forward_init)
    unused_mid, unused_res, stash_mid, stash_res, stash_center, stash_scale, out_rows = (
        forward_state
    )

    def backward_tick(tick_no, state_in):
        grad_mid, grad_res, weight_acc, gain_acc, bias_acc, input_acc = state_in
        micro_raw = tick_no - (pipe_count - 1 - section_idx)
        is_valid = (micro_raw >= 0) & (micro_raw < MB)
        micro_idx = jnp.clip(micro_raw, 0, MB - 1)
        gain_vec, bias_vec, mask_vec, gate_val, onehot = select_params(micro_idx)
        ops = (
            image_blocks[micro_idx],
            stash_mid[micro_idx],
            stash_res[micro_idx],
            stash_center[micro_idx],
            stash_scale[micro_idx],
            grad_mid,
            grad_res,
            cotangent[micro_idx],
            gain_vec,
            bias_vec,
            mask_vec,
            gate_val,
            is_valid,
        )
        first_buf, second_buf, third_buf, bias_one, gain_one = lax.switch(
            section_idx, bwd_first, ops
        )
        sum_bias_one, sum_gain_one = group_grad_sums(bias_one, gain_one)
        first_buf, second_buf, third_buf, bias_two, gain_two, weight_acc = lax.switch(
            section_idx,
            bwd_second,
            (ops, first_buf, second_buf, third_buf, sum_bias_one, sum_gain_one, weight_acc),
        )
        sum_bias_two, sum_gain_two = group_grad_sums(bias_two, gain_two)
        send_mid, send_res, weight_acc, side_out = lax.switch(
            section_idx,
            bwd_third,
            (
                ops,
                first_buf,
                second_buf,
                third_buf,
                sum_bias_one + sum_bias_two,
                sum_gain_one + sum_gain_two,
                weight_acc,
            ),
        )
        gain_grad = gain_one + gain_two
        bias_grad = bias_one + bias_two
        gain_acc = jnp.where(is_valid, gain_acc + onehot[:, None] * gain_grad[None, :], gain_acc)
        bias_acc = jnp.where(is_valid, bias_acc + onehot[:, None] * bias_grad[None, :], bias_acc)
        input_acc = jax.tree.map(
            lambda stored, fresh: stored.at[micro_idx].set(
                jnp.where(is_valid, fresh, stored[micro_idx])
            ),
            input_acc,
            side_out,
        )
        grad_mid, grad_res = (
            shifted(for_sending(send_mid), "pipe", -1).astype(send_mid.dtype),
            shifted(for_sending(send_res), "pipe", -1).astype(send_res.dtype),
        )
        return (grad_mid, grad_res, weight_acc, gain_acc, bias_acc, input_acc)

    side_init = jnp.zeros((MB, IMG_B, PIX_IN, C_IN), jnp.float32)
    backward_init = (
        zero_mid,
        zero_res,
        jnp.zeros((P_SIZE,), jnp.float32),
        jnp.zeros((NSETS, wide), jnp.float32),
        jnp.zeros((NSETS, wide), jnp.float32),
        side_init,
    )
    backward_state = lax.fori_loop(0, MB + pipe_count - 1, backward_tick, backward_init)
    unused_gmid, unused_gres, weight_acc, gain_acc, bias_acc, input_acc = backward_state
    grad_images, output_sum = (
        lax.psum_scatter(
            input_acc.reshape(IMG_DEV, PIX_IN, C_IN).astype(jnp.bfloat16),
            "pipe",
            scatter_dimension=2,
            tiled=True,
        ).astype(jnp.float32),
        lax.psum_scatter(
            out_rows.astype(jnp.bfloat16), "pipe", scatter_dimension=2, tiled=True
        ).astype(jnp.float32),
    )
    output_part = output_sum.astype(jnp.bfloat16)
    norm_grads = jnp.concatenate([gain_acc.reshape(-1), bias_acc.reshape(-1)])
    weight_sum, norm_sum = lax.psum((weight_acc, norm_grads), ("dp", "rep"))
    grad_gain = norm_sum[: NSETS * wide].reshape(1, NSETS, wide)
    grad_bias = norm_sum[NSETS * wide :].reshape(1, NSETS, wide)
    return (output_part, grad_images, weight_sum.reshape(1, P_SIZE), grad_gain, grad_bias)


PP = PIX_OUT + 1
RW = 8 * PP
RV = 8 * PIX_OUT
BLK = 512
SUB = 65536
F32 = jnp.float32
BF16 = jnp.bfloat16
MESH = pl.DeviceIdType.MESH

E_WIDE, E_WIDE_NEXT = 2, 6
C_H2, C_H4, C_D5, C_D4, C_DH = range(10, 15)
C_O1, C_SHARE, C_GI, C_GP = 15, 19, 22, 25
C_PAR2, C_PAR3, C_DG2, C_DG3, C_BN1, C_BN2, C_BN3, C_BN4 = range(28, 36)
N_SEM = 36
N_PIECE = 17
W_OWN, W_PEER, W_Z, W_ON, W_VIA = range(5)
VIA, HALF = 8, 11
W_BASE = (0, 17, 34, 45, -VIA)
S_CORE, S_IN, S_OUT, S_HAND, S_BACK, S_DONE, S_ACROSS, N_SUM_SEND = 0, 1, 2, 3, 4, 5, 9, 25
R_CORE, R_Z, R_ACROSS, R_GIVE = (0, 8), (8, 24), (32, 16), (48, 4)
R_DONE, R_BACK, R_BACK_HUB, R_HAND, N_SUM_RECV = 52, 53, 54, 55, 75
HUB_GUEST = 8704
RING = 8
SUBS = 2
SUB_ROWS = 256 // SUBS
HOPS = 2
HOP_ROWS = SUB_ROWS // HOPS
Z1_ZERO = 3136
ACROSS_LAG, OUT_LAG = 3 * SUBS // 2 + 1, 4 * SUBS
LAST_TURN = OUT_LAG - 2


def nn(a, b):
    return jnp.dot(a, b, preferred_element_type=F32)


def nt(a, b):
    return lax.dot_general(a, b, (((1,), (1,)), ((), ())), preferred_element_type=F32)


def tn(a, b):
    return lax.dot_general(a, b, (((0,), (0,)), ((), ())), preferred_element_type=F32)


def sigmoid(v):
    return 0.5 + 0.5 * jnp.tanh(0.5 * v)


def rows(start, size):
    return pl.ds(start if isinstance(start, int) else pl.multiple_of(start, 16), size)


def whole_kernel(
    img, wts, gain_in, bias_in, width, sets, gates, cot,
    out, gi, dw, dgb_out,
    imgb, raw, st, wh, wx, f0, f1, f2, f3, fs, pb, pt, u0, u1, u2, sx, cotb,
    h2, h4, h5, d5, d4, dh, r0, r1, ob, tx, rx, inv, par, parx, dg, dgx, sb, rd, bz, dgs, dgb, v_out, gain, bias,
    ls, ss, rs, wss, ass, ars, ready, go,
):
    p, d, r = lax.axis_index("pipe"), lax.axis_index("dp"), lax.axis_index("rep")
    peer = (p, 1 - d, r)
    z_pair = r + 1 - 2 * lax.rem(r, 2)
    quarter = 2 * lax.rem(r, 2) + d

    def remote(src, dst, send, recv, device):
        return pltpu.make_async_remote_copy(
            src_ref=src, dst_ref=dst, send_sem=ss.at[send], recv_sem=rs.at[recv],
            device_id=device, device_id_type=MESH,
        )

    def sync(event, first, count):
        part = pl.ds(first, count)
        copy = remote(tx.at[part], rx.at[part], event, event, peer)
        copy.start()
        copy.wait()

    def exchange_of(event, first, count):
        part = pl.ds(first, count)
        return remote(tx.at[part], rx.at[part], event, event, peer)

    def both(slot):
        return tx[slot] + rx[slot]

    def moments(slot_sum, slot_square, total, inv_slot):
        center = both(slot_sum) * (1.0 / total)
        scale = lax.rsqrt(both(slot_square) * (1.0 / total) - center * center + EPSILON)
        inv[inv_slot] = scale
        return center, scale

    def silu(v):
        return v * sigmoid(v)

    def slope(v):
        s = sigmoid(v)
        return s + v * s * (1.0 - s)

    def clear_pad(ref, first):
        tile = ref[rows(first + RW - 16, 16), :].astype(F32)
        keep = lax.broadcasted_iota(jnp.int32, tile.shape, 0) < 8
        ref[rows(first + RW - 16, 16), :] = jnp.where(keep, tile, 0.0).astype(BF16)

    def per_row(value_of):
        row = lax.broadcasted_iota(jnp.int32, (8, BLK), 0)
        out = jnp.zeros((8, BLK), jnp.int32)
        for m in range(MB):
            out = jnp.where(row == m, value_of(m), out)
        return out

    def mask_of(block):
        lane = lax.broadcasted_iota(jnp.int32, (8, BLK), 1)
        return (lane < per_row(lambda m: width[block, m])).astype(F32)

    def five(body, init=0, unrolled=False):
        if unrolled:
            for c in range(5):
                init = body(pl.ds(c * 10, 10), c, init)
            return init
        return lax.fori_loop(0, 5, lambda c, carry: body(pl.ds(c * 10, 10), c, carry), init)

    def add_stats(carry, a, b):
        return carry[0] + jnp.sum(a, axis=0), carry[1] + jnp.sum(b, axis=0)

    zero_stats = (jnp.zeros((8, BLK), F32), jnp.zeros((8, BLK), F32))

    def store_z(ref, first, z, slot_sum, slot_square):
        z3 = z.reshape(PP, 8, BLK)
        ref[pl.ds(first, PP)] = z3
        tx[slot_sum] = jnp.sum(z3, axis=0)
        tx[slot_square] = jnp.sum(z3 * z3, axis=0)

    def raw_copy(turn, element_of):
        slot = lax.rem(turn, RING)
        return pltpu.make_async_copy(
            wts.at[:, pl.ds(pl.multiple_of(element_of(turn) * SUB, SUB), SUB)], raw.at[slot], ls.at[8 + slot]
        )

    def open_weights(element_of, total):
        for turn in range(min(RING - 1, total)):
            raw_copy(turn, element_of).start()

    def load_weights(element_of, total, first, count, put):
        def body(k, carry):
            turn = first + k

            @pl.when(turn + RING - 1 < total)
            def _():
                raw_copy(turn + RING - 1, element_of).start()

            raw_copy(turn, element_of).wait()
            st[0:512] = raw[lax.rem(turn, RING)].astype(F32).reshape(512, 128)
            put(turn)
            return carry

        lax.fori_loop(0, count, body, 0)

    def put_narrow(ref, row_of):
        def put(i):
            for j in range(4):
                ref[rows(row_of(i), 128), j * 128 : (j + 1) * 128] = st[
                    pl.ds(j, 128, stride=4), :
                ].astype(BF16)

        return put

    def put_wide(ref, base, block_rows, first):
        def put(i):
            for n in range(4):
                for j in range(4):
                    ref[rows(base + n * block_rows + (i - first) * 32, 32), j * 128 : (j + 1) * 128] = st[
                        pl.ds(4 * n + j, 32, stride=16), :
                    ].astype(BF16)

        return put

    def put_chunk(row, n, block):
        size = SUB_ROWS // 4
        for part in range(2 * SUBS):
            wh[rows(row + part * SUB_ROWS + n * size, size), :] = block[part * size : (part + 1) * size].astype(BF16)

    def plain(turn):
        return turn

    def own_parts(turn):
        late = turn - HALF
        return jnp.where(late < 0, 4 * turn + quarter, 4 * HALF + (late // 2) * 4 + 2 * d + lax.rem(late, 2))

    def half_rows(turn):
        return 8 * d + turn

    def piece_copy(kind, i, q, device):
        part = wx.at[rows(i * 512 + q * 128, 128)]
        return pltpu.make_async_remote_copy(
            src_ref=part, dst_ref=part, send_sem=wss.at[kind], recv_sem=ars.at[W_BASE[kind] + i],
            device_id=device, device_id_type=MESH,
        )

    def half_copy(kind, i, which, device):
        part = wx.at[rows(i * 512 + which * 256, 256)]
        order = min(i, 13) if kind == W_VIA else i
        return pltpu.make_async_remote_copy(
            src_ref=part, dst_ref=part, send_sem=wss.at[kind], recv_sem=ars.at[W_BASE[kind] + order],
            device_id=device, device_id_type=MESH,
        )

    def all_sent(semaphore, ref):
        pltpu.make_async_remote_copy(
            src_ref=ref, dst_ref=ref, send_sem=semaphore, recv_sem=rs.at[0], device_id=peer, device_id_type=MESH
        ).wait_send()

    def all_here(semaphore, ref):
        pltpu.make_async_remote_copy(
            src_ref=ref, dst_ref=ref, send_sem=ss.at[0], recv_sem=semaphore, device_id=peer, device_id_type=MESH
        ).wait_recv()

    def o1_copy(n, chip):
        part = u0.at[n * RW : (n + 1) * RW]
        return remote(part, part, C_O1 + n, C_O1 + n, (chip, d, r))

    def each(work, first, last):
        def body(i, carry):
            work(i)
            return carry

        lax.fori_loop(first, last, body, 0)

    def img_copy(q, slot):
        return pltpu.make_async_copy(img.at[pl.ds(q * 28, 28)], imgb.at[slot], ls.at[slot])

    def open_images():
        for q in range(3):
            img_copy(q, q).start()

    def over_images(body, init):
        def step(q, carry):
            slot = lax.rem(q, 4)

            @pl.when(q + 3 < 7)
            def _():
                img_copy(q + 3, lax.rem(q + 3, 4)).start()

            img_copy(q, slot).wait()
            return body(q, slot, carry)

        return lax.fori_loop(0, 7, step, init)

    outer = (r == 0) | (r == 3)
    inner = jnp.logical_not(outer)
    z_dev, across = (p, d, z_pair), (p, d, 3 - r)

    def grad_copy(send, recv, src, dst, device):
        return pltpu.make_async_remote_copy(
            src_ref=src, dst_ref=dst, send_sem=ass.at[send], recv_sem=ars.at[recv],
            device_id=device, device_id_type=MESH,
        )

    def in_turn(ring, u):
        return ring[0] + lax.rem(u, ring[1])

    def zero_rest(first, source):
        source[...] = jnp.zeros(source.shape, BF16)

        def body(i, carry):
            copy = pltpu.make_async_copy(source, dw.at[pl.ds((first + i) * 4, 4)], ls.at[18])
            copy.start()
            copy.wait()
            return carry

        lax.fori_loop(0, 13 - first, body, 0)

    def bn_sums():
        for k in range(NSETS):
            hot = (set_of == k).astype(F32)
            for n in range(8):
                cols = slice(n * BLK, (n + 1) * BLK)
                dgs[k : k + 1, cols] = jnp.sum(dg[n] * hot, axis=0, keepdims=True)
                dgs[4 + k : 5 + k, cols] = jnp.sum(dg[8 + n] * hot, axis=0, keepdims=True)

    def norm_half(channels):
        return pl.ds(pl.multiple_of(d * (channels // 2), 512), channels // 2)

    def bn_in(cols):
        return remote(dgs.at[:, cols], bz.at[0, :, cols], C_BN1, C_BN1, z_dev)

    def bn_across(cols):
        return remote(dgs.at[:, cols], bz.at[1, :, cols], C_BN2, C_BN2, across)

    def bn_out(cols):
        return remote(dgb.at[:, cols], bz.at[0, :, cols], C_BN3, C_BN3, z_dev)

    def bn_core(cols):
        return remote(dgb.at[:, cols], dgb.at[:, cols], C_BN4, C_BN4, peer)

    def say_ready():
        pl.semaphore_signal(ready.at[0], inc=1, device_id=z_dev, device_id_type=MESH)

        @pl.when(inner)
        def _():
            pl.semaphore_signal(ready.at[1], inc=1, device_id=across, device_id_type=MESH)

    def sum_gradients(
        count, compute, at_row, chunk_of, wide, z1, extra,
        lend=(), passed=(), helper=None, helper_turn=None, helper_row=None, handed_in=None, lent_by=None, computed=None, packed_here=None,
        norms_at=0, norms=4096, after=None, back=R_BACK, late_back=0,
    ):
        turns = SUBS * count
        last_lent = SUBS * (count + len(lend))
        last_given = last_lent + SUBS * len(passed)
        computed = (0, count) if computed is None else computed
        packed_here = (0, count) if packed_here is None else packed_here
        cols = norm_half(norms)
        first_own, own_turns = packed_here[0] * SUBS, packed_here[1] * SUBS
        z2 = z1 + last_given * SUB_ROWS

        def when_own(u, work):
            if handed_in is None:
                work()
            else:
                pl.when(jnp.logical_not(handed_in(u // SUBS)))(work)

        def when_handed(u, work):
            if handed_in is not None:
                pl.when(handed_in(u // SUBS))(work)

        def when_kept(u, work):
            if lent_by is None:
                work()
            else:
                pl.when(jnp.logical_not(lent_by[0](u // SUBS)))(work)

        def when_lent(u, work):
            if lent_by is not None:
                pl.when(lent_by[0](u // SUBS))(work)

        def half(u, which):
            return wh.at[rows(at_row(u // SUBS) + which * 256 + lax.rem(u, SUBS) * SUB_ROWS, SUB_ROWS)]

        def half_part(u, k):
            first = at_row(u // SUBS) + d * 256 + lax.rem(u, SUBS) * SUB_ROWS + k * HOP_ROWS
            return wh.at[rows(first, HOP_ROWS)]

        def from_z(u):
            return wx.at[rows(z1 + u * SUB_ROWS, SUB_ROWS)]

        def from_z_part(u, k):
            return wx.at[rows(z1 + u * SUB_ROWS + k * HOP_ROWS, HOP_ROWS)]

        def from_across(u, k):
            return wx.at[rows(z2 + u * SUB_ROWS + k * HOP_ROWS, HOP_ROWS)]

        def from_core(u):
            return rd.at[rows(u * SUB_ROWS, SUB_ROWS)]

        def to_core(u):
            recv = jnp.where(u < turns, in_turn(R_CORE, u), in_turn(R_GIVE, u))
            return grad_copy(S_CORE, recv, half(u, 1 - d), from_core(u), peer)

        def inwards(u, k):
            return grad_copy(S_IN, in_turn(R_Z, u * HOPS + k), half_part(u, k), from_z_part(u, k), z_dev)

        def exchange(u, k):
            turn = u * HOPS + k
            return grad_copy(
                S_ACROSS + lax.rem(turn, 16), in_turn(R_ACROSS, turn), half_part(u, k), from_across(u, k), across
            )

        def outwards(u, k):
            return grad_copy(S_OUT, in_turn(R_Z, u * HOPS + k), half_part(u, k), from_z_part(u, k), z_dev)

        def packed(u, which):
            return dw.at[chunk_of(u // SUBS) * 4 + which * 2 + lax.rem(u, SUBS)]

        def done_core(u, turn):
            slot = lax.rem(turn, 4)
            return grad_copy(S_DONE + slot, R_DONE, sb.at[slot], packed(u, d), peer)

        def done_here(u, turn):
            slot = lax.rem(turn, 4)
            return pltpu.make_async_copy(sb.at[slot], packed(u, d), ls.at[4 + slot])

        def add(mine, other):
            sums = mine[...].astype(F32) + other[...].astype(F32)
            mine[...] = sums.astype(BF16)

        def pack(u, turn, ref):
            @pl.when(turn >= 4)
            def _():
                done_here(u, turn).wait()
                done_core(u, turn).wait_send()

            value = ref[...].astype(F32)
            for j in range(4):
                cols = slice(j * 128, (j + 1) * 128)
                if wide:
                    for n in range(4):
                        part = SUB_ROWS // 4
                        st[pl.ds(4 * n + j, part, stride=16), :] = value[n * part : (n + 1) * part, cols]
                else:
                    st[pl.ds(j, SUB_ROWS, stride=4), :] = value[:, cols]
            sb[lax.rem(turn, 4)] = st[...].astype(BF16)
            done_here(u, turn).start()
            done_core(u, turn).start()

        def hand(u):
            t, part = u // SUBS, lax.rem(u, SUBS)
            theirs = helper_turn(t) * SUBS + part
            row = helper_turn(t) * 512 if helper_row is None else helper_row(t)
            place = wh.at[rows(row + d * 256 + part * SUB_ROWS, SUB_ROWS)]
            return grad_copy(S_HAND, R_HAND + theirs, half(u, d), place, (helper(t), d, r))

        def handed(u):
            return grad_copy(S_HAND, R_HAND + u, half(u, d), half(u, d), (p, d, r))

        def give_back(u, ref):
            t = u // SUBS
            theirs = lent_by[2](t) * SUBS + lax.rem(u, SUBS)
            place = wx.at[rows(jnp.where(lent_by[1](t) == 0, Z1_ZERO, 0) + theirs * SUB_ROWS, SUB_ROWS)]
            return grad_copy(S_BACK, back, ref, place, (lent_by[1](t), d, r))

        def finish(u, ref):
            when_kept(u, lambda: pack(u, u - first_own, ref))
            when_lent(u, lambda: give_back(u, ref).start())

        def give(t):
            compute(t)
            for k in range(SUBS):
                to_core(t * SUBS + k).start()
            for k in range(SUBS):
                u = t * SUBS + k
                to_core(u).wait_recv()
                add(half(u, d), from_core(u))
                hand(u).start()

        def unit_rows(units):
            return wh.at[0 : units * SUB_ROWS]

        take_at = turns + OUT_LAG - (last_lent - turns)

        def step(it, carry):
            for when, work in extra.items():
                pl.when(it == when)(work)
            for k, when in enumerate(lend + passed):
                pl.when(it == when)(lambda k=k: give(jnp.int32(count + k)))

            def start():
                @pl.when(lax.rem(it, SUBS) == 0)
                def _():
                    compute(it // SUBS)

                to_core(it).start()

            @pl.when(it < turns)
            def _():
                when_own(it, start)

            u1 = it - 1

            @pl.when((u1 >= 0) & (u1 < turns))
            def _():
                def join_cores():
                    to_core(u1).wait_recv()
                    add(half(u1, d), from_core(u1))

                when_own(u1, join_cores)
                when_handed(u1, lambda: handed(u1).wait_recv())

                @pl.when(outer & (u1 == 0))
                def _():
                    pl.semaphore_wait(ready.at[0], 1)

                @pl.when(outer)
                def _():
                    for k in range(HOPS):
                        inwards(u1, k).start()

            u2 = it - 2

            @pl.when(inner & (u2 >= 0) & (u2 < turns))
            def _():
                @pl.when(u2 == 0)
                def _():
                    pl.semaphore_wait(ready.at[1], 1)

                for k in range(HOPS):
                    inwards(u2, k).wait_recv()
                    add(half_part(u2, k), from_z_part(u2, k))
                    exchange(u2, k).start()

            u4 = it - ACROSS_LAG

            @pl.when(inner & (u4 >= 0) & (u4 < turns))
            def _():
                @pl.when(u4 == 0)
                def _():
                    pl.semaphore_wait(ready.at[0], 1)

                for k in range(HOPS):
                    exchange(u4, k).wait()
                    add(half_part(u4, k), from_across(u4, k))
                    outwards(u4, k).start()

                finish(u4, half(u4, d))

            u8 = it - OUT_LAG

            @pl.when(outer & (u8 >= 0) & (u8 < turns))
            def _():
                for k in range(HOPS):
                    outwards(u8, k).wait_recv()

                finish(u8, from_z(u8))

            @pl.when(it == norms_at)
            def _():
                bn_sums()

                @pl.when(outer)
                def _():
                    bn_in(cols).start()

            @pl.when(inner & (it == norms_at + 4))
            def _():
                bn_in(cols).wait_recv()
                dgs[:, cols] += bz[0, :, cols]
                bn_across(cols).start()

            @pl.when(inner & (it == norms_at + 8))
            def _():
                bn_across(cols).wait()
                dgb[:, cols] = dgs[:, cols] + bz[1, :, cols]
                bn_out(cols).start()
                bn_core(cols).start()

            @pl.when(outer & (it == norms_at + 14))
            def _():
                bn_out(cols).wait_recv()
                dgb[:, cols] = bz[0, :, cols]
                bn_core(cols).start()

            for when, work in (after or {}).items():
                pl.when(it == when)(work)

            if lend:
                u_back = turns + it - take_at

                late_units = late_back * SUBS

                @pl.when(it == take_at)
                def _():
                    all_here(ars.at[R_BACK], unit_rows(last_lent - turns - late_units))

                if late_units:

                    @pl.when(u_back == last_lent - late_units)
                    def _():
                        all_here(ars.at[R_BACK_HUB], unit_rows(late_units))

                @pl.when((u_back >= turns) & (u_back < last_lent))
                def _():
                    pack(u_back, own_turns + u_back - turns, from_z(u_back))

            return carry

        lax.fori_loop(0, turns + OUT_LAG, step, 0)

        bn_core(cols).wait()

        @pl.when(outer)
        def _():
            bn_in(cols).wait_send()

        @pl.when(inner)
        def _():
            bn_out(cols).wait_send()

        @pl.when(outer)
        def _():
            all_sent(ass.at[S_IN], unit_rows(turns))

        @pl.when(inner)
        def _():
            all_sent(ass.at[S_OUT], unit_rows(turns))

        made = computed[1] * SUBS + last_given - turns
        if made:
            all_sent(ass.at[S_CORE], unit_rows(made))
        if last_given > turns:
            all_sent(ass.at[S_HAND], unit_rows(last_given - turns))
        if lent_by is not None:
            all_sent(ass.at[S_BACK], unit_rows(lent_by[3] * SUBS))
        all_here(ars.at[R_DONE], dw.at[pl.ds(0, own_turns + last_lent - turns)])
        for slot in range(4):
            done_here(first_own, jnp.int32(slot)).wait()
            done_core(first_own, jnp.int32(slot)).wait_send()

    tables = [
        pltpu.make_async_copy(gain_in, gain, ls.at[17]),
        pltpu.make_async_copy(bias_in, bias, ls.at[18]),
    ]
    for copy in tables:
        copy.start()

    @pl.when(p == 0)
    def _():
        open_weights(plain, 44)
        open_images()

    @pl.when(p == 1)
    def _():
        open_weights(plain, 48)
        open_images()
        pltpu.make_async_copy(cot, cotb.at[0:PIX_OUT], ls.at[16]).start()

    @pl.when(p == 2)
    def _():
        open_weights(own_parts, 15)

    @pl.when(p == 3)
    def _():
        open_weights(half_rows, 8)

    barrier = pltpu.get_barrier_semaphore()
    for device in (peer, (p, d, z_pair), (p, d, 3 - r)) + tuple((lax.rem(p + k, 4), d, r) for k in (1, 2, 3)):
        pl.semaphore_signal(barrier, inc=1, device_id=device, device_id_type=MESH)

    for copy in tables:
        copy.wait()
    block_two = p >= 2
    set_of = per_row(lambda m: jnp.where(block_two, sets[1, m], sets[0, m]))
    for k in range(NSETS):
        hot = (set_of == k).astype(F32)
        for n in range(8):
            g = hot * gain[k : k + 1, n * BLK : (n + 1) * BLK]
            b = hot * bias[k : k + 1, n * BLK : (n + 1) * BLK]
            if k == 0:
                par[n] = g
                par[8 + n] = b
            else:
                par[n] += g
                par[8 + n] += b
    dg[...] = jnp.zeros_like(dg)
    dgb[...] = jnp.zeros_like(dgb)
    pl.semaphore_wait(barrier, 6)

    total_in, total_out = 2.0 * PIX_IN, 2.0 * PIX_OUT

    def build_patches(base):
        def body(tap, carry):
            row, col = base(tap)
            window = pb[pl.ds(row, 7), pl.ds(col, 7)].reshape(RV, BLK)
            pt[tap, 0:RV, :] = window.astype(BF16)
            return carry

        lax.fori_loop(0, 9, body, 0)

    def clear_patch_pad():
        def body(tap, carry):
            pt[tap, RW - 16 : RW, :] = jnp.zeros((16, BLK), BF16)
            return carry

        lax.fori_loop(0, 9, body, 0)

    def strided_base(tap):
        di, dj = tap // 3, lax.rem(tap, 3)
        return lax.rem(di, 2) * 8 + di // 2, lax.rem(dj, 2) * 8 + dj // 2

    def plain_base(tap):
        return tap // 3, lax.rem(tap, 3)

    def conv(ref, first, target):
        target[...] = jnp.zeros_like(target)

        def body(tap, carry):
            z = nn(pt[tap], ref[rows(first + tap * BLK, BLK), :])
            target[...] += z.reshape(PP, 8, BLK)
            return carry

        lax.fori_loop(0, 9, body, 0)

    def conv_back(dz, ref, first, base, side):
        pb[0:side, 0:side] = jnp.zeros((side, side, 8, BLK), F32)

        def body(tap, carry):
            row, col = base(tap)
            part = nt(dz[0:RV, :], ref[rows(first + tap * BLK, BLK), :])
            pb[pl.ds(row, 7), pl.ds(col, 7)] += part.reshape(7, 7, 8, BLK)
            return carry

        lax.fori_loop(0, 9, body, 0)

    def stats_of_map(ref, slot_sum, slot_square):
        def body(c, _, carry):
            z = ref[c]
            return add_stats(carry, z, z * z)

        tx[slot_sum], tx[slot_square] = five(body, zero_stats)

    def act_to(ref, target, center, scale, g, b, mask):
        def body(c, i, carry):
            zhat = (ref[c] - center) * scale
            ref[c] = zhat
            h = silu(zhat * g + b) * mask
            target[rows(i * 80, 80), :] = h.reshape(80, BLK).astype(BF16)
            return carry

        five(body)
        clear_pad(target, 0)

    def upstream(target, grad, zhat_ref, g, b, mask, slot_sum, slot_gain):
        def body(c, i, carry):
            zhat = zhat_ref[c]
            du = grad[rows(i * 80, 80), :].astype(F32).reshape(10, 8, BLK) * mask * slope(zhat * g + b)
            target[c] = du
            return add_stats(carry, du, du * zhat)

        tx[slot_sum], tx[slot_gain] = five(body, zero_stats)

    def norm_back(target, first, du_ref, du_first, zhat_ref, zhat_first, gscale, mean_du, mean_dg, unrolled=False):
        def body(c, i, carry):
            du = du_ref[pl.ds(du_first + i * 10, 10)]
            zhat = zhat_ref[pl.ds(zhat_first + i * 10, 10)]
            dz = gscale * (du - mean_du - zhat * mean_dg)
            target[rows(first + i * 80, 80), :] = dz.reshape(80, BLK).astype(BF16)
            return carry

        five(body, unrolled=unrolled)
        clear_pad(target, first)

    def gi_copy():
        return pltpu.make_async_copy(f3.at[0:PIX_IN, :, 0:256], gi, ls.at[17])

    def out_copy():
        return pltpu.make_async_copy(v_out, out, ls.at[0])

    def dgb_copy():
        return pltpu.make_async_copy(dgb, dgb_out, ls.at[1])

    def final_part():
        @pl.when(p != 1)
        def _():
            remote(ob, ob, C_SHARE, C_SHARE, (p, d, r)).wait_recv()
            remote(r1, r1, C_GP, C_GP, (p, d, r)).wait_recv()

        @pl.when(p != 0)
        def _():
            remote(r0, r0, C_GI, C_GI, (p, d, r)).wait_recv()

        v_out[...] = ob[0:RV, :].astype(F32).reshape(PIX_OUT, 8, BLK).astype(BF16)
        out_copy().start()
        f0[0:PP, :, 0:256] = r1[...].astype(F32).reshape(PP, 8, 256)

        def place(a, carry):
            m = r0[rows(a * 224, 224), :].astype(F32).reshape(28, 8, 256)
            first = m[0:14].reshape(7, 2, 8, 256)
            even = first[:, 0] + f0[pl.ds(a * 7, 7), :, 0:256]
            f3[pl.ds(a * 28, 14), :, 0:256] = jnp.stack([even, first[:, 1]], axis=1).reshape(14, 8, 256)
            f3[pl.ds(a * 28 + 14, 14), :, 0:256] = m[14:28]
            return carry

        lax.fori_loop(0, 7, place, 0)
        gi_copy().start()

    @pl.when(p == 0)
    def _():
        mask = mask_of(0)

        def relay(i):
            piece_copy(W_VIA, i, quarter, (0, d, r)).wait_recv()
            piece_copy(W_OWN, i, quarter, (1, d, r)).start()

        def relay_half(i):
            half_copy(W_VIA, i, d, (0, d, r)).wait_recv()
            half_copy(W_OWN, i, d, (1, d, r)).start()

        put_w = put_narrow(wh, lambda i: i * 128)
        load_weights(plain, 44, 0, 8, put_w)

        def first_conv(q, slot, carry):
            rows_q = imgb[slot].astype(F32).reshape(224, 1024).astype(BF16)
            wx[rows(q * 224, 224), :] = rows_q[:, 0:512]
            wx[rows(1568 + q * 224, 224), :] = rows_q[:, 512:1024]
            z = nn(rows_q, wh[0:1024, :]).reshape(28, 8, BLK)
            f0[pl.ds(q * 28, 28)] = z
            load_weights(plain, 44, 8 + 5 * q, 5, put_w)
            return add_stats(carry, z, z * z)

        tx[0], tx[1] = over_images(first_conv, zero_stats)
        relay(VIA)
        exchange = remote(tx.at[pl.ds(0, 2)], rx.at[pl.ds(0, 2)], 0, 0, peer)
        exchange.start()
        pb[...] = jnp.zeros_like(pb)
        clear_patch_pad()
        load_weights(plain, 44, 43, 1, put_w)
        exchange.wait()

        center, scale = moments(0, 1, total_in, 0)
        g1, b1, g2, b2 = par[0], par[8], par[1], par[9]

        def hidden(i, carry):
            zhat = (f0[pl.ds(i * 14, 14)] - center) * scale
            f0[pl.ds(i * 14, 14)] = zhat
            h = (silu(zhat * g1 + b1) * mask).astype(BF16).astype(F32).reshape(7, 2, 8, BLK)
            u = i + 1
            row = lax.rem(u, 2) * 8 + u // 2
            pb[row, 8:15] = h[:, 0]
            pb[row, 1:8] = h[:, 1]
            return carry

        lax.fori_loop(0, 14, hidden, 0)
        relay(VIA + 1)
        build_patches(strided_base)
        conv(wh, 1024, fs.at[0])
        relay(VIA + 2)
        stats_of_map(fs.at[0], 2, 3)
        sync(1, 2, 2)
        center, scale = moments(2, 3, total_out, 1)
        act_to(fs.at[0], h2, center, scale, g2, b2, mask)
        send = remote(h2, h2, C_H2, C_H2, (1, d, r))
        send.start()
        for i in (HALF, HALF + 1, 16):
            relay_half(i)
        zero_rest(11, sb)
        send.wait_send()
        all_sent(wss.at[W_OWN], wx.at[0 : 3 * 128 + 3 * 256])
        say_ready()

        remote(dh, dh, C_DH, C_DH, (0, d, r)).wait_recv()
        upstream(fs.at[1], dh, fs.at[0], g2, b2, mask, 4, 5)
        sync(0, 4, 2)
        s_du, s_dg = both(4), both(5)
        dg[1], dg[9] = s_dg, s_du
        norm_back(d5, 0, fs.at[1], 0, fs.at[0], 0, g2 * inv[1], s_du * (1.0 / total_out), s_dg * (1.0 / total_out))
        def back_conv():
            conv_back(d5, wh, 1024, strided_base, 16)

        def slopes(i, carry):
            u = i + 1
            row = lax.rem(u, 2) * 8 + u // 2
            grad = jnp.stack([pb[row, 8:15], pb[row, 1:8]], axis=1).reshape(14, 8, BLK)
            zhat = f0[pl.ds(i * 14, 14)]
            du = grad * mask * slope(zhat * g1 + b1)
            f1[pl.ds(i * 14, 14)] = du
            return add_stats(carry, du, du * zhat)

        def first_slopes():
            tx[6], tx[7] = lax.fori_loop(0, 14, slopes, zero_stats)
            sync(1, 6, 2)
            dg[0], dg[8] = both(7), both(6)

        def first_back():
            s_du, s_dg = both(6), both(7)
            gscale, m_du, m_dg = g1 * inv[0], s_du * (1.0 / total_in), s_dg * (1.0 / total_in)

            def body(q, carry):
                part = pl.ds(q * 28, 28)
                dz = gscale * (f1[part] - m_du - f0[part] * m_dg)
                u1[rows(q * 224, 224), :] = dz.reshape(224, BLK).astype(BF16)
                return carry

            lax.fori_loop(0, 7, body, 0)

        def share(target, column, k):
            def body(q, carry):
                g = nt(u1[rows(q * 224, 224), :], wh[k * 256 : (k + 1) * 256, :])
                target[rows(q * 224, 224), column : column + 256] = g.astype(BF16)
                return carry

            lax.fori_loop(0, 7, body, 0)

        places = {1: (u0, 0), 2: (u0, 256), 3: (u2, 0)}

        def share_copy(k):
            target, column = places[k]
            return remote(target.at[0:1568, column : column + 256], r0, C_GI + k - 1, C_GI, (k, d, r))

        def share_out(k):
            share(*places[k], k)
            share_copy(k).start()

        def back_and_share():
            first_back()
            share_out(1)

        def compute(t):
            taps = (t < 6) | (t >= 8)

            @pl.when(taps)
            def _():
                tap = jnp.where(t < 6, t, t - 2)
                wh[rows(at_row(t), 512), :] = tn(pt[tap], d5[...]).astype(BF16)

            @pl.when(jnp.logical_not(taps))
            def _():
                block = tn(wx[rows((t - 6) * 1568, 1568), :], u1[0:1568, :])
                wh[rows(at_row(t), 512), :] = block.astype(BF16)

        def at_row(t):
            return jnp.where(t < 2, 5632 + t * 512, jnp.where(t < 8, t * 512, 2560 + t * 512))

        def chunk_of(t):
            return jnp.where(t < 6, t + 2, jnp.where(t < 8, t - 6, t))

        sum_gradients(
            8, compute, at_row, chunk_of, False, Z1_ZERO,
            {LAST_TURN + 8 * SUBS: final_part},
            lend=(5, 6, 7), helper=lambda t: jnp.where(t < 10, 2, 1), helper_turn=lambda t: jnp.where(t < 10, t - 1, 8),
            helper_row=lambda t: jnp.where(t < 10, (t - 1) * 512, HUB_GUEST), norms_at=4 * SUBS, norms=1024, late_back=1,
            after={
                1: back_conv,
                2: first_slopes,
                3: back_and_share,
                4: lambda: share(r0, 0, 0),
                8: lambda: share_out(3),
                10: lambda: share_out(2),
            },
        )
        for k in (1, 2, 3):
            share_copy(k).wait_send()

    @pl.when(p == 1)
    def _():
        mask = mask_of(1)
        gate_v = per_row(lambda m: gates[m]).astype(F32)
        cotb[PIX_OUT] = jnp.zeros((8, C_OUT), BF16)
        clear_patch_pad()
        load_weights(plain, 48, 0, 16, put_wide(wh, 0, 512, 0))
        load_weights(plain, 48, 16, 32, put_wide(wh, 2048, 1024, 16))

        def shorten(a, slot, carry):
            v = imgb[slot, 0:14].astype(F32).reshape(7, 2, 8, 1024)[:, 0]
            f0[pl.ds(a * 7, 7)] = v[:, :, 0:512]
            f0[pl.ds(PP + a * 7, 7)] = v[:, :, 512:1024]
            return carry

        other_z = 2 * (1 - lax.rem(r, 2))
        this_z = 2 * lax.rem(r, 2)

        def pass_own(i):
            piece_copy(W_OWN, i, quarter, (1, d, r)).wait_recv()
            piece_copy(W_PEER, i, quarter, peer).start()
            piece_copy(W_Z, i, quarter, z_dev).start()

        def pass_on(i):
            piece_copy(W_Z, i, other_z + d, peer).wait_recv()
            piece_copy(W_ON, i, other_z + d, peer).start()

        def have(i):
            piece_copy(W_PEER, i, this_z + 1 - d, peer).wait_recv()
            piece_copy(W_ON, i, other_z + 1 - d, peer).wait_recv()

        def pass_half(i):
            half_copy(W_OWN, i, d, (1, d, r)).wait_recv()
            half_copy(W_PEER, i, d, peer).start()

        def have_half(i):
            half_copy(W_PEER, i, 1 - d, peer).wait_recv()

        pass_own(0)
        over_images(shorten, 0)
        f0[PIX_OUT] = jnp.zeros((8, BLK), F32)
        f0[PP + PIX_OUT] = jnp.zeros((8, BLK), F32)
        sx[...] = f0[0 : 2 * PP].reshape(2 * RW, BLK).astype(BF16)

        def shortcut(n, carry):
            z = nn(sx[0:RW, :], wh[rows(2048 + n * 1024, 512), :]) + nn(
                sx[RW : 2 * RW, :], wh[rows(2560 + n * 1024, 512), :]
            )
            store_z(f1, n * PP, z, 4 * n + 2, 4 * n + 3)
            return carry

        pass_own(1)
        lax.fori_loop(0, 4, shortcut, 0)

        pass_own(2)
        pass_own(VIA)
        pass_on(0)
        pass_own(3)
        pass_on(1)
        pass_own(VIA + 1)
        pass_own(4)
        pl.semaphore_signal(go, inc=1, device_id=(3, d, r), device_id_type=MESH)
        pass_on(2)
        pass_own(VIA + 2)
        pass_own(5)
        pass_on(VIA)
        pass_own(6)
        pass_on(3)
        pass_own(7)
        pass_on(VIA + 1)
        remote(h2, h2, C_H2, C_H2, (1, d, r)).wait_recv()

        def third_conv(n, carry):
            store_z(f0, n * PP, nn(h2[...], wh[rows(n * 512, 512), :]), 4 * n, 4 * n + 1)
            exchange_of(E_WIDE + n, 4 * n, 4).start()
            return carry

        lax.fori_loop(0, 4, third_conv, 0)
        pass_on(4)

        def join(n, carry):
            exchange_of(E_WIDE + n, 4 * n, 4).wait()
            c3, s3 = moments(4 * n, 4 * n + 1, total_out, 2 + n)
            cp, sp = moments(4 * n + 2, 4 * n + 3, total_out, 6 + n)
            g3, gp, b = par[n], par[4 + n], par[8 + n] + par[12 + n]

            def body(_, i, carry):
                part = pl.ds(n * PP + i * 10, 10)
                a = (f0[part] - c3) * s3
                b_ = (f1[part] - cp) * sp
                f0[part] = a
                f1[part] = b_
                o = silu(a * g3 + b_ * gp + b)
                u0[rows(n * RW + i * 80, 80), :] = o.reshape(80, BLK).astype(BF16)
                return carry

            five(body)
            clear_pad(u0, n * RW)
            return carry

        lax.fori_loop(0, 4, join, 0)
        for n in (1, 2, 3):
            o1_copy(n, 3).start()
        pass_half(13)
        pass_on(VIA + 2)
        pass_half(HALF)
        each(have, 0, 4)
        zhat4, zhat5 = fs.at[0], fs.at[1]
        z = nn(u0[0:RW, :], wx[0:512, :])
        for n in range(1, 4):
            z += nn(u0[n * RW : (n + 1) * RW, :], wx[n * 512 : (n + 1) * 512, :])
        store_z(zhat4, 0, z, 16, 17)
        sync(0, 16, 2)
        remote(parx.at[0:4], parx.at[0:4], C_PAR2, C_PAR2, (1, d, r)).wait_recv()
        center, scale = moments(16, 17, total_out, 10)
        g4, g5, b4, b5 = parx[0], parx[1], parx[2], parx[3]
        pb[0:9, 0:9] = jnp.zeros((9, 9, 8, BLK), F32)

        def hidden(a, carry):
            part = pl.ds(a * 7, 7)
            zhat = (zhat4[part] - center) * scale
            zhat4[part] = zhat
            h = silu(zhat * g4 + b4) * mask
            pb[a + 1, 1:8] = h.astype(BF16).astype(F32)
            return carry

        lax.fori_loop(0, 7, hidden, 0)
        h4[0:RV, :] = pb[1:8, 1:8].reshape(RV, BLK).astype(BF16)
        h4_send = remote(h4, h4, C_H4, C_H4, (2, d, r))
        h4_send.start()

        o1_copy(0, 2).start()
        pass_on(5)
        build_patches(plain_base)

        def fifth_conv(taps):
            left = jnp.concatenate([pt[t] for t in taps], axis=1)
            right = jnp.concatenate([wx[2048 + t * 512 : 2560 + t * 512, :] for t in taps], axis=0)
            return nn(left, right).reshape(PP, 8, BLK)

        for i in (4, 5, VIA):
            have(i)
        zhat5[...] = fifth_conv((0, 1, 4))
        pass_half(14)
        pass_on(6)
        for i in (6, VIA + 1, VIA + 2):
            have(i)
        zhat5[...] += fifth_conv((2, 5, 6))
        pass_half(HALF + 1)
        pass_on(7)
        have(7)
        have_half(HALF)
        have_half(HALF + 1)
        zhat5[...] += fifth_conv((3, 7, 8))
        pass_half(15)
        stats_of_map(zhat5, 18, 19)
        sync(1, 18, 2)
        center, scale = moments(18, 19, total_out, 11)
        act_to(zhat5, h5, center, scale, g5, b5, mask)

        pass_half(16)

        def sixth_conv(n):
            have_half(13 + n)
            store_z(f2, n * PP, nn(h5[...], wx[6656 + n * 512 : 7168 + n * 512, :]), 20 + 2 * n, 21 + 2 * n)

        def exchange_z6(n):
            return exchange_of(E_WIDE_NEXT + n, 20 + 2 * n, 2)

        def exchange_d6(n):
            return exchange_of(E_WIDE + n, 28 + 2 * n, 2)

        def finish(n):
            center, scale = moments(20 + 2 * n, 21 + 2 * n, total_out, 12 + n)
            g6, b6 = parx[4 + n], parx[8 + n]

            def body(c, i, carry):
                part = pl.ds(n * PP + i * 10, 10)
                part_rows = rows(n * RW + i * 80, 80)
                zhat = (f2[part] - center) * scale
                f2[part] = zhat
                o = u0[part_rows, :].astype(F32).reshape(10, 8, BLK)
                q = o + zhat * g6 + b6
                s = sigmoid(q)
                act = q * s
                pt[n, rows(i * 80, 80), :] = (o + gate_v * (act - o)).reshape(80, BLK).astype(BF16)
                ct = cotb[c, :, n * BLK : (n + 1) * BLK].astype(F32)
                through = ct * gate_v
                dq = through * (s + act * (1.0 - s))
                f3[part] = dq
                u2[part_rows, :] = (dq + (ct - through)).reshape(80, BLK).astype(BF16)
                return add_stats(carry, dq, dq * zhat)

            tx[28 + 2 * n], tx[29 + 2 * n] = five(body, zero_stats, unrolled=True)

        for n in (0, 1):
            sixth_conv(n)
            exchange_z6(n).start()
        remote(parx.at[4:12], parx.at[4:12], C_PAR3, C_PAR3, (1, d, r)).wait_recv()
        pltpu.make_async_copy(cot, cotb.at[0:PIX_OUT], ls.at[16]).wait()
        for n in range(4):
            if n < 2:
                have_half(15 + n)
            exchange_z6(n).wait()
            if n < 2:
                store_z(
                    f2, (n + 2) * PP, nn(h5[...], wx[7680 + n * 512 : 8192 + n * 512, :]), 24 + 2 * n, 25 + 2 * n
                )
            finish(n)
            if n < 2:
                exchange_z6(n + 2).start()
            exchange_d6(n).start()
        ob[...] = pt[1]

        def output_copy(k):
            return remote(pt.at[k], ob, C_SHARE + k % 3, C_SHARE, (k, d, r))

        output_copy(3).start()


        def sixth_back(n):
            s_du, s_dg = both(28 + 2 * n), both(29 + 2 * n)
            dgx[4 + n] = s_dg
            dgx[8 + n] = s_du
            norm_back(
                u1, n * RW, f3, n * PP, f2, n * PP, parx[4 + n] * inv[12 + n],
                s_du * (1.0 / total_out), s_dg * (1.0 / total_out), unrolled=True,
            )

        for n in range(4):
            exchange_d6(n).wait()
        grad = jnp.zeros((RW, BLK), F32)
        for n in range(5):
            if n < 4:
                sixth_back(n)
            if n > 0:
                grad += nt(u1[(n - 1) * RW : n * RW, :], wx[6144 + n * 512 : 6656 + n * 512, :])
        dh[...] = grad.astype(BF16)

        upstream(f2, dh, zhat5, g5, b5, mask, 36, 37)
        sync(0, 36, 2)
        s_du, s_dg = both(36), both(37)
        dgx[1] = s_dg
        dgx[3] = s_du
        norm_back(d5, 0, f2, 0, zhat5, 0, g5 * inv[11], s_du * (1.0 / total_out), s_dg * (1.0 / total_out))
        d5_send = remote(d5, d5, C_D5, C_D5, (2, d, r))
        d5_send.start()
        pb[0:9, 0:9] = jnp.zeros((9, 9, 8, BLK), F32)
        for tap in range(9):
            row, col = tap // 3, tap % 3
            part = nt(d5[0:RV, :], wx[2048 + tap * 512 : 2560 + tap * 512, :])
            pb[row : row + 7, col : col + 7] += part.reshape(7, 7, 8, BLK)

        def fourth_slopes(a, carry):
            part = pl.ds(a * 7, 7)
            zhat = zhat4[part]
            du = pb[a + 1, 1:8] * mask * slope(zhat * g4 + b4)
            f2[part] = du
            return add_stats(carry, du, du * zhat)

        tx[38], tx[39] = lax.fori_loop(0, 7, fourth_slopes, zero_stats)
        sync(1, 38, 2)
        s_du, s_dg = both(38), both(39)
        dgx[0] = s_dg
        dgx[2] = s_du
        norm_back(d4, 0, f2, 0, zhat4, 0, g4 * inv[10], s_du * (1.0 / total_out), s_dg * (1.0 / total_out))

        def carried_back(n):
            z = nt(d4[...], wx[n * 512 : (n + 1) * 512, :])
            f2[(n % 2) * PP : (n % 2 + 1) * PP] = z.reshape(PP, 8, BLK)

        def exchange_d1(n):
            return exchange_of(E_WIDE_NEXT + n, 40 + 3 * n, 3)

        def first_block_slopes(n):
            g3, gp, b = par[n], par[4 + n], par[8 + n] + par[12 + n]

            def body(_, i, carry):
                part = pl.ds(n * PP + i * 10, 10)
                do = u2[n * RW + i * 80 : n * RW + (i + 1) * 80, :].astype(F32).reshape(10, 8, BLK)
                do += f2[pl.ds((n % 2) * PP + i * 10, 10)]
                a, b_ = f0[part], f1[part]
                dp = do.astype(BF16).astype(F32) * slope(a * g3 + b_ * gp + b)
                f3[part] = dp
                s0, s1, s2 = carry
                return s0 + jnp.sum(dp, axis=0), s1 + jnp.sum(dp * a, axis=0), s2 + jnp.sum(dp * b_, axis=0)

            first = 40 + 3 * n
            tx[first], tx[first + 1], tx[first + 2] = five(body, zero_stats + zero_stats[:1], unrolled=True)

        carried_back(0)
        for n in range(4):
            if n < 3:
                carried_back(n + 1)
            first_block_slopes(n)
            exchange_d1(n).start()

        def third_back(n):
            first = 40 + 3 * n
            m_du, m_dg = both(first) * (1.0 / total_out), both(first + 1) * (1.0 / total_out)
            norm_back(
                pt.at[4 + n], 0, f3, n * PP, f0, n * PP, par[n] * inv[2 + n], m_du, m_dg, unrolled=True
            )

        for n in range(4):
            exchange_d1(n).wait()
        grad = jnp.zeros((RW, BLK), F32)
        for n in range(5):
            if n < 4:
                third_back(n)
            if n > 0:
                grad += nt(pt[3 + n], wh[(n - 1) * 512 : n * 512, :])
        dh[...] = grad.astype(BF16)
        dh_send = remote(dh, dh, C_DH, C_DH, (0, d, r))
        dh_send.start()

        def shortcut_back(n, carry):
            first = 40 + 3 * n
            s_du, s_d3, s_dp = both(first), both(first + 1), both(first + 2)
            dg[n] = s_d3
            dg[4 + n] = s_dp
            dg[8 + n] = s_du
            dg[12 + n] = s_du
            m_du, m_dg = s_du * (1.0 / total_out), s_dp * (1.0 / total_out)
            norm_back(u2, n * RW, f3, n * PP, f1, n * PP, par[4 + n] * inv[6 + n], m_du, m_dg)
            return carry

        def all_shortcut_back():
            lax.fori_loop(0, 4, shortcut_back, 0)

        all_sent(wss.at[W_PEER], wx.at[0 : HALF * 128 + 6 * 256])
        all_sent(wss.at[W_Z], wx.at[0 : HALF * 128])
        all_sent(wss.at[W_ON], wx.at[0 : HALF * 128])
        say_ready()

        late = [remote(d4, d4, C_D4, C_D4, (2, d, r))]
        for first, last, sem, chip in ((0, 4, C_DG2, 2), (4, 12, C_DG3, 3)):
            late.append(remote(dgx.at[first:last], dgx.at[first:last], sem, sem, (chip, d, r)))

        def late_sends():
            dh_send.wait_send()
            for copy in late:
                copy.start()

        def shortcut_share(k):
            g = nt(u2[0:RW, :], wh[2048 + k * 256 : 2304 + k * 256, :])
            for n in range(1, 4):
                g += nt(u2[n * RW : (n + 1) * RW, :], wh[2048 + n * 1024 + k * 256 : 2304 + n * 1024 + k * 256, :])
            return g.astype(BF16)

        places = ((h4.at[:, 0:256], 0), (h4.at[:, 256:512], 2), (pt.at[8, :, 0:256], 3))

        def share_copy(slot):
            place, k = places[slot]
            return remote(place, r1, C_GP + slot, C_GP, (k, d, r))

        def shortcut_shares(slot):
            place, k = places[slot]
            if slot == 0:
                h4_send.wait_send()
            place[...] = shortcut_share(k)

        def shortcut_own():
            r1[...] = shortcut_share(1)


        def late_shares():
            for slot in range(3):
                share_copy(slot).start()

        def at_row(t):
            early = jnp.where(t == 8, HUB_GUEST, t * 512)
            return jnp.where(t < 11, early, jnp.where(t < 16, t * 512 + 512, 5632))

        def compute(t):
            @pl.when(t < 4)
            def _():
                left = h2[:, pl.ds(pl.multiple_of(t * 128, 128), 128)]
                for n in range(4):
                    put_chunk(at_row(t), n, tn(left, pt[4 + n]))

            @pl.when((t >= 4) & (t < 13))
            def _():
                m = jnp.where(t < 8, t - 4, t - 5)
                left = sx[rows((m // 4) * RW, RW), pl.ds(pl.multiple_of(lax.rem(m, 4) * 128, 128), 128)]
                for n in range(4):
                    put_chunk(at_row(t), n, tn(left, u2[n * RW : (n + 1) * RW, :]))

            @pl.when(t >= 13)
            def _():
                left = h5[:, pl.ds(pl.multiple_of((t - 13) * 128, 128), 128)]
                for n in range(4):
                    put_chunk(at_row(t), n, tn(left, u1[n * RW : (n + 1) * RW, :]))

        zero_rest(12, sb)
        sum_gradients(
            11, compute, at_row, lambda t: jnp.where(t < 8, t, t - 1), True, 0,
            {
                1: all_shortcut_back,
                2: lambda: shortcut_shares(0),
                4: lambda: shortcut_shares(1),
                5: late_sends,
                6: lambda: shortcut_shares(2),
                8: shortcut_own,
                7: lambda: output_copy(2).start(),
                11: lambda: output_copy(0).start(),
                15: late_shares,
                LAST_TURN + 11 * SUBS: final_part,
            },
            lend=(3, 5), passed=(7, 9, 11, 13), helper=lambda t: 3, helper_turn=lambda t: t - 7, norms_at=2,
            handed_in=lambda t: t == 8, lent_by=(lambda t: t == 8, lambda t: 0, lambda t: t + 2, 1), back=R_BACK_HUB,
            computed=(0, 10), packed_here=(0, 10),
        )
        for copy in [d5_send, o1_copy(0, 2)] + [o1_copy(n, 3) for n in (1, 2, 3)] + late:
            copy.wait_send()
        for slot in range(3):
            share_copy(slot).wait_send()
        for k in (0, 2, 3):
            output_copy(k).wait_send()


    @pl.when(p == 2)
    def _():
        for k, slot in ((0, 0), (1, 1), (2, 8), (3, 9)):
            parx[k] = par[slot]
        par_send = remote(parx.at[0:4], parx.at[0:4], C_PAR2, C_PAR2, (1, d, r))
        par_send.start()

        put_w = put_narrow(wx, lambda i: own_parts(i) * 128)

        def put(i):
            put_w(i)

            @pl.when(i < VIA)
            def _():
                piece_copy(W_OWN, i, quarter, (1, d, r)).start()

            @pl.when((i >= VIA) & (i < HALF))
            def _():
                piece_copy(W_VIA, i, quarter, (0, d, r)).start()

            for k in range(HALF, 13):
                @pl.when(i == HALF + 2 * (k - HALF) + 1)
                def _(k=k):
                    half_copy(W_VIA, k, d, (0, d, r)).start()

        load_weights(own_parts, 15, 0, 15, put)
        pb[...] = jnp.zeros_like(pb)
        clear_patch_pad()

        all_sent(wss.at[W_OWN], wx.at[0 : VIA * 128])
        all_sent(wss.at[W_VIA], wx.at[0 : 3 * 128 + 2 * 256])
        say_ready()
        remote(h4, h4, C_H4, C_H4, (2, d, r)).wait_recv()
        pb[1:8, 1:8] = h4[0:RV, :].astype(F32).reshape(7, 7, 8, BLK)
        build_patches(plain_base)
        remote(d5, d5, C_D5, C_D5, (2, d, r)).wait_recv()

        def compute(t):
            taps = (t < 5) | (t >= 11)

            @pl.when(taps)
            def _():
                tap = jnp.where(t < 5, t + 4, t - 11)
                wh[rows(t * 512, 512), :] = tn(pt[tap], d5[...]).astype(BF16)

            @pl.when(t == 5)
            def _():
                remote(d4, d4, C_D4, C_D4, (2, d, r)).wait_recv()
                for n in range(4):
                    o1_copy(n, 2).wait_recv()

            @pl.when(jnp.logical_not(taps))
            def _():
                n = jnp.where(t < 7, t - 5, t - 7)
                wh[rows(t * 512, 512), :] = tn(u0[rows(n * RW, RW), :], d4[...]).astype(BF16)

        def chunk_of(t):
            return jnp.where(t < 5, t + 8, jnp.where(t < 7, t - 5, t - 7))

        def norm_grads():
            remote(dgx.at[0:4], dgx.at[0:4], C_DG2, C_DG2, (2, d, r)).wait_recv()
            dg[0], dg[1], dg[8], dg[9] = dgx[0], dgx[1], dgx[2], dgx[3]

        sum_gradients(
            11, compute, lambda t: t * 512, chunk_of, False, 0,
            {6 * SUBS: norm_grads, LAST_TURN + 11 * SUBS: final_part},
            lend=(2, 3, 4, 6), helper=lambda t: 3, helper_turn=lambda t: t - 11,
            handed_in=lambda t: (t >= 7) & (t < 9),
            lent_by=(lambda t: (t >= 7) & (t < 9), lambda t: 0, lambda t: t + 1, 2),
            computed=(0, 9), packed_here=(0, 9), norms_at=6 * SUBS, norms=1024,
        )
        par_send.wait_send()

    @pl.when(p == 3)
    def _():
        for k in range(4):
            parx[4 + k] = par[k]
            parx[8 + k] = par[8 + k]
        par_send = remote(parx.at[4:12], parx.at[4:12], C_PAR3, C_PAR3, (1, d, r))
        par_send.start()
        say_ready()

        def put(i):
            for n in range(4):
                for j in range(4):
                    wx[rows(6656 + n * 512 + d * 256 + i * 32, 32), j * 128 : (j + 1) * 128] = st[
                        pl.ds(4 * n + j, 32, stride=16), :
                    ].astype(BF16)

        load_weights(half_rows, 8, 0, 8, put)
        zero_rest(4, sb)
        pl.semaphore_wait(go, 1)

        half_copy(W_VIA, 16, d, (0, d, r)).start()
        for i in (13, 14, 15):
            half_copy(W_OWN, i, d, (1, d, r)).start()
        for n in (1, 2, 3):
            o1_copy(n, 3).wait_recv()
            o1_copy(n, 2).start()
        def norm_grads():
            remote(dgx.at[4:12], dgx.at[4:12], C_DG3, C_DG3, (3, d, r)).wait_recv()
            for k in range(4):
                dg[k] = dgx[4 + k]
                dg[8 + k] = dgx[8 + k]

        sum_gradients(
            10, lambda t: None, lambda t: t * 512, lambda t: t - 6, True, 0,
            {5 * SUBS: norm_grads, LAST_TURN + 10 * SUBS: final_part},
            handed_in=lambda t: t >= 0,
            lent_by=(lambda t: t < 6, lambda t: jnp.where(t < 4, 2, 1), lambda t: jnp.where(t < 4, t + 11, t + 7), 6),
            computed=(0, 0), packed_here=(6, 4), norms_at=5 * SUBS, norms=2048,
        )
        for n in (1, 2, 3):
            o1_copy(n, 2).wait_send()
        all_sent(wss.at[W_VIA], wx.at[0:256])
        all_sent(wss.at[W_OWN], wx.at[0 : 3 * 256])
        par_send.wait_send()

    dgb_copy().start()
    gi_copy().wait()
    out_copy().wait()
    dgb_copy().wait()


def widen_kernel(out_in, gi_in, dw_in, dgb_in, out, gi, dw, gain, bias, v_out, v_gi, v_dw, v_wide, v_dgb, sin, sout):
    count = v_dw.shape[0] // 2048

    def part(i):
        return pl.ds(i * 2048, 2048)

    loads = [pltpu.make_async_copy(dw_in.at[part(i)], v_dw.at[part(i)], sin.at[i]) for i in range(count)]
    others = (
        (dgb_in, v_dgb, ((v_dgb.at[0:4], gain), (v_dgb.at[4:8], bias))),
        (out_in, v_out, ((v_out, out),)),
        (gi_in, v_gi, ((v_gi, gi),)),
    )
    more = [pltpu.make_async_copy(a, b, sin.at[count + k]) for k, (a, b, _) in enumerate(others)]
    for copy in loads + more:
        copy.start()
    stores = []
    for i in range(count):
        loads[i].wait()
        v_wide[part(i)] = v_dw[part(i)].astype(F32)
        stores.append(pltpu.make_async_copy(v_wide.at[part(i)], dw.at[part(i)], sout.at[i]))
        stores[-1].start()
    for k, (_, _, ends) in enumerate(others):
        more[k].wait()
        for a, b in ends:
            stores.append(pltpu.make_async_copy(a, b, sout.at[len(stores)]))
            stores[-1].start()
    for copy in stores:
        copy.wait()


def widen(out, gi, dw, dgb):
    count = P_SIZE // 128 // 2048
    any_space = pl.BlockSpec(memory_space=pl.ANY)
    return pl.pallas_call(
        widen_kernel,
        out_shape=(
            jax.ShapeDtypeStruct(out.shape, out.dtype),
            jax.ShapeDtypeStruct(gi.shape, gi.dtype),
            jax.ShapeDtypeStruct(dw.shape, F32),
            jax.ShapeDtypeStruct((4, 4096), F32),
            jax.ShapeDtypeStruct((4, 4096), F32),
        ),
        in_specs=[any_space] * 4,
        out_specs=(any_space,) * 5,
        scratch_shapes=[
            pltpu.VMEM(out.shape, out.dtype),
            pltpu.VMEM(gi.shape, gi.dtype),
            pltpu.VMEM(dw.shape, BF16),
            pltpu.VMEM(dw.shape, F32),
            pltpu.VMEM(dgb.shape, F32),
            pltpu.SemaphoreType.DMA((count + 3,)),
            pltpu.SemaphoreType.DMA((count + 4,)),
        ],
        compiler_params=pltpu.CompilerParams(vmem_limit_bytes=64 * 1024 * 1024),
    )(out, gi, dw, dgb)


def one_kernel(images, section_weights, bn_gain, bn_bias, width, bn_set, gate, cotangent):
    any_space = pl.BlockSpec(memory_space=pl.ANY)
    smem = pl.BlockSpec(memory_space=pltpu.SMEM)
    out, gi, dw, dgb = pl.pallas_call(
        whole_kernel,
        out_shape=(
            jax.ShapeDtypeStruct((PIX_OUT, 8, BLK), BF16),
            jax.ShapeDtypeStruct((PIX_IN, 8, 256), F32),
            jax.ShapeDtypeStruct((P_SIZE // SUB, 512, 128), BF16),
            jax.ShapeDtypeStruct((8, 4096), F32),
        ),
        in_specs=[any_space, any_space, any_space, any_space, smem, smem, smem, any_space],
        out_specs=(any_space,) * 4,
        scratch_shapes=[
            pltpu.VMEM((4, 28, 8, 1024), BF16),
            pltpu.VMEM((RING, 1, SUB), BF16),
            pltpu.VMEM((512, 128), F32),
            pltpu.VMEM((9216, BLK), BF16),
            pltpu.VMEM((8768, BLK), BF16),
            pltpu.VMEM((4 * PP, 8, BLK), F32),
            pltpu.VMEM((4 * PP, 8, BLK), F32),
            pltpu.VMEM((4 * PP, 8, BLK), F32),
            pltpu.VMEM((4 * PP, 8, BLK), F32),
            pltpu.VMEM((2, PP, 8, BLK), F32),
            pltpu.VMEM((16, 16, 8, BLK), F32),
            pltpu.VMEM((9, RW, BLK), BF16),
            pltpu.VMEM((4 * RW, BLK), BF16),
            pltpu.VMEM((4 * RW, BLK), BF16),
            pltpu.VMEM((4 * RW, BLK), BF16),
            pltpu.VMEM((2 * RW, BLK), BF16),
            pltpu.VMEM((PP, 8, C_OUT), BF16),
            pltpu.VMEM((RW, BLK), BF16),
            pltpu.VMEM((RW, BLK), BF16),
            pltpu.VMEM((RW, BLK), BF16),
            pltpu.VMEM((RW, BLK), BF16),
            pltpu.VMEM((RW, BLK), BF16),
            pltpu.VMEM((RW, BLK), BF16),
            pltpu.VMEM((8 * PIX_IN, 256), BF16),
            pltpu.VMEM((RW, 256), BF16),
            pltpu.VMEM((RW, BLK), BF16),
            pltpu.VMEM((52, 8, BLK), F32),
            pltpu.VMEM((52, 8, BLK), F32),
            pltpu.VMEM((16, 8, BLK), F32),
            pltpu.VMEM((16, 8, BLK), F32),
            pltpu.VMEM((12, 8, BLK), F32),
            pltpu.VMEM((16, 8, BLK), F32),
            pltpu.VMEM((12, 8, BLK), F32),
            pltpu.VMEM((4, 512, 128), BF16),
            pltpu.VMEM((4352, BLK), BF16),
            pltpu.VMEM((2, 8, 4096), F32),
            pltpu.VMEM((8, 4096), F32),
            pltpu.VMEM((8, 4096), F32),
            pltpu.VMEM((PIX_OUT, 8, BLK), BF16),
            pltpu.VMEM((NSETS, 4096), F32),
            pltpu.VMEM((NSETS, 4096), F32),
            pltpu.SemaphoreType.DMA((19,)),
            pltpu.SemaphoreType.DMA((N_SEM,)),
            pltpu.SemaphoreType.DMA((N_SEM,)),
            pltpu.SemaphoreType.DMA((5,)),
            pltpu.SemaphoreType.DMA((N_SUM_SEND,)),
            pltpu.SemaphoreType.DMA((N_SUM_RECV,)),
            pltpu.SemaphoreType.REGULAR((2,)),
            pltpu.SemaphoreType.REGULAR,
        ],
        compiler_params=pltpu.CompilerParams(
            collective_id=0, has_side_effects=True, vmem_limit_bytes=64 * 1024 * 1024
        ),
    )(
        jnp.transpose(images, (1, 0, 2)),
        section_weights,
        bn_gain[0],
        bn_bias[0],
        width.T,
        bn_set.T,
        gate,
        jnp.transpose(cotangent, (1, 0, 2)),
    )
    out, gi, dw, gain_sum, bias_sum = widen(out, gi, dw.reshape(P_SIZE // 128, 128), dgb)
    return (
        jnp.transpose(out, (1, 0, 2)),
        jnp.transpose(gi, (1, 0, 2)),
        dw.reshape(1, P_SIZE),
        gain_sum[None],
        bias_sum[None],
    )


def solution(mesh):
    sizes = dict(mesh.shape)
    fits = sizes["pipe"] == 4 and sizes["dp"] == 2 and sizes["rep"] == 4
    placed = (
        P(("dp", "rep"), None, None),
        P("pipe", None),
        P("pipe", None, None),
        P("pipe", None, None),
        P(),
        P(),
        P(),
        P(("dp", "rep"), None, None),
    )
    return jax.shard_map(
        one_kernel if fits else on_device,
        mesh=mesh,
        in_specs=placed,
        out_specs=(
            P(("dp", "rep"), None, "pipe"),
            P(("dp", "rep"), None, "pipe"),
            P("pipe", None),
            P("pipe", None, None),
            P("pipe", None, None),
        ),
        check_vma=False,
    )
```

```python
import jax
import jax.numpy as jnp
from jax import lax
from jax.experimental import pallas as pl
from jax.experimental.pallas import tpu as pltpu
from jax.sharding import PartitionSpec as P

C_IN = 1024
C_MID = 512
C_OUT = 2048
SIDE = 14
NSETS = 4
MB = 8
IMG_B = 1
OSIDE = 7
PIX_IN = 196
PIX_OUT = 49
IMG_DEV = 8
P_SIZE = 3407872


EPSILON = 1e-05


def for_sending(array):

    def short(part):
        return part.astype(jnp.bfloat16) if part.dtype == jnp.float32 else part

    return jax.tree.map(short, array)


def shifted(value, axis, steps):
    count = lax.axis_size(axis)
    first, last = (max(0, -steps), min(count, count - steps))
    return lax.ppermute(value, axis, [(source, source + steps) for source in range(first, last)])


def smooth(inputs):
    return inputs * jax.nn.sigmoid(inputs)


def smooth_slope(inputs):
    gate_sig = jax.nn.sigmoid(inputs)
    return gate_sig * (1.0 + inputs * (1.0 - gate_sig))


def matmul(left_op, right_op):
    return jnp.dot(left_op, right_op, preferred_element_type=jnp.float32)


def matmul_left_t(left_op, right_op):
    return lax.dot_general(
        left_op, right_op, (((0,), (0,)), ((), ())), preferred_element_type=jnp.float32
    )


def matmul_right_t(left_op, right_op):
    return lax.dot_general(
        left_op, right_op, (((1,), (1,)), ((), ())), preferred_element_type=jnp.float32
    )


def patches(planes, stride):
    images, side_len, channels = (planes.shape[0], planes.shape[1], planes.shape[3])
    out_side = side_len // stride
    padded = jnp.pad(planes, ((0, 0), (1, 1), (1, 1), (0, 0)))
    pieces = []
    for row_off in range(3):
        for col_off in range(3):
            pieces.append(
                padded[
                    :,
                    row_off : row_off + stride * (out_side - 1) + 1 : stride,
                    col_off : col_off + stride * (out_side - 1) + 1 : stride,
                    :,
                ]
            )
    return jnp.concatenate(pieces, axis=3).reshape(images * out_side * out_side, 9 * channels)


def unpatch(columns, images, side_len, stride, channels):
    out_side = side_len // stride
    pieces = columns.reshape(images, out_side, out_side, 9, channels)
    padded = jnp.zeros((images, side_len + 2, side_len + 2, channels), jnp.float32)
    for row_off in range(3):
        for col_off in range(3):
            padded = padded.at[
                :,
                row_off : row_off + stride * (out_side - 1) + 1 : stride,
                col_off : col_off + stride * (out_side - 1) + 1 : stride,
                :,
            ].add(pieces[:, :, :, row_off * 3 + col_off, :])
    return padded[:, 1 : side_len + 1, 1 : side_len + 1, :]


def group_moments(sums_local, squares_local):
    return (
        lax.psum(sums_local.astype(jnp.bfloat16), "dp").astype(jnp.float32),
        lax.psum(squares_local.astype(jnp.bfloat16), "dp").astype(jnp.float32),
    )


def group_grad_sums(bias_local, gain_local):
    return (
        lax.psum(bias_local.astype(jnp.bfloat16), "dp").astype(jnp.float32),
        lax.psum(gain_local.astype(jnp.bfloat16), "dp").astype(jnp.float32),
    )


def stats_of(sum_all, square_all, start, count, row_total):
    center = sum_all[start : start + count] / row_total
    inv_std = lax.rsqrt(square_all[start : start + count] / row_total - center * center + EPSILON)
    return (center, inv_std)


def norm_grad(slope_in, normed, gain_vec, inv_std, sum_bias, sum_gain, row_total):
    return (
        gain_vec * inv_std * (slope_in - sum_bias / row_total - normed * (sum_gain / row_total))
    ).astype(jnp.bfloat16)


def on_device(images, section_weights, bn_gain, bn_bias, width, bn_set, gate, cotangent):
    section_idx = lax.axis_index("pipe")
    pipe_count = lax.axis_size("pipe")
    dp_count = lax.axis_size("dp")
    flat_weights = section_weights[0]
    gain_table = bn_gain[0]
    bias_table = bn_bias[0]
    rows_in = IMG_B * PIX_IN
    rows_out = IMG_B * PIX_OUT
    total_in = float(rows_in * dp_count)
    total_out = float(rows_out * dp_count)
    wide = 2 * C_OUT
    scr_len = IMG_B * max(PIX_IN * C_MID, PIX_OUT * wide)
    image_blocks = images.reshape(MB, IMG_B, PIX_IN, C_IN)
    pad_mid = jnp.zeros((wide - 2 * C_MID,), jnp.float32)
    zero_wide = jnp.zeros((wide,), jnp.float32)
    zero_scr = jnp.zeros((scr_len,), jnp.float32)
    zero_mid = jnp.zeros((rows_out, C_MID), jnp.bfloat16)
    zero_res = jnp.zeros((rows_out, C_OUT), jnp.bfloat16)
    zero_rows = jnp.zeros((rows_out, C_OUT), jnp.float32)
    zero_input = jnp.zeros((IMG_B, PIX_IN, C_IN), jnp.float32)

    def pack(values):
        flat = values.reshape(-1).astype(jnp.float32)
        return jnp.pad(flat, (0, scr_len - flat.shape[0]))

    def unpack(buffer, rows, cols):
        return buffer[: rows * cols].reshape(rows, cols)

    def place(vec, start):
        return jnp.pad(vec, (start, wide - start - vec.shape[0]))

    def add_weight(acc, grad, offset, valid):
        flat = grad.reshape(-1)
        return acc.at[offset : offset + flat.shape[0]].add(jnp.where(valid, flat, 0.0))

    def weights_zero():
        split_at = C_IN * C_MID
        return (
            flat_weights[:split_at].reshape(C_IN, C_MID),
            flat_weights[split_at : split_at + 9 * C_MID * C_MID].reshape(9 * C_MID, C_MID),
        )

    def weights_one():
        split_at = C_MID * C_OUT
        return (
            flat_weights[:split_at].reshape(C_MID, C_OUT),
            flat_weights[split_at : split_at + C_IN * C_OUT].reshape(C_IN, C_OUT),
        )

    def weights_two():
        split_at = C_OUT * C_MID
        return (
            flat_weights[:split_at].reshape(C_OUT, C_MID),
            flat_weights[split_at : split_at + 9 * C_MID * C_MID].reshape(9 * C_MID, C_MID),
        )

    def short_rows(image_block):
        return image_block.reshape(IMG_B, SIDE, SIDE, C_IN)[:, ::2, ::2, :].reshape(rows_out, C_IN)

    def local_stats(values, start):
        return (
            place(jnp.sum(values, axis=0), start),
            place(jnp.sum(values * values, axis=0), start),
        )

    def fwd_a_zero(ops):
        conv_a, conv_b = weights_zero()
        pre_one = matmul(ops[0].reshape(rows_in, C_IN), conv_a)
        sums_local, squares_local = local_stats(pre_one, 0)
        return (pack(pre_one), sums_local, squares_local)

    def fwd_a_one(ops):
        conv_a, conv_b = weights_one()
        pre_both = jnp.concatenate(
            [matmul(ops[1], conv_a), matmul(short_rows(ops[0]), conv_b)], axis=1
        )
        sums_local, squares_local = local_stats(pre_both, 0)
        return (pack(pre_both), sums_local, squares_local)

    def fwd_a_two(ops):
        conv_a, conv_b = weights_two()
        pre_four = matmul(ops[2], conv_a)
        sums_local, squares_local = local_stats(pre_four, 0)
        return (pack(pre_four), sums_local, squares_local)

    def fwd_a_three(ops):
        conv_a = flat_weights[: C_MID * C_OUT].reshape(C_MID, C_OUT)
        pre_six = matmul(ops[1], conv_a)
        sums_local, squares_local = local_stats(pre_six, 0)
        return (pack(pre_six), sums_local, squares_local)

    def fwd_b_zero(args):
        ops, scratch, sum_all, square_all = args
        conv_a, conv_b = weights_zero()
        gain_vec, bias_vec, mask_vec = (ops[3], ops[4], ops[5])
        pre_one = unpack(scratch, rows_in, C_MID)
        center_one, inv_one = stats_of(sum_all, square_all, 0, C_MID, total_in)
        hidden_one = (
            smooth((pre_one - center_one) * inv_one * gain_vec[:C_MID] + bias_vec[:C_MID])
            * mask_vec
        ).astype(jnp.bfloat16)
        pre_two = matmul(patches(hidden_one.reshape(IMG_B, SIDE, SIDE, C_MID), 2), conv_b)
        sums_local, squares_local = local_stats(pre_two, C_MID)
        return (pack(pre_two), sums_local, squares_local)

    def fwd_b_pass(args):
        return (args[1], zero_wide, zero_wide)

    def fwd_b_two(args):
        ops, scratch, sum_all, square_all = args
        conv_a, conv_b = weights_two()
        gain_vec, bias_vec, mask_vec = (ops[3], ops[4], ops[5])
        pre_four = unpack(scratch, rows_out, C_MID)
        center_four, inv_four = stats_of(sum_all, square_all, 0, C_MID, total_out)
        hidden_four = (
            smooth((pre_four - center_four) * inv_four * gain_vec[:C_MID] + bias_vec[:C_MID])
            * mask_vec
        ).astype(jnp.bfloat16)
        pre_five = matmul(patches(hidden_four.reshape(IMG_B, OSIDE, OSIDE, C_MID), 1), conv_b)
        sums_local, squares_local = local_stats(pre_five, C_MID)
        return (pack(pre_five), sums_local, squares_local)

    def fwd_c_double(args, first_total, send_res):
        ops, scratch, sum_all, square_all = args
        gain_vec, bias_vec, mask_vec = (ops[3], ops[4], ops[5])
        pre_two = unpack(scratch, rows_out, C_MID)
        center_one, inv_one = stats_of(sum_all, square_all, 0, C_MID, first_total)
        center_two, inv_two = stats_of(sum_all, square_all, C_MID, C_MID, total_out)
        hidden_two = (
            smooth(
                (pre_two - center_two) * inv_two * gain_vec[C_MID : 2 * C_MID]
                + bias_vec[C_MID : 2 * C_MID]
            )
            * mask_vec
        ).astype(jnp.bfloat16)
        centers = jnp.concatenate([center_one, center_two, pad_mid])
        scales = jnp.concatenate([inv_one, inv_two, pad_mid])
        return (hidden_two, send_res, centers, scales, zero_rows)

    def fwd_c_zero(args):
        return fwd_c_double(args, total_in, zero_res)

    def fwd_c_two(args):
        return fwd_c_double(args, total_out, args[0][2])

    def fwd_c_one(args):
        ops, scratch, sum_all, square_all = args
        gain_vec, bias_vec = (ops[3], ops[4])
        pre_both = unpack(scratch, rows_out, wide)
        centers, scales = stats_of(sum_all, square_all, 0, wide, total_out)
        activ = (pre_both - centers) * scales * gain_vec + bias_vec
        block_out = smooth(activ[:, :C_OUT] + activ[:, C_OUT:]).astype(jnp.bfloat16)
        return (zero_mid, block_out, centers, scales, zero_rows)

    def fwd_c_three(args):
        ops, scratch, sum_all, square_all = args
        gain_vec, bias_vec, gate_val = (ops[3], ops[4], ops[6])
        pre_six = unpack(scratch, rows_out, C_OUT)
        centers, scales = stats_of(sum_all, square_all, 0, wide, total_out)
        residual = ops[2].astype(jnp.float32)
        merged = smooth(
            residual
            + (pre_six - centers[:C_OUT]) * scales[:C_OUT] * gain_vec[:C_OUT]
            + bias_vec[:C_OUT]
        )
        result = gate_val * merged + (1.0 - gate_val) * residual
        return (zero_mid, zero_res, centers, scales, result)

    def bwd_a_double(ops, flat_in, conv_a, conv_b, side_len, stride):
        centers, scales, grad_mid = (ops[3], ops[4], ops[5])
        gain_vec, bias_vec, mask_vec = (ops[8], ops[9], ops[10])
        norm_one = (matmul(flat_in, conv_a) - centers[:C_MID]) * scales[:C_MID]
        hidden_one = (smooth(norm_one * gain_vec[:C_MID] + bias_vec[:C_MID]) * mask_vec).astype(
            jnp.bfloat16
        )
        columns = patches(hidden_one.reshape(IMG_B, side_len, side_len, C_MID), stride)
        norm_two = (matmul(columns, conv_b) - centers[C_MID : 2 * C_MID]) * scales[
            C_MID : 2 * C_MID
        ]
        act_two = norm_two * gain_vec[C_MID : 2 * C_MID] + bias_vec[C_MID : 2 * C_MID]
        slope_two = grad_mid.astype(jnp.float32) * mask_vec * smooth_slope(act_two)
        return (
            pack(slope_two),
            pack(norm_two),
            pack(norm_one),
            place(jnp.sum(slope_two, axis=0), C_MID),
            place(jnp.sum(slope_two * norm_two, axis=0), C_MID),
        )

    def bwd_a_zero(ops):
        conv_a, conv_b = weights_zero()
        return bwd_a_double(ops, ops[0].reshape(rows_in, C_IN), conv_a, conv_b, SIDE, 2)

    def bwd_a_two(ops):
        conv_a, conv_b = weights_two()
        return bwd_a_double(ops, ops[2], conv_a, conv_b, OSIDE, 1)

    def bwd_a_one(ops):
        conv_a, conv_b = weights_one()
        centers, scales, grad_res = (ops[3], ops[4], ops[6])
        gain_vec, bias_vec = (ops[8], ops[9])
        pre_both = jnp.concatenate(
            [matmul(ops[1], conv_a), matmul(short_rows(ops[0]), conv_b)], axis=1
        )
        normed = (pre_both - centers) * scales
        activ = normed * gain_vec + bias_vec
        slope_in = grad_res.astype(jnp.float32) * smooth_slope(activ[:, :C_OUT] + activ[:, C_OUT:])
        both = jnp.concatenate([slope_in, slope_in], axis=1)
        return (
            pack(both),
            pack(normed),
            zero_scr,
            jnp.sum(both, axis=0),
            jnp.sum(both * normed, axis=0),
        )

    def bwd_a_three(ops):
        conv_a = flat_weights[: C_MID * C_OUT].reshape(C_MID, C_OUT)
        centers, scales = (ops[3], ops[4])
        gain_vec, bias_vec, gate_val = (ops[8], ops[9], ops[11])
        normed = (matmul(ops[1], conv_a) - centers[:C_OUT]) * scales[:C_OUT]
        joined = ops[2].astype(jnp.float32) + normed * gain_vec[:C_OUT] + bias_vec[:C_OUT]
        through = ops[7].astype(jnp.float32) * gate_val * smooth_slope(joined)
        return (
            pack(through),
            pack(normed),
            zero_scr,
            place(jnp.sum(through, axis=0), 0),
            place(jnp.sum(through * normed, axis=0), 0),
        )

    def bwd_b_double(args, conv_b, rows_first, side_len, stride, offset):
        ops, first_buf, second_buf, third_buf, sum_bias, sum_gain, acc = args
        scales = ops[4]
        gain_vec, bias_vec, mask_vec, valid = (ops[8], ops[9], ops[10], ops[12])
        slope_two = unpack(first_buf, rows_out, C_MID)
        norm_two = unpack(second_buf, rows_out, C_MID)
        norm_one = unpack(third_buf, rows_first, C_MID)
        grad_two = norm_grad(
            slope_two,
            norm_two,
            gain_vec[C_MID : 2 * C_MID],
            scales[C_MID : 2 * C_MID],
            sum_bias[C_MID : 2 * C_MID],
            sum_gain[C_MID : 2 * C_MID],
            total_out,
        )
        act_one = norm_one * gain_vec[:C_MID] + bias_vec[:C_MID]
        hidden_one = (smooth(act_one) * mask_vec).astype(jnp.bfloat16)
        columns = patches(hidden_one.reshape(IMG_B, side_len, side_len, C_MID), stride)
        acc = add_weight(acc, matmul_left_t(columns, grad_two), offset, valid)
        hid_grad = unpatch(
            matmul_right_t(grad_two, conv_b), IMG_B, side_len, stride, C_MID
        ).reshape(rows_first, C_MID)
        slope_one = hid_grad * mask_vec * smooth_slope(act_one)
        return (
            pack(slope_one),
            second_buf,
            third_buf,
            place(jnp.sum(slope_one, axis=0), 0),
            place(jnp.sum(slope_one * norm_one, axis=0), 0),
            acc,
        )

    def bwd_b_zero(args):
        conv_a, conv_b = weights_zero()
        return bwd_b_double(args, conv_b, rows_in, SIDE, 2, C_IN * C_MID)

    def bwd_b_two(args):
        conv_a, conv_b = weights_two()
        return bwd_b_double(args, conv_b, rows_out, OSIDE, 1, C_OUT * C_MID)

    def bwd_b_pass(args):
        return (args[1], args[2], args[3], zero_wide, zero_wide, args[6])

    def side_none():
        return zero_input

    def bwd_c_zero(args):
        ops, first_buf, second_buf, third_buf, sum_bias, sum_gain, acc = args
        conv_a, conv_b = weights_zero()
        scales, gain_vec, valid = (ops[4], ops[8], ops[12])
        flat_in = ops[0].reshape(rows_in, C_IN)
        slope_one = unpack(first_buf, rows_in, C_MID)
        norm_one = unpack(third_buf, rows_in, C_MID)
        grad_one = norm_grad(
            slope_one,
            norm_one,
            gain_vec[:C_MID],
            scales[:C_MID],
            sum_bias[:C_MID],
            sum_gain[:C_MID],
            total_in,
        )
        acc = add_weight(acc, matmul_left_t(flat_in, grad_one), 0, valid)
        side_out = matmul_right_t(grad_one, conv_a).reshape(IMG_B, PIX_IN, C_IN)
        return (zero_mid, zero_res, acc, side_out)

    def bwd_c_one(args):
        ops, first_buf, second_buf, third_buf, sum_bias, sum_gain, acc = args
        conv_a, conv_b = weights_one()
        scales, gain_vec, valid = (ops[4], ops[8], ops[12])
        short_in = short_rows(ops[0])
        both = unpack(first_buf, rows_out, wide)
        normed = unpack(second_buf, rows_out, wide)
        grad_both = norm_grad(both, normed, gain_vec, scales, sum_bias, sum_gain, total_out)
        acc = add_weight(acc, matmul_left_t(ops[1], grad_both[:, :C_OUT]), 0, valid)
        acc = add_weight(acc, matmul_left_t(short_in, grad_both[:, C_OUT:]), C_MID * C_OUT, valid)
        mid_grad = matmul_right_t(grad_both[:, :C_OUT], conv_a).astype(jnp.bfloat16)
        short_grad = matmul_right_t(grad_both[:, C_OUT:], conv_b).reshape(
            IMG_B, OSIDE, 1, OSIDE, 1, C_IN
        )
        side_out = jnp.pad(short_grad, ((0, 0), (0, 0), (0, 1), (0, 0), (0, 1), (0, 0))).reshape(
            IMG_B, PIX_IN, C_IN
        )
        return (mid_grad, zero_res, acc, side_out)

    def bwd_c_two(args):
        ops, first_buf, second_buf, third_buf, sum_bias, sum_gain, acc = args
        conv_a, conv_b = weights_two()
        scales, grad_res, gain_vec, valid = (ops[4], ops[6], ops[8], ops[12])
        slope_four = unpack(first_buf, rows_out, C_MID)
        norm_four = unpack(third_buf, rows_out, C_MID)
        grad_four = norm_grad(
            slope_four,
            norm_four,
            gain_vec[:C_MID],
            scales[:C_MID],
            sum_bias[:C_MID],
            sum_gain[:C_MID],
            total_out,
        )
        acc = add_weight(acc, matmul_left_t(ops[2], grad_four), 0, valid)
        carried_grad = (grad_res.astype(jnp.float32) + matmul_right_t(grad_four, conv_a)).astype(
            jnp.bfloat16
        )
        return (zero_mid, carried_grad, acc, side_none())

    def bwd_c_three(args):
        ops, first_buf, second_buf, third_buf, sum_bias, sum_gain, acc = args
        conv_a = flat_weights[: C_MID * C_OUT].reshape(C_MID, C_OUT)
        scales, gain_vec, gate_val, valid = (ops[4], ops[8], ops[11], ops[12])
        through = unpack(first_buf, rows_out, C_OUT)
        normed = unpack(second_buf, rows_out, C_OUT)
        res_grad = (through + (1.0 - gate_val) * ops[7].astype(jnp.float32)).astype(jnp.bfloat16)
        grad_six = norm_grad(
            through,
            normed,
            gain_vec[:C_OUT],
            scales[:C_OUT],
            sum_bias[:C_OUT],
            sum_gain[:C_OUT],
            total_out,
        )
        acc = add_weight(acc, matmul_left_t(ops[1], grad_six), 0, valid)
        mid_grad = matmul_right_t(grad_six, conv_a).astype(jnp.bfloat16)
        return (mid_grad, res_grad, acc, side_none())

    def select_params(micro_idx):
        block_id = section_idx // 2
        width_val = width[micro_idx, block_id]
        set_val = bn_set[micro_idx, block_id]
        onehot = (jnp.arange(NSETS) == set_val).astype(jnp.float32)
        gain_vec = jnp.sum(onehot[:, None] * gain_table, axis=0)
        bias_vec = jnp.sum(onehot[:, None] * bias_table, axis=0)
        mask_vec = (jnp.arange(C_MID) < width_val).astype(jnp.float32)
        gate_val = gate[micro_idx].astype(jnp.float32)
        return (gain_vec, bias_vec, mask_vec, gate_val, onehot)

    fwd_first = [fwd_a_zero, fwd_a_one, fwd_a_two, fwd_a_three]
    fwd_second = [fwd_b_zero, fwd_b_pass, fwd_b_two, fwd_b_pass]
    fwd_third = [fwd_c_zero, fwd_c_one, fwd_c_two, fwd_c_three]
    bwd_first = [bwd_a_zero, bwd_a_one, bwd_a_two, bwd_a_three]
    bwd_second = [bwd_b_zero, bwd_b_pass, bwd_b_two, bwd_b_pass]
    bwd_third = [bwd_c_zero, bwd_c_one, bwd_c_two, bwd_c_three]

    def forward_tick(tick_no, state_in):
        recv_mid, recv_res, stash_mid, stash_res, stash_center, stash_scale, out_rows = state_in
        micro_raw = tick_no - section_idx
        is_valid = (micro_raw >= 0) & (micro_raw < MB)
        micro_idx = jnp.clip(micro_raw, 0, MB - 1)
        gain_vec, bias_vec, mask_vec, gate_val, onehot = select_params(micro_idx)
        ops = (image_blocks[micro_idx], recv_mid, recv_res, gain_vec, bias_vec, mask_vec, gate_val)
        scratch, sums_local, squares_local = lax.switch(section_idx, fwd_first, ops)
        sum_first, square_first = group_moments(sums_local, squares_local)
        scratch, sums_local, squares_local = lax.switch(
            section_idx, fwd_second, (ops, scratch, sum_first, square_first)
        )
        sum_second, square_second = group_moments(sums_local, squares_local)
        send_mid, send_res, centers, scales, result = lax.switch(
            section_idx,
            fwd_third,
            (ops, scratch, sum_first + sum_second, square_first + square_second),
        )
        stash_mid = stash_mid.at[micro_idx].set(jnp.where(is_valid, recv_mid, stash_mid[micro_idx]))
        stash_res = stash_res.at[micro_idx].set(jnp.where(is_valid, recv_res, stash_res[micro_idx]))
        stash_center = stash_center.at[micro_idx].set(
            jnp.where(is_valid, centers, stash_center[micro_idx])
        )
        stash_scale = stash_scale.at[micro_idx].set(
            jnp.where(is_valid, scales, stash_scale[micro_idx])
        )
        out_rows = out_rows.at[micro_idx].set(jnp.where(is_valid, result, out_rows[micro_idx]))
        recv_mid, recv_res = (
            shifted(for_sending(send_mid), "pipe", 1).astype(send_mid.dtype),
            shifted(for_sending(send_res), "pipe", 1).astype(send_res.dtype),
        )
        return (recv_mid, recv_res, stash_mid, stash_res, stash_center, stash_scale, out_rows)

    forward_init = (
        zero_mid,
        zero_res,
        jnp.zeros((MB, rows_out, C_MID), jnp.bfloat16),
        jnp.zeros((MB, rows_out, C_OUT), jnp.bfloat16),
        jnp.zeros((MB, wide), jnp.float32),
        jnp.zeros((MB, wide), jnp.float32),
        jnp.zeros((MB, rows_out, C_OUT), jnp.float32),
    )
    forward_state = lax.fori_loop(0, MB + pipe_count - 1, forward_tick, forward_init)
    unused_mid, unused_res, stash_mid, stash_res, stash_center, stash_scale, out_rows = (
        forward_state
    )

    def backward_tick(tick_no, state_in):
        grad_mid, grad_res, weight_acc, gain_acc, bias_acc, input_acc = state_in
        micro_raw = tick_no - (pipe_count - 1 - section_idx)
        is_valid = (micro_raw >= 0) & (micro_raw < MB)
        micro_idx = jnp.clip(micro_raw, 0, MB - 1)
        gain_vec, bias_vec, mask_vec, gate_val, onehot = select_params(micro_idx)
        ops = (
            image_blocks[micro_idx],
            stash_mid[micro_idx],
            stash_res[micro_idx],
            stash_center[micro_idx],
            stash_scale[micro_idx],
            grad_mid,
            grad_res,
            cotangent[micro_idx],
            gain_vec,
            bias_vec,
            mask_vec,
            gate_val,
            is_valid,
        )
        first_buf, second_buf, third_buf, bias_one, gain_one = lax.switch(
            section_idx, bwd_first, ops
        )
        sum_bias_one, sum_gain_one = group_grad_sums(bias_one, gain_one)
        first_buf, second_buf, third_buf, bias_two, gain_two, weight_acc = lax.switch(
            section_idx,
            bwd_second,
            (ops, first_buf, second_buf, third_buf, sum_bias_one, sum_gain_one, weight_acc),
        )
        sum_bias_two, sum_gain_two = group_grad_sums(bias_two, gain_two)
        send_mid, send_res, weight_acc, side_out = lax.switch(
            section_idx,
            bwd_third,
            (
                ops,
                first_buf,
                second_buf,
                third_buf,
                sum_bias_one + sum_bias_two,
                sum_gain_one + sum_gain_two,
                weight_acc,
            ),
        )
        gain_grad = gain_one + gain_two
        bias_grad = bias_one + bias_two
        gain_acc = jnp.where(is_valid, gain_acc + onehot[:, None] * gain_grad[None, :], gain_acc)
        bias_acc = jnp.where(is_valid, bias_acc + onehot[:, None] * bias_grad[None, :], bias_acc)
        input_acc = jax.tree.map(
            lambda stored, fresh: stored.at[micro_idx].set(
                jnp.where(is_valid, fresh, stored[micro_idx])
            ),
            input_acc,
            side_out,
        )
        grad_mid, grad_res = (
            shifted(for_sending(send_mid), "pipe", -1).astype(send_mid.dtype),
            shifted(for_sending(send_res), "pipe", -1).astype(send_res.dtype),
        )
        return (grad_mid, grad_res, weight_acc, gain_acc, bias_acc, input_acc)

    side_init = jnp.zeros((MB, IMG_B, PIX_IN, C_IN), jnp.float32)
    backward_init = (
        zero_mid,
        zero_res,
        jnp.zeros((P_SIZE,), jnp.float32),
        jnp.zeros((NSETS, wide), jnp.float32),
        jnp.zeros((NSETS, wide), jnp.float32),
        side_init,
    )
    backward_state = lax.fori_loop(0, MB + pipe_count - 1, backward_tick, backward_init)
    unused_gmid, unused_gres, weight_acc, gain_acc, bias_acc, input_acc = backward_state
    grad_images, output_sum = (
        lax.psum_scatter(
            input_acc.reshape(IMG_DEV, PIX_IN, C_IN).astype(jnp.bfloat16),
            "pipe",
            scatter_dimension=2,
            tiled=True,
        ).astype(jnp.float32),
        lax.psum_scatter(
            out_rows.astype(jnp.bfloat16), "pipe", scatter_dimension=2, tiled=True
        ).astype(jnp.float32),
    )
    output_part = output_sum.astype(jnp.bfloat16)
    norm_grads = jnp.concatenate([gain_acc.reshape(-1), bias_acc.reshape(-1)])
    weight_sum, norm_sum = lax.psum((weight_acc, norm_grads), ("dp", "rep"))
    grad_gain = norm_sum[: NSETS * wide].reshape(1, NSETS, wide)
    grad_bias = norm_sum[NSETS * wide :].reshape(1, NSETS, wide)
    return (output_part, grad_images, weight_sum.reshape(1, P_SIZE), grad_gain, grad_bias)


PP = PIX_OUT + 1
RW = 8 * PP
RV = 8 * PIX_OUT
BLK = 512
SUB = 65536
F32 = jnp.float32
BF16 = jnp.bfloat16
MESH = pl.DeviceIdType.MESH

E_WIDE, E_WIDE_NEXT = 2, 6
C_H2, C_H4, C_D5, C_D4, C_DH = range(10, 15)
C_O1, C_SHARE, C_GI, C_GP = 15, 19, 22, 25
C_PAR2, C_PAR3, C_DG2, C_DG3, C_BN1, C_BN2, C_BN3, C_BN4 = range(28, 36)
N_SEM = 36
N_PIECE = 17
W_OWN, W_PEER, W_Z, W_ON, W_VIA = range(5)
VIA, HALF = 8, 11
W_BASE = (0, 17, 34, 45, -VIA)
S_CORE, S_IN, S_OUT, S_HAND, S_BACK, S_DONE, S_ACROSS, N_SUM_SEND = 0, 1, 2, 3, 4, 5, 9, 25
R_CORE, R_Z, R_ACROSS, R_GIVE = (0, 8), (8, 24), (32, 16), (48, 4)
R_DONE, R_BACK, R_BACK_HUB, R_HAND, N_SUM_RECV = 52, 53, 54, 55, 75
HUB_GUEST = 8704
RING = 8
SUBS = 2
SUB_ROWS = 256 // SUBS
HOPS = 2
HOP_ROWS = SUB_ROWS // HOPS
Z1_ZERO = 3136
ACROSS_LAG, OUT_LAG = 3 * SUBS // 2 + 1, 4 * SUBS
LAST_TURN = OUT_LAG - 2


def nn(a, b):
    return jnp.dot(a, b, preferred_element_type=F32)


def nt(a, b):
    return lax.dot_general(a, b, (((1,), (1,)), ((), ())), preferred_element_type=F32)


def tn(a, b):
    return lax.dot_general(a, b, (((0,), (0,)), ((), ())), preferred_element_type=F32)


def sigmoid(v):
    return 0.5 + 0.5 * jnp.tanh(0.5 * v)


def rows(start, size):
    return pl.ds(start if isinstance(start, int) else pl.multiple_of(start, 16), size)


def whole_kernel(
    img, wts, gain_in, bias_in, width, sets, gates, cot,
    out, gi, dw, dgb_out,
    imgb, raw, st, wh, wx, f0, f1, f2, f3, fs, pb, pt, u0, u1, u2, sx, cotb,
    h2, h4, h5, d5, d4, dh, r0, r1, ob, tx, rx, inv, par, parx, dg, dgx, sb, rd, bz, dgs, dgb, v_out, gain, bias,
    ls, ss, rs, wss, ass, ars, ready, go,
):
    p, d, r = lax.axis_index("pipe"), lax.axis_index("dp"), lax.axis_index("rep")
    peer = (p, 1 - d, r)
    z_pair = r + 1 - 2 * lax.rem(r, 2)
    quarter = 2 * lax.rem(r, 2) + d

    def remote(src, dst, send, recv, device):
        return pltpu.make_async_remote_copy(
            src_ref=src, dst_ref=dst, send_sem=ss.at[send], recv_sem=rs.at[recv],
            device_id=device, device_id_type=MESH,
        )

    def sync(event, first, count):
        part = pl.ds(first, count)
        copy = remote(tx.at[part], rx.at[part], event, event, peer)
        copy.start()
        copy.wait()

    def exchange_of(event, first, count):
        part = pl.ds(first, count)
        return remote(tx.at[part], rx.at[part], event, event, peer)

    def both(slot):
        return tx[slot] + rx[slot]

    def moments(slot_sum, slot_square, total, inv_slot):
        center = both(slot_sum) * (1.0 / total)
        scale = lax.rsqrt(both(slot_square) * (1.0 / total) - center * center + EPSILON)
        inv[inv_slot] = scale
        return center, scale

    def silu(v):
        return v * sigmoid(v)

    def slope(v):
        s = sigmoid(v)
        return s + v * s * (1.0 - s)

    def clear_pad(ref, first):
        tile = ref[rows(first + RW - 16, 16), :].astype(F32)
        keep = lax.broadcasted_iota(jnp.int32, tile.shape, 0) < 8
        ref[rows(first + RW - 16, 16), :] = jnp.where(keep, tile, 0.0).astype(BF16)

    def per_row(value_of):
        row = lax.broadcasted_iota(jnp.int32, (8, BLK), 0)
        out = jnp.zeros((8, BLK), jnp.int32)
        for m in range(MB):
            out = jnp.where(row == m, value_of(m), out)
        return out

    def mask_of(block):
        lane = lax.broadcasted_iota(jnp.int32, (8, BLK), 1)
        return (lane < per_row(lambda m: width[block, m])).astype(F32)

    def five(body, init=0, unrolled=False):
        if unrolled:
            for c in range(5):
                init = body(pl.ds(c * 10, 10), c, init)
            return init
        return lax.fori_loop(0, 5, lambda c, carry: body(pl.ds(c * 10, 10), c, carry), init)

    def add_stats(carry, a, b):
        return carry[0] + jnp.sum(a, axis=0), carry[1] + jnp.sum(b, axis=0)

    zero_stats = (jnp.zeros((8, BLK), F32), jnp.zeros((8, BLK), F32))

    def store_z(ref, first, z, slot_sum, slot_square):
        z3 = z.reshape(PP, 8, BLK) if z.ndim == 2 else z
        ref[pl.ds(first, PP)] = z3
        tx[slot_sum] = jnp.sum(z3, axis=0)
        tx[slot_square] = jnp.sum(z3 * z3, axis=0)

    def raw_copy(turn, element_of):
        slot = lax.rem(turn, RING)
        return pltpu.make_async_copy(
            wts.at[:, pl.ds(pl.multiple_of(element_of(turn) * SUB, SUB), SUB)], raw.at[slot], ls.at[8 + slot]
        )

    def open_weights(element_of, total):
        for turn in range(min(RING - 1, total)):
            raw_copy(turn, element_of).start()

    def load_weights(element_of, total, first, count, put):
        def body(k, carry):
            turn = first + k

            @pl.when(turn + RING - 1 < total)
            def _():
                raw_copy(turn + RING - 1, element_of).start()

            raw_copy(turn, element_of).wait()
            st[0:512] = raw[lax.rem(turn, RING)].astype(F32).reshape(512, 128)
            put(turn)
            return carry

        lax.fori_loop(0, count, body, 0)

    def put_narrow(ref, row_of):
        def put(i):
            for j in range(4):
                ref[rows(row_of(i), 128), j * 128 : (j + 1) * 128] = st[
                    pl.ds(j, 128, stride=4), :
                ].astype(BF16)

        return put

    def put_wide(ref, base, block_rows, first):
        def put(i):
            for n in range(4):
                for j in range(4):
                    ref[rows(base + n * block_rows + (i - first) * 32, 32), j * 128 : (j + 1) * 128] = st[
                        pl.ds(4 * n + j, 32, stride=16), :
                    ].astype(BF16)

        return put

    def put_chunk(row, n, block):
        size = SUB_ROWS // 4
        for part in range(2 * SUBS):
            wh[rows(row + part * SUB_ROWS + n * size, size), :] = block[part * size : (part + 1) * size].astype(BF16)

    def plain(turn):
        return turn

    def own_parts(turn):
        late = turn - HALF
        return jnp.where(late < 0, 4 * turn + quarter, 4 * HALF + (late // 2) * 4 + 2 * d + lax.rem(late, 2))

    def half_rows(turn):
        return 8 * d + turn

    def piece_copy(kind, i, q, device):
        part = wx.at[rows(i * 512 + q * 128, 128)]
        return pltpu.make_async_remote_copy(
            src_ref=part, dst_ref=part, send_sem=wss.at[kind], recv_sem=ars.at[W_BASE[kind] + i],
            device_id=device, device_id_type=MESH,
        )

    def half_copy(kind, i, which, device):
        part = wx.at[rows(i * 512 + which * 256, 256)]
        order = min(i, 13) if kind == W_VIA else i
        return pltpu.make_async_remote_copy(
            src_ref=part, dst_ref=part, send_sem=wss.at[kind], recv_sem=ars.at[W_BASE[kind] + order],
            device_id=device, device_id_type=MESH,
        )

    def all_sent(semaphore, ref):
        pltpu.make_async_remote_copy(
            src_ref=ref, dst_ref=ref, send_sem=semaphore, recv_sem=rs.at[0], device_id=peer, device_id_type=MESH
        ).wait_send()

    def all_here(semaphore, ref):
        pltpu.make_async_remote_copy(
            src_ref=ref, dst_ref=ref, send_sem=ss.at[0], recv_sem=semaphore, device_id=peer, device_id_type=MESH
        ).wait_recv()

    def o1_copy(n, chip):
        part = u0.at[n * RW : (n + 1) * RW]
        return remote(part, part, C_O1 + n, C_O1 + n, (chip, d, r))

    def each(work, first, last):
        def body(i, carry):
            work(i)
            return carry

        lax.fori_loop(first, last, body, 0)

    def img_copy(q, slot):
        return pltpu.make_async_copy(img.at[pl.ds(q * 28, 28)], imgb.at[slot], ls.at[slot])

    def open_images():
        for q in range(3):
            img_copy(q, q).start()

    def over_images(body, init):
        def step(q, carry):
            slot = lax.rem(q, 4)

            @pl.when(q + 3 < 7)
            def _():
                img_copy(q + 3, lax.rem(q + 3, 4)).start()

            img_copy(q, slot).wait()
            return body(q, slot, carry)

        return lax.fori_loop(0, 7, step, init)

    outer = (r == 0) | (r == 3)
    inner = jnp.logical_not(outer)
    z_dev, across = (p, d, z_pair), (p, d, 3 - r)

    def grad_copy(send, recv, src, dst, device):
        return pltpu.make_async_remote_copy(
            src_ref=src, dst_ref=dst, send_sem=ass.at[send], recv_sem=ars.at[recv],
            device_id=device, device_id_type=MESH,
        )

    def in_turn(ring, u):
        return ring[0] + lax.rem(u, ring[1])

    def zero_rest(first, source):
        source[...] = jnp.zeros(source.shape, BF16)

        def body(i, carry):
            copy = pltpu.make_async_copy(source, dw.at[pl.ds((first + i) * 4, 4)], ls.at[18])
            copy.start()
            copy.wait()
            return carry

        lax.fori_loop(0, 13 - first, body, 0)

    def bn_sums():
        for k in range(NSETS):
            hot = (set_of == k).astype(F32)
            for n in range(8):
                cols = slice(n * BLK, (n + 1) * BLK)
                dgs[k : k + 1, cols] = jnp.sum(dg[n] * hot, axis=0, keepdims=True)
                dgs[4 + k : 5 + k, cols] = jnp.sum(dg[8 + n] * hot, axis=0, keepdims=True)

    def norm_half(channels):
        return pl.ds(pl.multiple_of(d * (channels // 2), 512), channels // 2)

    def bn_in(cols):
        return remote(dgs.at[:, cols], bz.at[0, :, cols], C_BN1, C_BN1, z_dev)

    def bn_across(cols):
        return remote(dgs.at[:, cols], bz.at[1, :, cols], C_BN2, C_BN2, across)

    def bn_out(cols):
        return remote(dgb.at[:, cols], bz.at[0, :, cols], C_BN3, C_BN3, z_dev)

    def bn_core(cols):
        return remote(dgb.at[:, cols], dgb.at[:, cols], C_BN4, C_BN4, peer)

    def say_ready():
        pl.semaphore_signal(ready.at[0], inc=1, device_id=z_dev, device_id_type=MESH)

        @pl.when(inner)
        def _():
            pl.semaphore_signal(ready.at[1], inc=1, device_id=across, device_id_type=MESH)

    def sum_gradients(
        count, compute, at_row, chunk_of, wide, z1, extra,
        lend=(), passed=(), helper=None, helper_turn=None, helper_row=None, handed_in=None, lent_by=None, computed=None, packed_here=None,
        norms_at=0, norms=4096, after=None, back=R_BACK, late_back=0,
    ):
        turns = SUBS * count
        last_lent = SUBS * (count + len(lend))
        last_given = last_lent + SUBS * len(passed)
        computed = (0, count) if computed is None else computed
        packed_here = (0, count) if packed_here is None else packed_here
        cols = norm_half(norms)
        first_own, own_turns = packed_here[0] * SUBS, packed_here[1] * SUBS
        z2 = z1 + last_given * SUB_ROWS

        def when_own(u, work):
            if handed_in is None:
                work()
            else:
                pl.when(jnp.logical_not(handed_in(u // SUBS)))(work)

        def when_handed(u, work):
            if handed_in is not None:
                pl.when(handed_in(u // SUBS))(work)

        def when_kept(u, work):
            if lent_by is None:
                work()
            else:
                pl.when(jnp.logical_not(lent_by[0](u // SUBS)))(work)

        def when_lent(u, work):
            if lent_by is not None:
                pl.when(lent_by[0](u // SUBS))(work)

        def half(u, which):
            return wh.at[rows(at_row(u // SUBS) + which * 256 + lax.rem(u, SUBS) * SUB_ROWS, SUB_ROWS)]

        def half_part(u, k):
            first = at_row(u // SUBS) + d * 256 + lax.rem(u, SUBS) * SUB_ROWS + k * HOP_ROWS
            return wh.at[rows(first, HOP_ROWS)]

        def from_z(u):
            return wx.at[rows(z1 + u * SUB_ROWS, SUB_ROWS)]

        def from_z_part(u, k):
            return wx.at[rows(z1 + u * SUB_ROWS + k * HOP_ROWS, HOP_ROWS)]

        def from_across(u, k):
            return wx.at[rows(z2 + u * SUB_ROWS + k * HOP_ROWS, HOP_ROWS)]

        def from_core(u):
            return rd.at[rows(u * SUB_ROWS, SUB_ROWS)]

        def to_core(u):
            recv = jnp.where(u < turns, in_turn(R_CORE, u), in_turn(R_GIVE, u))
            return grad_copy(S_CORE, recv, half(u, 1 - d), from_core(u), peer)

        def inwards(u, k):
            return grad_copy(S_IN, in_turn(R_Z, u * HOPS + k), half_part(u, k), from_z_part(u, k), z_dev)

        def exchange(u, k):
            turn = u * HOPS + k
            return grad_copy(
                S_ACROSS + lax.rem(turn, 16), in_turn(R_ACROSS, turn), half_part(u, k), from_across(u, k), across
            )

        def outwards(u, k):
            return grad_copy(S_OUT, in_turn(R_Z, u * HOPS + k), half_part(u, k), from_z_part(u, k), z_dev)

        def packed(u, which):
            return dw.at[chunk_of(u // SUBS) * 4 + which * 2 + lax.rem(u, SUBS)]

        def done_core(u, turn):
            slot = lax.rem(turn, 4)
            return grad_copy(S_DONE + slot, R_DONE, sb.at[slot], packed(u, d), peer)

        def done_here(u, turn):
            slot = lax.rem(turn, 4)
            return pltpu.make_async_copy(sb.at[slot], packed(u, d), ls.at[4 + slot])

        def add(mine, other):
            sums = mine[...].astype(F32) + other[...].astype(F32)
            mine[...] = sums.astype(BF16)

        def pack(u, turn, ref):
            @pl.when(turn >= 4)
            def _():
                done_here(u, turn).wait()
                done_core(u, turn).wait_send()

            value = ref[...].astype(F32)
            for j in range(4):
                cols = slice(j * 128, (j + 1) * 128)
                if wide:
                    for n in range(4):
                        part = SUB_ROWS // 4
                        st[pl.ds(4 * n + j, part, stride=16), :] = value[n * part : (n + 1) * part, cols]
                else:
                    st[pl.ds(j, SUB_ROWS, stride=4), :] = value[:, cols]
            sb[lax.rem(turn, 4)] = st[...].astype(BF16)
            done_here(u, turn).start()
            done_core(u, turn).start()

        def hand(u):
            t, part = u // SUBS, lax.rem(u, SUBS)
            theirs = helper_turn(t) * SUBS + part
            row = helper_turn(t) * 512 if helper_row is None else helper_row(t)
            place = wh.at[rows(row + d * 256 + part * SUB_ROWS, SUB_ROWS)]
            return grad_copy(S_HAND, R_HAND + theirs, half(u, d), place, (helper(t), d, r))

        def handed(u):
            return grad_copy(S_HAND, R_HAND + u, half(u, d), half(u, d), (p, d, r))

        def give_back(u, ref):
            t = u // SUBS
            theirs = lent_by[2](t) * SUBS + lax.rem(u, SUBS)
            place = wx.at[rows(jnp.where(lent_by[1](t) == 0, Z1_ZERO, 0) + theirs * SUB_ROWS, SUB_ROWS)]
            return grad_copy(S_BACK, back, ref, place, (lent_by[1](t), d, r))

        def finish(u, ref):
            when_kept(u, lambda: pack(u, u - first_own, ref))
            when_lent(u, lambda: give_back(u, ref).start())

        def give(t):
            compute(t)
            for k in range(SUBS):
                to_core(t * SUBS + k).start()
            for k in range(SUBS):
                u = t * SUBS + k
                to_core(u).wait_recv()
                add(half(u, d), from_core(u))
                hand(u).start()

        def unit_rows(units):
            return wh.at[0 : units * SUB_ROWS]

        take_at = turns + OUT_LAG - (last_lent - turns)

        def step(it, carry):
            for when, work in extra.items():
                pl.when(it == when)(work)
            for k, when in enumerate(lend + passed):
                pl.when(it == when)(lambda k=k: give(jnp.int32(count + k)))

            def start():
                @pl.when(lax.rem(it, SUBS) == 0)
                def _():
                    compute(it // SUBS)

                to_core(it).start()

            @pl.when(it < turns)
            def _():
                when_own(it, start)

            u1 = it - 1

            @pl.when((u1 >= 0) & (u1 < turns))
            def _():
                def join_cores():
                    to_core(u1).wait_recv()
                    add(half(u1, d), from_core(u1))

                when_own(u1, join_cores)
                when_handed(u1, lambda: handed(u1).wait_recv())

                @pl.when(outer & (u1 == 0))
                def _():
                    pl.semaphore_wait(ready.at[0], 1)

                @pl.when(outer)
                def _():
                    for k in range(HOPS):
                        inwards(u1, k).start()

            u2 = it - 2

            @pl.when(inner & (u2 >= 0) & (u2 < turns))
            def _():
                @pl.when(u2 == 0)
                def _():
                    pl.semaphore_wait(ready.at[1], 1)

                for k in range(HOPS):
                    inwards(u2, k).wait_recv()
                    add(half_part(u2, k), from_z_part(u2, k))
                    exchange(u2, k).start()

            u4 = it - ACROSS_LAG

            @pl.when(inner & (u4 >= 0) & (u4 < turns))
            def _():
                @pl.when(u4 == 0)
                def _():
                    pl.semaphore_wait(ready.at[0], 1)

                for k in range(HOPS):
                    exchange(u4, k).wait()
                    add(half_part(u4, k), from_across(u4, k))
                    outwards(u4, k).start()

                finish(u4, half(u4, d))

            u8 = it - OUT_LAG

            @pl.when(outer & (u8 >= 0) & (u8 < turns))
            def _():
                for k in range(HOPS):
                    outwards(u8, k).wait_recv()

                finish(u8, from_z(u8))

            @pl.when(it == norms_at)
            def _():
                bn_sums()

                @pl.when(outer)
                def _():
                    bn_in(cols).start()

            @pl.when(inner & (it == norms_at + 4))
            def _():
                bn_in(cols).wait_recv()
                dgs[:, cols] += bz[0, :, cols]
                bn_across(cols).start()

            @pl.when(inner & (it == norms_at + 8))
            def _():
                bn_across(cols).wait()
                dgb[:, cols] = dgs[:, cols] + bz[1, :, cols]
                bn_out(cols).start()
                bn_core(cols).start()

            @pl.when(outer & (it == norms_at + 14))
            def _():
                bn_out(cols).wait_recv()
                dgb[:, cols] = bz[0, :, cols]
                bn_core(cols).start()

            for when, work in (after or {}).items():
                pl.when(it == when)(work)

            if lend:
                u_back = turns + it - take_at

                late_units = late_back * SUBS

                @pl.when(it == take_at)
                def _():
                    all_here(ars.at[R_BACK], unit_rows(last_lent - turns - late_units))

                if late_units:

                    @pl.when(u_back == last_lent - late_units)
                    def _():
                        all_here(ars.at[R_BACK_HUB], unit_rows(late_units))

                @pl.when((u_back >= turns) & (u_back < last_lent))
                def _():
                    pack(u_back, own_turns + u_back - turns, from_z(u_back))

            return carry

        lax.fori_loop(0, turns + OUT_LAG, step, 0)

        bn_core(cols).wait()

        @pl.when(outer)
        def _():
            bn_in(cols).wait_send()

        @pl.when(inner)
        def _():
            bn_out(cols).wait_send()

        @pl.when(outer)
        def _():
            all_sent(ass.at[S_IN], unit_rows(turns))

        @pl.when(inner)
        def _():
            all_sent(ass.at[S_OUT], unit_rows(turns))

        made = computed[1] * SUBS + last_given - turns
        if made:
            all_sent(ass.at[S_CORE], unit_rows(made))
        if last_given > turns:
            all_sent(ass.at[S_HAND], unit_rows(last_given - turns))
        if lent_by is not None:
            all_sent(ass.at[S_BACK], unit_rows(lent_by[3] * SUBS))
        all_here(ars.at[R_DONE], dw.at[pl.ds(0, own_turns + last_lent - turns)])
        for slot in range(4):
            done_here(first_own, jnp.int32(slot)).wait()
            done_core(first_own, jnp.int32(slot)).wait_send()

    tables = [
        pltpu.make_async_copy(gain_in, gain, ls.at[17]),
        pltpu.make_async_copy(bias_in, bias, ls.at[18]),
    ]
    for copy in tables:
        copy.start()

    @pl.when(p == 0)
    def _():
        open_weights(plain, 44)
        open_images()

    @pl.when(p == 1)
    def _():
        open_weights(plain, 48)
        open_images()
        pltpu.make_async_copy(cot, cotb.at[0:PIX_OUT], ls.at[16]).start()

    @pl.when(p == 2)
    def _():
        open_weights(own_parts, 15)

    @pl.when(p == 3)
    def _():
        open_weights(half_rows, 8)

    barrier = pltpu.get_barrier_semaphore()
    for device in (peer, (p, d, z_pair), (p, d, 3 - r)) + tuple((lax.rem(p + k, 4), d, r) for k in (1, 2, 3)):
        pl.semaphore_signal(barrier, inc=1, device_id=device, device_id_type=MESH)

    for copy in tables:
        copy.wait()
    block_two = p >= 2
    set_of = per_row(lambda m: jnp.where(block_two, sets[1, m], sets[0, m]))
    for k in range(NSETS):
        hot = (set_of == k).astype(F32)
        for n in range(8):
            g = hot * gain[k : k + 1, n * BLK : (n + 1) * BLK]
            b = hot * bias[k : k + 1, n * BLK : (n + 1) * BLK]
            if k == 0:
                par[n] = g
                par[8 + n] = b
            else:
                par[n] += g
                par[8 + n] += b
    dg[...] = jnp.zeros_like(dg)
    dgb[...] = jnp.zeros_like(dgb)
    pl.semaphore_wait(barrier, 6)

    total_in, total_out = 2.0 * PIX_IN, 2.0 * PIX_OUT

    def build_patches(base):
        def body(tap, carry):
            row, col = base(tap)
            window = pb[pl.ds(row, 7), pl.ds(col, 7)].reshape(RV, BLK)
            pt[tap, 0:RV, :] = window.astype(BF16)
            return carry

        lax.fori_loop(0, 9, body, 0)

    def clear_patch_pad():
        def body(tap, carry):
            pt[tap, RW - 16 : RW, :] = jnp.zeros((16, BLK), BF16)
            return carry

        lax.fori_loop(0, 9, body, 0)

    def strided_base(tap):
        di, dj = tap // 3, lax.rem(tap, 3)
        return lax.rem(di, 2) * 8 + di // 2, lax.rem(dj, 2) * 8 + dj // 2

    def plain_base(tap):
        return tap // 3, lax.rem(tap, 3)

    def conv(ref, first, target):
        target[...] = jnp.zeros_like(target)

        def body(tap, carry):
            z = nn(pt[tap], ref[rows(first + tap * BLK, BLK), :])
            target[...] += z.reshape(PP, 8, BLK)
            return carry

        lax.fori_loop(0, 9, body, 0)

    def conv_back(dz, ref, first, base, side):
        pb[0:side, 0:side] = jnp.zeros((side, side, 8, BLK), F32)

        def body(tap, carry):
            row, col = base(tap)
            part = nt(dz[0:RV, :], ref[rows(first + tap * BLK, BLK), :])
            pb[pl.ds(row, 7), pl.ds(col, 7)] += part.reshape(7, 7, 8, BLK)
            return carry

        lax.fori_loop(0, 9, body, 0)

    def stats_of_map(ref, slot_sum, slot_square):
        def body(c, _, carry):
            z = ref[c]
            return add_stats(carry, z, z * z)

        tx[slot_sum], tx[slot_square] = five(body, zero_stats)

    def act_to(ref, target, center, scale, g, b, mask):
        def body(c, i, carry):
            zhat = (ref[c] - center) * scale
            ref[c] = zhat
            h = silu(zhat * g + b) * mask
            target[rows(i * 80, 80), :] = h.reshape(80, BLK).astype(BF16)
            return carry

        five(body)
        clear_pad(target, 0)

    def upstream(target, grad, zhat_ref, g, b, mask, slot_sum, slot_gain):
        def body(c, i, carry):
            zhat = zhat_ref[c]
            du = grad[rows(i * 80, 80), :].astype(F32).reshape(10, 8, BLK) * mask * slope(zhat * g + b)
            target[c] = du
            return add_stats(carry, du, du * zhat)

        tx[slot_sum], tx[slot_gain] = five(body, zero_stats)

    def norm_back(target, first, du_ref, du_first, zhat_ref, zhat_first, gscale, mean_du, mean_dg, unrolled=False):
        def body(c, i, carry):
            du = du_ref[pl.ds(du_first + i * 10, 10)]
            zhat = zhat_ref[pl.ds(zhat_first + i * 10, 10)]
            dz = gscale * (du - mean_du - zhat * mean_dg)
            target[rows(first + i * 80, 80), :] = dz.reshape(80, BLK).astype(BF16)
            return carry

        five(body, unrolled=unrolled)
        clear_pad(target, first)

    def gi_copy():
        return pltpu.make_async_copy(f3.at[0:PIX_IN, :, 0:256], gi, ls.at[17])

    def out_copy():
        return pltpu.make_async_copy(v_out, out, ls.at[0])

    def dgb_copy():
        return pltpu.make_async_copy(dgb, dgb_out, ls.at[1])

    def final_part():
        @pl.when(p != 1)
        def _():
            remote(ob, ob, C_SHARE, C_SHARE, (p, d, r)).wait_recv()
            remote(r1, r1, C_GP, C_GP, (p, d, r)).wait_recv()

        @pl.when(p != 0)
        def _():
            remote(r0, r0, C_GI, C_GI, (p, d, r)).wait_recv()

        v_out[...] = ob[0:RV, :].astype(F32).reshape(PIX_OUT, 8, BLK).astype(BF16)
        out_copy().start()
        f0[0:PP, :, 0:256] = r1[...].astype(F32).reshape(PP, 8, 256)

        def place(a, carry):
            m = r0[rows(a * 224, 224), :].astype(F32).reshape(28, 8, 256)
            first = m[0:14].reshape(7, 2, 8, 256)
            even = first[:, 0] + f0[pl.ds(a * 7, 7), :, 0:256]
            f3[pl.ds(a * 28, 14), :, 0:256] = jnp.stack([even, first[:, 1]], axis=1).reshape(14, 8, 256)
            f3[pl.ds(a * 28 + 14, 14), :, 0:256] = m[14:28]
            return carry

        lax.fori_loop(0, 7, place, 0)
        gi_copy().start()

    @pl.when(p == 0)
    def _():
        mask = mask_of(0)

        def relay(i):
            piece_copy(W_VIA, i, quarter, (0, d, r)).wait_recv()
            piece_copy(W_OWN, i, quarter, (1, d, r)).start()

        def relay_half(i):
            half_copy(W_VIA, i, d, (0, d, r)).wait_recv()
            half_copy(W_OWN, i, d, (1, d, r)).start()

        put_w = put_narrow(wh, lambda i: i * 128)
        load_weights(plain, 44, 0, 8, put_w)

        def first_conv(q, slot, carry):
            rows_q = imgb[slot].astype(F32).reshape(224, 1024).astype(BF16)
            wx[rows(q * 224, 224), :] = rows_q[:, 0:512]
            wx[rows(1568 + q * 224, 224), :] = rows_q[:, 512:1024]
            z = nn(rows_q, wh[0:1024, :]).reshape(28, 8, BLK)
            f0[pl.ds(q * 28, 28)] = z
            load_weights(plain, 44, 8 + 5 * q, 5, put_w)
            return add_stats(carry, z, z * z)

        tx[0], tx[1] = over_images(first_conv, zero_stats)
        relay(VIA)
        exchange = remote(tx.at[pl.ds(0, 2)], rx.at[pl.ds(0, 2)], 0, 0, peer)
        exchange.start()
        pb[...] = jnp.zeros_like(pb)
        clear_patch_pad()
        load_weights(plain, 44, 43, 1, put_w)
        exchange.wait()

        center, scale = moments(0, 1, total_in, 0)
        g1, b1, g2, b2 = par[0], par[8], par[1], par[9]

        def hidden(i, carry):
            zhat = (f0[pl.ds(i * 14, 14)] - center) * scale
            f0[pl.ds(i * 14, 14)] = zhat
            h = (silu(zhat * g1 + b1) * mask).astype(BF16).astype(F32).reshape(7, 2, 8, BLK)
            u = i + 1
            row = lax.rem(u, 2) * 8 + u // 2
            pb[row, 8:15] = h[:, 0]
            pb[row, 1:8] = h[:, 1]
            return carry

        lax.fori_loop(0, 14, hidden, 0)
        relay(VIA + 1)
        build_patches(strided_base)
        conv(wh, 1024, fs.at[0])
        relay(VIA + 2)
        stats_of_map(fs.at[0], 2, 3)
        sync(1, 2, 2)
        center, scale = moments(2, 3, total_out, 1)
        act_to(fs.at[0], h2, center, scale, g2, b2, mask)
        send = remote(h2, h2, C_H2, C_H2, (1, d, r))
        send.start()
        for i in (HALF, HALF + 1, 16):
            relay_half(i)
        zero_rest(11, sb)
        send.wait_send()
        all_sent(wss.at[W_OWN], wx.at[0 : 3 * 128 + 3 * 256])
        say_ready()

        remote(dh, dh, C_DH, C_DH, (0, d, r)).wait_recv()
        upstream(fs.at[1], dh, fs.at[0], g2, b2, mask, 4, 5)
        sync(0, 4, 2)
        s_du, s_dg = both(4), both(5)
        dg[1], dg[9] = s_dg, s_du
        norm_back(d5, 0, fs.at[1], 0, fs.at[0], 0, g2 * inv[1], s_du * (1.0 / total_out), s_dg * (1.0 / total_out))
        def back_conv():
            conv_back(d5, wh, 1024, strided_base, 16)

        def slopes(i, carry):
            u = i + 1
            row = lax.rem(u, 2) * 8 + u // 2
            grad = jnp.stack([pb[row, 8:15], pb[row, 1:8]], axis=1).reshape(14, 8, BLK)
            zhat = f0[pl.ds(i * 14, 14)]
            du = grad * mask * slope(zhat * g1 + b1)
            f1[pl.ds(i * 14, 14)] = du
            return add_stats(carry, du, du * zhat)

        def first_slopes():
            tx[6], tx[7] = lax.fori_loop(0, 14, slopes, zero_stats)
            sync(1, 6, 2)
            dg[0], dg[8] = both(7), both(6)

        def first_back():
            s_du, s_dg = both(6), both(7)
            gscale, m_du, m_dg = g1 * inv[0], s_du * (1.0 / total_in), s_dg * (1.0 / total_in)

            def body(q, carry):
                part = pl.ds(q * 28, 28)
                dz = gscale * (f1[part] - m_du - f0[part] * m_dg)
                u1[rows(q * 224, 224), :] = dz.reshape(224, BLK).astype(BF16)
                return carry

            lax.fori_loop(0, 7, body, 0)

        def share(target, column, k):
            def body(q, carry):
                g = nt(u1[rows(q * 224, 224), :], wh[k * 256 : (k + 1) * 256, :])
                target[rows(q * 224, 224), column : column + 256] = g.astype(BF16)
                return carry

            lax.fori_loop(0, 7, body, 0)

        places = {1: (u0, 0), 2: (u0, 256), 3: (u2, 0)}

        def share_copy(k):
            target, column = places[k]
            return remote(target.at[0:1568, column : column + 256], r0, C_GI + k - 1, C_GI, (k, d, r))

        def share_out(k):
            share(*places[k], k)
            share_copy(k).start()

        def back_and_share():
            first_back()
            share_out(1)

        def compute(t):
            taps = (t < 6) | (t >= 8)

            @pl.when(taps)
            def _():
                tap = jnp.where(t < 6, t, t - 2)
                wh[rows(at_row(t), 512), :] = tn(pt[tap], d5[...]).astype(BF16)

            @pl.when(jnp.logical_not(taps))
            def _():
                block = tn(wx[rows((t - 6) * 1568, 1568), :], u1[0:1568, :])
                wh[rows(at_row(t), 512), :] = block.astype(BF16)

        def at_row(t):
            return jnp.where(t < 2, 5632 + t * 512, jnp.where(t < 8, t * 512, 2560 + t * 512))

        def chunk_of(t):
            return jnp.where(t < 6, t + 2, jnp.where(t < 8, t - 6, t))

        sum_gradients(
            8, compute, at_row, chunk_of, False, Z1_ZERO,
            {LAST_TURN + 8 * SUBS: final_part},
            lend=(5, 6, 7), helper=lambda t: jnp.where(t < 10, 2, 1), helper_turn=lambda t: jnp.where(t < 10, t - 1, 8),
            helper_row=lambda t: jnp.where(t < 10, (t - 1) * 512, HUB_GUEST), norms_at=4 * SUBS, norms=1024, late_back=1,
            after={
                1: back_conv,
                2: first_slopes,
                3: back_and_share,
                4: lambda: share(r0, 0, 0),
                8: lambda: share_out(3),
                10: lambda: share_out(2),
            },
        )
        for k in (1, 2, 3):
            share_copy(k).wait_send()

    @pl.when(p == 1)
    def _():
        mask = mask_of(1)
        gate_v = per_row(lambda m: gates[m]).astype(F32)
        cotb[PIX_OUT] = jnp.zeros((8, C_OUT), BF16)
        clear_patch_pad()
        load_weights(plain, 48, 0, 16, put_wide(wh, 0, 512, 0))
        load_weights(plain, 48, 16, 32, put_wide(wh, 2048, 1024, 16))

        def shorten(a, slot, carry):
            v = imgb[slot, 0:14].astype(F32).reshape(7, 2, 8, 1024)[:, 0]
            f0[pl.ds(a * 7, 7)] = v[:, :, 0:512]
            f0[pl.ds(PP + a * 7, 7)] = v[:, :, 512:1024]
            return carry

        other_z = 2 * (1 - lax.rem(r, 2))
        this_z = 2 * lax.rem(r, 2)

        def pass_own(i):
            piece_copy(W_OWN, i, quarter, (1, d, r)).wait_recv()
            piece_copy(W_PEER, i, quarter, peer).start()
            piece_copy(W_Z, i, quarter, z_dev).start()

        def pass_on(i):
            piece_copy(W_Z, i, other_z + d, peer).wait_recv()
            piece_copy(W_ON, i, other_z + d, peer).start()

        def have(i):
            piece_copy(W_PEER, i, this_z + 1 - d, peer).wait_recv()
            piece_copy(W_ON, i, other_z + 1 - d, peer).wait_recv()

        def pass_half(i):
            half_copy(W_OWN, i, d, (1, d, r)).wait_recv()
            half_copy(W_PEER, i, d, peer).start()

        def have_half(i):
            half_copy(W_PEER, i, 1 - d, peer).wait_recv()

        pass_own(0)
        over_images(shorten, 0)
        f0[PIX_OUT] = jnp.zeros((8, BLK), F32)
        f0[PP + PIX_OUT] = jnp.zeros((8, BLK), F32)
        sx[...] = f0[0 : 2 * PP].reshape(2 * RW, BLK).astype(BF16)

        def shortcut(n, carry):
            z = nn(sx[0:RW, :], wh[rows(2048 + n * 1024, 512), :]) + nn(
                sx[RW : 2 * RW, :], wh[rows(2560 + n * 1024, 512), :]
            )
            store_z(f1, n * PP, z, 4 * n + 2, 4 * n + 3)
            return carry

        pass_own(1)
        lax.fori_loop(0, 4, shortcut, 0)

        pass_own(2)
        pass_own(VIA)
        pass_on(0)
        pass_own(3)
        pass_on(1)
        pass_own(VIA + 1)
        pass_own(4)
        pl.semaphore_signal(go, inc=1, device_id=(3, d, r), device_id_type=MESH)
        pass_on(2)
        pass_own(VIA + 2)
        pass_own(5)
        pass_on(VIA)
        pass_own(6)
        pass_on(3)
        pass_own(7)
        pass_on(VIA + 1)
        remote(h2, h2, C_H2, C_H2, (1, d, r)).wait_recv()

        def third_conv(n, carry):
            store_z(f0, n * PP, nn(h2[...], wh[rows(n * 512, 512), :]), 4 * n, 4 * n + 1)
            exchange_of(E_WIDE + n, 4 * n, 4).start()
            return carry

        lax.fori_loop(0, 4, third_conv, 0)
        pass_on(4)

        def join(n, carry):
            exchange_of(E_WIDE + n, 4 * n, 4).wait()
            c3, s3 = moments(4 * n, 4 * n + 1, total_out, 2 + n)
            cp, sp = moments(4 * n + 2, 4 * n + 3, total_out, 6 + n)
            g3, gp, b = par[n], par[4 + n], par[8 + n] + par[12 + n]

            def body(_, i, carry):
                part = pl.ds(n * PP + i * 10, 10)
                a = (f0[part] - c3) * s3
                b_ = (f1[part] - cp) * sp
                f0[part] = a
                f1[part] = b_
                o = silu(a * g3 + b_ * gp + b)
                u0[rows(n * RW + i * 80, 80), :] = o.reshape(80, BLK).astype(BF16)
                return carry

            five(body)
            clear_pad(u0, n * RW)
            return carry

        lax.fori_loop(0, 4, join, 0)
        for n in (1, 2, 3):
            o1_copy(n, 3).start()
        pass_half(13)
        pass_on(VIA + 2)
        pass_half(HALF)
        each(have, 0, 4)
        zhat4, zhat5 = fs.at[0], fs.at[1]
        z = nn(u0[0:RW, :], wx[0:512, :])
        for n in range(1, 4):
            z += nn(u0[n * RW : (n + 1) * RW, :], wx[n * 512 : (n + 1) * 512, :])
        store_z(zhat4, 0, z, 16, 17)
        sync(0, 16, 2)
        remote(parx.at[0:4], parx.at[0:4], C_PAR2, C_PAR2, (1, d, r)).wait_recv()
        center, scale = moments(16, 17, total_out, 10)
        g4, g5, b4, b5 = parx[0], parx[1], parx[2], parx[3]
        pb[0:9, 0:9] = jnp.zeros((9, 9, 8, BLK), F32)

        def hidden(a, carry):
            part = pl.ds(a * 7, 7)
            zhat = (zhat4[part] - center) * scale
            zhat4[part] = zhat
            h = silu(zhat * g4 + b4) * mask
            pb[a + 1, 1:8] = h.astype(BF16).astype(F32)
            return carry

        lax.fori_loop(0, 7, hidden, 0)
        h4[0:RV, :] = pb[1:8, 1:8].reshape(RV, BLK).astype(BF16)
        h4_send = remote(h4, h4, C_H4, C_H4, (2, d, r))
        h4_send.start()

        o1_copy(0, 2).start()
        pass_on(5)
        build_patches(plain_base)
        pass_on(6)

        def fifth_conv(taps):
            left = jnp.concatenate([pt[t] for t in taps], axis=1)
            right = jnp.concatenate([wx[2048 + t * 512 : 2560 + t * 512, :] for t in taps], axis=0)
            return nn(left, right).reshape(PP, 8, BLK)

        for i in (4, 5, VIA):
            have(i)
        zhat5[...] = fifth_conv((0, 1, 4))
        pass_half(HALF + 1)
        pass_on(7)
        for i in (6, VIA + 1, VIA + 2):
            have(i)
        zhat5[...] += fifth_conv((2, 5, 6))
        have(7)
        have_half(HALF)
        have_half(HALF + 1)
        store_z(zhat5, 0, zhat5[...] + fifth_conv((3, 7, 8)), 18, 19)
        exchange_z5 = exchange_of(1, 18, 2)
        exchange_z5.start()
        pass_half(14)
        exchange_z5.wait()
        center, scale = moments(18, 19, total_out, 11)
        act_to(zhat5, h5, center, scale, g5, b5, mask)


        def sixth_conv(n):
            have_half(13 + n)
            store_z(f2, n * PP, nn(h5[...], wx[6656 + n * 512 : 7168 + n * 512, :]), 20 + 2 * n, 21 + 2 * n)

        def exchange_z6(n):
            return exchange_of(E_WIDE_NEXT + n, 20 + 2 * n, 2)

        def exchange_d6(n):
            return exchange_of(E_WIDE + n, 28 + 2 * n, 2)

        def finish(n):
            center, scale = moments(20 + 2 * n, 21 + 2 * n, total_out, 12 + n)
            g6, b6 = parx[4 + n], parx[8 + n]

            def body(c, i, carry):
                part = pl.ds(n * PP + i * 10, 10)
                part_rows = rows(n * RW + i * 80, 80)
                zhat = (f2[part] - center) * scale
                f2[part] = zhat
                o = u0[part_rows, :].astype(F32).reshape(10, 8, BLK)
                q = o + zhat * g6 + b6
                s = sigmoid(q)
                act = q * s
                pt[n, rows(i * 80, 80), :] = (o + gate_v * (act - o)).reshape(80, BLK).astype(BF16)
                ct = cotb[c, :, n * BLK : (n + 1) * BLK].astype(F32)
                through = ct * gate_v
                dq = through * (s + act * (1.0 - s))
                f3[part] = dq
                u2[part_rows, :] = (dq + (ct - through)).reshape(80, BLK).astype(BF16)
                return add_stats(carry, dq, dq * zhat)

            tx[28 + 2 * n], tx[29 + 2 * n] = five(body, zero_stats, unrolled=True)

        for n in (0, 1):
            sixth_conv(n)
            exchange_z6(n).start()
        remote(parx.at[4:12], parx.at[4:12], C_PAR3, C_PAR3, (1, d, r)).wait_recv()
        pltpu.make_async_copy(cot, cotb.at[0:PIX_OUT], ls.at[16]).wait()
        pass_half(15)
        exchange_z6(0).wait()
        finish(0)
        exchange_d6(0).start()
        pass_half(16)
        exchange_z6(1).wait()
        finish(1)
        exchange_d6(1).start()
        have_half(15)
        store_z(f2, 2 * PP, nn(h5[...], wx[7680:8192, :]), 24, 25)
        exchange_z6(2).start()
        have_half(16)
        store_z(f2, 3 * PP, nn(h5[...], wx[8192:8704, :]), 26, 27)
        exchange_z6(3).start()
        exchange_z6(2).wait()
        finish(2)
        exchange_d6(2).start()
        exchange_z6(3).wait()
        finish(3)
        exchange_d6(3).start()
        ob[...] = pt[1]

        def output_copy(k):
            return remote(pt.at[k], ob, C_SHARE + k % 3, C_SHARE, (k, d, r))

        output_copy(3).start()


        def sixth_back(n):
            s_du, s_dg = both(28 + 2 * n), both(29 + 2 * n)
            dgx[4 + n] = s_dg
            dgx[8 + n] = s_du
            norm_back(
                u1, n * RW, f3, n * PP, f2, n * PP, parx[4 + n] * inv[12 + n],
                s_du * (1.0 / total_out), s_dg * (1.0 / total_out), unrolled=True,
            )

        for n in range(4):
            exchange_d6(n).wait()
        grad = jnp.zeros((RW, BLK), F32)
        for n in range(5):
            if n < 4:
                sixth_back(n)
            if n > 0:
                grad += nt(u1[(n - 1) * RW : n * RW, :], wx[6144 + n * 512 : 6656 + n * 512, :])
        dh[...] = grad.astype(BF16)

        upstream(f2, dh, zhat5, g5, b5, mask, 36, 37)
        sync(0, 36, 2)
        s_du, s_dg = both(36), both(37)
        dgx[1] = s_dg
        dgx[3] = s_du
        norm_back(d5, 0, f2, 0, zhat5, 0, g5 * inv[11], s_du * (1.0 / total_out), s_dg * (1.0 / total_out))
        d5_send = remote(d5, d5, C_D5, C_D5, (2, d, r))
        d5_send.start()
        pb[0:9, 0:9] = jnp.zeros((9, 9, 8, BLK), F32)
        for tap in range(9):
            row, col = tap // 3, tap % 3
            part = nt(d5[0:RV, :], wx[2048 + tap * 512 : 2560 + tap * 512, :])
            pb[row : row + 7, col : col + 7] += part.reshape(7, 7, 8, BLK)

        def fourth_slopes(a, carry):
            part = pl.ds(a * 7, 7)
            zhat = zhat4[part]
            du = pb[a + 1, 1:8] * mask * slope(zhat * g4 + b4)
            f2[part] = du
            return add_stats(carry, du, du * zhat)

        tx[38], tx[39] = lax.fori_loop(0, 7, fourth_slopes, zero_stats)
        sync(1, 38, 2)
        s_du, s_dg = both(38), both(39)
        dgx[0] = s_dg
        dgx[2] = s_du
        norm_back(d4, 0, f2, 0, zhat4, 0, g4 * inv[10], s_du * (1.0 / total_out), s_dg * (1.0 / total_out))

        def carried_back(n):
            z = nt(d4[...], wx[n * 512 : (n + 1) * 512, :])
            f2[(n % 2) * PP : (n % 2 + 1) * PP] = z.reshape(PP, 8, BLK)

        def exchange_d1(n):
            return exchange_of(E_WIDE_NEXT + n, 40 + 3 * n, 3)

        def first_block_slopes(n):
            g3, gp, b = par[n], par[4 + n], par[8 + n] + par[12 + n]

            def body(_, i, carry):
                part = pl.ds(n * PP + i * 10, 10)
                do = u2[n * RW + i * 80 : n * RW + (i + 1) * 80, :].astype(F32).reshape(10, 8, BLK)
                do += f2[pl.ds((n % 2) * PP + i * 10, 10)]
                a, b_ = f0[part], f1[part]
                dp = do.astype(BF16).astype(F32) * slope(a * g3 + b_ * gp + b)
                f3[part] = dp
                s0, s1, s2 = carry
                return s0 + jnp.sum(dp, axis=0), s1 + jnp.sum(dp * a, axis=0), s2 + jnp.sum(dp * b_, axis=0)

            first = 40 + 3 * n
            tx[first], tx[first + 1], tx[first + 2] = five(body, zero_stats + zero_stats[:1], unrolled=True)

        carried_back(0)
        for n in range(4):
            if n < 3:
                carried_back(n + 1)
            first_block_slopes(n)
            exchange_d1(n).start()

        def third_back(n):
            first = 40 + 3 * n
            m_du, m_dg = both(first) * (1.0 / total_out), both(first + 1) * (1.0 / total_out)
            norm_back(
                pt.at[4 + n], 0, f3, n * PP, f0, n * PP, par[n] * inv[2 + n], m_du, m_dg, unrolled=True
            )

        for n in range(4):
            exchange_d1(n).wait()
        grad = jnp.zeros((RW, BLK), F32)
        for n in range(5):
            if n < 4:
                third_back(n)
            if n > 0:
                grad += nt(pt[3 + n], wh[(n - 1) * 512 : n * 512, :])
        dh[...] = grad.astype(BF16)
        dh_send = remote(dh, dh, C_DH, C_DH, (0, d, r))
        dh_send.start()

        def shortcut_back(n, carry):
            first = 40 + 3 * n
            s_du, s_d3, s_dp = both(first), both(first + 1), both(first + 2)
            dg[n] = s_d3
            dg[4 + n] = s_dp
            dg[8 + n] = s_du
            dg[12 + n] = s_du
            m_du, m_dg = s_du * (1.0 / total_out), s_dp * (1.0 / total_out)
            norm_back(u2, n * RW, f3, n * PP, f1, n * PP, par[4 + n] * inv[6 + n], m_du, m_dg)
            return carry

        def all_shortcut_back():
            lax.fori_loop(0, 4, shortcut_back, 0)

        all_sent(wss.at[W_PEER], wx.at[0 : HALF * 128 + 6 * 256])
        all_sent(wss.at[W_Z], wx.at[0 : HALF * 128])
        all_sent(wss.at[W_ON], wx.at[0 : HALF * 128])
        say_ready()

        late = [remote(d4, d4, C_D4, C_D4, (2, d, r))]
        for first, last, sem, chip in ((0, 4, C_DG2, 2), (4, 12, C_DG3, 3)):
            late.append(remote(dgx.at[first:last], dgx.at[first:last], sem, sem, (chip, d, r)))

        def late_sends():
            dh_send.wait_send()
            for copy in late:
                copy.start()

        def shortcut_share(k):
            g = nt(u2[0:RW, :], wh[2048 + k * 256 : 2304 + k * 256, :])
            for n in range(1, 4):
                g += nt(u2[n * RW : (n + 1) * RW, :], wh[2048 + n * 1024 + k * 256 : 2304 + n * 1024 + k * 256, :])
            return g.astype(BF16)

        places = ((h4.at[:, 0:256], 0), (h4.at[:, 256:512], 2), (pt.at[8, :, 0:256], 3))

        def share_copy(slot):
            place, k = places[slot]
            return remote(place, r1, C_GP + slot, C_GP, (k, d, r))

        def shortcut_shares(slot):
            place, k = places[slot]
            if slot == 0:
                h4_send.wait_send()
            place[...] = shortcut_share(k)

        def shortcut_own():
            r1[...] = shortcut_share(1)


        def late_shares():
            for slot in range(3):
                share_copy(slot).start()

        def at_row(t):
            early = jnp.where(t == 8, HUB_GUEST, t * 512)
            return jnp.where(t < 11, early, jnp.where(t < 16, t * 512 + 512, 5632))

        def compute(t):
            @pl.when(t < 4)
            def _():
                left = h2[:, pl.ds(pl.multiple_of(t * 128, 128), 128)]
                for n in range(4):
                    put_chunk(at_row(t), n, tn(left, pt[4 + n]))

            @pl.when((t >= 4) & (t < 13))
            def _():
                m = jnp.where(t < 8, t - 4, t - 5)
                left = sx[rows((m // 4) * RW, RW), pl.ds(pl.multiple_of(lax.rem(m, 4) * 128, 128), 128)]
                for n in range(4):
                    put_chunk(at_row(t), n, tn(left, u2[n * RW : (n + 1) * RW, :]))

            @pl.when(t >= 13)
            def _():
                left = h5[:, pl.ds(pl.multiple_of((t - 13) * 128, 128), 128)]
                for n in range(4):
                    put_chunk(at_row(t), n, tn(left, u1[n * RW : (n + 1) * RW, :]))

        zero_rest(12, sb)
        sum_gradients(
            11, compute, at_row, lambda t: jnp.where(t < 8, t, t - 1), True, 0,
            {
                1: all_shortcut_back,
                2: lambda: shortcut_shares(0),
                4: lambda: shortcut_shares(1),
                5: late_sends,
                6: lambda: shortcut_shares(2),
                8: shortcut_own,
                7: lambda: output_copy(2).start(),
                11: lambda: output_copy(0).start(),
                15: late_shares,
                LAST_TURN + 11 * SUBS: final_part,
            },
            lend=(3, 5), passed=(7, 9, 11, 13), helper=lambda t: 3, helper_turn=lambda t: t - 7, norms_at=2,
            handed_in=lambda t: t == 8, lent_by=(lambda t: t == 8, lambda t: 0, lambda t: t + 2, 1), back=R_BACK_HUB,
            computed=(0, 10), packed_here=(0, 10),
        )
        for copy in [d5_send, o1_copy(0, 2)] + [o1_copy(n, 3) for n in (1, 2, 3)] + late:
            copy.wait_send()
        for slot in range(3):
            share_copy(slot).wait_send()
        for k in (0, 2, 3):
            output_copy(k).wait_send()


    @pl.when(p == 2)
    def _():
        for k, slot in ((0, 0), (1, 1), (2, 8), (3, 9)):
            parx[k] = par[slot]
        par_send = remote(parx.at[0:4], parx.at[0:4], C_PAR2, C_PAR2, (1, d, r))
        par_send.start()

        put_w = put_narrow(wx, lambda i: own_parts(i) * 128)

        def put(i):
            put_w(i)

            @pl.when(i < VIA)
            def _():
                piece_copy(W_OWN, i, quarter, (1, d, r)).start()

            @pl.when((i >= VIA) & (i < HALF))
            def _():
                piece_copy(W_VIA, i, quarter, (0, d, r)).start()

            for k in range(HALF, 13):
                @pl.when(i == HALF + 2 * (k - HALF) + 1)
                def _(k=k):
                    half_copy(W_VIA, k, d, (0, d, r)).start()

        load_weights(own_parts, 15, 0, 15, put)
        pb[...] = jnp.zeros_like(pb)
        clear_patch_pad()

        all_sent(wss.at[W_OWN], wx.at[0 : VIA * 128])
        all_sent(wss.at[W_VIA], wx.at[0 : 3 * 128 + 2 * 256])
        say_ready()
        remote(h4, h4, C_H4, C_H4, (2, d, r)).wait_recv()
        pb[1:8, 1:8] = h4[0:RV, :].astype(F32).reshape(7, 7, 8, BLK)
        build_patches(plain_base)
        remote(d5, d5, C_D5, C_D5, (2, d, r)).wait_recv()

        def compute(t):
            taps = (t < 5) | (t >= 11)

            @pl.when(taps)
            def _():
                tap = jnp.where(t < 5, t + 4, t - 11)
                wh[rows(t * 512, 512), :] = tn(pt[tap], d5[...]).astype(BF16)

            @pl.when(t == 5)
            def _():
                remote(d4, d4, C_D4, C_D4, (2, d, r)).wait_recv()
                for n in range(4):
                    o1_copy(n, 2).wait_recv()

            @pl.when(jnp.logical_not(taps))
            def _():
                n = jnp.where(t < 7, t - 5, t - 7)
                wh[rows(t * 512, 512), :] = tn(u0[rows(n * RW, RW), :], d4[...]).astype(BF16)

        def chunk_of(t):
            return jnp.where(t < 5, t + 8, jnp.where(t < 7, t - 5, t - 7))

        def norm_grads():
            remote(dgx.at[0:4], dgx.at[0:4], C_DG2, C_DG2, (2, d, r)).wait_recv()
            dg[0], dg[1], dg[8], dg[9] = dgx[0], dgx[1], dgx[2], dgx[3]

        sum_gradients(
            11, compute, lambda t: t * 512, chunk_of, False, 0,
            {6 * SUBS: norm_grads, LAST_TURN + 11 * SUBS: final_part},
            lend=(2, 3, 4, 6), helper=lambda t: 3, helper_turn=lambda t: t - 11,
            handed_in=lambda t: (t >= 7) & (t < 9),
            lent_by=(lambda t: (t >= 7) & (t < 9), lambda t: 0, lambda t: t + 1, 2),
            computed=(0, 9), packed_here=(0, 9), norms_at=6 * SUBS, norms=1024,
        )
        par_send.wait_send()

    @pl.when(p == 3)
    def _():
        for k in range(4):
            parx[4 + k] = par[k]
            parx[8 + k] = par[8 + k]
        par_send = remote(parx.at[4:12], parx.at[4:12], C_PAR3, C_PAR3, (1, d, r))
        par_send.start()
        say_ready()

        def put(i):
            for n in range(4):
                for j in range(4):
                    wx[rows(6656 + n * 512 + d * 256 + i * 32, 32), j * 128 : (j + 1) * 128] = st[
                        pl.ds(4 * n + j, 32, stride=16), :
                    ].astype(BF16)

        load_weights(half_rows, 8, 0, 8, put)
        zero_rest(4, sb)
        pl.semaphore_wait(go, 1)

        half_copy(W_VIA, 16, d, (0, d, r)).start()
        for i in (13, 14, 15):
            half_copy(W_OWN, i, d, (1, d, r)).start()
        for n in (1, 2, 3):
            o1_copy(n, 3).wait_recv()
            o1_copy(n, 2).start()
        def norm_grads():
            remote(dgx.at[4:12], dgx.at[4:12], C_DG3, C_DG3, (3, d, r)).wait_recv()
            for k in range(4):
                dg[k] = dgx[4 + k]
                dg[8 + k] = dgx[8 + k]

        sum_gradients(
            10, lambda t: None, lambda t: t * 512, lambda t: t - 6, True, 0,
            {5 * SUBS: norm_grads, LAST_TURN + 10 * SUBS: final_part},
            handed_in=lambda t: t >= 0,
            lent_by=(lambda t: t < 6, lambda t: jnp.where(t < 4, 2, 1), lambda t: jnp.where(t < 4, t + 11, t + 7), 6),
            computed=(0, 0), packed_here=(6, 4), norms_at=5 * SUBS, norms=2048,
        )
        for n in (1, 2, 3):
            o1_copy(n, 2).wait_send()
        all_sent(wss.at[W_VIA], wx.at[0:256])
        all_sent(wss.at[W_OWN], wx.at[0 : 3 * 256])
        par_send.wait_send()

    dgb_copy().start()
    gi_copy().wait()
    out_copy().wait()
    dgb_copy().wait()


def widen_kernel(out_in, gi_in, dw_in, dgb_in, out, gi, dw, gain, bias, v_out, v_gi, v_dw, v_wide, v_dgb, sin, sout):
    count = v_dw.shape[0] // 2048

    def part(i):
        return pl.ds(i * 2048, 2048)

    loads = [pltpu.make_async_copy(dw_in.at[part(i)], v_dw.at[part(i)], sin.at[i]) for i in range(count)]
    others = (
        (dgb_in, v_dgb, ((v_dgb.at[0:4], gain), (v_dgb.at[4:8], bias))),
        (out_in, v_out, ((v_out, out),)),
        (gi_in, v_gi, ((v_gi, gi),)),
    )
    more = [pltpu.make_async_copy(a, b, sin.at[count + k]) for k, (a, b, _) in enumerate(others)]
    for copy in loads + more:
        copy.start()
    stores = []
    for i in range(count):
        loads[i].wait()
        v_wide[part(i)] = v_dw[part(i)].astype(F32)
        stores.append(pltpu.make_async_copy(v_wide.at[part(i)], dw.at[part(i)], sout.at[i]))
        stores[-1].start()
    for k, (_, _, ends) in enumerate(others):
        more[k].wait()
        for a, b in ends:
            stores.append(pltpu.make_async_copy(a, b, sout.at[len(stores)]))
            stores[-1].start()
    for copy in stores:
        copy.wait()


def widen(out, gi, dw, dgb):
    count = P_SIZE // 128 // 2048
    any_space = pl.BlockSpec(memory_space=pl.ANY)
    return pl.pallas_call(
        widen_kernel,
        out_shape=(
            jax.ShapeDtypeStruct(out.shape, out.dtype),
            jax.ShapeDtypeStruct(gi.shape, gi.dtype),
            jax.ShapeDtypeStruct(dw.shape, F32),
            jax.ShapeDtypeStruct((4, 4096), F32),
            jax.ShapeDtypeStruct((4, 4096), F32),
        ),
        in_specs=[any_space] * 4,
        out_specs=(any_space,) * 5,
        scratch_shapes=[
            pltpu.VMEM(out.shape, out.dtype),
            pltpu.VMEM(gi.shape, gi.dtype),
            pltpu.VMEM(dw.shape, BF16),
            pltpu.VMEM(dw.shape, F32),
            pltpu.VMEM(dgb.shape, F32),
            pltpu.SemaphoreType.DMA((count + 3,)),
            pltpu.SemaphoreType.DMA((count + 4,)),
        ],
        compiler_params=pltpu.CompilerParams(vmem_limit_bytes=64 * 1024 * 1024),
    )(out, gi, dw, dgb)


def one_kernel(images, section_weights, bn_gain, bn_bias, width, bn_set, gate, cotangent):
    any_space = pl.BlockSpec(memory_space=pl.ANY)
    smem = pl.BlockSpec(memory_space=pltpu.SMEM)
    out, gi, dw, dgb = pl.pallas_call(
        whole_kernel,
        out_shape=(
            jax.ShapeDtypeStruct((PIX_OUT, 8, BLK), BF16),
            jax.ShapeDtypeStruct((PIX_IN, 8, 256), F32),
            jax.ShapeDtypeStruct((P_SIZE // SUB, 512, 128), BF16),
            jax.ShapeDtypeStruct((8, 4096), F32),
        ),
        in_specs=[any_space, any_space, any_space, any_space, smem, smem, smem, any_space],
        out_specs=(any_space,) * 4,
        scratch_shapes=[
            pltpu.VMEM((4, 28, 8, 1024), BF16),
            pltpu.VMEM((RING, 1, SUB), BF16),
            pltpu.VMEM((512, 128), F32),
            pltpu.VMEM((9216, BLK), BF16),
            pltpu.VMEM((8768, BLK), BF16),
            pltpu.VMEM((4 * PP, 8, BLK), F32),
            pltpu.VMEM((4 * PP, 8, BLK), F32),
            pltpu.VMEM((4 * PP, 8, BLK), F32),
            pltpu.VMEM((4 * PP, 8, BLK), F32),
            pltpu.VMEM((2, PP, 8, BLK), F32),
            pltpu.VMEM((16, 16, 8, BLK), F32),
            pltpu.VMEM((9, RW, BLK), BF16),
            pltpu.VMEM((4 * RW, BLK), BF16),
            pltpu.VMEM((4 * RW, BLK), BF16),
            pltpu.VMEM((4 * RW, BLK), BF16),
            pltpu.VMEM((2 * RW, BLK), BF16),
            pltpu.VMEM((PP, 8, C_OUT), BF16),
            pltpu.VMEM((RW, BLK), BF16),
            pltpu.VMEM((RW, BLK), BF16),
            pltpu.VMEM((RW, BLK), BF16),
            pltpu.VMEM((RW, BLK), BF16),
            pltpu.VMEM((RW, BLK), BF16),
            pltpu.VMEM((RW, BLK), BF16),
            pltpu.VMEM((8 * PIX_IN, 256), BF16),
            pltpu.VMEM((RW, 256), BF16),
            pltpu.VMEM((RW, BLK), BF16),
            pltpu.VMEM((52, 8, BLK), F32),
            pltpu.VMEM((52, 8, BLK), F32),
            pltpu.VMEM((16, 8, BLK), F32),
            pltpu.VMEM((16, 8, BLK), F32),
            pltpu.VMEM((12, 8, BLK), F32),
            pltpu.VMEM((16, 8, BLK), F32),
            pltpu.VMEM((12, 8, BLK), F32),
            pltpu.VMEM((4, 512, 128), BF16),
            pltpu.VMEM((4352, BLK), BF16),
            pltpu.VMEM((2, 8, 4096), F32),
            pltpu.VMEM((8, 4096), F32),
            pltpu.VMEM((8, 4096), F32),
            pltpu.VMEM((PIX_OUT, 8, BLK), BF16),
            pltpu.VMEM((NSETS, 4096), F32),
            pltpu.VMEM((NSETS, 4096), F32),
            pltpu.SemaphoreType.DMA((19,)),
            pltpu.SemaphoreType.DMA((N_SEM,)),
            pltpu.SemaphoreType.DMA((N_SEM,)),
            pltpu.SemaphoreType.DMA((5,)),
            pltpu.SemaphoreType.DMA((N_SUM_SEND,)),
            pltpu.SemaphoreType.DMA((N_SUM_RECV,)),
            pltpu.SemaphoreType.REGULAR((2,)),
            pltpu.SemaphoreType.REGULAR,
        ],
        compiler_params=pltpu.CompilerParams(
            collective_id=0, has_side_effects=True, vmem_limit_bytes=64 * 1024 * 1024
        ),
    )(
        jnp.transpose(images, (1, 0, 2)),
        section_weights,
        bn_gain[0],
        bn_bias[0],
        width.T,
        bn_set.T,
        gate,
        jnp.transpose(cotangent, (1, 0, 2)),
    )
    out, gi, dw, gain_sum, bias_sum = widen(out, gi, dw.reshape(P_SIZE // 128, 128), dgb)
    return (
        jnp.transpose(out, (1, 0, 2)),
        jnp.transpose(gi, (1, 0, 2)),
        dw.reshape(1, P_SIZE),
        gain_sum[None],
        bias_sum[None],
    )


def solution(mesh):
    sizes = dict(mesh.shape)
    fits = sizes["pipe"] == 4 and sizes["dp"] == 2 and sizes["rep"] == 4
    placed = (
        P(("dp", "rep"), None, None),
        P("pipe", None),
        P("pipe", None, None),
        P("pipe", None, None),
        P(),
        P(),
        P(),
        P(("dp", "rep"), None, None),
    )
    return jax.shard_map(
        one_kernel if fits else on_device,
        mesh=mesh,
        in_specs=placed,
        out_specs=(
            P(("dp", "rep"), None, "pipe"),
            P(("dp", "rep"), None, "pipe"),
            P("pipe", None),
            P("pipe", None, None),
            P("pipe", None, None),
        ),
        check_vma=False,
    )
```

```python
import jax
import jax.numpy as jnp
from jax import lax
from jax.experimental import pallas as pl
from jax.experimental.pallas import tpu as pltpu
from jax.sharding import PartitionSpec as P

C_IN = 1024
C_MID = 512
C_OUT = 2048
SIDE = 14
NSETS = 4
MB = 8
IMG_B = 1
OSIDE = 7
PIX_IN = 196
PIX_OUT = 49
IMG_DEV = 8
P_SIZE = 3407872


EPSILON = 1e-05


def for_sending(array):

    def short(part):
        return part.astype(jnp.bfloat16) if part.dtype == jnp.float32 else part

    return jax.tree.map(short, array)


def shifted(value, axis, steps):
    count = lax.axis_size(axis)
    first, last = (max(0, -steps), min(count, count - steps))
    return lax.ppermute(value, axis, [(source, source + steps) for source in range(first, last)])


def smooth(inputs):
    return inputs * jax.nn.sigmoid(inputs)


def smooth_slope(inputs):
    gate_sig = jax.nn.sigmoid(inputs)
    return gate_sig * (1.0 + inputs * (1.0 - gate_sig))


def matmul(left_op, right_op):
    return jnp.dot(left_op, right_op, preferred_element_type=jnp.float32)


def matmul_left_t(left_op, right_op):
    return lax.dot_general(
        left_op, right_op, (((0,), (0,)), ((), ())), preferred_element_type=jnp.float32
    )


def matmul_right_t(left_op, right_op):
    return lax.dot_general(
        left_op, right_op, (((1,), (1,)), ((), ())), preferred_element_type=jnp.float32
    )


def patches(planes, stride):
    images, side_len, channels = (planes.shape[0], planes.shape[1], planes.shape[3])
    out_side = side_len // stride
    padded = jnp.pad(planes, ((0, 0), (1, 1), (1, 1), (0, 0)))
    pieces = []
    for row_off in range(3):
        for col_off in range(3):
            pieces.append(
                padded[
                    :,
                    row_off : row_off + stride * (out_side - 1) + 1 : stride,
                    col_off : col_off + stride * (out_side - 1) + 1 : stride,
                    :,
                ]
            )
    return jnp.concatenate(pieces, axis=3).reshape(images * out_side * out_side, 9 * channels)


def unpatch(columns, images, side_len, stride, channels):
    out_side = side_len // stride
    pieces = columns.reshape(images, out_side, out_side, 9, channels)
    padded = jnp.zeros((images, side_len + 2, side_len + 2, channels), jnp.float32)
    for row_off in range(3):
        for col_off in range(3):
            padded = padded.at[
                :,
                row_off : row_off + stride * (out_side - 1) + 1 : stride,
                col_off : col_off + stride * (out_side - 1) + 1 : stride,
                :,
            ].add(pieces[:, :, :, row_off * 3 + col_off, :])
    return padded[:, 1 : side_len + 1, 1 : side_len + 1, :]


def group_moments(sums_local, squares_local):
    return (
        lax.psum(sums_local.astype(jnp.bfloat16), "dp").astype(jnp.float32),
        lax.psum(squares_local.astype(jnp.bfloat16), "dp").astype(jnp.float32),
    )


def group_grad_sums(bias_local, gain_local):
    return (
        lax.psum(bias_local.astype(jnp.bfloat16), "dp").astype(jnp.float32),
        lax.psum(gain_local.astype(jnp.bfloat16), "dp").astype(jnp.float32),
    )


def stats_of(sum_all, square_all, start, count, row_total):
    center = sum_all[start : start + count] / row_total
    inv_std = lax.rsqrt(square_all[start : start + count] / row_total - center * center + EPSILON)
    return (center, inv_std)


def norm_grad(slope_in, normed, gain_vec, inv_std, sum_bias, sum_gain, row_total):
    return (
        gain_vec * inv_std * (slope_in - sum_bias / row_total - normed * (sum_gain / row_total))
    ).astype(jnp.bfloat16)


def on_device(images, section_weights, bn_gain, bn_bias, width, bn_set, gate, cotangent):
    section_idx = lax.axis_index("pipe")
    pipe_count = lax.axis_size("pipe")
    dp_count = lax.axis_size("dp")
    flat_weights = section_weights[0]
    gain_table = bn_gain[0]
    bias_table = bn_bias[0]
    rows_in = IMG_B * PIX_IN
    rows_out = IMG_B * PIX_OUT
    total_in = float(rows_in * dp_count)
    total_out = float(rows_out * dp_count)
    wide = 2 * C_OUT
    scr_len = IMG_B * max(PIX_IN * C_MID, PIX_OUT * wide)
    image_blocks = images.reshape(MB, IMG_B, PIX_IN, C_IN)
    pad_mid = jnp.zeros((wide - 2 * C_MID,), jnp.float32)
    zero_wide = jnp.zeros((wide,), jnp.float32)
    zero_scr = jnp.zeros((scr_len,), jnp.float32)
    zero_mid = jnp.zeros((rows_out, C_MID), jnp.bfloat16)
    zero_res = jnp.zeros((rows_out, C_OUT), jnp.bfloat16)
    zero_rows = jnp.zeros((rows_out, C_OUT), jnp.float32)
    zero_input = jnp.zeros((IMG_B, PIX_IN, C_IN), jnp.float32)

    def pack(values):
        flat = values.reshape(-1).astype(jnp.float32)
        return jnp.pad(flat, (0, scr_len - flat.shape[0]))

    def unpack(buffer, rows, cols):
        return buffer[: rows * cols].reshape(rows, cols)

    def place(vec, start):
        return jnp.pad(vec, (start, wide - start - vec.shape[0]))

    def add_weight(acc, grad, offset, valid):
        flat = grad.reshape(-1)
        return acc.at[offset : offset + flat.shape[0]].add(jnp.where(valid, flat, 0.0))

    def weights_zero():
        split_at = C_IN * C_MID
        return (
            flat_weights[:split_at].reshape(C_IN, C_MID),
            flat_weights[split_at : split_at + 9 * C_MID * C_MID].reshape(9 * C_MID, C_MID),
        )

    def weights_one():
        split_at = C_MID * C_OUT
        return (
            flat_weights[:split_at].reshape(C_MID, C_OUT),
            flat_weights[split_at : split_at + C_IN * C_OUT].reshape(C_IN, C_OUT),
        )

    def weights_two():
        split_at = C_OUT * C_MID
        return (
            flat_weights[:split_at].reshape(C_OUT, C_MID),
            flat_weights[split_at : split_at + 9 * C_MID * C_MID].reshape(9 * C_MID, C_MID),
        )

    def short_rows(image_block):
        return image_block.reshape(IMG_B, SIDE, SIDE, C_IN)[:, ::2, ::2, :].reshape(rows_out, C_IN)

    def local_stats(values, start):
        return (
            place(jnp.sum(values, axis=0), start),
            place(jnp.sum(values * values, axis=0), start),
        )

    def fwd_a_zero(ops):
        conv_a, conv_b = weights_zero()
        pre_one = matmul(ops[0].reshape(rows_in, C_IN), conv_a)
        sums_local, squares_local = local_stats(pre_one, 0)
        return (pack(pre_one), sums_local, squares_local)

    def fwd_a_one(ops):
        conv_a, conv_b = weights_one()
        pre_both = jnp.concatenate(
            [matmul(ops[1], conv_a), matmul(short_rows(ops[0]), conv_b)], axis=1
        )
        sums_local, squares_local = local_stats(pre_both, 0)
        return (pack(pre_both), sums_local, squares_local)

    def fwd_a_two(ops):
        conv_a, conv_b = weights_two()
        pre_four = matmul(ops[2], conv_a)
        sums_local, squares_local = local_stats(pre_four, 0)
        return (pack(pre_four), sums_local, squares_local)

    def fwd_a_three(ops):
        conv_a = flat_weights[: C_MID * C_OUT].reshape(C_MID, C_OUT)
        pre_six = matmul(ops[1], conv_a)
        sums_local, squares_local = local_stats(pre_six, 0)
        return (pack(pre_six), sums_local, squares_local)

    def fwd_b_zero(args):
        ops, scratch, sum_all, square_all = args
        conv_a, conv_b = weights_zero()
        gain_vec, bias_vec, mask_vec = (ops[3], ops[4], ops[5])
        pre_one = unpack(scratch, rows_in, C_MID)
        center_one, inv_one = stats_of(sum_all, square_all, 0, C_MID, total_in)
        hidden_one = (
            smooth((pre_one - center_one) * inv_one * gain_vec[:C_MID] + bias_vec[:C_MID])
            * mask_vec
        ).astype(jnp.bfloat16)
        pre_two = matmul(patches(hidden_one.reshape(IMG_B, SIDE, SIDE, C_MID), 2), conv_b)
        sums_local, squares_local = local_stats(pre_two, C_MID)
        return (pack(pre_two), sums_local, squares_local)

    def fwd_b_pass(args):
        return (args[1], zero_wide, zero_wide)

    def fwd_b_two(args):
        ops, scratch, sum_all, square_all = args
        conv_a, conv_b = weights_two()
        gain_vec, bias_vec, mask_vec = (ops[3], ops[4], ops[5])
        pre_four = unpack(scratch, rows_out, C_MID)
        center_four, inv_four = stats_of(sum_all, square_all, 0, C_MID, total_out)
        hidden_four = (
            smooth((pre_four - center_four) * inv_four * gain_vec[:C_MID] + bias_vec[:C_MID])
            * mask_vec
        ).astype(jnp.bfloat16)
        pre_five = matmul(patches(hidden_four.reshape(IMG_B, OSIDE, OSIDE, C_MID), 1), conv_b)
        sums_local, squares_local = local_stats(pre_five, C_MID)
        return (pack(pre_five), sums_local, squares_local)

    def fwd_c_double(args, first_total, send_res):
        ops, scratch, sum_all, square_all = args
        gain_vec, bias_vec, mask_vec = (ops[3], ops[4], ops[5])
        pre_two = unpack(scratch, rows_out, C_MID)
        center_one, inv_one = stats_of(sum_all, square_all, 0, C_MID, first_total)
        center_two, inv_two = stats_of(sum_all, square_all, C_MID, C_MID, total_out)
        hidden_two = (
            smooth(
                (pre_two - center_two) * inv_two * gain_vec[C_MID : 2 * C_MID]
                + bias_vec[C_MID : 2 * C_MID]
            )
            * mask_vec
        ).astype(jnp.bfloat16)
        centers = jnp.concatenate([center_one, center_two, pad_mid])
        scales = jnp.concatenate([inv_one, inv_two, pad_mid])
        return (hidden_two, send_res, centers, scales, zero_rows)

    def fwd_c_zero(args):
        return fwd_c_double(args, total_in, zero_res)

    def fwd_c_two(args):
        return fwd_c_double(args, total_out, args[0][2])

    def fwd_c_one(args):
        ops, scratch, sum_all, square_all = args
        gain_vec, bias_vec = (ops[3], ops[4])
        pre_both = unpack(scratch, rows_out, wide)
        centers, scales = stats_of(sum_all, square_all, 0, wide, total_out)
        activ = (pre_both - centers) * scales * gain_vec + bias_vec
        block_out = smooth(activ[:, :C_OUT] + activ[:, C_OUT:]).astype(jnp.bfloat16)
        return (zero_mid, block_out, centers, scales, zero_rows)

    def fwd_c_three(args):
        ops, scratch, sum_all, square_all = args
        gain_vec, bias_vec, gate_val = (ops[3], ops[4], ops[6])
        pre_six = unpack(scratch, rows_out, C_OUT)
        centers, scales = stats_of(sum_all, square_all, 0, wide, total_out)
        residual = ops[2].astype(jnp.float32)
        merged = smooth(
            residual
            + (pre_six - centers[:C_OUT]) * scales[:C_OUT] * gain_vec[:C_OUT]
            + bias_vec[:C_OUT]
        )
        result = gate_val * merged + (1.0 - gate_val) * residual
        return (zero_mid, zero_res, centers, scales, result)

    def bwd_a_double(ops, flat_in, conv_a, conv_b, side_len, stride):
        centers, scales, grad_mid = (ops[3], ops[4], ops[5])
        gain_vec, bias_vec, mask_vec = (ops[8], ops[9], ops[10])
        norm_one = (matmul(flat_in, conv_a) - centers[:C_MID]) * scales[:C_MID]
        hidden_one = (smooth(norm_one * gain_vec[:C_MID] + bias_vec[:C_MID]) * mask_vec).astype(
            jnp.bfloat16
        )
        columns = patches(hidden_one.reshape(IMG_B, side_len, side_len, C_MID), stride)
        norm_two = (matmul(columns, conv_b) - centers[C_MID : 2 * C_MID]) * scales[
            C_MID : 2 * C_MID
        ]
        act_two = norm_two * gain_vec[C_MID : 2 * C_MID] + bias_vec[C_MID : 2 * C_MID]
        slope_two = grad_mid.astype(jnp.float32) * mask_vec * smooth_slope(act_two)
        return (
            pack(slope_two),
            pack(norm_two),
            pack(norm_one),
            place(jnp.sum(slope_two, axis=0), C_MID),
            place(jnp.sum(slope_two * norm_two, axis=0), C_MID),
        )

    def bwd_a_zero(ops):
        conv_a, conv_b = weights_zero()
        return bwd_a_double(ops, ops[0].reshape(rows_in, C_IN), conv_a, conv_b, SIDE, 2)

    def bwd_a_two(ops):
        conv_a, conv_b = weights_two()
        return bwd_a_double(ops, ops[2], conv_a, conv_b, OSIDE, 1)

    def bwd_a_one(ops):
        conv_a, conv_b = weights_one()
        centers, scales, grad_res = (ops[3], ops[4], ops[6])
        gain_vec, bias_vec = (ops[8], ops[9])
        pre_both = jnp.concatenate(
            [matmul(ops[1], conv_a), matmul(short_rows(ops[0]), conv_b)], axis=1
        )
        normed = (pre_both - centers) * scales
        activ = normed * gain_vec + bias_vec
        slope_in = grad_res.astype(jnp.float32) * smooth_slope(activ[:, :C_OUT] + activ[:, C_OUT:])
        both = jnp.concatenate([slope_in, slope_in], axis=1)
        return (
            pack(both),
            pack(normed),
            zero_scr,
            jnp.sum(both, axis=0),
            jnp.sum(both * normed, axis=0),
        )

    def bwd_a_three(ops):
        conv_a = flat_weights[: C_MID * C_OUT].reshape(C_MID, C_OUT)
        centers, scales = (ops[3], ops[4])
        gain_vec, bias_vec, gate_val = (ops[8], ops[9], ops[11])
        normed = (matmul(ops[1], conv_a) - centers[:C_OUT]) * scales[:C_OUT]
        joined = ops[2].astype(jnp.float32) + normed * gain_vec[:C_OUT] + bias_vec[:C_OUT]
        through = ops[7].astype(jnp.float32) * gate_val * smooth_slope(joined)
        return (
            pack(through),
            pack(normed),
            zero_scr,
            place(jnp.sum(through, axis=0), 0),
            place(jnp.sum(through * normed, axis=0), 0),
        )

    def bwd_b_double(args, conv_b, rows_first, side_len, stride, offset):
        ops, first_buf, second_buf, third_buf, sum_bias, sum_gain, acc = args
        scales = ops[4]
        gain_vec, bias_vec, mask_vec, valid = (ops[8], ops[9], ops[10], ops[12])
        slope_two = unpack(first_buf, rows_out, C_MID)
        norm_two = unpack(second_buf, rows_out, C_MID)
        norm_one = unpack(third_buf, rows_first, C_MID)
        grad_two = norm_grad(
            slope_two,
            norm_two,
            gain_vec[C_MID : 2 * C_MID],
            scales[C_MID : 2 * C_MID],
            sum_bias[C_MID : 2 * C_MID],
            sum_gain[C_MID : 2 * C_MID],
            total_out,
        )
        act_one = norm_one * gain_vec[:C_MID] + bias_vec[:C_MID]
        hidden_one = (smooth(act_one) * mask_vec).astype(jnp.bfloat16)
        columns = patches(hidden_one.reshape(IMG_B, side_len, side_len, C_MID), stride)
        acc = add_weight(acc, matmul_left_t(columns, grad_two), offset, valid)
        hid_grad = unpatch(
            matmul_right_t(grad_two, conv_b), IMG_B, side_len, stride, C_MID
        ).reshape(rows_first, C_MID)
        slope_one = hid_grad * mask_vec * smooth_slope(act_one)
        return (
            pack(slope_one),
            second_buf,
            third_buf,
            place(jnp.sum(slope_one, axis=0), 0),
            place(jnp.sum(slope_one * norm_one, axis=0), 0),
            acc,
        )

    def bwd_b_zero(args):
        conv_a, conv_b = weights_zero()
        return bwd_b_double(args, conv_b, rows_in, SIDE, 2, C_IN * C_MID)

    def bwd_b_two(args):
        conv_a, conv_b = weights_two()
        return bwd_b_double(args, conv_b, rows_out, OSIDE, 1, C_OUT * C_MID)

    def bwd_b_pass(args):
        return (args[1], args[2], args[3], zero_wide, zero_wide, args[6])

    def side_none():
        return zero_input

    def bwd_c_zero(args):
        ops, first_buf, second_buf, third_buf, sum_bias, sum_gain, acc = args
        conv_a, conv_b = weights_zero()
        scales, gain_vec, valid = (ops[4], ops[8], ops[12])
        flat_in = ops[0].reshape(rows_in, C_IN)
        slope_one = unpack(first_buf, rows_in, C_MID)
        norm_one = unpack(third_buf, rows_in, C_MID)
        grad_one = norm_grad(
            slope_one,
            norm_one,
            gain_vec[:C_MID],
            scales[:C_MID],
            sum_bias[:C_MID],
            sum_gain[:C_MID],
            total_in,
        )
        acc = add_weight(acc, matmul_left_t(flat_in, grad_one), 0, valid)
        side_out = matmul_right_t(grad_one, conv_a).reshape(IMG_B, PIX_IN, C_IN)
        return (zero_mid, zero_res, acc, side_out)

    def bwd_c_one(args):
        ops, first_buf, second_buf, third_buf, sum_bias, sum_gain, acc = args
        conv_a, conv_b = weights_one()
        scales, gain_vec, valid = (ops[4], ops[8], ops[12])
        short_in = short_rows(ops[0])
        both = unpack(first_buf, rows_out, wide)
        normed = unpack(second_buf, rows_out, wide)
        grad_both = norm_grad(both, normed, gain_vec, scales, sum_bias, sum_gain, total_out)
        acc = add_weight(acc, matmul_left_t(ops[1], grad_both[:, :C_OUT]), 0, valid)
        acc = add_weight(acc, matmul_left_t(short_in, grad_both[:, C_OUT:]), C_MID * C_OUT, valid)
        mid_grad = matmul_right_t(grad_both[:, :C_OUT], conv_a).astype(jnp.bfloat16)
        short_grad = matmul_right_t(grad_both[:, C_OUT:], conv_b).reshape(
            IMG_B, OSIDE, 1, OSIDE, 1, C_IN
        )
        side_out = jnp.pad(short_grad, ((0, 0), (0, 0), (0, 1), (0, 0), (0, 1), (0, 0))).reshape(
            IMG_B, PIX_IN, C_IN
        )
        return (mid_grad, zero_res, acc, side_out)

    def bwd_c_two(args):
        ops, first_buf, second_buf, third_buf, sum_bias, sum_gain, acc = args
        conv_a, conv_b = weights_two()
        scales, grad_res, gain_vec, valid = (ops[4], ops[6], ops[8], ops[12])
        slope_four = unpack(first_buf, rows_out, C_MID)
        norm_four = unpack(third_buf, rows_out, C_MID)
        grad_four = norm_grad(
            slope_four,
            norm_four,
            gain_vec[:C_MID],
            scales[:C_MID],
            sum_bias[:C_MID],
            sum_gain[:C_MID],
            total_out,
        )
        acc = add_weight(acc, matmul_left_t(ops[2], grad_four), 0, valid)
        carried_grad = (grad_res.astype(jnp.float32) + matmul_right_t(grad_four, conv_a)).astype(
            jnp.bfloat16
        )
        return (zero_mid, carried_grad, acc, side_none())

    def bwd_c_three(args):
        ops, first_buf, second_buf, third_buf, sum_bias, sum_gain, acc = args
        conv_a = flat_weights[: C_MID * C_OUT].reshape(C_MID, C_OUT)
        scales, gain_vec, gate_val, valid = (ops[4], ops[8], ops[11], ops[12])
        through = unpack(first_buf, rows_out, C_OUT)
        normed = unpack(second_buf, rows_out, C_OUT)
        res_grad = (through + (1.0 - gate_val) * ops[7].astype(jnp.float32)).astype(jnp.bfloat16)
        grad_six = norm_grad(
            through,
            normed,
            gain_vec[:C_OUT],
            scales[:C_OUT],
            sum_bias[:C_OUT],
            sum_gain[:C_OUT],
            total_out,
        )
        acc = add_weight(acc, matmul_left_t(ops[1], grad_six), 0, valid)
        mid_grad = matmul_right_t(grad_six, conv_a).astype(jnp.bfloat16)
        return (mid_grad, res_grad, acc, side_none())

    def select_params(micro_idx):
        block_id = section_idx // 2
        width_val = width[micro_idx, block_id]
        set_val = bn_set[micro_idx, block_id]
        onehot = (jnp.arange(NSETS) == set_val).astype(jnp.float32)
        gain_vec = jnp.sum(onehot[:, None] * gain_table, axis=0)
        bias_vec = jnp.sum(onehot[:, None] * bias_table, axis=0)
        mask_vec = (jnp.arange(C_MID) < width_val).astype(jnp.float32)
        gate_val = gate[micro_idx].astype(jnp.float32)
        return (gain_vec, bias_vec, mask_vec, gate_val, onehot)

    fwd_first = [fwd_a_zero, fwd_a_one, fwd_a_two, fwd_a_three]
    fwd_second = [fwd_b_zero, fwd_b_pass, fwd_b_two, fwd_b_pass]
    fwd_third = [fwd_c_zero, fwd_c_one, fwd_c_two, fwd_c_three]
    bwd_first = [bwd_a_zero, bwd_a_one, bwd_a_two, bwd_a_three]
    bwd_second = [bwd_b_zero, bwd_b_pass, bwd_b_two, bwd_b_pass]
    bwd_third = [bwd_c_zero, bwd_c_one, bwd_c_two, bwd_c_three]

    def forward_tick(tick_no, state_in):
        recv_mid, recv_res, stash_mid, stash_res, stash_center, stash_scale, out_rows = state_in
        micro_raw = tick_no - section_idx
        is_valid = (micro_raw >= 0) & (micro_raw < MB)
        micro_idx = jnp.clip(micro_raw, 0, MB - 1)
        gain_vec, bias_vec, mask_vec, gate_val, onehot = select_params(micro_idx)
        ops = (image_blocks[micro_idx], recv_mid, recv_res, gain_vec, bias_vec, mask_vec, gate_val)
        scratch, sums_local, squares_local = lax.switch(section_idx, fwd_first, ops)
        sum_first, square_first = group_moments(sums_local, squares_local)
        scratch, sums_local, squares_local = lax.switch(
            section_idx, fwd_second, (ops, scratch, sum_first, square_first)
        )
        sum_second, square_second = group_moments(sums_local, squares_local)
        send_mid, send_res, centers, scales, result = lax.switch(
            section_idx,
            fwd_third,
            (ops, scratch, sum_first + sum_second, square_first + square_second),
        )
        stash_mid = stash_mid.at[micro_idx].set(jnp.where(is_valid, recv_mid, stash_mid[micro_idx]))
        stash_res = stash_res.at[micro_idx].set(jnp.where(is_valid, recv_res, stash_res[micro_idx]))
        stash_center = stash_center.at[micro_idx].set(
            jnp.where(is_valid, centers, stash_center[micro_idx])
        )
        stash_scale = stash_scale.at[micro_idx].set(
            jnp.where(is_valid, scales, stash_scale[micro_idx])
        )
        out_rows = out_rows.at[micro_idx].set(jnp.where(is_valid, result, out_rows[micro_idx]))
        recv_mid, recv_res = (
            shifted(for_sending(send_mid), "pipe", 1).astype(send_mid.dtype),
            shifted(for_sending(send_res), "pipe", 1).astype(send_res.dtype),
        )
        return (recv_mid, recv_res, stash_mid, stash_res, stash_center, stash_scale, out_rows)

    forward_init = (
        zero_mid,
        zero_res,
        jnp.zeros((MB, rows_out, C_MID), jnp.bfloat16),
        jnp.zeros((MB, rows_out, C_OUT), jnp.bfloat16),
        jnp.zeros((MB, wide), jnp.float32),
        jnp.zeros((MB, wide), jnp.float32),
        jnp.zeros((MB, rows_out, C_OUT), jnp.float32),
    )
    forward_state = lax.fori_loop(0, MB + pipe_count - 1, forward_tick, forward_init)
    unused_mid, unused_res, stash_mid, stash_res, stash_center, stash_scale, out_rows = (
        forward_state
    )

    def backward_tick(tick_no, state_in):
        grad_mid, grad_res, weight_acc, gain_acc, bias_acc, input_acc = state_in
        micro_raw = tick_no - (pipe_count - 1 - section_idx)
        is_valid = (micro_raw >= 0) & (micro_raw < MB)
        micro_idx = jnp.clip(micro_raw, 0, MB - 1)
        gain_vec, bias_vec, mask_vec, gate_val, onehot = select_params(micro_idx)
        ops = (
            image_blocks[micro_idx],
            stash_mid[micro_idx],
            stash_res[micro_idx],
            stash_center[micro_idx],
            stash_scale[micro_idx],
            grad_mid,
            grad_res,
            cotangent[micro_idx],
            gain_vec,
            bias_vec,
            mask_vec,
            gate_val,
            is_valid,
        )
        first_buf, second_buf, third_buf, bias_one, gain_one = lax.switch(
            section_idx, bwd_first, ops
        )
        sum_bias_one, sum_gain_one = group_grad_sums(bias_one, gain_one)
        first_buf, second_buf, third_buf, bias_two, gain_two, weight_acc = lax.switch(
            section_idx,
            bwd_second,
            (ops, first_buf, second_buf, third_buf, sum_bias_one, sum_gain_one, weight_acc),
        )
        sum_bias_two, sum_gain_two = group_grad_sums(bias_two, gain_two)
        send_mid, send_res, weight_acc, side_out = lax.switch(
            section_idx,
            bwd_third,
            (
                ops,
                first_buf,
                second_buf,
                third_buf,
                sum_bias_one + sum_bias_two,
                sum_gain_one + sum_gain_two,
                weight_acc,
            ),
        )
        gain_grad = gain_one + gain_two
        bias_grad = bias_one + bias_two
        gain_acc = jnp.where(is_valid, gain_acc + onehot[:, None] * gain_grad[None, :], gain_acc)
        bias_acc = jnp.where(is_valid, bias_acc + onehot[:, None] * bias_grad[None, :], bias_acc)
        input_acc = jax.tree.map(
            lambda stored, fresh: stored.at[micro_idx].set(
                jnp.where(is_valid, fresh, stored[micro_idx])
            ),
            input_acc,
            side_out,
        )
        grad_mid, grad_res = (
            shifted(for_sending(send_mid), "pipe", -1).astype(send_mid.dtype),
            shifted(for_sending(send_res), "pipe", -1).astype(send_res.dtype),
        )
        return (grad_mid, grad_res, weight_acc, gain_acc, bias_acc, input_acc)

    side_init = jnp.zeros((MB, IMG_B, PIX_IN, C_IN), jnp.float32)
    backward_init = (
        zero_mid,
        zero_res,
        jnp.zeros((P_SIZE,), jnp.float32),
        jnp.zeros((NSETS, wide), jnp.float32),
        jnp.zeros((NSETS, wide), jnp.float32),
        side_init,
    )
    backward_state = lax.fori_loop(0, MB + pipe_count - 1, backward_tick, backward_init)
    unused_gmid, unused_gres, weight_acc, gain_acc, bias_acc, input_acc = backward_state
    grad_images, output_sum = (
        lax.psum_scatter(
            input_acc.reshape(IMG_DEV, PIX_IN, C_IN).astype(jnp.bfloat16),
            "pipe",
            scatter_dimension=2,
            tiled=True,
        ).astype(jnp.float32),
        lax.psum_scatter(
            out_rows.astype(jnp.bfloat16), "pipe", scatter_dimension=2, tiled=True
        ).astype(jnp.float32),
    )
    output_part = output_sum.astype(jnp.bfloat16)
    norm_grads = jnp.concatenate([gain_acc.reshape(-1), bias_acc.reshape(-1)])
    weight_sum, norm_sum = lax.psum((weight_acc, norm_grads), ("dp", "rep"))
    grad_gain = norm_sum[: NSETS * wide].reshape(1, NSETS, wide)
    grad_bias = norm_sum[NSETS * wide :].reshape(1, NSETS, wide)
    return (output_part, grad_images, weight_sum.reshape(1, P_SIZE), grad_gain, grad_bias)


PP = PIX_OUT + 1
RW = 8 * PP
RV = 8 * PIX_OUT
BLK = 512
SUB = 65536
F32 = jnp.float32
BF16 = jnp.bfloat16
MESH = pl.DeviceIdType.MESH

E_WIDE, E_WIDE_NEXT = 2, 6
C_H2, C_H4, C_D5, C_D4, C_DH = range(10, 15)
C_O1, C_SHARE, C_GI, C_GP = 15, 19, 22, 25
C_PAR2, C_PAR3, C_DG2, C_DG3, C_BN1, C_BN2, C_BN3, C_BN4 = range(28, 36)
N_SEM = 36
N_PIECE = 17
W_OWN, W_PEER, W_Z, W_ON, W_VIA = range(5)
VIA, HALF = 8, 11
W_BASE = (0, 17, 34, 45, -VIA)
S_CORE, S_IN, S_OUT, S_HAND, S_BACK, S_DONE, S_ACROSS, N_SUM_SEND = 0, 1, 2, 3, 4, 5, 9, 25
R_CORE, R_Z, R_ACROSS, R_GIVE = (0, 8), (8, 24), (32, 16), (48, 4)
R_DONE, R_BACK, R_BACK_HUB, R_HAND, N_SUM_RECV = 52, 53, 54, 55, 75
HUB_GUEST = 8704
RING = 8
SUBS = 2
SUB_ROWS = 256 // SUBS
HOPS = 2
HOP_ROWS = SUB_ROWS // HOPS
Z1_ZERO = 3136
ACROSS_LAG, OUT_LAG = 3 * SUBS // 2 + 1, 4 * SUBS
LAST_TURN = OUT_LAG - 2


def nn(a, b):
    return jnp.dot(a, b, preferred_element_type=F32)


def nt(a, b):
    return lax.dot_general(a, b, (((1,), (1,)), ((), ())), preferred_element_type=F32)


def tn(a, b):
    return lax.dot_general(a, b, (((0,), (0,)), ((), ())), preferred_element_type=F32)


def sigmoid(v):
    return 0.5 + 0.5 * jnp.tanh(0.5 * v)


def rows(start, size):
    return pl.ds(start if isinstance(start, int) else pl.multiple_of(start, 16), size)


def whole_kernel(
    img, wts, gain_in, bias_in, width, sets, gates, cot,
    out, gi, dw, dgb_out,
    imgb, raw, st, wh, wx, f0, f1, f2, f3, fs, pb, pt, u0, u1, u2, sx, cotb,
    h2, h4, h5, d5, d4, dh, r0, r1, ob, tx, rx, inv, par, parx, dg, dgx, sb, rd, bz, dgs, dgb, v_out, gain, bias,
    ls, ss, rs, wss, ass, ars, ready, go,
):
    p, d, r = lax.axis_index("pipe"), lax.axis_index("dp"), lax.axis_index("rep")
    peer = (p, 1 - d, r)
    z_pair = r + 1 - 2 * lax.rem(r, 2)
    quarter = 2 * lax.rem(r, 2) + d

    def remote(src, dst, send, recv, device):
        return pltpu.make_async_remote_copy(
            src_ref=src, dst_ref=dst, send_sem=ss.at[send], recv_sem=rs.at[recv],
            device_id=device, device_id_type=MESH,
        )

    def sync(event, first, count):
        part = pl.ds(first, count)
        copy = remote(tx.at[part], rx.at[part], event, event, peer)
        copy.start()
        copy.wait()

    def exchange_of(event, first, count):
        part = pl.ds(first, count)
        return remote(tx.at[part], rx.at[part], event, event, peer)

    def both(slot):
        return tx[slot] + rx[slot]

    def moments(slot_sum, slot_square, total, inv_slot):
        center = both(slot_sum) * (1.0 / total)
        scale = lax.rsqrt(both(slot_square) * (1.0 / total) - center * center + EPSILON)
        inv[inv_slot] = scale
        return center, scale

    def silu(v):
        return v * sigmoid(v)

    def slope(v):
        s = sigmoid(v)
        return s + v * s * (1.0 - s)

    def clear_pad(ref, first):
        tile = ref[rows(first + RW - 16, 16), :].astype(F32)
        keep = lax.broadcasted_iota(jnp.int32, tile.shape, 0) < 8
        ref[rows(first + RW - 16, 16), :] = jnp.where(keep, tile, 0.0).astype(BF16)

    def per_row(value_of):
        row = lax.broadcasted_iota(jnp.int32, (8, BLK), 0)
        out = jnp.zeros((8, BLK), jnp.int32)
        for m in range(MB):
            out = jnp.where(row == m, value_of(m), out)
        return out

    def mask_of(block):
        lane = lax.broadcasted_iota(jnp.int32, (8, BLK), 1)
        return (lane < per_row(lambda m: width[block, m])).astype(F32)

    def five(body, init=0, unrolled=False):
        if unrolled:
            for c in range(5):
                init = body(pl.ds(c * 10, 10), c, init)
            return init
        return lax.fori_loop(0, 5, lambda c, carry: body(pl.ds(c * 10, 10), c, carry), init)

    def add_stats(carry, a, b):
        return carry[0] + jnp.sum(a, axis=0), carry[1] + jnp.sum(b, axis=0)

    zero_stats = (jnp.zeros((8, BLK), F32), jnp.zeros((8, BLK), F32))

    def store_z(ref, first, z, slot_sum, slot_square):
        z3 = z.reshape(PP, 8, BLK) if z.ndim == 2 else z
        ref[pl.ds(first, PP)] = z3
        tx[slot_sum] = jnp.sum(z3, axis=0)
        tx[slot_square] = jnp.sum(z3 * z3, axis=0)

    def raw_copy(turn, element_of):
        slot = lax.rem(turn, RING)
        return pltpu.make_async_copy(
            wts.at[:, pl.ds(pl.multiple_of(element_of(turn) * SUB, SUB), SUB)], raw.at[slot], ls.at[8 + slot]
        )

    def open_weights(element_of, total):
        for turn in range(min(RING - 1, total)):
            raw_copy(turn, element_of).start()

    def load_weights(element_of, total, first, count, put):
        def body(k, carry):
            turn = first + k

            @pl.when(turn + RING - 1 < total)
            def _():
                raw_copy(turn + RING - 1, element_of).start()

            raw_copy(turn, element_of).wait()
            st[0:512] = raw[lax.rem(turn, RING)].astype(F32).reshape(512, 128)
            put(turn)
            return carry

        lax.fori_loop(0, count, body, 0)

    def put_narrow(ref, row_of):
        def put(i):
            for j in range(4):
                ref[rows(row_of(i), 128), j * 128 : (j + 1) * 128] = st[
                    pl.ds(j, 128, stride=4), :
                ].astype(BF16)

        return put

    def put_wide(ref, base, block_rows, first):
        def put(i):
            for n in range(4):
                for j in range(4):
                    ref[rows(base + n * block_rows + (i - first) * 32, 32), j * 128 : (j + 1) * 128] = st[
                        pl.ds(4 * n + j, 32, stride=16), :
                    ].astype(BF16)

        return put

    def put_chunk(row, n, block):
        size = SUB_ROWS // 4
        for part in range(2 * SUBS):
            wh[rows(row + part * SUB_ROWS + n * size, size), :] = block[part * size : (part + 1) * size].astype(BF16)

    def plain(turn):
        return turn

    def own_parts(turn):
        late = turn - HALF
        return jnp.where(late < 0, 4 * turn + quarter, 4 * HALF + (late // 2) * 4 + 2 * d + lax.rem(late, 2))

    def half_rows(turn):
        return 8 * d + turn

    def piece_copy(kind, i, q, device):
        part = wx.at[rows(i * 512 + q * 128, 128)]
        return pltpu.make_async_remote_copy(
            src_ref=part, dst_ref=part, send_sem=wss.at[kind], recv_sem=ars.at[W_BASE[kind] + i],
            device_id=device, device_id_type=MESH,
        )

    def half_copy(kind, i, which, device):
        part = wx.at[rows(i * 512 + which * 256, 256)]
        order = min(i, 13) if kind == W_VIA else i
        return pltpu.make_async_remote_copy(
            src_ref=part, dst_ref=part, send_sem=wss.at[kind], recv_sem=ars.at[W_BASE[kind] + order],
            device_id=device, device_id_type=MESH,
        )

    def all_sent(semaphore, ref):
        pltpu.make_async_remote_copy(
            src_ref=ref, dst_ref=ref, send_sem=semaphore, recv_sem=rs.at[0], device_id=peer, device_id_type=MESH
        ).wait_send()

    def all_here(semaphore, ref):
        pltpu.make_async_remote_copy(
            src_ref=ref, dst_ref=ref, send_sem=ss.at[0], recv_sem=semaphore, device_id=peer, device_id_type=MESH
        ).wait_recv()

    def o1_copy(n, chip):
        part = u0.at[n * RW : (n + 1) * RW]
        return remote(part, part, C_O1 + n, C_O1 + n, (chip, d, r))

    def each(work, first, last):
        def body(i, carry):
            work(i)
            return carry

        lax.fori_loop(first, last, body, 0)

    def img_copy(q, slot):
        return pltpu.make_async_copy(img.at[pl.ds(q * 28, 28)], imgb.at[slot], ls.at[slot])

    def open_images():
        for q in range(3):
            img_copy(q, q).start()

    def over_images(body, init):
        def step(q, carry):
            slot = lax.rem(q, 4)

            @pl.when(q + 3 < 7)
            def _():
                img_copy(q + 3, lax.rem(q + 3, 4)).start()

            img_copy(q, slot).wait()
            return body(q, slot, carry)

        return lax.fori_loop(0, 7, step, init)

    outer = (r == 0) | (r == 3)
    inner = jnp.logical_not(outer)
    z_dev, across = (p, d, z_pair), (p, d, 3 - r)

    def grad_copy(send, recv, src, dst, device):
        return pltpu.make_async_remote_copy(
            src_ref=src, dst_ref=dst, send_sem=ass.at[send], recv_sem=ars.at[recv],
            device_id=device, device_id_type=MESH,
        )

    def in_turn(ring, u):
        return ring[0] + lax.rem(u, ring[1])

    def zero_rest(first, source):
        source[...] = jnp.zeros(source.shape, BF16)

        def body(i, carry):
            copy = pltpu.make_async_copy(source, dw.at[pl.ds((first + i) * 4, 4)], ls.at[18])
            copy.start()
            copy.wait()
            return carry

        lax.fori_loop(0, 13 - first, body, 0)

    def bn_sums():
        for k in range(NSETS):
            hot = (set_of == k).astype(F32)
            for n in range(8):
                cols = slice(n * BLK, (n + 1) * BLK)
                dgs[k : k + 1, cols] = jnp.sum(dg[n] * hot, axis=0, keepdims=True)
                dgs[4 + k : 5 + k, cols] = jnp.sum(dg[8 + n] * hot, axis=0, keepdims=True)

    def norm_half(channels):
        return pl.ds(pl.multiple_of(d * (channels // 2), 512), channels // 2)

    def bn_in(cols):
        return remote(dgs.at[:, cols], bz.at[0, :, cols], C_BN1, C_BN1, z_dev)

    def bn_across(cols):
        return remote(dgs.at[:, cols], bz.at[1, :, cols], C_BN2, C_BN2, across)

    def bn_out(cols):
        return remote(dgb.at[:, cols], bz.at[0, :, cols], C_BN3, C_BN3, z_dev)

    def bn_core(cols):
        return remote(dgb.at[:, cols], dgb.at[:, cols], C_BN4, C_BN4, peer)

    def say_ready():
        pl.semaphore_signal(ready.at[0], inc=1, device_id=z_dev, device_id_type=MESH)

        @pl.when(inner)
        def _():
            pl.semaphore_signal(ready.at[1], inc=1, device_id=across, device_id_type=MESH)

    def sum_gradients(
        count, compute, at_row, chunk_of, wide, z1, extra,
        lend=(), passed=(), helper=None, helper_turn=None, helper_row=None, handed_in=None, lent_by=None, computed=None, packed_here=None,
        norms_at=0, norms=4096, after=None, back=R_BACK, late_back=0,
    ):
        turns = SUBS * count
        last_lent = SUBS * (count + len(lend))
        last_given = last_lent + SUBS * len(passed)
        computed = (0, count) if computed is None else computed
        packed_here = (0, count) if packed_here is None else packed_here
        cols = norm_half(norms)
        first_own, own_turns = packed_here[0] * SUBS, packed_here[1] * SUBS
        z2 = z1 + last_given * SUB_ROWS

        def when_own(u, work):
            if handed_in is None:
                work()
            else:
                pl.when(jnp.logical_not(handed_in(u // SUBS)))(work)

        def when_handed(u, work):
            if handed_in is not None:
                pl.when(handed_in(u // SUBS))(work)

        def when_kept(u, work):
            if lent_by is None:
                work()
            else:
                pl.when(jnp.logical_not(lent_by[0](u // SUBS)))(work)

        def when_lent(u, work):
            if lent_by is not None:
                pl.when(lent_by[0](u // SUBS))(work)

        def half(u, which):
            return wh.at[rows(at_row(u // SUBS) + which * 256 + lax.rem(u, SUBS) * SUB_ROWS, SUB_ROWS)]

        def half_part(u, k):
            first = at_row(u // SUBS) + d * 256 + lax.rem(u, SUBS) * SUB_ROWS + k * HOP_ROWS
            return wh.at[rows(first, HOP_ROWS)]

        def from_z(u):
            return wx.at[rows(z1 + u * SUB_ROWS, SUB_ROWS)]

        def from_z_part(u, k):
            return wx.at[rows(z1 + u * SUB_ROWS + k * HOP_ROWS, HOP_ROWS)]

        def from_across(u, k):
            return wx.at[rows(z2 + u * SUB_ROWS + k * HOP_ROWS, HOP_ROWS)]

        def from_core(u):
            return rd.at[rows(u * SUB_ROWS, SUB_ROWS)]

        def to_core(u):
            recv = jnp.where(u < turns, in_turn(R_CORE, u), in_turn(R_GIVE, u))
            return grad_copy(S_CORE, recv, half(u, 1 - d), from_core(u), peer)

        def inwards(u, k):
            return grad_copy(S_IN, in_turn(R_Z, u * HOPS + k), half_part(u, k), from_z_part(u, k), z_dev)

        def exchange(u, k):
            turn = u * HOPS + k
            return grad_copy(
                S_ACROSS + lax.rem(turn, 16), in_turn(R_ACROSS, turn), half_part(u, k), from_across(u, k), across
            )

        def outwards(u, k):
            return grad_copy(S_OUT, in_turn(R_Z, u * HOPS + k), half_part(u, k), from_z_part(u, k), z_dev)

        def packed(u, which):
            return dw.at[chunk_of(u // SUBS) * 4 + which * 2 + lax.rem(u, SUBS)]

        def done_core(u, turn):
            slot = lax.rem(turn, 4)
            return grad_copy(S_DONE + slot, R_DONE, sb.at[slot], packed(u, d), peer)

        def done_here(u, turn):
            slot = lax.rem(turn, 4)
            return pltpu.make_async_copy(sb.at[slot], packed(u, d), ls.at[4 + slot])

        def add(mine, other):
            sums = mine[...].astype(F32) + other[...].astype(F32)
            mine[...] = sums.astype(BF16)

        def pack(u, turn, ref):
            @pl.when(turn >= 4)
            def _():
                done_here(u, turn).wait()
                done_core(u, turn).wait_send()

            value = ref[...].astype(F32)
            for j in range(4):
                cols = slice(j * 128, (j + 1) * 128)
                if wide:
                    for n in range(4):
                        part = SUB_ROWS // 4
                        st[pl.ds(4 * n + j, part, stride=16), :] = value[n * part : (n + 1) * part, cols]
                else:
                    st[pl.ds(j, SUB_ROWS, stride=4), :] = value[:, cols]
            sb[lax.rem(turn, 4)] = st[...].astype(BF16)
            done_here(u, turn).start()
            done_core(u, turn).start()

        def hand(u):
            t, part = u // SUBS, lax.rem(u, SUBS)
            theirs = helper_turn(t) * SUBS + part
            row = helper_turn(t) * 512 if helper_row is None else helper_row(t)
            place = wh.at[rows(row + d * 256 + part * SUB_ROWS, SUB_ROWS)]
            return grad_copy(S_HAND, R_HAND + theirs, half(u, d), place, (helper(t), d, r))

        def handed(u):
            return grad_copy(S_HAND, R_HAND + u, half(u, d), half(u, d), (p, d, r))

        def give_back(u, ref):
            t = u // SUBS
            theirs = lent_by[2](t) * SUBS + lax.rem(u, SUBS)
            place = wx.at[rows(jnp.where(lent_by[1](t) == 0, Z1_ZERO, 0) + theirs * SUB_ROWS, SUB_ROWS)]
            return grad_copy(S_BACK, back, ref, place, (lent_by[1](t), d, r))

        def finish(u, ref):
            when_kept(u, lambda: pack(u, u - first_own, ref))
            when_lent(u, lambda: give_back(u, ref).start())

        def give(t):
            compute(t)
            for k in range(SUBS):
                to_core(t * SUBS + k).start()
            for k in range(SUBS):
                u = t * SUBS + k
                to_core(u).wait_recv()
                add(half(u, d), from_core(u))
                hand(u).start()

        def unit_rows(units):
            return wh.at[0 : units * SUB_ROWS]

        take_at = turns + OUT_LAG - (last_lent - turns)

        def step(it, carry):
            for when, work in extra.items():
                pl.when(it == when)(work)
            for k, when in enumerate(lend + passed):
                pl.when(it == when)(lambda k=k: give(jnp.int32(count + k)))

            def start():
                @pl.when(lax.rem(it, SUBS) == 0)
                def _():
                    compute(it // SUBS)

                to_core(it).start()

            @pl.when(it < turns)
            def _():
                when_own(it, start)

            u1 = it - 1

            @pl.when((u1 >= 0) & (u1 < turns))
            def _():
                def join_cores():
                    to_core(u1).wait_recv()
                    add(half(u1, d), from_core(u1))

                when_own(u1, join_cores)
                when_handed(u1, lambda: handed(u1).wait_recv())

                @pl.when(outer & (u1 == 0))
                def _():
                    pl.semaphore_wait(ready.at[0], 1)

                @pl.when(outer)
                def _():
                    for k in range(HOPS):
                        inwards(u1, k).start()

            u2 = it - 2

            @pl.when(inner & (u2 >= 0) & (u2 < turns))
            def _():
                @pl.when(u2 == 0)
                def _():
                    pl.semaphore_wait(ready.at[1], 1)

                for k in range(HOPS):
                    inwards(u2, k).wait_recv()
                    add(half_part(u2, k), from_z_part(u2, k))
                    exchange(u2, k).start()

            u4 = it - ACROSS_LAG

            @pl.when(inner & (u4 >= 0) & (u4 < turns))
            def _():
                @pl.when(u4 == 0)
                def _():
                    pl.semaphore_wait(ready.at[0], 1)

                for k in range(HOPS):
                    exchange(u4, k).wait()
                    add(half_part(u4, k), from_across(u4, k))
                    outwards(u4, k).start()

                finish(u4, half(u4, d))

            u8 = it - OUT_LAG

            @pl.when(outer & (u8 >= 0) & (u8 < turns))
            def _():
                for k in range(HOPS):
                    outwards(u8, k).wait_recv()

                finish(u8, from_z(u8))

            @pl.when(it == norms_at)
            def _():
                bn_sums()

                @pl.when(outer)
                def _():
                    bn_in(cols).start()

            @pl.when(inner & (it == norms_at + 4))
            def _():
                bn_in(cols).wait_recv()
                dgs[:, cols] += bz[0, :, cols]
                bn_across(cols).start()

            @pl.when(inner & (it == norms_at + 8))
            def _():
                bn_across(cols).wait()
                dgb[:, cols] = dgs[:, cols] + bz[1, :, cols]
                bn_out(cols).start()
                bn_core(cols).start()

            @pl.when(outer & (it == norms_at + 14))
            def _():
                bn_out(cols).wait_recv()
                dgb[:, cols] = bz[0, :, cols]
                bn_core(cols).start()

            for when, work in (after or {}).items():
                pl.when(it == when)(work)

            if lend:
                u_back = turns + it - take_at

                late_units = late_back * SUBS

                @pl.when(it == take_at)
                def _():
                    all_here(ars.at[R_BACK], unit_rows(last_lent - turns - late_units))

                if late_units:

                    @pl.when(u_back == last_lent - late_units)
                    def _():
                        all_here(ars.at[R_BACK_HUB], unit_rows(late_units))

                @pl.when((u_back >= turns) & (u_back < last_lent))
                def _():
                    pack(u_back, own_turns + u_back - turns, from_z(u_back))

            return carry

        lax.fori_loop(0, turns + OUT_LAG, step, 0)

        bn_core(cols).wait()

        @pl.when(outer)
        def _():
            bn_in(cols).wait_send()

        @pl.when(inner)
        def _():
            bn_out(cols).wait_send()

        @pl.when(outer)
        def _():
            all_sent(ass.at[S_IN], unit_rows(turns))

        @pl.when(inner)
        def _():
            all_sent(ass.at[S_OUT], unit_rows(turns))

        made = computed[1] * SUBS + last_given - turns
        if made:
            all_sent(ass.at[S_CORE], unit_rows(made))
        if last_given > turns:
            all_sent(ass.at[S_HAND], unit_rows(last_given - turns))
        if lent_by is not None:
            all_sent(ass.at[S_BACK], unit_rows(lent_by[3] * SUBS))
        all_here(ars.at[R_DONE], dw.at[pl.ds(0, own_turns + last_lent - turns)])
        for slot in range(4):
            done_here(first_own, jnp.int32(slot)).wait()
            done_core(first_own, jnp.int32(slot)).wait_send()

    tables = [
        pltpu.make_async_copy(gain_in, gain, ls.at[17]),
        pltpu.make_async_copy(bias_in, bias, ls.at[18]),
    ]
    for copy in tables:
        copy.start()

    @pl.when(p == 0)
    def _():
        open_weights(plain, 44)
        open_images()

    @pl.when(p == 1)
    def _():
        open_weights(plain, 48)
        open_images()
        pltpu.make_async_copy(cot, cotb.at[0:PIX_OUT], ls.at[16]).start()

    @pl.when(p == 2)
    def _():
        open_weights(own_parts, 15)

    @pl.when(p == 3)
    def _():
        open_weights(half_rows, 8)

    barrier = pltpu.get_barrier_semaphore()
    for device in (peer, (p, d, z_pair), (p, d, 3 - r)) + tuple((lax.rem(p + k, 4), d, r) for k in (1, 2, 3)):
        pl.semaphore_signal(barrier, inc=1, device_id=device, device_id_type=MESH)

    for copy in tables:
        copy.wait()
    block_two = p >= 2
    set_of = per_row(lambda m: jnp.where(block_two, sets[1, m], sets[0, m]))
    for k in range(NSETS):
        hot = (set_of == k).astype(F32)
        for n in range(8):
            g = hot * gain[k : k + 1, n * BLK : (n + 1) * BLK]
            b = hot * bias[k : k + 1, n * BLK : (n + 1) * BLK]
            if k == 0:
                par[n] = g
                par[8 + n] = b
            else:
                par[n] += g
                par[8 + n] += b
    dg[...] = jnp.zeros_like(dg)
    dgb[...] = jnp.zeros_like(dgb)
    pl.semaphore_wait(barrier, 6)

    total_in, total_out = 2.0 * PIX_IN, 2.0 * PIX_OUT

    def build_patches(base):
        def body(tap, carry):
            row, col = base(tap)
            window = pb[pl.ds(row, 7), pl.ds(col, 7)].reshape(RV, BLK)
            pt[tap, 0:RV, :] = window.astype(BF16)
            return carry

        lax.fori_loop(0, 9, body, 0)

    def clear_patch_pad():
        def body(tap, carry):
            pt[tap, RW - 16 : RW, :] = jnp.zeros((16, BLK), BF16)
            return carry

        lax.fori_loop(0, 9, body, 0)

    def strided_base(tap):
        di, dj = tap // 3, lax.rem(tap, 3)
        return lax.rem(di, 2) * 8 + di // 2, lax.rem(dj, 2) * 8 + dj // 2

    def plain_base(tap):
        return tap // 3, lax.rem(tap, 3)

    def conv(ref, first, target):
        target[...] = jnp.zeros_like(target)

        def body(tap, carry):
            z = nn(pt[tap], ref[rows(first + tap * BLK, BLK), :])
            target[...] += z.reshape(PP, 8, BLK)
            return carry

        lax.fori_loop(0, 9, body, 0)

    def conv_back(dz, ref, first, base, side):
        pb[0:side, 0:side] = jnp.zeros((side, side, 8, BLK), F32)

        def body(tap, carry):
            row, col = base(tap)
            part = nt(dz[0:RV, :], ref[rows(first + tap * BLK, BLK), :])
            pb[pl.ds(row, 7), pl.ds(col, 7)] += part.reshape(7, 7, 8, BLK)
            return carry

        lax.fori_loop(0, 9, body, 0)

    def stats_of_map(ref, slot_sum, slot_square):
        def body(c, _, carry):
            z = ref[c]
            return add_stats(carry, z, z * z)

        tx[slot_sum], tx[slot_square] = five(body, zero_stats)

    def act_to(ref, target, center, scale, g, b, mask):
        def body(c, i, carry):
            zhat = (ref[c] - center) * scale
            ref[c] = zhat
            h = silu(zhat * g + b) * mask
            target[rows(i * 80, 80), :] = h.reshape(80, BLK).astype(BF16)
            return carry

        five(body)
        clear_pad(target, 0)

    def upstream(target, grad, zhat_ref, g, b, mask, slot_sum, slot_gain):
        def body(c, i, carry):
            zhat = zhat_ref[c]
            du = grad[rows(i * 80, 80), :].astype(F32).reshape(10, 8, BLK) * mask * slope(zhat * g + b)
            target[c] = du
            return add_stats(carry, du, du * zhat)

        tx[slot_sum], tx[slot_gain] = five(body, zero_stats)

    def norm_back(target, first, du_ref, du_first, zhat_ref, zhat_first, gscale, mean_du, mean_dg, unrolled=False):
        def body(c, i, carry):
            du = du_ref[pl.ds(du_first + i * 10, 10)]
            zhat = zhat_ref[pl.ds(zhat_first + i * 10, 10)]
            dz = gscale * (du - mean_du - zhat * mean_dg)
            target[rows(first + i * 80, 80), :] = dz.reshape(80, BLK).astype(BF16)
            return carry

        five(body, unrolled=unrolled)
        clear_pad(target, first)

    def gi_copy():
        return pltpu.make_async_copy(f3.at[0:PIX_IN, :, 0:256], gi, ls.at[17])

    def out_copy():
        return pltpu.make_async_copy(v_out, out, ls.at[0])

    def dgb_copy():
        return pltpu.make_async_copy(dgb, dgb_out, ls.at[1])

    def final_part():
        @pl.when(p != 1)
        def _():
            remote(ob, ob, C_SHARE, C_SHARE, (p, d, r)).wait_recv()
            remote(r1, r1, C_GP, C_GP, (p, d, r)).wait_recv()

        @pl.when(p != 0)
        def _():
            remote(r0, r0, C_GI, C_GI, (p, d, r)).wait_recv()

        v_out[...] = ob[0:RV, :].astype(F32).reshape(PIX_OUT, 8, BLK).astype(BF16)
        out_copy().start()
        f0[0:PP, :, 0:256] = r1[...].astype(F32).reshape(PP, 8, 256)

        def place(a, carry):
            m = r0[rows(a * 224, 224), :].astype(F32).reshape(28, 8, 256)
            first = m[0:14].reshape(7, 2, 8, 256)
            even = first[:, 0] + f0[pl.ds(a * 7, 7), :, 0:256]
            f3[pl.ds(a * 28, 14), :, 0:256] = jnp.stack([even, first[:, 1]], axis=1).reshape(14, 8, 256)
            f3[pl.ds(a * 28 + 14, 14), :, 0:256] = m[14:28]
            return carry

        lax.fori_loop(0, 7, place, 0)
        gi_copy().start()

    @pl.when(p == 0)
    def _():
        mask = mask_of(0)

        def relay(i):
            piece_copy(W_VIA, i, quarter, (0, d, r)).wait_recv()
            piece_copy(W_OWN, i, quarter, (1, d, r)).start()

        def relay_half(i):
            half_copy(W_VIA, i, d, (0, d, r)).wait_recv()
            half_copy(W_OWN, i, d, (1, d, r)).start()

        put_w = put_narrow(wh, lambda i: i * 128)
        load_weights(plain, 44, 0, 8, put_w)

        def first_conv(q, slot, carry):
            rows_q = imgb[slot].astype(F32).reshape(224, 1024).astype(BF16)
            wx[rows(q * 224, 224), :] = rows_q[:, 0:512]
            wx[rows(1568 + q * 224, 224), :] = rows_q[:, 512:1024]
            z = nn(rows_q, wh[0:1024, :]).reshape(28, 8, BLK)
            f0[pl.ds(q * 28, 28)] = z
            load_weights(plain, 44, 8 + 5 * q, 5, put_w)
            return add_stats(carry, z, z * z)

        tx[0], tx[1] = over_images(first_conv, zero_stats)
        relay(VIA)
        exchange = remote(tx.at[pl.ds(0, 2)], rx.at[pl.ds(0, 2)], 0, 0, peer)
        exchange.start()
        pb[...] = jnp.zeros_like(pb)
        clear_patch_pad()
        load_weights(plain, 44, 43, 1, put_w)
        exchange.wait()

        center, scale = moments(0, 1, total_in, 0)
        g1, b1, g2, b2 = par[0], par[8], par[1], par[9]

        def hidden(i, carry):
            zhat = (f0[pl.ds(i * 14, 14)] - center) * scale
            f0[pl.ds(i * 14, 14)] = zhat
            h = (silu(zhat * g1 + b1) * mask).astype(BF16).astype(F32).reshape(7, 2, 8, BLK)
            u = i + 1
            row = lax.rem(u, 2) * 8 + u // 2
            pb[row, 8:15] = h[:, 0]
            pb[row, 1:8] = h[:, 1]
            return carry

        lax.fori_loop(0, 14, hidden, 0)
        relay(VIA + 1)
        build_patches(strided_base)
        conv(wh, 1024, fs.at[0])
        relay(VIA + 2)
        stats_of_map(fs.at[0], 2, 3)
        sync(1, 2, 2)
        center, scale = moments(2, 3, total_out, 1)
        act_to(fs.at[0], h2, center, scale, g2, b2, mask)
        send = remote(h2, h2, C_H2, C_H2, (1, d, r))
        send.start()
        for i in (HALF, HALF + 1, 16):
            relay_half(i)
        zero_rest(11, sb)
        send.wait_send()
        all_sent(wss.at[W_OWN], wx.at[0 : 3 * 128 + 3 * 256])
        say_ready()

        remote(dh, dh, C_DH, C_DH, (0, d, r)).wait_recv()
        upstream(fs.at[1], dh, fs.at[0], g2, b2, mask, 4, 5)
        sync(0, 4, 2)
        s_du, s_dg = both(4), both(5)
        dg[1], dg[9] = s_dg, s_du
        norm_back(d5, 0, fs.at[1], 0, fs.at[0], 0, g2 * inv[1], s_du * (1.0 / total_out), s_dg * (1.0 / total_out))
        def back_conv():
            conv_back(d5, wh, 1024, strided_base, 16)

        def slopes(i, carry):
            u = i + 1
            row = lax.rem(u, 2) * 8 + u // 2
            grad = jnp.stack([pb[row, 8:15], pb[row, 1:8]], axis=1).reshape(14, 8, BLK)
            zhat = f0[pl.ds(i * 14, 14)]
            du = grad * mask * slope(zhat * g1 + b1)
            f1[pl.ds(i * 14, 14)] = du
            return add_stats(carry, du, du * zhat)

        def first_slopes():
            tx[6], tx[7] = lax.fori_loop(0, 14, slopes, zero_stats)
            sync(1, 6, 2)
            dg[0], dg[8] = both(7), both(6)

        def first_back():
            s_du, s_dg = both(6), both(7)
            gscale, m_du, m_dg = g1 * inv[0], s_du * (1.0 / total_in), s_dg * (1.0 / total_in)

            def body(q, carry):
                part = pl.ds(q * 28, 28)
                dz = gscale * (f1[part] - m_du - f0[part] * m_dg)
                u1[rows(q * 224, 224), :] = dz.reshape(224, BLK).astype(BF16)
                return carry

            lax.fori_loop(0, 7, body, 0)

        def share(target, column, k):
            def body(q, carry):
                g = nt(u1[rows(q * 224, 224), :], wh[k * 256 : (k + 1) * 256, :])
                target[rows(q * 224, 224), column : column + 256] = g.astype(BF16)
                return carry

            lax.fori_loop(0, 7, body, 0)

        places = {1: (u0, 0), 2: (u0, 256), 3: (u2, 0)}

        def share_copy(k):
            target, column = places[k]
            return remote(target.at[0:1568, column : column + 256], r0, C_GI + k - 1, C_GI, (k, d, r))

        def share_out(k):
            share(*places[k], k)
            share_copy(k).start()

        def back_and_share():
            first_back()
            share_out(1)

        def compute(t):
            taps = (t < 6) | (t >= 8)

            @pl.when(taps)
            def _():
                tap = jnp.where(t < 6, t, t - 2)
                wh[rows(at_row(t), 512), :] = tn(pt[tap], d5[...]).astype(BF16)

            @pl.when(jnp.logical_not(taps))
            def _():
                block = tn(wx[rows((t - 6) * 1568, 1568), :], u1[0:1568, :])
                wh[rows(at_row(t), 512), :] = block.astype(BF16)

        def at_row(t):
            return jnp.where(t < 2, 5632 + t * 512, jnp.where(t < 8, t * 512, 2560 + t * 512))

        def chunk_of(t):
            return jnp.where(t < 6, t + 2, jnp.where(t < 8, t - 6, t))

        sum_gradients(
            8, compute, at_row, chunk_of, False, Z1_ZERO,
            {LAST_TURN + 8 * SUBS: final_part},
            lend=(5, 6, 7), helper=lambda t: jnp.where(t < 10, 2, 1), helper_turn=lambda t: jnp.where(t < 10, t - 1, 8),
            helper_row=lambda t: jnp.where(t < 10, (t - 1) * 512, HUB_GUEST), norms_at=4 * SUBS, norms=1024, late_back=1,
            after={
                1: back_conv,
                2: first_slopes,
                3: back_and_share,
                4: lambda: share(r0, 0, 0),
                8: lambda: share_out(3),
                10: lambda: share_out(2),
            },
        )
        for k in (1, 2, 3):
            share_copy(k).wait_send()

    @pl.when(p == 1)
    def _():
        mask = mask_of(1)
        gate_v = per_row(lambda m: gates[m]).astype(F32)
        cotb[PIX_OUT] = jnp.zeros((8, C_OUT), BF16)
        clear_patch_pad()
        load_weights(plain, 48, 0, 16, put_wide(wh, 0, 512, 0))
        load_weights(plain, 48, 16, 32, put_wide(wh, 2048, 1024, 16))

        def shorten(a, slot, carry):
            v = imgb[slot, 0:14].astype(F32).reshape(7, 2, 8, 1024)[:, 0]
            f0[pl.ds(a * 7, 7)] = v[:, :, 0:512]
            f0[pl.ds(PP + a * 7, 7)] = v[:, :, 512:1024]
            return carry

        other_z = 2 * (1 - lax.rem(r, 2))
        this_z = 2 * lax.rem(r, 2)

        def pass_own(i):
            piece_copy(W_OWN, i, quarter, (1, d, r)).wait_recv()
            piece_copy(W_PEER, i, quarter, peer).start()
            piece_copy(W_Z, i, quarter, z_dev).start()

        def pass_on(i):
            piece_copy(W_Z, i, other_z + d, peer).wait_recv()
            piece_copy(W_ON, i, other_z + d, peer).start()

        def have(i):
            piece_copy(W_PEER, i, this_z + 1 - d, peer).wait_recv()
            piece_copy(W_ON, i, other_z + 1 - d, peer).wait_recv()

        def pass_half(i):
            half_copy(W_OWN, i, d, (1, d, r)).wait_recv()
            half_copy(W_PEER, i, d, peer).start()

        def have_half(i):
            half_copy(W_PEER, i, 1 - d, peer).wait_recv()

        pass_own(0)
        over_images(shorten, 0)
        f0[PIX_OUT] = jnp.zeros((8, BLK), F32)
        f0[PP + PIX_OUT] = jnp.zeros((8, BLK), F32)
        sx[...] = f0[0 : 2 * PP].reshape(2 * RW, BLK).astype(BF16)

        def shortcut(n, carry):
            z = nn(sx[0:RW, :], wh[rows(2048 + n * 1024, 512), :]) + nn(
                sx[RW : 2 * RW, :], wh[rows(2560 + n * 1024, 512), :]
            )
            store_z(f1, n * PP, z, 4 * n + 2, 4 * n + 3)
            return carry

        pass_own(1)
        lax.fori_loop(0, 4, shortcut, 0)

        pass_own(2)
        pass_own(VIA)
        pass_on(0)
        pass_own(3)
        pass_on(1)
        pass_own(VIA + 1)
        pass_own(4)
        pl.semaphore_signal(go, inc=1, device_id=(3, d, r), device_id_type=MESH)
        pass_on(2)
        pass_own(VIA + 2)
        pass_own(5)
        pass_on(VIA)
        pass_own(6)
        pass_on(3)
        pass_own(7)
        pass_on(VIA + 1)
        remote(h2, h2, C_H2, C_H2, (1, d, r)).wait_recv()

        def third_conv(n, carry):
            store_z(f0, n * PP, nn(h2[...], wh[rows(n * 512, 512), :]), 4 * n, 4 * n + 1)
            exchange_of(E_WIDE + n, 4 * n, 4).start()
            return carry

        lax.fori_loop(0, 4, third_conv, 0)
        pass_on(4)

        def join(n, carry):
            exchange_of(E_WIDE + n, 4 * n, 4).wait()
            c3, s3 = moments(4 * n, 4 * n + 1, total_out, 2 + n)
            cp, sp = moments(4 * n + 2, 4 * n + 3, total_out, 6 + n)
            g3, gp, b = par[n], par[4 + n], par[8 + n] + par[12 + n]

            def body(_, i, carry):
                part = pl.ds(n * PP + i * 10, 10)
                a = (f0[part] - c3) * s3
                b_ = (f1[part] - cp) * sp
                f0[part] = a
                f1[part] = b_
                o = silu(a * g3 + b_ * gp + b)
                u0[rows(n * RW + i * 80, 80), :] = o.reshape(80, BLK).astype(BF16)
                return carry

            five(body)
            clear_pad(u0, n * RW)
            return carry

        lax.fori_loop(0, 4, join, 0)
        for n in (1, 2, 3):
            o1_copy(n, 3).start()
        pass_half(13)
        pass_on(VIA + 2)
        pass_half(HALF)
        each(have, 0, 4)
        zhat4, zhat5 = fs.at[0], fs.at[1]
        z = nn(u0[0:RW, :], wx[0:512, :])
        for n in range(1, 4):
            z += nn(u0[n * RW : (n + 1) * RW, :], wx[n * 512 : (n + 1) * 512, :])
        store_z(zhat4, 0, z, 16, 17)
        sync(0, 16, 2)
        remote(parx.at[0:4], parx.at[0:4], C_PAR2, C_PAR2, (1, d, r)).wait_recv()
        center, scale = moments(16, 17, total_out, 10)
        g4, g5, b4, b5 = parx[0], parx[1], parx[2], parx[3]
        pb[0:9, 0:9] = jnp.zeros((9, 9, 8, BLK), F32)

        def hidden(a, carry):
            part = pl.ds(a * 7, 7)
            zhat = (zhat4[part] - center) * scale
            zhat4[part] = zhat
            h = silu(zhat * g4 + b4) * mask
            pb[a + 1, 1:8] = h.astype(BF16).astype(F32)
            return carry

        lax.fori_loop(0, 7, hidden, 0)
        h4[0:RV, :] = pb[1:8, 1:8].reshape(RV, BLK).astype(BF16)
        h4_send = remote(h4, h4, C_H4, C_H4, (2, d, r))
        h4_send.start()

        o1_copy(0, 2).start()
        pass_on(5)
        build_patches(plain_base)
        pass_on(6)

        def fifth_conv(taps):
            left = jnp.concatenate([pt[t] for t in taps], axis=1)
            right = jnp.concatenate([wx[2048 + t * 512 : 2560 + t * 512, :] for t in taps], axis=0)
            return nn(left, right).reshape(PP, 8, BLK)

        for i in (4, 5, VIA):
            have(i)
        zhat5[...] = fifth_conv((0, 1, 4))
        pass_half(HALF + 1)
        pass_on(7)
        for i in (6, VIA + 1, VIA + 2):
            have(i)
        zhat5[...] += fifth_conv((2, 5, 6))
        have(7)
        have_half(HALF)
        have_half(HALF + 1)
        store_z(zhat5, 0, zhat5[...] + fifth_conv((3, 7, 8)), 18, 19)
        exchange_z5 = exchange_of(1, 18, 2)
        exchange_z5.start()
        pass_half(14)
        exchange_z5.wait()
        center, scale = moments(18, 19, total_out, 11)
        act_to(zhat5, h5, center, scale, g5, b5, mask)


        def sixth_conv(n):
            have_half(13 + n)
            store_z(f2, n * PP, nn(h5[...], wx[6656 + n * 512 : 7168 + n * 512, :]), 20 + 2 * n, 21 + 2 * n)

        def exchange_z6(n):
            return exchange_of(E_WIDE_NEXT + n, 20 + 2 * n, 2)

        def exchange_d6(n):
            return exchange_of(E_WIDE + n, 28 + 2 * n, 2)

        def finish(n):
            center, scale = moments(20 + 2 * n, 21 + 2 * n, total_out, 12 + n)
            g6, b6 = parx[4 + n], parx[8 + n]

            def body(c, i, carry):
                part = pl.ds(n * PP + i * 10, 10)
                part_rows = rows(n * RW + i * 80, 80)
                zhat = (f2[part] - center) * scale
                f2[part] = zhat
                o = u0[part_rows, :].astype(F32).reshape(10, 8, BLK)
                q = o + zhat * g6 + b6
                s = sigmoid(q)
                act = q * s
                pt[n, rows(i * 80, 80), :] = (o + gate_v * (act - o)).reshape(80, BLK).astype(BF16)
                ct = cotb[c, :, n * BLK : (n + 1) * BLK].astype(F32)
                through = ct * gate_v
                dq = through * (s + act * (1.0 - s))
                f3[part] = dq
                u2[part_rows, :] = (dq + (ct - through)).reshape(80, BLK).astype(BF16)
                return add_stats(carry, dq, dq * zhat)

            tx[28 + 2 * n], tx[29 + 2 * n] = five(body, zero_stats, unrolled=True)

        for n in (0, 1):
            sixth_conv(n)
            exchange_z6(n).start()
        remote(parx.at[4:12], parx.at[4:12], C_PAR3, C_PAR3, (1, d, r)).wait_recv()
        pltpu.make_async_copy(cot, cotb.at[0:PIX_OUT], ls.at[16]).wait()
        pass_half(15)
        exchange_z6(0).wait()
        finish(0)
        exchange_d6(0).start()
        pass_half(16)
        exchange_z6(1).wait()
        finish(1)
        exchange_d6(1).start()
        have_half(15)
        store_z(f2, 2 * PP, nn(h5[...], wx[7680:8192, :]), 24, 25)
        exchange_z6(2).start()
        have_half(16)
        store_z(f2, 3 * PP, nn(h5[...], wx[8192:8704, :]), 26, 27)
        exchange_z6(3).start()
        exchange_z6(2).wait()
        finish(2)
        exchange_d6(2).start()
        exchange_z6(3).wait()
        finish(3)
        exchange_d6(3).start()
        ob[...] = pt[1]

        def output_copy(k):
            return remote(pt.at[k], ob, C_SHARE + k % 3, C_SHARE, (k, d, r))

        output_copy(3).start()


        def sixth_back(n):
            s_du, s_dg = both(28 + 2 * n), both(29 + 2 * n)
            dgx[4 + n] = s_dg
            dgx[8 + n] = s_du
            norm_back(
                u1, n * RW, f3, n * PP, f2, n * PP, parx[4 + n] * inv[12 + n],
                s_du * (1.0 / total_out), s_dg * (1.0 / total_out), unrolled=True,
            )

        grad = jnp.zeros((RW, BLK), F32)
        for n in range(5):
            if n < 4:
                exchange_d6(n).wait()
                sixth_back(n)
            if n > 0:
                grad += nt(u1[(n - 1) * RW : n * RW, :], wx[6144 + n * 512 : 6656 + n * 512, :])
        dh[...] = grad.astype(BF16)

        upstream(f2, dh, zhat5, g5, b5, mask, 36, 37)
        sync(0, 36, 2)
        s_du, s_dg = both(36), both(37)
        dgx[1] = s_dg
        dgx[3] = s_du
        norm_back(d5, 0, f2, 0, zhat5, 0, g5 * inv[11], s_du * (1.0 / total_out), s_dg * (1.0 / total_out))
        d5_send = remote(d5, d5, C_D5, C_D5, (2, d, r))
        d5_send.start()
        pb[0:9, 0:9] = jnp.zeros((9, 9, 8, BLK), F32)
        for tap in range(9):
            row, col = tap // 3, tap % 3
            part = nt(d5[0:RV, :], wx[2048 + tap * 512 : 2560 + tap * 512, :])
            pb[row : row + 7, col : col + 7] += part.reshape(7, 7, 8, BLK)

        def fourth_slopes(a, carry):
            part = pl.ds(a * 7, 7)
            zhat = zhat4[part]
            du = pb[a + 1, 1:8] * mask * slope(zhat * g4 + b4)
            f2[part] = du
            return add_stats(carry, du, du * zhat)

        tx[38], tx[39] = lax.fori_loop(0, 7, fourth_slopes, zero_stats)
        sync(1, 38, 2)
        s_du, s_dg = both(38), both(39)
        dgx[0] = s_dg
        dgx[2] = s_du
        norm_back(d4, 0, f2, 0, zhat4, 0, g4 * inv[10], s_du * (1.0 / total_out), s_dg * (1.0 / total_out))

        def carried_back(n):
            z = nt(d4[...], wx[n * 512 : (n + 1) * 512, :])
            f2[(n % 2) * PP : (n % 2 + 1) * PP] = z.reshape(PP, 8, BLK)

        def exchange_d1(n):
            return exchange_of(E_WIDE_NEXT + n, 40 + 3 * n, 3)

        def first_block_slopes(n):
            g3, gp, b = par[n], par[4 + n], par[8 + n] + par[12 + n]

            def body(_, i, carry):
                part = pl.ds(n * PP + i * 10, 10)
                do = u2[n * RW + i * 80 : n * RW + (i + 1) * 80, :].astype(F32).reshape(10, 8, BLK)
                do += f2[pl.ds((n % 2) * PP + i * 10, 10)]
                a, b_ = f0[part], f1[part]
                dp = do.astype(BF16).astype(F32) * slope(a * g3 + b_ * gp + b)
                f3[part] = dp
                s0, s1, s2 = carry
                return s0 + jnp.sum(dp, axis=0), s1 + jnp.sum(dp * a, axis=0), s2 + jnp.sum(dp * b_, axis=0)

            first = 40 + 3 * n
            tx[first], tx[first + 1], tx[first + 2] = five(body, zero_stats + zero_stats[:1], unrolled=True)

        carried_back(0)
        for n in range(4):
            if n < 3:
                carried_back(n + 1)
            first_block_slopes(n)
            exchange_d1(n).start()

        def third_back(n):
            first = 40 + 3 * n
            m_du, m_dg = both(first) * (1.0 / total_out), both(first + 1) * (1.0 / total_out)
            norm_back(
                pt.at[4 + n], 0, f3, n * PP, f0, n * PP, par[n] * inv[2 + n], m_du, m_dg, unrolled=True
            )

        grad = jnp.zeros((RW, BLK), F32)
        for n in range(5):
            if n < 4:
                exchange_d1(n).wait()
                third_back(n)
            if n > 0:
                grad += nt(pt[3 + n], wh[(n - 1) * 512 : n * 512, :])
        dh[...] = grad.astype(BF16)
        dh_send = remote(dh, dh, C_DH, C_DH, (0, d, r))
        dh_send.start()

        def shortcut_back(n, carry):
            first = 40 + 3 * n
            s_du, s_d3, s_dp = both(first), both(first + 1), both(first + 2)
            dg[n] = s_d3
            dg[4 + n] = s_dp
            dg[8 + n] = s_du
            dg[12 + n] = s_du
            m_du, m_dg = s_du * (1.0 / total_out), s_dp * (1.0 / total_out)
            norm_back(u2, n * RW, f3, n * PP, f1, n * PP, par[4 + n] * inv[6 + n], m_du, m_dg)
            return carry

        def all_shortcut_back():
            lax.fori_loop(0, 4, shortcut_back, 0)

        all_sent(wss.at[W_PEER], wx.at[0 : HALF * 128 + 6 * 256])
        all_sent(wss.at[W_Z], wx.at[0 : HALF * 128])
        all_sent(wss.at[W_ON], wx.at[0 : HALF * 128])
        say_ready()

        late = [remote(d4, d4, C_D4, C_D4, (2, d, r))]
        for first, last, sem, chip in ((0, 4, C_DG2, 2), (4, 12, C_DG3, 3)):
            late.append(remote(dgx.at[first:last], dgx.at[first:last], sem, sem, (chip, d, r)))

        def late_sends():
            dh_send.wait_send()
            for copy in late:
                copy.start()

        def shortcut_share(k):
            g = nt(u2[0:RW, :], wh[2048 + k * 256 : 2304 + k * 256, :])
            for n in range(1, 4):
                g += nt(u2[n * RW : (n + 1) * RW, :], wh[2048 + n * 1024 + k * 256 : 2304 + n * 1024 + k * 256, :])
            return g.astype(BF16)

        places = ((h4.at[:, 0:256], 0), (h4.at[:, 256:512], 2), (pt.at[8, :, 0:256], 3))

        def share_copy(slot):
            place, k = places[slot]
            return remote(place, r1, C_GP + slot, C_GP, (k, d, r))

        def shortcut_shares(slot):
            place, k = places[slot]
            if slot == 0:
                h4_send.wait_send()
            place[...] = shortcut_share(k)

        def shortcut_own():
            r1[...] = shortcut_share(1)


        def own_and_output():
            shortcut_own()
            output_copy(2).start()

        def late_shares():
            for slot in range(3):
                share_copy(slot).start()

        def at_row(t):
            early = jnp.where(t == 8, HUB_GUEST, t * 512)
            return jnp.where(t < 11, early, jnp.where(t < 16, t * 512 + 512, 5632))

        def compute(t):
            @pl.when(t < 4)
            def _():
                left = h2[:, pl.ds(pl.multiple_of(t * 128, 128), 128)]
                for n in range(4):
                    put_chunk(at_row(t), n, tn(left, pt[4 + n]))

            @pl.when((t >= 4) & (t < 13))
            def _():
                m = jnp.where(t < 8, t - 4, t - 5)
                left = sx[rows((m // 4) * RW, RW), pl.ds(pl.multiple_of(lax.rem(m, 4) * 128, 128), 128)]
                for n in range(4):
                    put_chunk(at_row(t), n, tn(left, u2[n * RW : (n + 1) * RW, :]))

            @pl.when(t >= 13)
            def _():
                left = h5[:, pl.ds(pl.multiple_of((t - 13) * 128, 128), 128)]
                for n in range(4):
                    put_chunk(at_row(t), n, tn(left, u1[n * RW : (n + 1) * RW, :]))

        zero_rest(12, sb)
        sum_gradients(
            11, compute, at_row, lambda t: jnp.where(t < 8, t, t - 1), True, 0,
            {LAST_TURN + 11 * SUBS: final_part},
            after={
                1: all_shortcut_back,
                2: lambda: shortcut_shares(0),
                4: lambda: shortcut_shares(1),
                5: late_sends,
                6: lambda: shortcut_shares(2),
                7: own_and_output,
                11: lambda: output_copy(0).start(),
                15: late_shares,
            },
            lend=(3, 5), passed=(7, 9, 11, 13), helper=lambda t: 3, helper_turn=lambda t: t - 7, norms_at=2,
            handed_in=lambda t: t == 8, lent_by=(lambda t: t == 8, lambda t: 0, lambda t: t + 2, 1), back=R_BACK_HUB,
            computed=(0, 10), packed_here=(0, 10),
        )
        for copy in [d5_send, o1_copy(0, 2)] + [o1_copy(n, 3) for n in (1, 2, 3)] + late:
            copy.wait_send()
        for slot in range(3):
            share_copy(slot).wait_send()
        for k in (0, 2, 3):
            output_copy(k).wait_send()


    @pl.when(p == 2)
    def _():
        for k, slot in ((0, 0), (1, 1), (2, 8), (3, 9)):
            parx[k] = par[slot]
        par_send = remote(parx.at[0:4], parx.at[0:4], C_PAR2, C_PAR2, (1, d, r))
        par_send.start()

        put_w = put_narrow(wx, lambda i: own_parts(i) * 128)

        def put(i):
            put_w(i)

            @pl.when(i < VIA)
            def _():
                piece_copy(W_OWN, i, quarter, (1, d, r)).start()

            @pl.when((i >= VIA) & (i < HALF))
            def _():
                piece_copy(W_VIA, i, quarter, (0, d, r)).start()

            for k in range(HALF, 13):
                @pl.when(i == HALF + 2 * (k - HALF) + 1)
                def _(k=k):
                    half_copy(W_VIA, k, d, (0, d, r)).start()

        load_weights(own_parts, 15, 0, 15, put)
        pb[...] = jnp.zeros_like(pb)
        clear_patch_pad()

        all_sent(wss.at[W_OWN], wx.at[0 : VIA * 128])
        all_sent(wss.at[W_VIA], wx.at[0 : 3 * 128 + 2 * 256])
        say_ready()
        remote(h4, h4, C_H4, C_H4, (2, d, r)).wait_recv()
        pb[1:8, 1:8] = h4[0:RV, :].astype(F32).reshape(7, 7, 8, BLK)
        build_patches(plain_base)
        remote(d5, d5, C_D5, C_D5, (2, d, r)).wait_recv()

        def compute(t):
            taps = (t < 5) | (t >= 11)

            @pl.when(taps)
            def _():
                tap = jnp.where(t < 5, t + 4, t - 11)
                wh[rows(t * 512, 512), :] = tn(pt[tap], d5[...]).astype(BF16)

            @pl.when(t == 5)
            def _():
                remote(d4, d4, C_D4, C_D4, (2, d, r)).wait_recv()
                for n in range(4):
                    o1_copy(n, 2).wait_recv()

            @pl.when(jnp.logical_not(taps))
            def _():
                n = jnp.where(t < 7, t - 5, t - 7)
                wh[rows(t * 512, 512), :] = tn(u0[rows(n * RW, RW), :], d4[...]).astype(BF16)

        def chunk_of(t):
            return jnp.where(t < 5, t + 8, jnp.where(t < 7, t - 5, t - 7))

        def norm_grads():
            remote(dgx.at[0:4], dgx.at[0:4], C_DG2, C_DG2, (2, d, r)).wait_recv()
            dg[0], dg[1], dg[8], dg[9] = dgx[0], dgx[1], dgx[2], dgx[3]

        sum_gradients(
            11, compute, lambda t: t * 512, chunk_of, False, 0,
            {6 * SUBS: norm_grads, LAST_TURN + 11 * SUBS: final_part},
            lend=(2, 3, 4, 6), helper=lambda t: 3, helper_turn=lambda t: t - 11,
            handed_in=lambda t: (t >= 7) & (t < 9),
            lent_by=(lambda t: (t >= 7) & (t < 9), lambda t: 0, lambda t: t + 1, 2),
            computed=(0, 9), packed_here=(0, 9), norms_at=6 * SUBS, norms=1024,
        )
        par_send.wait_send()

    @pl.when(p == 3)
    def _():
        for k in range(4):
            parx[4 + k] = par[k]
            parx[8 + k] = par[8 + k]
        par_send = remote(parx.at[4:12], parx.at[4:12], C_PAR3, C_PAR3, (1, d, r))
        par_send.start()
        say_ready()

        def put(i):
            for n in range(4):
                for j in range(4):
                    wx[rows(6656 + n * 512 + d * 256 + i * 32, 32), j * 128 : (j + 1) * 128] = st[
                        pl.ds(4 * n + j, 32, stride=16), :
                    ].astype(BF16)

        load_weights(half_rows, 8, 0, 8, put)
        zero_rest(4, sb)
        pl.semaphore_wait(go, 1)

        half_copy(W_VIA, 16, d, (0, d, r)).start()
        for i in (13, 14, 15):
            half_copy(W_OWN, i, d, (1, d, r)).start()
        for n in (1, 2, 3):
            o1_copy(n, 3).wait_recv()
            o1_copy(n, 2).start()
        def norm_grads():
            remote(dgx.at[4:12], dgx.at[4:12], C_DG3, C_DG3, (3, d, r)).wait_recv()
            for k in range(4):
                dg[k] = dgx[4 + k]
                dg[8 + k] = dgx[8 + k]

        sum_gradients(
            10, lambda t: None, lambda t: t * 512, lambda t: t - 6, True, 0,
            {5 * SUBS: norm_grads, LAST_TURN + 10 * SUBS: final_part},
            handed_in=lambda t: t >= 0,
            lent_by=(lambda t: t < 6, lambda t: jnp.where(t < 4, 2, 1), lambda t: jnp.where(t < 4, t + 11, t + 7), 6),
            computed=(0, 0), packed_here=(6, 4), norms_at=5 * SUBS, norms=2048,
        )
        for n in (1, 2, 3):
            o1_copy(n, 2).wait_send()
        all_sent(wss.at[W_VIA], wx.at[0:256])
        all_sent(wss.at[W_OWN], wx.at[0 : 3 * 256])
        par_send.wait_send()

    dgb_copy().start()
    gi_copy().wait()
    out_copy().wait()
    dgb_copy().wait()


def widen_kernel(out_in, gi_in, dw_in, dgb_in, out, gi, dw, gain, bias, v_out, v_gi, v_dw, v_wide, v_dgb, sin, sout):
    count = v_dw.shape[0] // 3328

    def part(i):
        return pl.ds(i * 3328, 3328)

    loads = [pltpu.make_async_copy(dw_in.at[part(i)], v_dw.at[part(i)], sin.at[i]) for i in range(count)]
    others = (
        (dgb_in, v_dgb, ((v_dgb.at[0:4], gain), (v_dgb.at[4:8], bias))),
        (out_in, v_out, ((v_out, out),)),
        (gi_in, v_gi, ((v_gi, gi),)),
    )
    more = [pltpu.make_async_copy(a, b, sin.at[count + k]) for k, (a, b, _) in enumerate(others)]
    for copy in more + loads:
        copy.start()
    stores = []
    for i in range(count):
        loads[i].wait()
        v_wide[part(i)] = v_dw[part(i)].astype(F32)
        stores.append(pltpu.make_async_copy(v_wide.at[part(i)], dw.at[part(i)], sout.at[i]))
        stores[-1].start()
    for k, (_, _, ends) in enumerate(others):
        more[k].wait()
        for a, b in ends:
            stores.append(pltpu.make_async_copy(a, b, sout.at[len(stores)]))
            stores[-1].start()
    for copy in stores:
        copy.wait()


def widen(out, gi, dw, dgb):
    count = P_SIZE // 128 // 3328
    any_space = pl.BlockSpec(memory_space=pl.ANY)
    return pl.pallas_call(
        widen_kernel,
        out_shape=(
            jax.ShapeDtypeStruct(out.shape, out.dtype),
            jax.ShapeDtypeStruct(gi.shape, gi.dtype),
            jax.ShapeDtypeStruct(dw.shape, F32),
            jax.ShapeDtypeStruct((4, 4096), F32),
            jax.ShapeDtypeStruct((4, 4096), F32),
        ),
        in_specs=[any_space] * 4,
        out_specs=(any_space,) * 5,
        scratch_shapes=[
            pltpu.VMEM(out.shape, out.dtype),
            pltpu.VMEM(gi.shape, gi.dtype),
            pltpu.VMEM(dw.shape, BF16),
            pltpu.VMEM(dw.shape, F32),
            pltpu.VMEM(dgb.shape, F32),
            pltpu.SemaphoreType.DMA((count + 3,)),
            pltpu.SemaphoreType.DMA((count + 4,)),
        ],
        compiler_params=pltpu.CompilerParams(vmem_limit_bytes=64 * 1024 * 1024),
    )(out, gi, dw, dgb)


def one_kernel(images, section_weights, bn_gain, bn_bias, width, bn_set, gate, cotangent):
    any_space = pl.BlockSpec(memory_space=pl.ANY)
    smem = pl.BlockSpec(memory_space=pltpu.SMEM)
    out, gi, dw, dgb = pl.pallas_call(
        whole_kernel,
        out_shape=(
            jax.ShapeDtypeStruct((PIX_OUT, 8, BLK), BF16),
            jax.ShapeDtypeStruct((PIX_IN, 8, 256), F32),
            jax.ShapeDtypeStruct((P_SIZE // SUB, 512, 128), BF16),
            jax.ShapeDtypeStruct((8, 4096), F32),
        ),
        in_specs=[any_space, any_space, any_space, any_space, smem, smem, smem, any_space],
        out_specs=(any_space,) * 4,
        scratch_shapes=[
            pltpu.VMEM((4, 28, 8, 1024), BF16),
            pltpu.VMEM((RING, 1, SUB), BF16),
            pltpu.VMEM((512, 128), F32),
            pltpu.VMEM((9216, BLK), BF16),
            pltpu.VMEM((8768, BLK), BF16),
            pltpu.VMEM((4 * PP, 8, BLK), F32),
            pltpu.VMEM((4 * PP, 8, BLK), F32),
            pltpu.VMEM((4 * PP, 8, BLK), F32),
            pltpu.VMEM((4 * PP, 8, BLK), F32),
            pltpu.VMEM((2, PP, 8, BLK), F32),
            pltpu.VMEM((16, 16, 8, BLK), F32),
            pltpu.VMEM((9, RW, BLK), BF16),
            pltpu.VMEM((4 * RW, BLK), BF16),
            pltpu.VMEM((4 * RW, BLK), BF16),
            pltpu.VMEM((4 * RW, BLK), BF16),
            pltpu.VMEM((2 * RW, BLK), BF16),
            pltpu.VMEM((PP, 8, C_OUT), BF16),
            pltpu.VMEM((RW, BLK), BF16),
            pltpu.VMEM((RW, BLK), BF16),
            pltpu.VMEM((RW, BLK), BF16),
            pltpu.VMEM((RW, BLK), BF16),
            pltpu.VMEM((RW, BLK), BF16),
            pltpu.VMEM((RW, BLK), BF16),
            pltpu.VMEM((8 * PIX_IN, 256), BF16),
            pltpu.VMEM((RW, 256), BF16),
            pltpu.VMEM((RW, BLK), BF16),
            pltpu.VMEM((52, 8, BLK), F32),
            pltpu.VMEM((52, 8, BLK), F32),
            pltpu.VMEM((16, 8, BLK), F32),
            pltpu.VMEM((16, 8, BLK), F32),
            pltpu.VMEM((12, 8, BLK), F32),
            pltpu.VMEM((16, 8, BLK), F32),
            pltpu.VMEM((12, 8, BLK), F32),
            pltpu.VMEM((4, 512, 128), BF16),
            pltpu.VMEM((4352, BLK), BF16),
            pltpu.VMEM((2, 8, 4096), F32),
            pltpu.VMEM((8, 4096), F32),
            pltpu.VMEM((8, 4096), F32),
            pltpu.VMEM((PIX_OUT, 8, BLK), BF16),
            pltpu.VMEM((NSETS, 4096), F32),
            pltpu.VMEM((NSETS, 4096), F32),
            pltpu.SemaphoreType.DMA((19,)),
            pltpu.SemaphoreType.DMA((N_SEM,)),
            pltpu.SemaphoreType.DMA((N_SEM,)),
            pltpu.SemaphoreType.DMA((5,)),
            pltpu.SemaphoreType.DMA((N_SUM_SEND,)),
            pltpu.SemaphoreType.DMA((N_SUM_RECV,)),
            pltpu.SemaphoreType.REGULAR((2,)),
            pltpu.SemaphoreType.REGULAR,
        ],
        compiler_params=pltpu.CompilerParams(
            collective_id=0, has_side_effects=True, vmem_limit_bytes=64 * 1024 * 1024
        ),
    )(
        jnp.transpose(images, (1, 0, 2)),
        section_weights,
        bn_gain[0],
        bn_bias[0],
        width.T,
        bn_set.T,
        gate,
        jnp.transpose(cotangent, (1, 0, 2)),
    )
    out, gi, dw, gain_sum, bias_sum = widen(out, gi, dw.reshape(P_SIZE // 128, 128), dgb)
    return (
        jnp.transpose(out, (1, 0, 2)),
        jnp.transpose(gi, (1, 0, 2)),
        dw.reshape(1, P_SIZE),
        gain_sum[None],
        bias_sum[None],
    )


def solution(mesh):
    sizes = dict(mesh.shape)
    fits = sizes["pipe"] == 4 and sizes["dp"] == 2 and sizes["rep"] == 4
    placed = (
        P(("dp", "rep"), None, None),
        P("pipe", None),
        P("pipe", None, None),
        P("pipe", None, None),
        P(),
        P(),
        P(),
        P(("dp", "rep"), None, None),
    )
    return jax.shard_map(
        one_kernel if fits else on_device,
        mesh=mesh,
        in_specs=placed,
        out_specs=(
            P(("dp", "rep"), None, "pipe"),
            P(("dp", "rep"), None, "pipe"),
            P("pipe", None),
            P("pipe", None, None),
            P("pipe", None, None),
        ),
        check_vma=False,
    )
```

```python
import jax
import jax.numpy as jnp
from jax import lax
from jax.experimental import pallas as pl
from jax.experimental.pallas import tpu as pltpu
from jax.sharding import PartitionSpec as P

C_IN = 1024
C_MID = 512
C_OUT = 2048
SIDE = 14
NSETS = 4
MB = 8
IMG_B = 1
OSIDE = 7
PIX_IN = 196
PIX_OUT = 49
IMG_DEV = 8
P_SIZE = 3407872


EPSILON = 1e-05


def for_sending(array):

    def short(part):
        return part.astype(jnp.bfloat16) if part.dtype == jnp.float32 else part

    return jax.tree.map(short, array)


def shifted(value, axis, steps):
    count = lax.axis_size(axis)
    first, last = (max(0, -steps), min(count, count - steps))
    return lax.ppermute(value, axis, [(source, source + steps) for source in range(first, last)])


def smooth(inputs):
    return inputs * jax.nn.sigmoid(inputs)


def smooth_slope(inputs):
    gate_sig = jax.nn.sigmoid(inputs)
    return gate_sig * (1.0 + inputs * (1.0 - gate_sig))


def matmul(left_op, right_op):
    return jnp.dot(left_op, right_op, preferred_element_type=jnp.float32)


def matmul_left_t(left_op, right_op):
    return lax.dot_general(
        left_op, right_op, (((0,), (0,)), ((), ())), preferred_element_type=jnp.float32
    )


def matmul_right_t(left_op, right_op):
    return lax.dot_general(
        left_op, right_op, (((1,), (1,)), ((), ())), preferred_element_type=jnp.float32
    )


def patches(planes, stride):
    images, side_len, channels = (planes.shape[0], planes.shape[1], planes.shape[3])
    out_side = side_len // stride
    padded = jnp.pad(planes, ((0, 0), (1, 1), (1, 1), (0, 0)))
    pieces = []
    for row_off in range(3):
        for col_off in range(3):
            pieces.append(
                padded[
                    :,
                    row_off : row_off + stride * (out_side - 1) + 1 : stride,
                    col_off : col_off + stride * (out_side - 1) + 1 : stride,
                    :,
                ]
            )
    return jnp.concatenate(pieces, axis=3).reshape(images * out_side * out_side, 9 * channels)


def unpatch(columns, images, side_len, stride, channels):
    out_side = side_len // stride
    pieces = columns.reshape(images, out_side, out_side, 9, channels)
    padded = jnp.zeros((images, side_len + 2, side_len + 2, channels), jnp.float32)
    for row_off in range(3):
        for col_off in range(3):
            padded = padded.at[
                :,
                row_off : row_off + stride * (out_side - 1) + 1 : stride,
                col_off : col_off + stride * (out_side - 1) + 1 : stride,
                :,
            ].add(pieces[:, :, :, row_off * 3 + col_off, :])
    return padded[:, 1 : side_len + 1, 1 : side_len + 1, :]


def group_moments(sums_local, squares_local):
    return (
        lax.psum(sums_local.astype(jnp.bfloat16), "dp").astype(jnp.float32),
        lax.psum(squares_local.astype(jnp.bfloat16), "dp").astype(jnp.float32),
    )


def group_grad_sums(bias_local, gain_local):
    return (
        lax.psum(bias_local.astype(jnp.bfloat16), "dp").astype(jnp.float32),
        lax.psum(gain_local.astype(jnp.bfloat16), "dp").astype(jnp.float32),
    )


def stats_of(sum_all, square_all, start, count, row_total):
    center = sum_all[start : start + count] / row_total
    inv_std = lax.rsqrt(square_all[start : start + count] / row_total - center * center + EPSILON)
    return (center, inv_std)


def norm_grad(slope_in, normed, gain_vec, inv_std, sum_bias, sum_gain, row_total):
    return (
        gain_vec * inv_std * (slope_in - sum_bias / row_total - normed * (sum_gain / row_total))
    ).astype(jnp.bfloat16)


def on_device(images, section_weights, bn_gain, bn_bias, width, bn_set, gate, cotangent):
    section_idx = lax.axis_index("pipe")
    pipe_count = lax.axis_size("pipe")
    dp_count = lax.axis_size("dp")
    flat_weights = section_weights[0]
    gain_table = bn_gain[0]
    bias_table = bn_bias[0]
    rows_in = IMG_B * PIX_IN
    rows_out = IMG_B * PIX_OUT
    total_in = float(rows_in * dp_count)
    total_out = float(rows_out * dp_count)
    wide = 2 * C_OUT
    scr_len = IMG_B * max(PIX_IN * C_MID, PIX_OUT * wide)
    image_blocks = images.reshape(MB, IMG_B, PIX_IN, C_IN)
    pad_mid = jnp.zeros((wide - 2 * C_MID,), jnp.float32)
    zero_wide = jnp.zeros((wide,), jnp.float32)
    zero_scr = jnp.zeros((scr_len,), jnp.float32)
    zero_mid = jnp.zeros((rows_out, C_MID), jnp.bfloat16)
    zero_res = jnp.zeros((rows_out, C_OUT), jnp.bfloat16)
    zero_rows = jnp.zeros((rows_out, C_OUT), jnp.float32)
    zero_input = jnp.zeros((IMG_B, PIX_IN, C_IN), jnp.float32)

    def pack(values):
        flat = values.reshape(-1).astype(jnp.float32)
        return jnp.pad(flat, (0, scr_len - flat.shape[0]))

    def unpack(buffer, rows, cols):
        return buffer[: rows * cols].reshape(rows, cols)

    def place(vec, start):
        return jnp.pad(vec, (start, wide - start - vec.shape[0]))

    def add_weight(acc, grad, offset, valid):
        flat = grad.reshape(-1)
        return acc.at[offset : offset + flat.shape[0]].add(jnp.where(valid, flat, 0.0))

    def weights_zero():
        split_at = C_IN * C_MID
        return (
            flat_weights[:split_at].reshape(C_IN, C_MID),
            flat_weights[split_at : split_at + 9 * C_MID * C_MID].reshape(9 * C_MID, C_MID),
        )

    def weights_one():
        split_at = C_MID * C_OUT
        return (
            flat_weights[:split_at].reshape(C_MID, C_OUT),
            flat_weights[split_at : split_at + C_IN * C_OUT].reshape(C_IN, C_OUT),
        )

    def weights_two():
        split_at = C_OUT * C_MID
        return (
            flat_weights[:split_at].reshape(C_OUT, C_MID),
            flat_weights[split_at : split_at + 9 * C_MID * C_MID].reshape(9 * C_MID, C_MID),
        )

    def short_rows(image_block):
        return image_block.reshape(IMG_B, SIDE, SIDE, C_IN)[:, ::2, ::2, :].reshape(rows_out, C_IN)

    def local_stats(values, start):
        return (
            place(jnp.sum(values, axis=0), start),
            place(jnp.sum(values * values, axis=0), start),
        )

    def fwd_a_zero(ops):
        conv_a, conv_b = weights_zero()
        pre_one = matmul(ops[0].reshape(rows_in, C_IN), conv_a)
        sums_local, squares_local = local_stats(pre_one, 0)
        return (pack(pre_one), sums_local, squares_local)

    def fwd_a_one(ops):
        conv_a, conv_b = weights_one()
        pre_both = jnp.concatenate(
            [matmul(ops[1], conv_a), matmul(short_rows(ops[0]), conv_b)], axis=1
        )
        sums_local, squares_local = local_stats(pre_both, 0)
        return (pack(pre_both), sums_local, squares_local)

    def fwd_a_two(ops):
        conv_a, conv_b = weights_two()
        pre_four = matmul(ops[2], conv_a)
        sums_local, squares_local = local_stats(pre_four, 0)
        return (pack(pre_four), sums_local, squares_local)

    def fwd_a_three(ops):
        conv_a = flat_weights[: C_MID * C_OUT].reshape(C_MID, C_OUT)
        pre_six = matmul(ops[1], conv_a)
        sums_local, squares_local = local_stats(pre_six, 0)
        return (pack(pre_six), sums_local, squares_local)

    def fwd_b_zero(args):
        ops, scratch, sum_all, square_all = args
        conv_a, conv_b = weights_zero()
        gain_vec, bias_vec, mask_vec = (ops[3], ops[4], ops[5])
        pre_one = unpack(scratch, rows_in, C_MID)
        center_one, inv_one = stats_of(sum_all, square_all, 0, C_MID, total_in)
        hidden_one = (
            smooth((pre_one - center_one) * inv_one * gain_vec[:C_MID] + bias_vec[:C_MID])
            * mask_vec
        ).astype(jnp.bfloat16)
        pre_two = matmul(patches(hidden_one.reshape(IMG_B, SIDE, SIDE, C_MID), 2), conv_b)
        sums_local, squares_local = local_stats(pre_two, C_MID)
        return (pack(pre_two), sums_local, squares_local)

    def fwd_b_pass(args):
        return (args[1], zero_wide, zero_wide)

    def fwd_b_two(args):
        ops, scratch, sum_all, square_all = args
        conv_a, conv_b = weights_two()
        gain_vec, bias_vec, mask_vec = (ops[3], ops[4], ops[5])
        pre_four = unpack(scratch, rows_out, C_MID)
        center_four, inv_four = stats_of(sum_all, square_all, 0, C_MID, total_out)
        hidden_four = (
            smooth((pre_four - center_four) * inv_four * gain_vec[:C_MID] + bias_vec[:C_MID])
            * mask_vec
        ).astype(jnp.bfloat16)
        pre_five = matmul(patches(hidden_four.reshape(IMG_B, OSIDE, OSIDE, C_MID), 1), conv_b)
        sums_local, squares_local = local_stats(pre_five, C_MID)
        return (pack(pre_five), sums_local, squares_local)

    def fwd_c_double(args, first_total, send_res):
        ops, scratch, sum_all, square_all = args
        gain_vec, bias_vec, mask_vec = (ops[3], ops[4], ops[5])
        pre_two = unpack(scratch, rows_out, C_MID)
        center_one, inv_one = stats_of(sum_all, square_all, 0, C_MID, first_total)
        center_two, inv_two = stats_of(sum_all, square_all, C_MID, C_MID, total_out)
        hidden_two = (
            smooth(
                (pre_two - center_two) * inv_two * gain_vec[C_MID : 2 * C_MID]
                + bias_vec[C_MID : 2 * C_MID]
            )
            * mask_vec
        ).astype(jnp.bfloat16)
        centers = jnp.concatenate([center_one, center_two, pad_mid])
        scales = jnp.concatenate([inv_one, inv_two, pad_mid])
        return (hidden_two, send_res, centers, scales, zero_rows)

    def fwd_c_zero(args):
        return fwd_c_double(args, total_in, zero_res)

    def fwd_c_two(args):
        return fwd_c_double(args, total_out, args[0][2])

    def fwd_c_one(args):
        ops, scratch, sum_all, square_all = args
        gain_vec, bias_vec = (ops[3], ops[4])
        pre_both = unpack(scratch, rows_out, wide)
        centers, scales = stats_of(sum_all, square_all, 0, wide, total_out)
        activ = (pre_both - centers) * scales * gain_vec + bias_vec
        block_out = smooth(activ[:, :C_OUT] + activ[:, C_OUT:]).astype(jnp.bfloat16)
        return (zero_mid, block_out, centers, scales, zero_rows)

    def fwd_c_three(args):
        ops, scratch, sum_all, square_all = args
        gain_vec, bias_vec, gate_val = (ops[3], ops[4], ops[6])
        pre_six = unpack(scratch, rows_out, C_OUT)
        centers, scales = stats_of(sum_all, square_all, 0, wide, total_out)
        residual = ops[2].astype(jnp.float32)
        merged = smooth(
            residual
            + (pre_six - centers[:C_OUT]) * scales[:C_OUT] * gain_vec[:C_OUT]
            + bias_vec[:C_OUT]
        )
        result = gate_val * merged + (1.0 - gate_val) * residual
        return (zero_mid, zero_res, centers, scales, result)

    def bwd_a_double(ops, flat_in, conv_a, conv_b, side_len, stride):
        centers, scales, grad_mid = (ops[3], ops[4], ops[5])
        gain_vec, bias_vec, mask_vec = (ops[8], ops[9], ops[10])
        norm_one = (matmul(flat_in, conv_a) - centers[:C_MID]) * scales[:C_MID]
        hidden_one = (smooth(norm_one * gain_vec[:C_MID] + bias_vec[:C_MID]) * mask_vec).astype(
            jnp.bfloat16
        )
        columns = patches(hidden_one.reshape(IMG_B, side_len, side_len, C_MID), stride)
        norm_two = (matmul(columns, conv_b) - centers[C_MID : 2 * C_MID]) * scales[
            C_MID : 2 * C_MID
        ]
        act_two = norm_two * gain_vec[C_MID : 2 * C_MID] + bias_vec[C_MID : 2 * C_MID]
        slope_two = grad_mid.astype(jnp.float32) * mask_vec * smooth_slope(act_two)
        return (
            pack(slope_two),
            pack(norm_two),
            pack(norm_one),
            place(jnp.sum(slope_two, axis=0), C_MID),
            place(jnp.sum(slope_two * norm_two, axis=0), C_MID),
        )

    def bwd_a_zero(ops):
        conv_a, conv_b = weights_zero()
        return bwd_a_double(ops, ops[0].reshape(rows_in, C_IN), conv_a, conv_b, SIDE, 2)

    def bwd_a_two(ops):
        conv_a, conv_b = weights_two()
        return bwd_a_double(ops, ops[2], conv_a, conv_b, OSIDE, 1)

    def bwd_a_one(ops):
        conv_a, conv_b = weights_one()
        centers, scales, grad_res = (ops[3], ops[4], ops[6])
        gain_vec, bias_vec = (ops[8], ops[9])
        pre_both = jnp.concatenate(
            [matmul(ops[1], conv_a), matmul(short_rows(ops[0]), conv_b)], axis=1
        )
        normed = (pre_both - centers) * scales
        activ = normed * gain_vec + bias_vec
        slope_in = grad_res.astype(jnp.float32) * smooth_slope(activ[:, :C_OUT] + activ[:, C_OUT:])
        both = jnp.concatenate([slope_in, slope_in], axis=1)
        return (
            pack(both),
            pack(normed),
            zero_scr,
            jnp.sum(both, axis=0),
            jnp.sum(both * normed, axis=0),
        )

    def bwd_a_three(ops):
        conv_a = flat_weights[: C_MID * C_OUT].reshape(C_MID, C_OUT)
        centers, scales = (ops[3], ops[4])
        gain_vec, bias_vec, gate_val = (ops[8], ops[9], ops[11])
        normed = (matmul(ops[1], conv_a) - centers[:C_OUT]) * scales[:C_OUT]
        joined = ops[2].astype(jnp.float32) + normed * gain_vec[:C_OUT] + bias_vec[:C_OUT]
        through = ops[7].astype(jnp.float32) * gate_val * smooth_slope(joined)
        return (
            pack(through),
            pack(normed),
            zero_scr,
            place(jnp.sum(through, axis=0), 0),
            place(jnp.sum(through * normed, axis=0), 0),
        )

    def bwd_b_double(args, conv_b, rows_first, side_len, stride, offset):
        ops, first_buf, second_buf, third_buf, sum_bias, sum_gain, acc = args
        scales = ops[4]
        gain_vec, bias_vec, mask_vec, valid = (ops[8], ops[9], ops[10], ops[12])
        slope_two = unpack(first_buf, rows_out, C_MID)
        norm_two = unpack(second_buf, rows_out, C_MID)
        norm_one = unpack(third_buf, rows_first, C_MID)
        grad_two = norm_grad(
            slope_two,
            norm_two,
            gain_vec[C_MID : 2 * C_MID],
            scales[C_MID : 2 * C_MID],
            sum_bias[C_MID : 2 * C_MID],
            sum_gain[C_MID : 2 * C_MID],
            total_out,
        )
        act_one = norm_one * gain_vec[:C_MID] + bias_vec[:C_MID]
        hidden_one = (smooth(act_one) * mask_vec).astype(jnp.bfloat16)
        columns = patches(hidden_one.reshape(IMG_B, side_len, side_len, C_MID), stride)
        acc = add_weight(acc, matmul_left_t(columns, grad_two), offset, valid)
        hid_grad = unpatch(
            matmul_right_t(grad_two, conv_b), IMG_B, side_len, stride, C_MID
        ).reshape(rows_first, C_MID)
        slope_one = hid_grad * mask_vec * smooth_slope(act_one)
        return (
            pack(slope_one),
            second_buf,
            third_buf,
            place(jnp.sum(slope_one, axis=0), 0),
            place(jnp.sum(slope_one * norm_one, axis=0), 0),
            acc,
        )

    def bwd_b_zero(args):
        conv_a, conv_b = weights_zero()
        return bwd_b_double(args, conv_b, rows_in, SIDE, 2, C_IN * C_MID)

    def bwd_b_two(args):
        conv_a, conv_b = weights_two()
        return bwd_b_double(args, conv_b, rows_out, OSIDE, 1, C_OUT * C_MID)

    def bwd_b_pass(args):
        return (args[1], args[2], args[3], zero_wide, zero_wide, args[6])

    def side_none():
        return zero_input

    def bwd_c_zero(args):
        ops, first_buf, second_buf, third_buf, sum_bias, sum_gain, acc = args
        conv_a, conv_b = weights_zero()
        scales, gain_vec, valid = (ops[4], ops[8], ops[12])
        flat_in = ops[0].reshape(rows_in, C_IN)
        slope_one = unpack(first_buf, rows_in, C_MID)
        norm_one = unpack(third_buf, rows_in, C_MID)
        grad_one = norm_grad(
            slope_one,
            norm_one,
            gain_vec[:C_MID],
            scales[:C_MID],
            sum_bias[:C_MID],
            sum_gain[:C_MID],
            total_in,
        )
        acc = add_weight(acc, matmul_left_t(flat_in, grad_one), 0, valid)
        side_out = matmul_right_t(grad_one, conv_a).reshape(IMG_B, PIX_IN, C_IN)
        return (zero_mid, zero_res, acc, side_out)

    def bwd_c_one(args):
        ops, first_buf, second_buf, third_buf, sum_bias, sum_gain, acc = args
        conv_a, conv_b = weights_one()
        scales, gain_vec, valid = (ops[4], ops[8], ops[12])
        short_in = short_rows(ops[0])
        both = unpack(first_buf, rows_out, wide)
        normed = unpack(second_buf, rows_out, wide)
        grad_both = norm_grad(both, normed, gain_vec, scales, sum_bias, sum_gain, total_out)
        acc = add_weight(acc, matmul_left_t(ops[1], grad_both[:, :C_OUT]), 0, valid)
        acc = add_weight(acc, matmul_left_t(short_in, grad_both[:, C_OUT:]), C_MID * C_OUT, valid)
        mid_grad = matmul_right_t(grad_both[:, :C_OUT], conv_a).astype(jnp.bfloat16)
        short_grad = matmul_right_t(grad_both[:, C_OUT:], conv_b).reshape(
            IMG_B, OSIDE, 1, OSIDE, 1, C_IN
        )
        side_out = jnp.pad(short_grad, ((0, 0), (0, 0), (0, 1), (0, 0), (0, 1), (0, 0))).reshape(
            IMG_B, PIX_IN, C_IN
        )
        return (mid_grad, zero_res, acc, side_out)

    def bwd_c_two(args):
        ops, first_buf, second_buf, third_buf, sum_bias, sum_gain, acc = args
        conv_a, conv_b = weights_two()
        scales, grad_res, gain_vec, valid = (ops[4], ops[6], ops[8], ops[12])
        slope_four = unpack(first_buf, rows_out, C_MID)
        norm_four = unpack(third_buf, rows_out, C_MID)
        grad_four = norm_grad(
            slope_four,
            norm_four,
            gain_vec[:C_MID],
            scales[:C_MID],
            sum_bias[:C_MID],
            sum_gain[:C_MID],
            total_out,
        )
        acc = add_weight(acc, matmul_left_t(ops[2], grad_four), 0, valid)
        carried_grad = (grad_res.astype(jnp.float32) + matmul_right_t(grad_four, conv_a)).astype(
            jnp.bfloat16
        )
        return (zero_mid, carried_grad, acc, side_none())

    def bwd_c_three(args):
        ops, first_buf, second_buf, third_buf, sum_bias, sum_gain, acc = args
        conv_a = flat_weights[: C_MID * C_OUT].reshape(C_MID, C_OUT)
        scales, gain_vec, gate_val, valid = (ops[4], ops[8], ops[11], ops[12])
        through = unpack(first_buf, rows_out, C_OUT)
        normed = unpack(second_buf, rows_out, C_OUT)
        res_grad = (through + (1.0 - gate_val) * ops[7].astype(jnp.float32)).astype(jnp.bfloat16)
        grad_six = norm_grad(
            through,
            normed,
            gain_vec[:C_OUT],
            scales[:C_OUT],
            sum_bias[:C_OUT],
            sum_gain[:C_OUT],
            total_out,
        )
        acc = add_weight(acc, matmul_left_t(ops[1], grad_six), 0, valid)
        mid_grad = matmul_right_t(grad_six, conv_a).astype(jnp.bfloat16)
        return (mid_grad, res_grad, acc, side_none())

    def select_params(micro_idx):
        block_id = section_idx // 2
        width_val = width[micro_idx, block_id]
        set_val = bn_set[micro_idx, block_id]
        onehot = (jnp.arange(NSETS) == set_val).astype(jnp.float32)
        gain_vec = jnp.sum(onehot[:, None] * gain_table, axis=0)
        bias_vec = jnp.sum(onehot[:, None] * bias_table, axis=0)
        mask_vec = (jnp.arange(C_MID) < width_val).astype(jnp.float32)
        gate_val = gate[micro_idx].astype(jnp.float32)
        return (gain_vec, bias_vec, mask_vec, gate_val, onehot)

    fwd_first = [fwd_a_zero, fwd_a_one, fwd_a_two, fwd_a_three]
    fwd_second = [fwd_b_zero, fwd_b_pass, fwd_b_two, fwd_b_pass]
    fwd_third = [fwd_c_zero, fwd_c_one, fwd_c_two, fwd_c_three]
    bwd_first = [bwd_a_zero, bwd_a_one, bwd_a_two, bwd_a_three]
    bwd_second = [bwd_b_zero, bwd_b_pass, bwd_b_two, bwd_b_pass]
    bwd_third = [bwd_c_zero, bwd_c_one, bwd_c_two, bwd_c_three]

    def forward_tick(tick_no, state_in):
        recv_mid, recv_res, stash_mid, stash_res, stash_center, stash_scale, out_rows = state_in
        micro_raw = tick_no - section_idx
        is_valid = (micro_raw >= 0) & (micro_raw < MB)
        micro_idx = jnp.clip(micro_raw, 0, MB - 1)
        gain_vec, bias_vec, mask_vec, gate_val, onehot = select_params(micro_idx)
        ops = (image_blocks[micro_idx], recv_mid, recv_res, gain_vec, bias_vec, mask_vec, gate_val)
        scratch, sums_local, squares_local = lax.switch(section_idx, fwd_first, ops)
        sum_first, square_first = group_moments(sums_local, squares_local)
        scratch, sums_local, squares_local = lax.switch(
            section_idx, fwd_second, (ops, scratch, sum_first, square_first)
        )
        sum_second, square_second = group_moments(sums_local, squares_local)
        send_mid, send_res, centers, scales, result = lax.switch(
            section_idx,
            fwd_third,
            (ops, scratch, sum_first + sum_second, square_first + square_second),
        )
        stash_mid = stash_mid.at[micro_idx].set(jnp.where(is_valid, recv_mid, stash_mid[micro_idx]))
        stash_res = stash_res.at[micro_idx].set(jnp.where(is_valid, recv_res, stash_res[micro_idx]))
        stash_center = stash_center.at[micro_idx].set(
            jnp.where(is_valid, centers, stash_center[micro_idx])
        )
        stash_scale = stash_scale.at[micro_idx].set(
            jnp.where(is_valid, scales, stash_scale[micro_idx])
        )
        out_rows = out_rows.at[micro_idx].set(jnp.where(is_valid, result, out_rows[micro_idx]))
        recv_mid, recv_res = (
            shifted(for_sending(send_mid), "pipe", 1).astype(send_mid.dtype),
            shifted(for_sending(send_res), "pipe", 1).astype(send_res.dtype),
        )
        return (recv_mid, recv_res, stash_mid, stash_res, stash_center, stash_scale, out_rows)

    forward_init = (
        zero_mid,
        zero_res,
        jnp.zeros((MB, rows_out, C_MID), jnp.bfloat16),
        jnp.zeros((MB, rows_out, C_OUT), jnp.bfloat16),
        jnp.zeros((MB, wide), jnp.float32),
        jnp.zeros((MB, wide), jnp.float32),
        jnp.zeros((MB, rows_out, C_OUT), jnp.float32),
    )
    forward_state = lax.fori_loop(0, MB + pipe_count - 1, forward_tick, forward_init)
    unused_mid, unused_res, stash_mid, stash_res, stash_center, stash_scale, out_rows = (
        forward_state
    )

    def backward_tick(tick_no, state_in):
        grad_mid, grad_res, weight_acc, gain_acc, bias_acc, input_acc = state_in
        micro_raw = tick_no - (pipe_count - 1 - section_idx)
        is_valid = (micro_raw >= 0) & (micro_raw < MB)
        micro_idx = jnp.clip(micro_raw, 0, MB - 1)
        gain_vec, bias_vec, mask_vec, gate_val, onehot = select_params(micro_idx)
        ops = (
            image_blocks[micro_idx],
            stash_mid[micro_idx],
            stash_res[micro_idx],
            stash_center[micro_idx],
            stash_scale[micro_idx],
            grad_mid,
            grad_res,
            cotangent[micro_idx],
            gain_vec,
            bias_vec,
            mask_vec,
            gate_val,
            is_valid,
        )
        first_buf, second_buf, third_buf, bias_one, gain_one = lax.switch(
            section_idx, bwd_first, ops
        )
        sum_bias_one, sum_gain_one = group_grad_sums(bias_one, gain_one)
        first_buf, second_buf, third_buf, bias_two, gain_two, weight_acc = lax.switch(
            section_idx,
            bwd_second,
            (ops, first_buf, second_buf, third_buf, sum_bias_one, sum_gain_one, weight_acc),
        )
        sum_bias_two, sum_gain_two = group_grad_sums(bias_two, gain_two)
        send_mid, send_res, weight_acc, side_out = lax.switch(
            section_idx,
            bwd_third,
            (
                ops,
                first_buf,
                second_buf,
                third_buf,
                sum_bias_one + sum_bias_two,
                sum_gain_one + sum_gain_two,
                weight_acc,
            ),
        )
        gain_grad = gain_one + gain_two
        bias_grad = bias_one + bias_two
        gain_acc = jnp.where(is_valid, gain_acc + onehot[:, None] * gain_grad[None, :], gain_acc)
        bias_acc = jnp.where(is_valid, bias_acc + onehot[:, None] * bias_grad[None, :], bias_acc)
        input_acc = jax.tree.map(
            lambda stored, fresh: stored.at[micro_idx].set(
                jnp.where(is_valid, fresh, stored[micro_idx])
            ),
            input_acc,
            side_out,
        )
        grad_mid, grad_res = (
            shifted(for_sending(send_mid), "pipe", -1).astype(send_mid.dtype),
            shifted(for_sending(send_res), "pipe", -1).astype(send_res.dtype),
        )
        return (grad_mid, grad_res, weight_acc, gain_acc, bias_acc, input_acc)

    side_init = jnp.zeros((MB, IMG_B, PIX_IN, C_IN), jnp.float32)
    backward_init = (
        zero_mid,
        zero_res,
        jnp.zeros((P_SIZE,), jnp.float32),
        jnp.zeros((NSETS, wide), jnp.float32),
        jnp.zeros((NSETS, wide), jnp.float32),
        side_init,
    )
    backward_state = lax.fori_loop(0, MB + pipe_count - 1, backward_tick, backward_init)
    unused_gmid, unused_gres, weight_acc, gain_acc, bias_acc, input_acc = backward_state
    grad_images, output_sum = (
        lax.psum_scatter(
            input_acc.reshape(IMG_DEV, PIX_IN, C_IN).astype(jnp.bfloat16),
            "pipe",
            scatter_dimension=2,
            tiled=True,
        ).astype(jnp.float32),
        lax.psum_scatter(
            out_rows.astype(jnp.bfloat16), "pipe", scatter_dimension=2, tiled=True
        ).astype(jnp.float32),
    )
    output_part = output_sum.astype(jnp.bfloat16)
    norm_grads = jnp.concatenate([gain_acc.reshape(-1), bias_acc.reshape(-1)])
    weight_sum, norm_sum = lax.psum((weight_acc, norm_grads), ("dp", "rep"))
    grad_gain = norm_sum[: NSETS * wide].reshape(1, NSETS, wide)
    grad_bias = norm_sum[NSETS * wide :].reshape(1, NSETS, wide)
    return (output_part, grad_images, weight_sum.reshape(1, P_SIZE), grad_gain, grad_bias)


PP = PIX_OUT + 1
RW = 8 * PP
RV = 8 * PIX_OUT
BLK = 512
SUB = 65536
F32 = jnp.float32
BF16 = jnp.bfloat16
MESH = pl.DeviceIdType.MESH

E_WIDE, E_WIDE_NEXT = 2, 6
C_H2, C_H4, C_D5, C_D4, C_DH = range(10, 15)
C_O1, C_SHARE, C_GI, C_GP = 15, 19, 22, 25
C_PAR2, C_PAR3, C_DG2, C_DG3, C_BN1, C_BN2, C_BN3, C_BN4 = range(28, 36)
N_SEM = 36
N_PIECE = 17
W_OWN, W_PEER, W_Z, W_ON, W_VIA = range(5)
VIA, HALF = 8, 11
W_BASE = (0, 17, 34, 45, -VIA)
S_CORE, S_IN, S_OUT, S_HAND, S_BACK, S_DONE, S_ACROSS, N_SUM_SEND = 0, 1, 2, 3, 4, 5, 9, 25
R_CORE, R_Z, R_ACROSS, R_GIVE = (0, 8), (8, 24), (32, 16), (48, 4)
R_DONE, R_BACK, R_BACK_HUB, R_HAND, N_SUM_RECV = 52, 53, 54, 55, 75
HUB_GUEST = 8704
RING = 8
SUBS = 2
SUB_ROWS = 256 // SUBS
HOPS = 2
HOP_ROWS = SUB_ROWS // HOPS
Z1_ZERO = 3136
ACROSS_LAG, OUT_LAG = 3 * SUBS // 2 + 1, 4 * SUBS
LAST_TURN = OUT_LAG - 2


def nn(a, b):
    return jnp.dot(a, b, preferred_element_type=F32)


def nt(a, b):
    return lax.dot_general(a, b, (((1,), (1,)), ((), ())), preferred_element_type=F32)


def tn(a, b):
    return lax.dot_general(a, b, (((0,), (0,)), ((), ())), preferred_element_type=F32)


def sigmoid(v):
    return 0.5 + 0.5 * jnp.tanh(0.5 * v)


def rows(start, size):
    return pl.ds(start if isinstance(start, int) else pl.multiple_of(start, 16), size)


def whole_kernel(
    img, wts, gain_in, bias_in, width, sets, gates, cot,
    out, gi, dw, dgb_out,
    imgb, raw, st, wh, wx, f0, f1, f2, f3, fs, pb, pt, u0, u1, u2, sx, cotb,
    h2, h4, h5, d5, d4, dh, r0, r1, ob, tx, rx, inv, par, parx, dg, dgx, sb, rd, bz, dgs, dgb, v_out, gain, bias,
    ls, ss, rs, wss, ass, ars, ready, go,
):
    p, d, r = lax.axis_index("pipe"), lax.axis_index("dp"), lax.axis_index("rep")
    peer = (p, 1 - d, r)
    z_pair = r + 1 - 2 * lax.rem(r, 2)
    quarter = 2 * lax.rem(r, 2) + d

    def remote(src, dst, send, recv, device):
        return pltpu.make_async_remote_copy(
            src_ref=src, dst_ref=dst, send_sem=ss.at[send], recv_sem=rs.at[recv],
            device_id=device, device_id_type=MESH,
        )

    def sync(event, first, count):
        part = pl.ds(first, count)
        copy = remote(tx.at[part], rx.at[part], event, event, peer)
        copy.start()
        copy.wait()

    def exchange_of(event, first, count):
        part = pl.ds(first, count)
        return remote(tx.at[part], rx.at[part], event, event, peer)

    def both(slot):
        return tx[slot] + rx[slot]

    def moments(slot_sum, slot_square, total, inv_slot):
        center = both(slot_sum) * (1.0 / total)
        scale = lax.rsqrt(both(slot_square) * (1.0 / total) - center * center + EPSILON)
        inv[inv_slot] = scale
        return center, scale

    def silu(v):
        return v * sigmoid(v)

    def slope(v):
        s = sigmoid(v)
        return s + v * s * (1.0 - s)

    def clear_pad(ref, first):
        tile = ref[rows(first + RW - 16, 16), :].astype(F32)
        keep = lax.broadcasted_iota(jnp.int32, tile.shape, 0) < 8
        ref[rows(first + RW - 16, 16), :] = jnp.where(keep, tile, 0.0).astype(BF16)

    def per_row(value_of):
        row = lax.broadcasted_iota(jnp.int32, (8, BLK), 0)
        out = jnp.zeros((8, BLK), jnp.int32)
        for m in range(MB):
            out = jnp.where(row == m, value_of(m), out)
        return out

    def mask_of(block):
        lane = lax.broadcasted_iota(jnp.int32, (8, BLK), 1)
        return (lane < per_row(lambda m: width[block, m])).astype(F32)

    def five(body, init=0, unrolled=False):
        if unrolled:
            for c in range(5):
                init = body(pl.ds(c * 10, 10), c, init)
            return init
        return lax.fori_loop(0, 5, lambda c, carry: body(pl.ds(c * 10, 10), c, carry), init)

    def add_stats(carry, a, b):
        return carry[0] + jnp.sum(a, axis=0), carry[1] + jnp.sum(b, axis=0)

    zero_stats = (jnp.zeros((8, BLK), F32), jnp.zeros((8, BLK), F32))

    def store_z(ref, first, z, slot_sum, slot_square):
        z3 = z.reshape(PP, 8, BLK) if z.ndim == 2 else z
        ref[pl.ds(first, PP)] = z3
        tx[slot_sum] = jnp.sum(z3, axis=0)
        tx[slot_square] = jnp.sum(z3 * z3, axis=0)

    def raw_copy(turn, element_of):
        slot = lax.rem(turn, RING)
        return pltpu.make_async_copy(
            wts.at[:, pl.ds(pl.multiple_of(element_of(turn) * SUB, SUB), SUB)], raw.at[slot], ls.at[8 + slot]
        )

    def open_weights(element_of, total):
        for turn in range(min(RING - 1, total)):
            raw_copy(turn, element_of).start()

    def load_weights(element_of, total, first, count, put):
        def body(k, carry):
            turn = first + k

            @pl.when(turn + RING - 1 < total)
            def _():
                raw_copy(turn + RING - 1, element_of).start()

            raw_copy(turn, element_of).wait()
            st[0:512] = raw[lax.rem(turn, RING)].astype(F32).reshape(512, 128)
            put(turn)
            return carry

        lax.fori_loop(0, count, body, 0)

    def put_narrow(ref, row_of):
        def put(i):
            for j in range(4):
                ref[rows(row_of(i), 128), j * 128 : (j + 1) * 128] = st[
                    pl.ds(j, 128, stride=4), :
                ].astype(BF16)

        return put

    def put_wide(ref, base, block_rows, first):
        def put(i):
            for n in range(4):
                for j in range(4):
                    ref[rows(base + n * block_rows + (i - first) * 32, 32), j * 128 : (j + 1) * 128] = st[
                        pl.ds(4 * n + j, 32, stride=16), :
                    ].astype(BF16)

        return put

    def put_chunk(row, n, block):
        size = SUB_ROWS // 4
        for part in range(2 * SUBS):
            wh[rows(row + part * SUB_ROWS + n * size, size), :] = block[part * size : (part + 1) * size].astype(BF16)

    def plain(turn):
        return turn

    def own_parts(turn):
        late = turn - HALF
        return jnp.where(late < 0, 4 * turn + quarter, 4 * HALF + (late // 2) * 4 + 2 * d + lax.rem(late, 2))

    def half_rows(turn):
        return 8 * d + turn

    def piece_copy(kind, i, q, device):
        part = wx.at[rows(i * 512 + q * 128, 128)]
        return pltpu.make_async_remote_copy(
            src_ref=part, dst_ref=part, send_sem=wss.at[kind], recv_sem=ars.at[W_BASE[kind] + i],
            device_id=device, device_id_type=MESH,
        )

    def half_copy(kind, i, which, device):
        part = wx.at[rows(i * 512 + which * 256, 256)]
        order = min(i, 13) if kind == W_VIA else i
        return pltpu.make_async_remote_copy(
            src_ref=part, dst_ref=part, send_sem=wss.at[kind], recv_sem=ars.at[W_BASE[kind] + order],
            device_id=device, device_id_type=MESH,
        )

    def all_sent(semaphore, ref):
        pltpu.make_async_remote_copy(
            src_ref=ref, dst_ref=ref, send_sem=semaphore, recv_sem=rs.at[0], device_id=peer, device_id_type=MESH
        ).wait_send()

    def all_here(semaphore, ref):
        pltpu.make_async_remote_copy(
            src_ref=ref, dst_ref=ref, send_sem=ss.at[0], recv_sem=semaphore, device_id=peer, device_id_type=MESH
        ).wait_recv()

    def o1_copy(n, chip):
        part = u0.at[n * RW : (n + 1) * RW]
        return remote(part, part, C_O1 + n, C_O1 + n, (chip, d, r))

    def each(work, first, last):
        def body(i, carry):
            work(i)
            return carry

        lax.fori_loop(first, last, body, 0)

    def img_copy(q, slot):
        return pltpu.make_async_copy(img.at[pl.ds(q * 28, 28)], imgb.at[slot], ls.at[slot])

    def open_images():
        for q in range(3):
            img_copy(q, q).start()

    def over_images(body, init):
        def step(q, carry):
            slot = lax.rem(q, 4)

            @pl.when(q + 3 < 7)
            def _():
                img_copy(q + 3, lax.rem(q + 3, 4)).start()

            img_copy(q, slot).wait()
            return body(q, slot, carry)

        return lax.fori_loop(0, 7, step, init)

    outer = (r == 0) | (r == 3)
    inner = jnp.logical_not(outer)
    z_dev, across = (p, d, z_pair), (p, d, 3 - r)

    def grad_copy(send, recv, src, dst, device):
        return pltpu.make_async_remote_copy(
            src_ref=src, dst_ref=dst, send_sem=ass.at[send], recv_sem=ars.at[recv],
            device_id=device, device_id_type=MESH,
        )

    def in_turn(ring, u):
        return ring[0] + lax.rem(u, ring[1])

    def zero_rest(first, source):
        source[...] = jnp.zeros(source.shape, BF16)

        def body(i, carry):
            copy = pltpu.make_async_copy(source, dw.at[pl.ds((first + i) * 4, 4)], ls.at[18])
            copy.start()
            copy.wait()
            return carry

        lax.fori_loop(0, 13 - first, body, 0)

    def bn_sums():
        for k in range(NSETS):
            hot = (set_of == k).astype(F32)
            for n in range(8):
                cols = slice(n * BLK, (n + 1) * BLK)
                dgs[k : k + 1, cols] = jnp.sum(dg[n] * hot, axis=0, keepdims=True)
                dgs[4 + k : 5 + k, cols] = jnp.sum(dg[8 + n] * hot, axis=0, keepdims=True)

    def norm_half(channels):
        return pl.ds(pl.multiple_of(d * (channels // 2), 512), channels // 2)

    def bn_in(cols):
        return remote(dgs.at[:, cols], bz.at[0, :, cols], C_BN1, C_BN1, z_dev)

    def bn_across(cols):
        return remote(dgs.at[:, cols], bz.at[1, :, cols], C_BN2, C_BN2, across)

    def bn_out(cols):
        return remote(dgb.at[:, cols], bz.at[0, :, cols], C_BN3, C_BN3, z_dev)

    def bn_core(cols):
        return remote(dgb.at[:, cols], dgb.at[:, cols], C_BN4, C_BN4, peer)

    def say_ready():
        pl.semaphore_signal(ready.at[0], inc=1, device_id=z_dev, device_id_type=MESH)

        @pl.when(inner)
        def _():
            pl.semaphore_signal(ready.at[1], inc=1, device_id=across, device_id_type=MESH)

    def sum_gradients(
        count, compute, at_row, chunk_of, wide, z1, extra,
        lend=(), passed=(), helper=None, helper_turn=None, helper_row=None, handed_in=None, lent_by=None, computed=None, packed_here=None,
        norms_at=0, norms=4096, after=None, back=R_BACK, late_back=0,
    ):
        turns = SUBS * count
        last_lent = SUBS * (count + len(lend))
        last_given = last_lent + SUBS * len(passed)
        computed = (0, count) if computed is None else computed
        packed_here = (0, count) if packed_here is None else packed_here
        cols = norm_half(norms)
        first_own, own_turns = packed_here[0] * SUBS, packed_here[1] * SUBS
        z2 = z1 + last_given * SUB_ROWS

        def when_own(u, work):
            if handed_in is None:
                work()
            else:
                pl.when(jnp.logical_not(handed_in(u // SUBS)))(work)

        def when_handed(u, work):
            if handed_in is not None:
                pl.when(handed_in(u // SUBS))(work)

        def when_kept(u, work):
            if lent_by is None:
                work()
            else:
                pl.when(jnp.logical_not(lent_by[0](u // SUBS)))(work)

        def when_lent(u, work):
            if lent_by is not None:
                pl.when(lent_by[0](u // SUBS))(work)

        def half(u, which):
            return wh.at[rows(at_row(u // SUBS) + which * 256 + lax.rem(u, SUBS) * SUB_ROWS, SUB_ROWS)]

        def half_part(u, k):
            first = at_row(u // SUBS) + d * 256 + lax.rem(u, SUBS) * SUB_ROWS + k * HOP_ROWS
            return wh.at[rows(first, HOP_ROWS)]

        def from_z(u):
            return wx.at[rows(z1 + u * SUB_ROWS, SUB_ROWS)]

        def from_z_part(u, k):
            return wx.at[rows(z1 + u * SUB_ROWS + k * HOP_ROWS, HOP_ROWS)]

        def from_across(u, k):
            return wx.at[rows(z2 + u * SUB_ROWS + k * HOP_ROWS, HOP_ROWS)]

        def from_core(u):
            return rd.at[rows(u * SUB_ROWS, SUB_ROWS)]

        def to_core(u):
            recv = jnp.where(u < turns, in_turn(R_CORE, u), in_turn(R_GIVE, u))
            return grad_copy(S_CORE, recv, half(u, 1 - d), from_core(u), peer)

        def inwards(u, k):
            return grad_copy(S_IN, in_turn(R_Z, u * HOPS + k), half_part(u, k), from_z_part(u, k), z_dev)

        def exchange(u, k):
            turn = u * HOPS + k
            return grad_copy(
                S_ACROSS + lax.rem(turn, 16), in_turn(R_ACROSS, turn), half_part(u, k), from_across(u, k), across
            )

        def outwards(u, k):
            return grad_copy(S_OUT, in_turn(R_Z, u * HOPS + k), half_part(u, k), from_z_part(u, k), z_dev)

        def packed(u, which):
            return dw.at[chunk_of(u // SUBS) * 4 + which * 2 + lax.rem(u, SUBS)]

        def done_core(u, turn):
            slot = lax.rem(turn, 4)
            return grad_copy(S_DONE + slot, R_DONE, sb.at[slot], packed(u, d), peer)

        def done_here(u, turn):
            slot = lax.rem(turn, 4)
            return pltpu.make_async_copy(sb.at[slot], packed(u, d), ls.at[4 + slot])

        def add(mine, other):
            sums = mine[...].astype(F32) + other[...].astype(F32)
            mine[...] = sums.astype(BF16)

        def pack(u, turn, ref):
            @pl.when(turn >= 4)
            def _():
                done_here(u, turn).wait()
                done_core(u, turn).wait_send()

            value = ref[...].astype(F32)
            for j in range(4):
                cols = slice(j * 128, (j + 1) * 128)
                if wide:
                    for n in range(4):
                        part = SUB_ROWS // 4
                        st[pl.ds(4 * n + j, part, stride=16), :] = value[n * part : (n + 1) * part, cols]
                else:
                    st[pl.ds(j, SUB_ROWS, stride=4), :] = value[:, cols]
            sb[lax.rem(turn, 4)] = st[...].astype(BF16)
            done_here(u, turn).start()
            done_core(u, turn).start()

        def hand(u):
            t, part = u // SUBS, lax.rem(u, SUBS)
            theirs = helper_turn(t) * SUBS + part
            row = helper_turn(t) * 512 if helper_row is None else helper_row(t)
            place = wh.at[rows(row + d * 256 + part * SUB_ROWS, SUB_ROWS)]
            return grad_copy(S_HAND, R_HAND + theirs, half(u, d), place, (helper(t), d, r))

        def handed(u):
            return grad_copy(S_HAND, R_HAND + u, half(u, d), half(u, d), (p, d, r))

        def give_back(u, ref):
            t = u // SUBS
            theirs = lent_by[2](t) * SUBS + lax.rem(u, SUBS)
            place = wx.at[rows(jnp.where(lent_by[1](t) == 0, Z1_ZERO, 0) + theirs * SUB_ROWS, SUB_ROWS)]
            return grad_copy(S_BACK, back, ref, place, (lent_by[1](t), d, r))

        def finish(u, ref):
            when_kept(u, lambda: pack(u, u - first_own, ref))
            when_lent(u, lambda: give_back(u, ref).start())

        def give(t):
            compute(t)
            for k in range(SUBS):
                to_core(t * SUBS + k).start()
            for k in range(SUBS):
                u = t * SUBS + k
                to_core(u).wait_recv()
                add(half(u, d), from_core(u))
                hand(u).start()

        def unit_rows(units):
            return wh.at[0 : units * SUB_ROWS]

        take_at = turns + OUT_LAG - (last_lent - turns)

        def step(it, carry):
            for when, work in extra.items():
                pl.when(it == when)(work)
            for k, when in enumerate(lend + passed):
                pl.when(it == when)(lambda k=k: give(jnp.int32(count + k)))

            def start():
                @pl.when(lax.rem(it, SUBS) == 0)
                def _():
                    compute(it // SUBS)

                to_core(it).start()

            @pl.when(it < turns)
            def _():
                when_own(it, start)

            u1 = it - 1

            @pl.when((u1 >= 0) & (u1 < turns))
            def _():
                def join_cores():
                    to_core(u1).wait_recv()
                    add(half(u1, d), from_core(u1))

                when_own(u1, join_cores)
                when_handed(u1, lambda: handed(u1).wait_recv())

                @pl.when(outer & (u1 == 0))
                def _():
                    pl.semaphore_wait(ready.at[0], 1)

                @pl.when(outer)
                def _():
                    for k in range(HOPS):
                        inwards(u1, k).start()

            u2 = it - 2

            @pl.when(inner & (u2 >= 0) & (u2 < turns))
            def _():
                @pl.when(u2 == 0)
                def _():
                    pl.semaphore_wait(ready.at[1], 1)

                for k in range(HOPS):
                    inwards(u2, k).wait_recv()
                    add(half_part(u2, k), from_z_part(u2, k))
                    exchange(u2, k).start()

            u4 = it - ACROSS_LAG

            @pl.when(inner & (u4 >= 0) & (u4 < turns))
            def _():
                @pl.when(u4 == 0)
                def _():
                    pl.semaphore_wait(ready.at[0], 1)

                for k in range(HOPS):
                    exchange(u4, k).wait()
                    add(half_part(u4, k), from_across(u4, k))
                    outwards(u4, k).start()

                finish(u4, half(u4, d))

            u8 = it - OUT_LAG

            @pl.when(outer & (u8 >= 0) & (u8 < turns))
            def _():
                for k in range(HOPS):
                    outwards(u8, k).wait_recv()

                finish(u8, from_z(u8))

            @pl.when(it == norms_at)
            def _():
                bn_sums()

                @pl.when(outer)
                def _():
                    bn_in(cols).start()

            @pl.when(inner & (it == norms_at + 4))
            def _():
                bn_in(cols).wait_recv()
                dgs[:, cols] += bz[0, :, cols]
                bn_across(cols).start()

            @pl.when(inner & (it == norms_at + 8))
            def _():
                bn_across(cols).wait()
                dgb[:, cols] = dgs[:, cols] + bz[1, :, cols]
                bn_out(cols).start()
                bn_core(cols).start()

            @pl.when(outer & (it == norms_at + 14))
            def _():
                bn_out(cols).wait_recv()
                dgb[:, cols] = bz[0, :, cols]
                bn_core(cols).start()

            for when, work in (after or {}).items():
                pl.when(it == when)(work)

            if lend:
                u_back = turns + it - take_at

                late_units = late_back * SUBS

                @pl.when(it == take_at)
                def _():
                    all_here(ars.at[R_BACK], unit_rows(last_lent - turns - late_units))

                if late_units:

                    @pl.when(u_back == last_lent - late_units)
                    def _():
                        all_here(ars.at[R_BACK_HUB], unit_rows(late_units))

                @pl.when((u_back >= turns) & (u_back < last_lent))
                def _():
                    pack(u_back, own_turns + u_back - turns, from_z(u_back))

            return carry

        lax.fori_loop(0, turns + OUT_LAG, step, 0)

        bn_core(cols).wait()

        @pl.when(outer)
        def _():
            bn_in(cols).wait_send()

        @pl.when(inner)
        def _():
            bn_out(cols).wait_send()

        @pl.when(outer)
        def _():
            all_sent(ass.at[S_IN], unit_rows(turns))

        @pl.when(inner)
        def _():
            all_sent(ass.at[S_OUT], unit_rows(turns))

        made = computed[1] * SUBS + last_given - turns
        if made:
            all_sent(ass.at[S_CORE], unit_rows(made))
        if last_given > turns:
            all_sent(ass.at[S_HAND], unit_rows(last_given - turns))
        if lent_by is not None:
            all_sent(ass.at[S_BACK], unit_rows(lent_by[3] * SUBS))
        all_here(ars.at[R_DONE], dw.at[pl.ds(0, own_turns + last_lent - turns)])
        for slot in range(4):
            done_here(first_own, jnp.int32(slot)).wait()
            done_core(first_own, jnp.int32(slot)).wait_send()

    tables = [
        pltpu.make_async_copy(gain_in, gain, ls.at[17]),
        pltpu.make_async_copy(bias_in, bias, ls.at[18]),
    ]
    for copy in tables:
        copy.start()

    @pl.when(p == 0)
    def _():
        open_weights(plain, 44)
        open_images()

    @pl.when(p == 1)
    def _():
        open_weights(plain, 48)
        open_images()
        pltpu.make_async_copy(cot, cotb.at[0:PIX_OUT], ls.at[16]).start()

    @pl.when(p == 2)
    def _():
        open_weights(own_parts, 15)

    @pl.when(p == 3)
    def _():
        open_weights(half_rows, 8)

    barrier = pltpu.get_barrier_semaphore()
    for device in (peer, (p, d, z_pair), (p, d, 3 - r)) + tuple((lax.rem(p + k, 4), d, r) for k in (1, 2, 3)):
        pl.semaphore_signal(barrier, inc=1, device_id=device, device_id_type=MESH)

    for copy in tables:
        copy.wait()
    block_two = p >= 2
    set_of = per_row(lambda m: jnp.where(block_two, sets[1, m], sets[0, m]))
    for k in range(NSETS):
        hot = (set_of == k).astype(F32)
        for n in range(8):
            g = hot * gain[k : k + 1, n * BLK : (n + 1) * BLK]
            b = hot * bias[k : k + 1, n * BLK : (n + 1) * BLK]
            if k == 0:
                par[n] = g
                par[8 + n] = b
            else:
                par[n] += g
                par[8 + n] += b
    dg[...] = jnp.zeros_like(dg)
    dgb[...] = jnp.zeros_like(dgb)
    pl.semaphore_wait(barrier, 6)

    total_in, total_out = 2.0 * PIX_IN, 2.0 * PIX_OUT

    def build_patches(base):
        def body(tap, carry):
            row, col = base(tap)
            window = pb[pl.ds(row, 7), pl.ds(col, 7)].reshape(RV, BLK)
            pt[tap, 0:RV, :] = window.astype(BF16)
            return carry

        lax.fori_loop(0, 9, body, 0)

    def clear_patch_pad():
        def body(tap, carry):
            pt[tap, RW - 16 : RW, :] = jnp.zeros((16, BLK), BF16)
            return carry

        lax.fori_loop(0, 9, body, 0)

    def strided_base(tap):
        di, dj = tap // 3, lax.rem(tap, 3)
        return lax.rem(di, 2) * 8 + di // 2, lax.rem(dj, 2) * 8 + dj // 2

    def plain_base(tap):
        return tap // 3, lax.rem(tap, 3)

    def conv(ref, first, target):
        target[...] = jnp.zeros_like(target)

        def body(tap, carry):
            z = nn(pt[tap], ref[rows(first + tap * BLK, BLK), :])
            target[...] += z.reshape(PP, 8, BLK)
            return carry

        lax.fori_loop(0, 9, body, 0)

    def conv_back(dz, ref, first, base, side):
        pb[0:side, 0:side] = jnp.zeros((side, side, 8, BLK), F32)

        def body(tap, carry):
            row, col = base(tap)
            part = nt(dz[0:RV, :], ref[rows(first + tap * BLK, BLK), :])
            pb[pl.ds(row, 7), pl.ds(col, 7)] += part.reshape(7, 7, 8, BLK)
            return carry

        lax.fori_loop(0, 9, body, 0)

    def stats_of_map(ref, slot_sum, slot_square):
        def body(c, _, carry):
            z = ref[c]
            return add_stats(carry, z, z * z)

        tx[slot_sum], tx[slot_square] = five(body, zero_stats)

    def act_to(ref, target, center, scale, g, b, mask):
        def body(c, i, carry):
            zhat = (ref[c] - center) * scale
            ref[c] = zhat
            h = silu(zhat * g + b) * mask
            target[rows(i * 80, 80), :] = h.reshape(80, BLK).astype(BF16)
            return carry

        five(body)
        clear_pad(target, 0)

    def upstream(target, grad, zhat_ref, g, b, mask, slot_sum, slot_gain):
        def body(c, i, carry):
            zhat = zhat_ref[c]
            du = grad[rows(i * 80, 80), :].astype(F32).reshape(10, 8, BLK) * mask * slope(zhat * g + b)
            target[c] = du
            return add_stats(carry, du, du * zhat)

        tx[slot_sum], tx[slot_gain] = five(body, zero_stats)

    def norm_back(target, first, du_ref, du_first, zhat_ref, zhat_first, gscale, mean_du, mean_dg, unrolled=False):
        def body(c, i, carry):
            du = du_ref[pl.ds(du_first + i * 10, 10)]
            zhat = zhat_ref[pl.ds(zhat_first + i * 10, 10)]
            dz = gscale * (du - mean_du - zhat * mean_dg)
            target[rows(first + i * 80, 80), :] = dz.reshape(80, BLK).astype(BF16)
            return carry

        five(body, unrolled=unrolled)
        clear_pad(target, first)

    def gi_copy():
        return pltpu.make_async_copy(f3.at[0:PIX_IN, :, 0:256], gi, ls.at[17])

    def out_copy():
        return pltpu.make_async_copy(v_out, out, ls.at[0])

    def dgb_copy():
        return pltpu.make_async_copy(dgb, dgb_out, ls.at[1])

    def final_part():
        @pl.when(p != 1)
        def _():
            remote(ob, ob, C_SHARE, C_SHARE, (p, d, r)).wait_recv()
            remote(r1, r1, C_GP, C_GP, (p, d, r)).wait_recv()

        @pl.when(p != 0)
        def _():
            remote(r0, r0, C_GI, C_GI, (p, d, r)).wait_recv()

        v_out[...] = ob[0:RV, :].astype(F32).reshape(PIX_OUT, 8, BLK).astype(BF16)
        out_copy().start()
        f0[0:PP, :, 0:256] = r1[...].astype(F32).reshape(PP, 8, 256)

        def place(a, carry):
            m = r0[rows(a * 224, 224), :].astype(F32).reshape(28, 8, 256)
            first = m[0:14].reshape(7, 2, 8, 256)
            even = first[:, 0] + f0[pl.ds(a * 7, 7), :, 0:256]
            f3[pl.ds(a * 28, 14), :, 0:256] = jnp.stack([even, first[:, 1]], axis=1).reshape(14, 8, 256)
            f3[pl.ds(a * 28 + 14, 14), :, 0:256] = m[14:28]
            return carry

        lax.fori_loop(0, 7, place, 0)
        gi_copy().start()

    @pl.when(p == 0)
    def _():
        mask = mask_of(0)

        def relay(i):
            piece_copy(W_VIA, i, quarter, (0, d, r)).wait_recv()
            piece_copy(W_OWN, i, quarter, (1, d, r)).start()

        def relay_half(i):
            half_copy(W_VIA, i, d, (0, d, r)).wait_recv()
            half_copy(W_OWN, i, d, (1, d, r)).start()

        put_w = put_narrow(wh, lambda i: i * 128)
        load_weights(plain, 44, 0, 8, put_w)

        def first_conv(q, slot, carry):
            rows_q = imgb[slot].astype(F32).reshape(224, 1024).astype(BF16)
            wx[rows(q * 224, 224), :] = rows_q[:, 0:512]
            wx[rows(1568 + q * 224, 224), :] = rows_q[:, 512:1024]
            z = nn(rows_q, wh[0:1024, :]).reshape(28, 8, BLK)
            f0[pl.ds(q * 28, 28)] = z
            load_weights(plain, 44, 8 + 5 * q, 5, put_w)

            @pl.when(q == 5)
            def _():
                relay(VIA)

            return add_stats(carry, z, z * z)

        tx[0], tx[1] = over_images(first_conv, zero_stats)
        exchange = remote(tx.at[pl.ds(0, 2)], rx.at[pl.ds(0, 2)], 0, 0, peer)
        exchange.start()
        pb[...] = jnp.zeros_like(pb)
        clear_patch_pad()
        load_weights(plain, 44, 43, 1, put_w)
        exchange.wait()

        center, scale = moments(0, 1, total_in, 0)
        g1, b1, g2, b2 = par[0], par[8], par[1], par[9]

        def hidden(i, carry):
            zhat = (f0[pl.ds(i * 14, 14)] - center) * scale
            f0[pl.ds(i * 14, 14)] = zhat
            h = (silu(zhat * g1 + b1) * mask).astype(BF16).astype(F32).reshape(7, 2, 8, BLK)
            u = i + 1
            row = lax.rem(u, 2) * 8 + u // 2
            pb[row, 8:15] = h[:, 0]
            pb[row, 1:8] = h[:, 1]
            return carry

        lax.fori_loop(0, 14, hidden, 0)
        relay(VIA + 1)
        build_patches(strided_base)
        conv(wh, 1024, fs.at[0])
        relay(VIA + 2)
        stats_of_map(fs.at[0], 2, 3)
        sync(1, 2, 2)
        center, scale = moments(2, 3, total_out, 1)
        act_to(fs.at[0], h2, center, scale, g2, b2, mask)
        send = remote(h2, h2, C_H2, C_H2, (1, d, r))
        send.start()
        for i in (HALF, HALF + 1, 16):
            relay_half(i)
        zero_rest(11, sb)
        send.wait_send()
        all_sent(wss.at[W_OWN], wx.at[0 : 3 * 128 + 3 * 256])
        say_ready()

        remote(dh, dh, C_DH, C_DH, (0, d, r)).wait_recv()
        upstream(fs.at[1], dh, fs.at[0], g2, b2, mask, 4, 5)
        sync(0, 4, 2)
        s_du, s_dg = both(4), both(5)
        dg[1], dg[9] = s_dg, s_du
        norm_back(d5, 0, fs.at[1], 0, fs.at[0], 0, g2 * inv[1], s_du * (1.0 / total_out), s_dg * (1.0 / total_out))
        def back_conv():
            conv_back(d5, wh, 1024, strided_base, 16)

        def slopes(i, carry):
            u = i + 1
            row = lax.rem(u, 2) * 8 + u // 2
            grad = jnp.stack([pb[row, 8:15], pb[row, 1:8]], axis=1).reshape(14, 8, BLK)
            zhat = f0[pl.ds(i * 14, 14)]
            du = grad * mask * slope(zhat * g1 + b1)
            f1[pl.ds(i * 14, 14)] = du
            return add_stats(carry, du, du * zhat)

        def first_slopes():
            tx[6], tx[7] = lax.fori_loop(0, 14, slopes, zero_stats)
            sync(1, 6, 2)
            dg[0], dg[8] = both(7), both(6)

        def first_back():
            s_du, s_dg = both(6), both(7)
            gscale, m_du, m_dg = g1 * inv[0], s_du * (1.0 / total_in), s_dg * (1.0 / total_in)

            def body(q, carry):
                part = pl.ds(q * 28, 28)
                dz = gscale * (f1[part] - m_du - f0[part] * m_dg)
                u1[rows(q * 224, 224), :] = dz.reshape(224, BLK).astype(BF16)
                return carry

            lax.fori_loop(0, 7, body, 0)

        def share(target, column, k):
            def body(q, carry):
                g = nt(u1[rows(q * 224, 224), :], wh[k * 256 : (k + 1) * 256, :])
                target[rows(q * 224, 224), column : column + 256] = g.astype(BF16)
                return carry

            lax.fori_loop(0, 7, body, 0)

        places = {1: (u0, 0), 2: (u0, 256), 3: (u2, 0)}

        def share_copy(k):
            target, column = places[k]
            return remote(target.at[0:1568, column : column + 256], r0, C_GI + k - 1, C_GI, (k, d, r))

        def share_out(k):
            share(*places[k], k)
            share_copy(k).start()

        def back_and_share():
            first_back()
            share_out(1)

        def compute(t):
            taps = (t < 6) | (t >= 8)

            @pl.when(taps)
            def _():
                tap = jnp.where(t < 6, t, t - 2)
                wh[rows(at_row(t), 512), :] = tn(pt[tap], d5[...]).astype(BF16)

            @pl.when(jnp.logical_not(taps))
            def _():
                block = tn(wx[rows((t - 6) * 1568, 1568), :], u1[0:1568, :])
                wh[rows(at_row(t), 512), :] = block.astype(BF16)

        def at_row(t):
            return jnp.where(t < 2, 5632 + t * 512, jnp.where(t < 8, t * 512, 2560 + t * 512))

        def chunk_of(t):
            return jnp.where(t < 6, t + 2, jnp.where(t < 8, t - 6, t))

        sum_gradients(
            8, compute, at_row, chunk_of, False, Z1_ZERO,
            {LAST_TURN + 8 * SUBS: final_part},
            lend=(5, 6, 7), helper=lambda t: jnp.where(t < 10, 2, 1), helper_turn=lambda t: jnp.where(t < 10, t - 1, 8),
            helper_row=lambda t: jnp.where(t < 10, (t - 1) * 512, HUB_GUEST), norms_at=4 * SUBS, norms=1024, late_back=1,
            after={
                1: back_conv,
                2: first_slopes,
                3: back_and_share,
                4: lambda: share(r0, 0, 0),
                8: lambda: share_out(3),
                10: lambda: share_out(2),
            },
        )
        for k in (1, 2, 3):
            share_copy(k).wait_send()

    @pl.when(p == 1)
    def _():
        mask = mask_of(1)
        gate_v = per_row(lambda m: gates[m]).astype(F32)
        cotb[PIX_OUT] = jnp.zeros((8, C_OUT), BF16)
        clear_patch_pad()
        load_weights(plain, 48, 0, 16, put_wide(wh, 0, 512, 0))
        load_weights(plain, 48, 16, 32, put_wide(wh, 2048, 1024, 16))

        def shorten(a, slot, carry):
            v = imgb[slot, 0:14].astype(F32).reshape(7, 2, 8, 1024)[:, 0]
            f0[pl.ds(a * 7, 7)] = v[:, :, 0:512]
            f0[pl.ds(PP + a * 7, 7)] = v[:, :, 512:1024]
            return carry

        other_z = 2 * (1 - lax.rem(r, 2))
        this_z = 2 * lax.rem(r, 2)

        def pass_own(i):
            piece_copy(W_OWN, i, quarter, (1, d, r)).wait_recv()
            piece_copy(W_PEER, i, quarter, peer).start()
            piece_copy(W_Z, i, quarter, z_dev).start()

        def pass_on(i):
            piece_copy(W_Z, i, other_z + d, peer).wait_recv()
            piece_copy(W_ON, i, other_z + d, peer).start()

        def have(i):
            piece_copy(W_PEER, i, this_z + 1 - d, peer).wait_recv()
            piece_copy(W_ON, i, other_z + 1 - d, peer).wait_recv()

        def pass_half(i):
            half_copy(W_OWN, i, d, (1, d, r)).wait_recv()
            half_copy(W_PEER, i, d, peer).start()

        def have_half(i):
            half_copy(W_PEER, i, 1 - d, peer).wait_recv()

        pass_own(0)
        over_images(shorten, 0)
        f0[PIX_OUT] = jnp.zeros((8, BLK), F32)
        f0[PP + PIX_OUT] = jnp.zeros((8, BLK), F32)
        sx[...] = f0[0 : 2 * PP].reshape(2 * RW, BLK).astype(BF16)

        def shortcut(n, carry):
            z = nn(sx[0:RW, :], wh[rows(2048 + n * 1024, 512), :]) + nn(
                sx[RW : 2 * RW, :], wh[rows(2560 + n * 1024, 512), :]
            )
            store_z(f1, n * PP, z, 4 * n + 2, 4 * n + 3)
            return carry

        pass_own(1)
        lax.fori_loop(0, 4, shortcut, 0)

        pass_own(2)
        pass_own(VIA)
        pass_on(0)
        pass_own(3)
        pass_on(1)
        pass_own(VIA + 1)
        pass_own(4)
        pl.semaphore_signal(go, inc=1, device_id=(3, d, r), device_id_type=MESH)
        pass_on(2)
        pass_own(VIA + 2)
        pass_own(5)
        pass_on(VIA)
        pass_own(6)
        pass_on(3)
        pass_own(7)
        pass_on(VIA + 1)
        remote(h2, h2, C_H2, C_H2, (1, d, r)).wait_recv()

        def third_conv(n, carry):
            store_z(f0, n * PP, nn(h2[...], wh[rows(n * 512, 512), :]), 4 * n, 4 * n + 1)
            exchange_of(E_WIDE + n, 4 * n, 4).start()
            return carry

        lax.fori_loop(0, 4, third_conv, 0)
        pass_on(4)

        def join(n, carry):
            exchange_of(E_WIDE + n, 4 * n, 4).wait()
            c3, s3 = moments(4 * n, 4 * n + 1, total_out, 2 + n)
            cp, sp = moments(4 * n + 2, 4 * n + 3, total_out, 6 + n)
            g3, gp, b = par[n], par[4 + n], par[8 + n] + par[12 + n]

            def body(_, i, carry):
                part = pl.ds(n * PP + i * 10, 10)
                a = (f0[part] - c3) * s3
                b_ = (f1[part] - cp) * sp
                f0[part] = a
                f1[part] = b_
                o = silu(a * g3 + b_ * gp + b)
                u0[rows(n * RW + i * 80, 80), :] = o.reshape(80, BLK).astype(BF16)
                return carry

            five(body)
            clear_pad(u0, n * RW)
            return carry

        lax.fori_loop(0, 4, join, 0)
        for n in (1, 2, 3):
            o1_copy(n, 3).start()
        pass_half(13)
        pass_on(VIA + 2)
        pass_half(HALF)
        each(have, 0, 4)
        zhat4, zhat5 = fs.at[0], fs.at[1]
        z = nn(u0[0:RW, :], wx[0:512, :])
        for n in range(1, 4):
            z += nn(u0[n * RW : (n + 1) * RW, :], wx[n * 512 : (n + 1) * 512, :])
        store_z(zhat4, 0, z, 16, 17)
        sync(0, 16, 2)
        remote(parx.at[0:4], parx.at[0:4], C_PAR2, C_PAR2, (1, d, r)).wait_recv()
        center, scale = moments(16, 17, total_out, 10)
        g4, g5, b4, b5 = parx[0], parx[1], parx[2], parx[3]
        pb[0:9, 0:9] = jnp.zeros((9, 9, 8, BLK), F32)

        def hidden(a, carry):
            part = pl.ds(a * 7, 7)
            zhat = (zhat4[part] - center) * scale
            zhat4[part] = zhat
            h = silu(zhat * g4 + b4) * mask
            pb[a + 1, 1:8] = h.astype(BF16).astype(F32)
            return carry

        lax.fori_loop(0, 7, hidden, 0)
        h4[0:RV, :] = pb[1:8, 1:8].reshape(RV, BLK).astype(BF16)
        h4_send = remote(h4, h4, C_H4, C_H4, (2, d, r))
        h4_send.start()

        o1_copy(0, 2).start()
        pass_on(5)
        build_patches(plain_base)
        pass_on(6)

        def fifth_conv(taps):
            left = jnp.concatenate([pt[t] for t in taps], axis=1)
            right = jnp.concatenate([wx[2048 + t * 512 : 2560 + t * 512, :] for t in taps], axis=0)
            return nn(left, right).reshape(PP, 8, BLK)

        for i in (4, 5, VIA):
            have(i)
        zhat5[...] = fifth_conv((0, 1, 4))
        pass_half(HALF + 1)
        pass_on(7)
        for i in (6, VIA + 1, VIA + 2):
            have(i)
        zhat5[...] += fifth_conv((2, 5, 6))
        have(7)
        have_half(HALF)
        have_half(HALF + 1)
        store_z(zhat5, 0, zhat5[...] + fifth_conv((3, 7, 8)), 18, 19)
        exchange_z5 = exchange_of(1, 18, 2)
        exchange_z5.start()
        pass_half(14)
        exchange_z5.wait()
        center, scale = moments(18, 19, total_out, 11)
        act_to(zhat5, h5, center, scale, g5, b5, mask)


        def sixth_conv(n):
            have_half(13 + n)
            store_z(f2, n * PP, nn(h5[...], wx[6656 + n * 512 : 7168 + n * 512, :]), 20 + 2 * n, 21 + 2 * n)

        def exchange_z6(n):
            return exchange_of(E_WIDE_NEXT + n, 20 + 2 * n, 2)

        def exchange_d6(n):
            return exchange_of(E_WIDE + n, 28 + 2 * n, 2)

        def finish(n):
            center, scale = moments(20 + 2 * n, 21 + 2 * n, total_out, 12 + n)
            g6, b6 = parx[4 + n], parx[8 + n]

            def body(c, i, carry):
                part = pl.ds(n * PP + i * 10, 10)
                part_rows = rows(n * RW + i * 80, 80)
                zhat = (f2[part] - center) * scale
                f2[part] = zhat
                o = u0[part_rows, :].astype(F32).reshape(10, 8, BLK)
                q = o + zhat * g6 + b6
                s = sigmoid(q)
                act = q * s
                pt[n, rows(i * 80, 80), :] = (o + gate_v * (act - o)).reshape(80, BLK).astype(BF16)
                ct = cotb[c, :, n * BLK : (n + 1) * BLK].astype(F32)
                through = ct * gate_v
                dq = through * (s + act * (1.0 - s))
                f3[part] = dq
                u2[part_rows, :] = (dq + (ct - through)).reshape(80, BLK).astype(BF16)
                return add_stats(carry, dq, dq * zhat)

            tx[28 + 2 * n], tx[29 + 2 * n] = five(body, zero_stats, unrolled=True)

        for n in (0, 1):
            sixth_conv(n)
            exchange_z6(n).start()
        remote(parx.at[4:12], parx.at[4:12], C_PAR3, C_PAR3, (1, d, r)).wait_recv()
        pltpu.make_async_copy(cot, cotb.at[0:PIX_OUT], ls.at[16]).wait()
        pass_half(15)
        exchange_z6(0).wait()
        finish(0)
        exchange_d6(0).start()
        pass_half(16)
        exchange_z6(1).wait()
        finish(1)
        exchange_d6(1).start()
        have_half(15)
        store_z(f2, 2 * PP, nn(h5[...], wx[7680:8192, :]), 24, 25)
        exchange_z6(2).start()
        have_half(16)
        store_z(f2, 3 * PP, nn(h5[...], wx[8192:8704, :]), 26, 27)
        exchange_z6(3).start()
        exchange_z6(2).wait()
        finish(2)
        exchange_d6(2).start()
        exchange_z6(3).wait()
        finish(3)
        exchange_d6(3).start()
        ob[...] = pt[1]

        def output_copy(k):
            return remote(pt.at[k], ob, C_SHARE + k % 3, C_SHARE, (k, d, r))

        output_copy(3).start()


        def sixth_back(n):
            s_du, s_dg = both(28 + 2 * n), both(29 + 2 * n)
            dgx[4 + n] = s_dg
            dgx[8 + n] = s_du
            norm_back(
                u1, n * RW, f3, n * PP, f2, n * PP, parx[4 + n] * inv[12 + n],
                s_du * (1.0 / total_out), s_dg * (1.0 / total_out), unrolled=True,
            )

        grad = jnp.zeros((RW, BLK), F32)
        for n in range(5):
            if n < 4:
                exchange_d6(n).wait()
                sixth_back(n)
            if n > 0:
                grad += nt(u1[(n - 1) * RW : n * RW, :], wx[6144 + n * 512 : 6656 + n * 512, :])
        dh[...] = grad.astype(BF16)

        upstream(f2, dh, zhat5, g5, b5, mask, 36, 37)
        sync(0, 36, 2)
        s_du, s_dg = both(36), both(37)
        dgx[1] = s_dg
        dgx[3] = s_du
        norm_back(d5, 0, f2, 0, zhat5, 0, g5 * inv[11], s_du * (1.0 / total_out), s_dg * (1.0 / total_out))
        d5_send = remote(d5, d5, C_D5, C_D5, (2, d, r))
        d5_send.start()
        pb[0:9, 0:9] = jnp.zeros((9, 9, 8, BLK), F32)
        for tap in range(9):
            row, col = tap // 3, tap % 3
            part = nt(d5[0:RV, :], wx[2048 + tap * 512 : 2560 + tap * 512, :])
            pb[row : row + 7, col : col + 7] += part.reshape(7, 7, 8, BLK)

        def fourth_slopes(a, carry):
            part = pl.ds(a * 7, 7)
            zhat = zhat4[part]
            du = pb[a + 1, 1:8] * mask * slope(zhat * g4 + b4)
            f2[part] = du
            return add_stats(carry, du, du * zhat)

        tx[38], tx[39] = lax.fori_loop(0, 7, fourth_slopes, zero_stats)
        sync(1, 38, 2)
        s_du, s_dg = both(38), both(39)
        dgx[0] = s_dg
        dgx[2] = s_du
        norm_back(d4, 0, f2, 0, zhat4, 0, g4 * inv[10], s_du * (1.0 / total_out), s_dg * (1.0 / total_out))

        def carried_back(n):
            z = nt(d4[...], wx[n * 512 : (n + 1) * 512, :])
            f2[(n % 2) * PP : (n % 2 + 1) * PP] = z.reshape(PP, 8, BLK)

        def exchange_d1(n):
            return exchange_of(E_WIDE_NEXT + n, 40 + 3 * n, 3)

        def first_block_slopes(n):
            g3, gp, b = par[n], par[4 + n], par[8 + n] + par[12 + n]

            def body(_, i, carry):
                part = pl.ds(n * PP + i * 10, 10)
                do = u2[n * RW + i * 80 : n * RW + (i + 1) * 80, :].astype(F32).reshape(10, 8, BLK)
                do += f2[pl.ds((n % 2) * PP + i * 10, 10)]
                a, b_ = f0[part], f1[part]
                dp = do.astype(BF16).astype(F32) * slope(a * g3 + b_ * gp + b)
                f3[part] = dp
                s0, s1, s2 = carry
                return s0 + jnp.sum(dp, axis=0), s1 + jnp.sum(dp * a, axis=0), s2 + jnp.sum(dp * b_, axis=0)

            first = 40 + 3 * n
            tx[first], tx[first + 1], tx[first + 2] = five(body, zero_stats + zero_stats[:1], unrolled=True)

        carried_back(0)
        for n in range(4):
            if n < 3:
                carried_back(n + 1)
            first_block_slopes(n)
            exchange_d1(n).start()
            if n == 2:
                all_sent(wss.at[W_PEER], wx.at[0 : HALF * 128 + 6 * 256])
                all_sent(wss.at[W_Z], wx.at[0 : HALF * 128])
                all_sent(wss.at[W_ON], wx.at[0 : HALF * 128])
                say_ready()

        def third_back(n):
            first = 40 + 3 * n
            m_du, m_dg = both(first) * (1.0 / total_out), both(first + 1) * (1.0 / total_out)
            norm_back(
                pt.at[4 + n], 0, f3, n * PP, f0, n * PP, par[n] * inv[2 + n], m_du, m_dg, unrolled=True
            )

        grad = jnp.zeros((RW, BLK), F32)
        for n in range(5):
            if n < 4:
                exchange_d1(n).wait()
                third_back(n)
            if n > 0:
                grad += nt(pt[3 + n], wh[(n - 1) * 512 : n * 512, :])
        dh[...] = grad.astype(BF16)
        dh_send = remote(dh, dh, C_DH, C_DH, (0, d, r))
        dh_send.start()

        def shortcut_back(n, carry):
            first = 40 + 3 * n
            s_du, s_d3, s_dp = both(first), both(first + 1), both(first + 2)
            dg[n] = s_d3
            dg[4 + n] = s_dp
            dg[8 + n] = s_du
            dg[12 + n] = s_du
            m_du, m_dg = s_du * (1.0 / total_out), s_dp * (1.0 / total_out)
            norm_back(u2, n * RW, f3, n * PP, f1, n * PP, par[4 + n] * inv[6 + n], m_du, m_dg)
            return carry

        def all_shortcut_back():
            lax.fori_loop(0, 4, shortcut_back, 0)


        late = [remote(d4, d4, C_D4, C_D4, (2, d, r))]
        for first, last, sem, chip in ((0, 4, C_DG2, 2), (4, 12, C_DG3, 3)):
            late.append(remote(dgx.at[first:last], dgx.at[first:last], sem, sem, (chip, d, r)))

        def late_sends():
            dh_send.wait_send()
            for copy in late:
                copy.start()

        def shortcut_share(k):
            g = nt(u2[0:RW, :], wh[2048 + k * 256 : 2304 + k * 256, :])
            for n in range(1, 4):
                g += nt(u2[n * RW : (n + 1) * RW, :], wh[2048 + n * 1024 + k * 256 : 2304 + n * 1024 + k * 256, :])
            return g.astype(BF16)

        places = ((h4.at[:, 0:256], 0), (h4.at[:, 256:512], 2), (pt.at[8, :, 0:256], 3))

        def share_copy(slot):
            place, k = places[slot]
            return remote(place, r1, C_GP + slot, C_GP, (k, d, r))

        def shortcut_shares(slot):
            place, k = places[slot]
            if slot == 0:
                h4_send.wait_send()
            place[...] = shortcut_share(k)

        def shortcut_own():
            r1[...] = shortcut_share(1)


        def own_and_output():
            shortcut_own()
            output_copy(2).start()

        def late_shares():
            for slot in range(3):
                share_copy(slot).start()

        def at_row(t):
            early = jnp.where(t == 8, HUB_GUEST, t * 512)
            return jnp.where(t < 11, early, jnp.where(t < 16, t * 512 + 512, 5632))

        def compute(t):
            @pl.when(t < 4)
            def _():
                left = h2[:, pl.ds(pl.multiple_of(t * 128, 128), 128)]
                for n in range(4):
                    put_chunk(at_row(t), n, tn(left, pt[4 + n]))

            @pl.when((t >= 4) & (t < 13))
            def _():
                m = jnp.where(t < 8, t - 4, t - 5)
                left = sx[rows((m // 4) * RW, RW), pl.ds(pl.multiple_of(lax.rem(m, 4) * 128, 128), 128)]
                for n in range(4):
                    put_chunk(at_row(t), n, tn(left, u2[n * RW : (n + 1) * RW, :]))

            @pl.when(t >= 13)
            def _():
                left = h5[:, pl.ds(pl.multiple_of((t - 13) * 128, 128), 128)]
                for n in range(4):
                    put_chunk(at_row(t), n, tn(left, u1[n * RW : (n + 1) * RW, :]))

        zero_rest(12, sb)
        sum_gradients(
            11, compute, at_row, lambda t: jnp.where(t < 8, t, t - 1), True, 0,
            {LAST_TURN + 11 * SUBS: final_part},
            after={
                1: all_shortcut_back,
                2: lambda: shortcut_shares(0),
                4: lambda: shortcut_shares(1),
                5: late_sends,
                6: lambda: shortcut_shares(2),
                7: own_and_output,
                11: lambda: output_copy(0).start(),
                15: late_shares,
            },
            lend=(3, 5), passed=(7, 9, 11, 13), helper=lambda t: 3, helper_turn=lambda t: t - 7, norms_at=2,
            handed_in=lambda t: t == 8, lent_by=(lambda t: t == 8, lambda t: 0, lambda t: t + 2, 1), back=R_BACK_HUB,
            computed=(0, 10), packed_here=(0, 10),
        )
        for copy in [d5_send, o1_copy(0, 2)] + [o1_copy(n, 3) for n in (1, 2, 3)] + late:
            copy.wait_send()
        for slot in range(3):
            share_copy(slot).wait_send()
        for k in (0, 2, 3):
            output_copy(k).wait_send()


    @pl.when(p == 2)
    def _():
        for k, slot in ((0, 0), (1, 1), (2, 8), (3, 9)):
            parx[k] = par[slot]
        par_send = remote(parx.at[0:4], parx.at[0:4], C_PAR2, C_PAR2, (1, d, r))
        par_send.start()

        put_w = put_narrow(wx, lambda i: own_parts(i) * 128)

        def put(i):
            put_w(i)

            @pl.when(i < VIA)
            def _():
                piece_copy(W_OWN, i, quarter, (1, d, r)).start()

            @pl.when((i >= VIA) & (i < HALF))
            def _():
                piece_copy(W_VIA, i, quarter, (0, d, r)).start()

            for k in range(HALF, 13):
                @pl.when(i == HALF + 2 * (k - HALF) + 1)
                def _(k=k):
                    half_copy(W_VIA, k, d, (0, d, r)).start()

        load_weights(own_parts, 15, 0, 15, put)
        pb[...] = jnp.zeros_like(pb)
        clear_patch_pad()

        all_sent(wss.at[W_OWN], wx.at[0 : VIA * 128])
        all_sent(wss.at[W_VIA], wx.at[0 : 3 * 128 + 2 * 256])
        say_ready()
        remote(h4, h4, C_H4, C_H4, (2, d, r)).wait_recv()
        pb[1:8, 1:8] = h4[0:RV, :].astype(F32).reshape(7, 7, 8, BLK)
        build_patches(plain_base)
        remote(d5, d5, C_D5, C_D5, (2, d, r)).wait_recv()

        def compute(t):
            taps = (t < 5) | (t >= 11)

            @pl.when(taps)
            def _():
                tap = jnp.where(t < 5, t + 4, t - 11)
                wh[rows(t * 512, 512), :] = tn(pt[tap], d5[...]).astype(BF16)

            @pl.when(t == 5)
            def _():
                remote(d4, d4, C_D4, C_D4, (2, d, r)).wait_recv()
                for n in range(4):
                    o1_copy(n, 2).wait_recv()

            @pl.when(jnp.logical_not(taps))
            def _():
                n = jnp.where(t < 7, t - 5, t - 7)
                wh[rows(t * 512, 512), :] = tn(u0[rows(n * RW, RW), :], d4[...]).astype(BF16)

        def chunk_of(t):
            return jnp.where(t < 5, t + 8, jnp.where(t < 7, t - 5, t - 7))

        def norm_grads():
            remote(dgx.at[0:4], dgx.at[0:4], C_DG2, C_DG2, (2, d, r)).wait_recv()
            dg[0], dg[1], dg[8], dg[9] = dgx[0], dgx[1], dgx[2], dgx[3]

        sum_gradients(
            11, compute, lambda t: t * 512, chunk_of, False, 0,
            {6 * SUBS: norm_grads, LAST_TURN + 11 * SUBS: final_part},
            lend=(2, 3, 4, 6), helper=lambda t: 3, helper_turn=lambda t: t - 11,
            handed_in=lambda t: (t >= 7) & (t < 9),
            lent_by=(lambda t: (t >= 7) & (t < 9), lambda t: 0, lambda t: t + 1, 2),
            computed=(0, 9), packed_here=(0, 9), norms_at=6 * SUBS, norms=1024,
        )
        par_send.wait_send()

    @pl.when(p == 3)
    def _():
        for k in range(4):
            parx[4 + k] = par[k]
            parx[8 + k] = par[8 + k]
        par_send = remote(parx.at[4:12], parx.at[4:12], C_PAR3, C_PAR3, (1, d, r))
        par_send.start()
        say_ready()

        def put(i):
            for n in range(4):
                for j in range(4):
                    wx[rows(6656 + n * 512 + d * 256 + i * 32, 32), j * 128 : (j + 1) * 128] = st[
                        pl.ds(4 * n + j, 32, stride=16), :
                    ].astype(BF16)

        load_weights(half_rows, 8, 0, 8, put)
        zero_rest(4, sb)
        pl.semaphore_wait(go, 1)

        half_copy(W_VIA, 16, d, (0, d, r)).start()
        for i in (13, 14, 15):
            half_copy(W_OWN, i, d, (1, d, r)).start()
        for n in (1, 2, 3):
            o1_copy(n, 3).wait_recv()
            o1_copy(n, 2).start()
        def norm_grads():
            remote(dgx.at[4:12], dgx.at[4:12], C_DG3, C_DG3, (3, d, r)).wait_recv()
            for k in range(4):
                dg[k] = dgx[4 + k]
                dg[8 + k] = dgx[8 + k]

        sum_gradients(
            10, lambda t: None, lambda t: t * 512, lambda t: t - 6, True, 0,
            {5 * SUBS: norm_grads, LAST_TURN + 10 * SUBS: final_part},
            handed_in=lambda t: t >= 0,
            lent_by=(lambda t: t < 6, lambda t: jnp.where(t < 4, 2, 1), lambda t: jnp.where(t < 4, t + 11, t + 7), 6),
            computed=(0, 0), packed_here=(6, 4), norms_at=5 * SUBS, norms=2048,
        )
        for n in (1, 2, 3):
            o1_copy(n, 2).wait_send()
        all_sent(wss.at[W_VIA], wx.at[0:256])
        all_sent(wss.at[W_OWN], wx.at[0 : 3 * 256])
        par_send.wait_send()

    dgb_copy().start()
    gi_copy().wait()
    out_copy().wait()
    dgb_copy().wait()


def widen_kernel(out_in, gi_in, dw_in, dgb_in, out, gi, dw, gain, bias, v_out, v_gi, v_dw, v_wide, v_dgb, sin, sout):
    count = v_dw.shape[0] // 3328

    def part(i):
        return pl.ds(i * 3328, 3328)

    loads = [pltpu.make_async_copy(dw_in.at[part(i)], v_dw.at[part(i)], sin.at[i]) for i in range(count)]
    others = (
        (dgb_in, v_dgb, ((v_dgb.at[0:4], gain), (v_dgb.at[4:8], bias))),
        (out_in, v_out, ((v_out, out),)),
        (gi_in, v_gi, ((v_gi, gi),)),
    )
    more = [pltpu.make_async_copy(a, b, sin.at[count + k]) for k, (a, b, _) in enumerate(others)]
    for copy in more + loads:
        copy.start()
    stores = []
    for i in range(count):
        loads[i].wait()
        v_wide[part(i)] = v_dw[part(i)].astype(F32)
        stores.append(pltpu.make_async_copy(v_wide.at[part(i)], dw.at[part(i)], sout.at[i]))
        stores[-1].start()
    for k, (_, _, ends) in enumerate(others):
        more[k].wait()
        for a, b in ends:
            stores.append(pltpu.make_async_copy(a, b, sout.at[len(stores)]))
            stores[-1].start()
    for copy in stores:
        copy.wait()


def widen(out, gi, dw, dgb):
    count = P_SIZE // 128 // 3328
    any_space = pl.BlockSpec(memory_space=pl.ANY)
    return pl.pallas_call(
        widen_kernel,
        out_shape=(
            jax.ShapeDtypeStruct(out.shape, out.dtype),
            jax.ShapeDtypeStruct(gi.shape, gi.dtype),
            jax.ShapeDtypeStruct(dw.shape, F32),
            jax.ShapeDtypeStruct((4, 4096), F32),
            jax.ShapeDtypeStruct((4, 4096), F32),
        ),
        in_specs=[any_space] * 4,
        out_specs=(any_space,) * 5,
        scratch_shapes=[
            pltpu.VMEM(out.shape, out.dtype),
            pltpu.VMEM(gi.shape, gi.dtype),
            pltpu.VMEM(dw.shape, BF16),
            pltpu.VMEM(dw.shape, F32),
            pltpu.VMEM(dgb.shape, F32),
            pltpu.SemaphoreType.DMA((count + 3,)),
            pltpu.SemaphoreType.DMA((count + 4,)),
        ],
        compiler_params=pltpu.CompilerParams(vmem_limit_bytes=64 * 1024 * 1024),
    )(out, gi, dw, dgb)


def one_kernel(images, section_weights, bn_gain, bn_bias, width, bn_set, gate, cotangent):
    any_space = pl.BlockSpec(memory_space=pl.ANY)
    smem = pl.BlockSpec(memory_space=pltpu.SMEM)
    out, gi, dw, dgb = pl.pallas_call(
        whole_kernel,
        out_shape=(
            jax.ShapeDtypeStruct((PIX_OUT, 8, BLK), BF16),
            jax.ShapeDtypeStruct((PIX_IN, 8, 256), F32),
            jax.ShapeDtypeStruct((P_SIZE // SUB, 512, 128), BF16),
            jax.ShapeDtypeStruct((8, 4096), F32),
        ),
        in_specs=[any_space, any_space, any_space, any_space, smem, smem, smem, any_space],
        out_specs=(any_space,) * 4,
        scratch_shapes=[
            pltpu.VMEM((4, 28, 8, 1024), BF16),
            pltpu.VMEM((RING, 1, SUB), BF16),
            pltpu.VMEM((512, 128), F32),
            pltpu.VMEM((9216, BLK), BF16),
            pltpu.VMEM((8768, BLK), BF16),
            pltpu.VMEM((4 * PP, 8, BLK), F32),
            pltpu.VMEM((4 * PP, 8, BLK), F32),
            pltpu.VMEM((4 * PP, 8, BLK), F32),
            pltpu.VMEM((4 * PP, 8, BLK), F32),
            pltpu.VMEM((2, PP, 8, BLK), F32),
            pltpu.VMEM((16, 16, 8, BLK), F32),
            pltpu.VMEM((9, RW, BLK), BF16),
            pltpu.VMEM((4 * RW, BLK), BF16),
            pltpu.VMEM((4 * RW, BLK), BF16),
            pltpu.VMEM((4 * RW, BLK), BF16),
            pltpu.VMEM((2 * RW, BLK), BF16),
            pltpu.VMEM((PP, 8, C_OUT), BF16),
            pltpu.VMEM((RW, BLK), BF16),
            pltpu.VMEM((RW, BLK), BF16),
            pltpu.VMEM((RW, BLK), BF16),
            pltpu.VMEM((RW, BLK), BF16),
            pltpu.VMEM((RW, BLK), BF16),
            pltpu.VMEM((RW, BLK), BF16),
            pltpu.VMEM((8 * PIX_IN, 256), BF16),
            pltpu.VMEM((RW, 256), BF16),
            pltpu.VMEM((RW, BLK), BF16),
            pltpu.VMEM((52, 8, BLK), F32),
            pltpu.VMEM((52, 8, BLK), F32),
            pltpu.VMEM((16, 8, BLK), F32),
            pltpu.VMEM((16, 8, BLK), F32),
            pltpu.VMEM((12, 8, BLK), F32),
            pltpu.VMEM((16, 8, BLK), F32),
            pltpu.VMEM((12, 8, BLK), F32),
            pltpu.VMEM((4, 512, 128), BF16),
            pltpu.VMEM((4352, BLK), BF16),
            pltpu.VMEM((2, 8, 4096), F32),
            pltpu.VMEM((8, 4096), F32),
            pltpu.VMEM((8, 4096), F32),
            pltpu.VMEM((PIX_OUT, 8, BLK), BF16),
            pltpu.VMEM((NSETS, 4096), F32),
            pltpu.VMEM((NSETS, 4096), F32),
            pltpu.SemaphoreType.DMA((19,)),
            pltpu.SemaphoreType.DMA((N_SEM,)),
            pltpu.SemaphoreType.DMA((N_SEM,)),
            pltpu.SemaphoreType.DMA((5,)),
            pltpu.SemaphoreType.DMA((N_SUM_SEND,)),
            pltpu.SemaphoreType.DMA((N_SUM_RECV,)),
            pltpu.SemaphoreType.REGULAR((2,)),
            pltpu.SemaphoreType.REGULAR,
        ],
        compiler_params=pltpu.CompilerParams(
            collective_id=0, has_side_effects=True, vmem_limit_bytes=64 * 1024 * 1024
        ),
    )(
        jnp.transpose(images, (1, 0, 2)),
        section_weights,
        bn_gain[0],
        bn_bias[0],
        width.T,
        bn_set.T,
        gate,
        jnp.transpose(cotangent, (1, 0, 2)),
    )
    out, gi, dw, gain_sum, bias_sum = widen(out, gi, dw.reshape(P_SIZE // 128, 128), dgb)
    return (
        jnp.transpose(out, (1, 0, 2)),
        jnp.transpose(gi, (1, 0, 2)),
        dw.reshape(1, P_SIZE),
        gain_sum[None],
        bias_sum[None],
    )


def solution(mesh):
    sizes = dict(mesh.shape)
    fits = sizes["pipe"] == 4 and sizes["dp"] == 2 and sizes["rep"] == 4
    placed = (
        P(("dp", "rep"), None, None),
        P("pipe", None),
        P("pipe", None, None),
        P("pipe", None, None),
        P(),
        P(),
        P(),
        P(("dp", "rep"), None, None),
    )
    return jax.shard_map(
        one_kernel if fits else on_device,
        mesh=mesh,
        in_specs=placed,
        out_specs=(
            P(("dp", "rep"), None, "pipe"),
            P(("dp", "rep"), None, "pipe"),
            P("pipe", None),
            P("pipe", None, None),
            P("pipe", None, None),
        ),
        check_vma=False,
    )
```

```python
import jax
import jax.numpy as jnp
from jax import lax
from jax.experimental import pallas as pl
from jax.experimental.pallas import tpu as pltpu
from jax.sharding import PartitionSpec as P

C_IN = 1024
C_MID = 512
C_OUT = 2048
SIDE = 14
NSETS = 4
MB = 8
IMG_B = 1
OSIDE = 7
PIX_IN = 196
PIX_OUT = 49
IMG_DEV = 8
P_SIZE = 3407872


EPSILON = 1e-05


def for_sending(array):

    def short(part):
        return part.astype(jnp.bfloat16) if part.dtype == jnp.float32 else part

    return jax.tree.map(short, array)


def shifted(value, axis, steps):
    count = lax.axis_size(axis)
    first, last = (max(0, -steps), min(count, count - steps))
    return lax.ppermute(value, axis, [(source, source + steps) for source in range(first, last)])


def smooth(inputs):
    return inputs * jax.nn.sigmoid(inputs)


def smooth_slope(inputs):
    gate_sig = jax.nn.sigmoid(inputs)
    return gate_sig * (1.0 + inputs * (1.0 - gate_sig))


def matmul(left_op, right_op):
    return jnp.dot(left_op, right_op, preferred_element_type=jnp.float32)


def matmul_left_t(left_op, right_op):
    return lax.dot_general(
        left_op, right_op, (((0,), (0,)), ((), ())), preferred_element_type=jnp.float32
    )


def matmul_right_t(left_op, right_op):
    return lax.dot_general(
        left_op, right_op, (((1,), (1,)), ((), ())), preferred_element_type=jnp.float32
    )


def patches(planes, stride):
    images, side_len, channels = (planes.shape[0], planes.shape[1], planes.shape[3])
    out_side = side_len // stride
    padded = jnp.pad(planes, ((0, 0), (1, 1), (1, 1), (0, 0)))
    pieces = []
    for row_off in range(3):
        for col_off in range(3):
            pieces.append(
                padded[
                    :,
                    row_off : row_off + stride * (out_side - 1) + 1 : stride,
                    col_off : col_off + stride * (out_side - 1) + 1 : stride,
                    :,
                ]
            )
    return jnp.concatenate(pieces, axis=3).reshape(images * out_side * out_side, 9 * channels)


def unpatch(columns, images, side_len, stride, channels):
    out_side = side_len // stride
    pieces = columns.reshape(images, out_side, out_side, 9, channels)
    padded = jnp.zeros((images, side_len + 2, side_len + 2, channels), jnp.float32)
    for row_off in range(3):
        for col_off in range(3):
            padded = padded.at[
                :,
                row_off : row_off + stride * (out_side - 1) + 1 : stride,
                col_off : col_off + stride * (out_side - 1) + 1 : stride,
                :,
            ].add(pieces[:, :, :, row_off * 3 + col_off, :])
    return padded[:, 1 : side_len + 1, 1 : side_len + 1, :]


def group_moments(sums_local, squares_local):
    return (
        lax.psum(sums_local.astype(jnp.bfloat16), "dp").astype(jnp.float32),
        lax.psum(squares_local.astype(jnp.bfloat16), "dp").astype(jnp.float32),
    )


def group_grad_sums(bias_local, gain_local):
    return (
        lax.psum(bias_local.astype(jnp.bfloat16), "dp").astype(jnp.float32),
        lax.psum(gain_local.astype(jnp.bfloat16), "dp").astype(jnp.float32),
    )


def stats_of(sum_all, square_all, start, count, row_total):
    center = sum_all[start : start + count] / row_total
    inv_std = lax.rsqrt(square_all[start : start + count] / row_total - center * center + EPSILON)
    return (center, inv_std)


def norm_grad(slope_in, normed, gain_vec, inv_std, sum_bias, sum_gain, row_total):
    return (
        gain_vec * inv_std * (slope_in - sum_bias / row_total - normed * (sum_gain / row_total))
    ).astype(jnp.bfloat16)


def on_device(images, section_weights, bn_gain, bn_bias, width, bn_set, gate, cotangent):
    section_idx = lax.axis_index("pipe")
    pipe_count = lax.axis_size("pipe")
    dp_count = lax.axis_size("dp")
    flat_weights = section_weights[0]
    gain_table = bn_gain[0]
    bias_table = bn_bias[0]
    rows_in = IMG_B * PIX_IN
    rows_out = IMG_B * PIX_OUT
    total_in = float(rows_in * dp_count)
    total_out = float(rows_out * dp_count)
    wide = 2 * C_OUT
    scr_len = IMG_B * max(PIX_IN * C_MID, PIX_OUT * wide)
    image_blocks = images.reshape(MB, IMG_B, PIX_IN, C_IN)
    pad_mid = jnp.zeros((wide - 2 * C_MID,), jnp.float32)
    zero_wide = jnp.zeros((wide,), jnp.float32)
    zero_scr = jnp.zeros((scr_len,), jnp.float32)
    zero_mid = jnp.zeros((rows_out, C_MID), jnp.bfloat16)
    zero_res = jnp.zeros((rows_out, C_OUT), jnp.bfloat16)
    zero_rows = jnp.zeros((rows_out, C_OUT), jnp.float32)
    zero_input = jnp.zeros((IMG_B, PIX_IN, C_IN), jnp.float32)

    def pack(values):
        flat = values.reshape(-1).astype(jnp.float32)
        return jnp.pad(flat, (0, scr_len - flat.shape[0]))

    def unpack(buffer, rows, cols):
        return buffer[: rows * cols].reshape(rows, cols)

    def place(vec, start):
        return jnp.pad(vec, (start, wide - start - vec.shape[0]))

    def add_weight(acc, grad, offset, valid):
        flat = grad.reshape(-1)
        return acc.at[offset : offset + flat.shape[0]].add(jnp.where(valid, flat, 0.0))

    def weights_zero():
        split_at = C_IN * C_MID
        return (
            flat_weights[:split_at].reshape(C_IN, C_MID),
            flat_weights[split_at : split_at + 9 * C_MID * C_MID].reshape(9 * C_MID, C_MID),
        )

    def weights_one():
        split_at = C_MID * C_OUT
        return (
            flat_weights[:split_at].reshape(C_MID, C_OUT),
            flat_weights[split_at : split_at + C_IN * C_OUT].reshape(C_IN, C_OUT),
        )

    def weights_two():
        split_at = C_OUT * C_MID
        return (
            flat_weights[:split_at].reshape(C_OUT, C_MID),
            flat_weights[split_at : split_at + 9 * C_MID * C_MID].reshape(9 * C_MID, C_MID),
        )

    def short_rows(image_block):
        return image_block.reshape(IMG_B, SIDE, SIDE, C_IN)[:, ::2, ::2, :].reshape(rows_out, C_IN)

    def local_stats(values, start):
        return (
            place(jnp.sum(values, axis=0), start),
            place(jnp.sum(values * values, axis=0), start),
        )

    def fwd_a_zero(ops):
        conv_a, conv_b = weights_zero()
        pre_one = matmul(ops[0].reshape(rows_in, C_IN), conv_a)
        sums_local, squares_local = local_stats(pre_one, 0)
        return (pack(pre_one), sums_local, squares_local)

    def fwd_a_one(ops):
        conv_a, conv_b = weights_one()
        pre_both = jnp.concatenate(
            [matmul(ops[1], conv_a), matmul(short_rows(ops[0]), conv_b)], axis=1
        )
        sums_local, squares_local = local_stats(pre_both, 0)
        return (pack(pre_both), sums_local, squares_local)

    def fwd_a_two(ops):
        conv_a, conv_b = weights_two()
        pre_four = matmul(ops[2], conv_a)
        sums_local, squares_local = local_stats(pre_four, 0)
        return (pack(pre_four), sums_local, squares_local)

    def fwd_a_three(ops):
        conv_a = flat_weights[: C_MID * C_OUT].reshape(C_MID, C_OUT)
        pre_six = matmul(ops[1], conv_a)
        sums_local, squares_local = local_stats(pre_six, 0)
        return (pack(pre_six), sums_local, squares_local)

    def fwd_b_zero(args):
        ops, scratch, sum_all, square_all = args
        conv_a, conv_b = weights_zero()
        gain_vec, bias_vec, mask_vec = (ops[3], ops[4], ops[5])
        pre_one = unpack(scratch, rows_in, C_MID)
        center_one, inv_one = stats_of(sum_all, square_all, 0, C_MID, total_in)
        hidden_one = (
            smooth((pre_one - center_one) * inv_one * gain_vec[:C_MID] + bias_vec[:C_MID])
            * mask_vec
        ).astype(jnp.bfloat16)
        pre_two = matmul(patches(hidden_one.reshape(IMG_B, SIDE, SIDE, C_MID), 2), conv_b)
        sums_local, squares_local = local_stats(pre_two, C_MID)
        return (pack(pre_two), sums_local, squares_local)

    def fwd_b_pass(args):
        return (args[1], zero_wide, zero_wide)

    def fwd_b_two(args):
        ops, scratch, sum_all, square_all = args
        conv_a, conv_b = weights_two()
        gain_vec, bias_vec, mask_vec = (ops[3], ops[4], ops[5])
        pre_four = unpack(scratch, rows_out, C_MID)
        center_four, inv_four = stats_of(sum_all, square_all, 0, C_MID, total_out)
        hidden_four = (
            smooth((pre_four - center_four) * inv_four * gain_vec[:C_MID] + bias_vec[:C_MID])
            * mask_vec
        ).astype(jnp.bfloat16)
        pre_five = matmul(patches(hidden_four.reshape(IMG_B, OSIDE, OSIDE, C_MID), 1), conv_b)
        sums_local, squares_local = local_stats(pre_five, C_MID)
        return (pack(pre_five), sums_local, squares_local)

    def fwd_c_double(args, first_total, send_res):
        ops, scratch, sum_all, square_all = args
        gain_vec, bias_vec, mask_vec = (ops[3], ops[4], ops[5])
        pre_two = unpack(scratch, rows_out, C_MID)
        center_one, inv_one = stats_of(sum_all, square_all, 0, C_MID, first_total)
        center_two, inv_two = stats_of(sum_all, square_all, C_MID, C_MID, total_out)
        hidden_two = (
            smooth(
                (pre_two - center_two) * inv_two * gain_vec[C_MID : 2 * C_MID]
                + bias_vec[C_MID : 2 * C_MID]
            )
            * mask_vec
        ).astype(jnp.bfloat16)
        centers = jnp.concatenate([center_one, center_two, pad_mid])
        scales = jnp.concatenate([inv_one, inv_two, pad_mid])
        return (hidden_two, send_res, centers, scales, zero_rows)

    def fwd_c_zero(args):
        return fwd_c_double(args, total_in, zero_res)

    def fwd_c_two(args):
        return fwd_c_double(args, total_out, args[0][2])

    def fwd_c_one(args):
        ops, scratch, sum_all, square_all = args
        gain_vec, bias_vec = (ops[3], ops[4])
        pre_both = unpack(scratch, rows_out, wide)
        centers, scales = stats_of(sum_all, square_all, 0, wide, total_out)
        activ = (pre_both - centers) * scales * gain_vec + bias_vec
        block_out = smooth(activ[:, :C_OUT] + activ[:, C_OUT:]).astype(jnp.bfloat16)
        return (zero_mid, block_out, centers, scales, zero_rows)

    def fwd_c_three(args):
        ops, scratch, sum_all, square_all = args
        gain_vec, bias_vec, gate_val = (ops[3], ops[4], ops[6])
        pre_six = unpack(scratch, rows_out, C_OUT)
        centers, scales = stats_of(sum_all, square_all, 0, wide, total_out)
        residual = ops[2].astype(jnp.float32)
        merged = smooth(
            residual
            + (pre_six - centers[:C_OUT]) * scales[:C_OUT] * gain_vec[:C_OUT]
            + bias_vec[:C_OUT]
        )
        result = gate_val * merged + (1.0 - gate_val) * residual
        return (zero_mid, zero_res, centers, scales, result)

    def bwd_a_double(ops, flat_in, conv_a, conv_b, side_len, stride):
        centers, scales, grad_mid = (ops[3], ops[4], ops[5])
        gain_vec, bias_vec, mask_vec = (ops[8], ops[9], ops[10])
        norm_one = (matmul(flat_in, conv_a) - centers[:C_MID]) * scales[:C_MID]
        hidden_one = (smooth(norm_one * gain_vec[:C_MID] + bias_vec[:C_MID]) * mask_vec).astype(
            jnp.bfloat16
        )
        columns = patches(hidden_one.reshape(IMG_B, side_len, side_len, C_MID), stride)
        norm_two = (matmul(columns, conv_b) - centers[C_MID : 2 * C_MID]) * scales[
            C_MID : 2 * C_MID
        ]
        act_two = norm_two * gain_vec[C_MID : 2 * C_MID] + bias_vec[C_MID : 2 * C_MID]
        slope_two = grad_mid.astype(jnp.float32) * mask_vec * smooth_slope(act_two)
        return (
            pack(slope_two),
            pack(norm_two),
            pack(norm_one),
            place(jnp.sum(slope_two, axis=0), C_MID),
            place(jnp.sum(slope_two * norm_two, axis=0), C_MID),
        )

    def bwd_a_zero(ops):
        conv_a, conv_b = weights_zero()
        return bwd_a_double(ops, ops[0].reshape(rows_in, C_IN), conv_a, conv_b, SIDE, 2)

    def bwd_a_two(ops):
        conv_a, conv_b = weights_two()
        return bwd_a_double(ops, ops[2], conv_a, conv_b, OSIDE, 1)

    def bwd_a_one(ops):
        conv_a, conv_b = weights_one()
        centers, scales, grad_res = (ops[3], ops[4], ops[6])
        gain_vec, bias_vec = (ops[8], ops[9])
        pre_both = jnp.concatenate(
            [matmul(ops[1], conv_a), matmul(short_rows(ops[0]), conv_b)], axis=1
        )
        normed = (pre_both - centers) * scales
        activ = normed * gain_vec + bias_vec
        slope_in = grad_res.astype(jnp.float32) * smooth_slope(activ[:, :C_OUT] + activ[:, C_OUT:])
        both = jnp.concatenate([slope_in, slope_in], axis=1)
        return (
            pack(both),
            pack(normed),
            zero_scr,
            jnp.sum(both, axis=0),
            jnp.sum(both * normed, axis=0),
        )

    def bwd_a_three(ops):
        conv_a = flat_weights[: C_MID * C_OUT].reshape(C_MID, C_OUT)
        centers, scales = (ops[3], ops[4])
        gain_vec, bias_vec, gate_val = (ops[8], ops[9], ops[11])
        normed = (matmul(ops[1], conv_a) - centers[:C_OUT]) * scales[:C_OUT]
        joined = ops[2].astype(jnp.float32) + normed * gain_vec[:C_OUT] + bias_vec[:C_OUT]
        through = ops[7].astype(jnp.float32) * gate_val * smooth_slope(joined)
        return (
            pack(through),
            pack(normed),
            zero_scr,
            place(jnp.sum(through, axis=0), 0),
            place(jnp.sum(through * normed, axis=0), 0),
        )

    def bwd_b_double(args, conv_b, rows_first, side_len, stride, offset):
        ops, first_buf, second_buf, third_buf, sum_bias, sum_gain, acc = args
        scales = ops[4]
        gain_vec, bias_vec, mask_vec, valid = (ops[8], ops[9], ops[10], ops[12])
        slope_two = unpack(first_buf, rows_out, C_MID)
        norm_two = unpack(second_buf, rows_out, C_MID)
        norm_one = unpack(third_buf, rows_first, C_MID)
        grad_two = norm_grad(
            slope_two,
            norm_two,
            gain_vec[C_MID : 2 * C_MID],
            scales[C_MID : 2 * C_MID],
            sum_bias[C_MID : 2 * C_MID],
            sum_gain[C_MID : 2 * C_MID],
            total_out,
        )
        act_one = norm_one * gain_vec[:C_MID] + bias_vec[:C_MID]
        hidden_one = (smooth(act_one) * mask_vec).astype(jnp.bfloat16)
        columns = patches(hidden_one.reshape(IMG_B, side_len, side_len, C_MID), stride)
        acc = add_weight(acc, matmul_left_t(columns, grad_two), offset, valid)
        hid_grad = unpatch(
            matmul_right_t(grad_two, conv_b), IMG_B, side_len, stride, C_MID
        ).reshape(rows_first, C_MID)
        slope_one = hid_grad * mask_vec * smooth_slope(act_one)
        return (
            pack(slope_one),
            second_buf,
            third_buf,
            place(jnp.sum(slope_one, axis=0), 0),
            place(jnp.sum(slope_one * norm_one, axis=0), 0),
            acc,
        )

    def bwd_b_zero(args):
        conv_a, conv_b = weights_zero()
        return bwd_b_double(args, conv_b, rows_in, SIDE, 2, C_IN * C_MID)

    def bwd_b_two(args):
        conv_a, conv_b = weights_two()
        return bwd_b_double(args, conv_b, rows_out, OSIDE, 1, C_OUT * C_MID)

    def bwd_b_pass(args):
        return (args[1], args[2], args[3], zero_wide, zero_wide, args[6])

    def side_none():
        return zero_input

    def bwd_c_zero(args):
        ops, first_buf, second_buf, third_buf, sum_bias, sum_gain, acc = args
        conv_a, conv_b = weights_zero()
        scales, gain_vec, valid = (ops[4], ops[8], ops[12])
        flat_in = ops[0].reshape(rows_in, C_IN)
        slope_one = unpack(first_buf, rows_in, C_MID)
        norm_one = unpack(third_buf, rows_in, C_MID)
        grad_one = norm_grad(
            slope_one,
            norm_one,
            gain_vec[:C_MID],
            scales[:C_MID],
            sum_bias[:C_MID],
            sum_gain[:C_MID],
            total_in,
        )
        acc = add_weight(acc, matmul_left_t(flat_in, grad_one), 0, valid)
        side_out = matmul_right_t(grad_one, conv_a).reshape(IMG_B, PIX_IN, C_IN)
        return (zero_mid, zero_res, acc, side_out)

    def bwd_c_one(args):
        ops, first_buf, second_buf, third_buf, sum_bias, sum_gain, acc = args
        conv_a, conv_b = weights_one()
        scales, gain_vec, valid = (ops[4], ops[8], ops[12])
        short_in = short_rows(ops[0])
        both = unpack(first_buf, rows_out, wide)
        normed = unpack(second_buf, rows_out, wide)
        grad_both = norm_grad(both, normed, gain_vec, scales, sum_bias, sum_gain, total_out)
        acc = add_weight(acc, matmul_left_t(ops[1], grad_both[:, :C_OUT]), 0, valid)
        acc = add_weight(acc, matmul_left_t(short_in, grad_both[:, C_OUT:]), C_MID * C_OUT, valid)
        mid_grad = matmul_right_t(grad_both[:, :C_OUT], conv_a).astype(jnp.bfloat16)
        short_grad = matmul_right_t(grad_both[:, C_OUT:], conv_b).reshape(
            IMG_B, OSIDE, 1, OSIDE, 1, C_IN
        )
        side_out = jnp.pad(short_grad, ((0, 0), (0, 0), (0, 1), (0, 0), (0, 1), (0, 0))).reshape(
            IMG_B, PIX_IN, C_IN
        )
        return (mid_grad, zero_res, acc, side_out)

    def bwd_c_two(args):
        ops, first_buf, second_buf, third_buf, sum_bias, sum_gain, acc = args
        conv_a, conv_b = weights_two()
        scales, grad_res, gain_vec, valid = (ops[4], ops[6], ops[8], ops[12])
        slope_four = unpack(first_buf, rows_out, C_MID)
        norm_four = unpack(third_buf, rows_out, C_MID)
        grad_four = norm_grad(
            slope_four,
            norm_four,
            gain_vec[:C_MID],
            scales[:C_MID],
            sum_bias[:C_MID],
            sum_gain[:C_MID],
            total_out,
        )
        acc = add_weight(acc, matmul_left_t(ops[2], grad_four), 0, valid)
        carried_grad = (grad_res.astype(jnp.float32) + matmul_right_t(grad_four, conv_a)).astype(
            jnp.bfloat16
        )
        return (zero_mid, carried_grad, acc, side_none())

    def bwd_c_three(args):
        ops, first_buf, second_buf, third_buf, sum_bias, sum_gain, acc = args
        conv_a = flat_weights[: C_MID * C_OUT].reshape(C_MID, C_OUT)
        scales, gain_vec, gate_val, valid = (ops[4], ops[8], ops[11], ops[12])
        through = unpack(first_buf, rows_out, C_OUT)
        normed = unpack(second_buf, rows_out, C_OUT)
        res_grad = (through + (1.0 - gate_val) * ops[7].astype(jnp.float32)).astype(jnp.bfloat16)
        grad_six = norm_grad(
            through,
            normed,
            gain_vec[:C_OUT],
            scales[:C_OUT],
            sum_bias[:C_OUT],
            sum_gain[:C_OUT],
            total_out,
        )
        acc = add_weight(acc, matmul_left_t(ops[1], grad_six), 0, valid)
        mid_grad = matmul_right_t(grad_six, conv_a).astype(jnp.bfloat16)
        return (mid_grad, res_grad, acc, side_none())

    def select_params(micro_idx):
        block_id = section_idx // 2
        width_val = width[micro_idx, block_id]
        set_val = bn_set[micro_idx, block_id]
        onehot = (jnp.arange(NSETS) == set_val).astype(jnp.float32)
        gain_vec = jnp.sum(onehot[:, None] * gain_table, axis=0)
        bias_vec = jnp.sum(onehot[:, None] * bias_table, axis=0)
        mask_vec = (jnp.arange(C_MID) < width_val).astype(jnp.float32)
        gate_val = gate[micro_idx].astype(jnp.float32)
        return (gain_vec, bias_vec, mask_vec, gate_val, onehot)

    fwd_first = [fwd_a_zero, fwd_a_one, fwd_a_two, fwd_a_three]
    fwd_second = [fwd_b_zero, fwd_b_pass, fwd_b_two, fwd_b_pass]
    fwd_third = [fwd_c_zero, fwd_c_one, fwd_c_two, fwd_c_three]
    bwd_first = [bwd_a_zero, bwd_a_one, bwd_a_two, bwd_a_three]
    bwd_second = [bwd_b_zero, bwd_b_pass, bwd_b_two, bwd_b_pass]
    bwd_third = [bwd_c_zero, bwd_c_one, bwd_c_two, bwd_c_three]

    def forward_tick(tick_no, state_in):
        recv_mid, recv_res, stash_mid, stash_res, stash_center, stash_scale, out_rows = state_in
        micro_raw = tick_no - section_idx
        is_valid = (micro_raw >= 0) & (micro_raw < MB)
        micro_idx = jnp.clip(micro_raw, 0, MB - 1)
        gain_vec, bias_vec, mask_vec, gate_val, onehot = select_params(micro_idx)
        ops = (image_blocks[micro_idx], recv_mid, recv_res, gain_vec, bias_vec, mask_vec, gate_val)
        scratch, sums_local, squares_local = lax.switch(section_idx, fwd_first, ops)
        sum_first, square_first = group_moments(sums_local, squares_local)
        scratch, sums_local, squares_local = lax.switch(
            section_idx, fwd_second, (ops, scratch, sum_first, square_first)
        )
        sum_second, square_second = group_moments(sums_local, squares_local)
        send_mid, send_res, centers, scales, result = lax.switch(
            section_idx,
            fwd_third,
            (ops, scratch, sum_first + sum_second, square_first + square_second),
        )
        stash_mid = stash_mid.at[micro_idx].set(jnp.where(is_valid, recv_mid, stash_mid[micro_idx]))
        stash_res = stash_res.at[micro_idx].set(jnp.where(is_valid, recv_res, stash_res[micro_idx]))
        stash_center = stash_center.at[micro_idx].set(
            jnp.where(is_valid, centers, stash_center[micro_idx])
        )
        stash_scale = stash_scale.at[micro_idx].set(
            jnp.where(is_valid, scales, stash_scale[micro_idx])
        )
        out_rows = out_rows.at[micro_idx].set(jnp.where(is_valid, result, out_rows[micro_idx]))
        recv_mid, recv_res = (
            shifted(for_sending(send_mid), "pipe", 1).astype(send_mid.dtype),
            shifted(for_sending(send_res), "pipe", 1).astype(send_res.dtype),
        )
        return (recv_mid, recv_res, stash_mid, stash_res, stash_center, stash_scale, out_rows)

    forward_init = (
        zero_mid,
        zero_res,
        jnp.zeros((MB, rows_out, C_MID), jnp.bfloat16),
        jnp.zeros((MB, rows_out, C_OUT), jnp.bfloat16),
        jnp.zeros((MB, wide), jnp.float32),
        jnp.zeros((MB, wide), jnp.float32),
        jnp.zeros((MB, rows_out, C_OUT), jnp.float32),
    )
    forward_state = lax.fori_loop(0, MB + pipe_count - 1, forward_tick, forward_init)
    unused_mid, unused_res, stash_mid, stash_res, stash_center, stash_scale, out_rows = (
        forward_state
    )

    def backward_tick(tick_no, state_in):
        grad_mid, grad_res, weight_acc, gain_acc, bias_acc, input_acc = state_in
        micro_raw = tick_no - (pipe_count - 1 - section_idx)
        is_valid = (micro_raw >= 0) & (micro_raw < MB)
        micro_idx = jnp.clip(micro_raw, 0, MB - 1)
        gain_vec, bias_vec, mask_vec, gate_val, onehot = select_params(micro_idx)
        ops = (
            image_blocks[micro_idx],
            stash_mid[micro_idx],
            stash_res[micro_idx],
            stash_center[micro_idx],
            stash_scale[micro_idx],
            grad_mid,
            grad_res,
            cotangent[micro_idx],
            gain_vec,
            bias_vec,
            mask_vec,
            gate_val,
            is_valid,
        )
        first_buf, second_buf, third_buf, bias_one, gain_one = lax.switch(
            section_idx, bwd_first, ops
        )
        sum_bias_one, sum_gain_one = group_grad_sums(bias_one, gain_one)
        first_buf, second_buf, third_buf, bias_two, gain_two, weight_acc = lax.switch(
            section_idx,
            bwd_second,
            (ops, first_buf, second_buf, third_buf, sum_bias_one, sum_gain_one, weight_acc),
        )
        sum_bias_two, sum_gain_two = group_grad_sums(bias_two, gain_two)
        send_mid, send_res, weight_acc, side_out = lax.switch(
            section_idx,
            bwd_third,
            (
                ops,
                first_buf,
                second_buf,
                third_buf,
                sum_bias_one + sum_bias_two,
                sum_gain_one + sum_gain_two,
                weight_acc,
            ),
        )
        gain_grad = gain_one + gain_two
        bias_grad = bias_one + bias_two
        gain_acc = jnp.where(is_valid, gain_acc + onehot[:, None] * gain_grad[None, :], gain_acc)
        bias_acc = jnp.where(is_valid, bias_acc + onehot[:, None] * bias_grad[None, :], bias_acc)
        input_acc = jax.tree.map(
            lambda stored, fresh: stored.at[micro_idx].set(
                jnp.where(is_valid, fresh, stored[micro_idx])
            ),
            input_acc,
            side_out,
        )
        grad_mid, grad_res = (
            shifted(for_sending(send_mid), "pipe", -1).astype(send_mid.dtype),
            shifted(for_sending(send_res), "pipe", -1).astype(send_res.dtype),
        )
        return (grad_mid, grad_res, weight_acc, gain_acc, bias_acc, input_acc)

    side_init = jnp.zeros((MB, IMG_B, PIX_IN, C_IN), jnp.float32)
    backward_init = (
        zero_mid,
        zero_res,
        jnp.zeros((P_SIZE,), jnp.float32),
        jnp.zeros((NSETS, wide), jnp.float32),
        jnp.zeros((NSETS, wide), jnp.float32),
        side_init,
    )
    backward_state = lax.fori_loop(0, MB + pipe_count - 1, backward_tick, backward_init)
    unused_gmid, unused_gres, weight_acc, gain_acc, bias_acc, input_acc = backward_state
    grad_images, output_sum = (
        lax.psum_scatter(
            input_acc.reshape(IMG_DEV, PIX_IN, C_IN).astype(jnp.bfloat16),
            "pipe",
            scatter_dimension=2,
            tiled=True,
        ).astype(jnp.float32),
        lax.psum_scatter(
            out_rows.astype(jnp.bfloat16), "pipe", scatter_dimension=2, tiled=True
        ).astype(jnp.float32),
    )
    output_part = output_sum.astype(jnp.bfloat16)
    norm_grads = jnp.concatenate([gain_acc.reshape(-1), bias_acc.reshape(-1)])
    weight_sum, norm_sum = lax.psum((weight_acc, norm_grads), ("dp", "rep"))
    grad_gain = norm_sum[: NSETS * wide].reshape(1, NSETS, wide)
    grad_bias = norm_sum[NSETS * wide :].reshape(1, NSETS, wide)
    return (output_part, grad_images, weight_sum.reshape(1, P_SIZE), grad_gain, grad_bias)


PP = PIX_OUT + 1
RW = 8 * PP
RV = 8 * PIX_OUT
BLK = 512
SUB = 65536
F32 = jnp.float32
BF16 = jnp.bfloat16
MESH = pl.DeviceIdType.MESH

E_WIDE, E_WIDE_NEXT = 2, 6
C_H2, C_H4, C_D5, C_D4, C_DH = range(10, 15)
C_O1, C_SHARE, C_GI, C_GP = 15, 19, 22, 25
C_PAR2, C_PAR3, C_DG2, C_DG3, C_BN1, C_BN2, C_BN3, C_BN4 = range(28, 36)
N_SEM = 36
N_PIECE = 17
W_OWN, W_PEER, W_Z, W_ON, W_VIA = range(5)
VIA, HALF = 8, 11
W_BASE = (0, 17, 34, 45, -VIA)
S_CORE, S_IN, S_OUT, S_HAND, S_BACK, S_DONE, S_ACROSS, N_SUM_SEND = 0, 1, 2, 3, 4, 5, 9, 25
R_CORE, R_Z, R_ACROSS, R_GIVE = (0, 8), (8, 24), (32, 16), (48, 4)
R_DONE, R_BACK, R_BACK_HUB, R_HAND, N_SUM_RECV = 52, 53, 54, 55, 75
HUB_GUEST = 8704
RING = 8
SUBS = 2
SUB_ROWS = 256 // SUBS
HOPS = 2
HOP_ROWS = SUB_ROWS // HOPS
Z1_ZERO = 3136
ACROSS_LAG, OUT_LAG = 3 * SUBS // 2 + 1, 4 * SUBS
LAST_TURN = OUT_LAG - 2


def nn(a, b):
    return jnp.dot(a, b, preferred_element_type=F32)


def nt(a, b):
    return lax.dot_general(a, b, (((1,), (1,)), ((), ())), preferred_element_type=F32)


def tn(a, b):
    return lax.dot_general(a, b, (((0,), (0,)), ((), ())), preferred_element_type=F32)


def sigmoid(v):
    return 0.5 + 0.5 * jnp.tanh(0.5 * v)


def rows(start, size):
    return pl.ds(start if isinstance(start, int) else pl.multiple_of(start, 16), size)


def whole_kernel(
    img, wts, gain_in, bias_in, width, sets, gates, cot,
    out, gi, dw, dgb_out,
    imgb, raw, st, wh, wx, f0, f1, f2, f3, fs, pb, pt, u0, u1, u2, sx, cotb,
    h2, h4, h5, d5, d4, dh, r0, r1, ob, tx, rx, inv, par, parx, dg, dgx, sb, rd, bz, dgs, dgb, v_out, gain, bias,
    ls, ss, rs, wss, ass, ars, ready, go,
):
    p, d, r = lax.axis_index("pipe"), lax.axis_index("dp"), lax.axis_index("rep")
    peer = (p, 1 - d, r)
    z_pair = r + 1 - 2 * lax.rem(r, 2)
    quarter = 2 * lax.rem(r, 2) + d

    def remote(src, dst, send, recv, device):
        return pltpu.make_async_remote_copy(
            src_ref=src, dst_ref=dst, send_sem=ss.at[send], recv_sem=rs.at[recv],
            device_id=device, device_id_type=MESH,
        )

    def sync(event, first, count):
        part = pl.ds(first, count)
        copy = remote(tx.at[part], rx.at[part], event, event, peer)
        copy.start()
        copy.wait()

    def exchange_of(event, first, count):
        part = pl.ds(first, count)
        return remote(tx.at[part], rx.at[part], event, event, peer)

    def both(slot):
        return tx[slot] + rx[slot]

    def moments(slot_sum, slot_square, total, inv_slot):
        center = both(slot_sum) * (1.0 / total)
        scale = lax.rsqrt(both(slot_square) * (1.0 / total) - center * center + EPSILON)
        inv[inv_slot] = scale
        return center, scale

    def silu(v):
        return v * sigmoid(v)

    def slope(v):
        s = sigmoid(v)
        return s + v * s * (1.0 - s)

    def clear_pad(ref, first):
        tile = ref[rows(first + RW - 16, 16), :].astype(F32)
        keep = lax.broadcasted_iota(jnp.int32, tile.shape, 0) < 8
        ref[rows(first + RW - 16, 16), :] = jnp.where(keep, tile, 0.0).astype(BF16)

    def per_row(value_of):
        row = lax.broadcasted_iota(jnp.int32, (8, BLK), 0)
        out = jnp.zeros((8, BLK), jnp.int32)
        for m in range(MB):
            out = jnp.where(row == m, value_of(m), out)
        return out

    def mask_of(block):
        lane = lax.broadcasted_iota(jnp.int32, (8, BLK), 1)
        return (lane < per_row(lambda m: width[block, m])).astype(F32)

    def five(body, init=0, unrolled=False):
        if unrolled:
            for c in range(5):
                init = body(pl.ds(c * 10, 10), c, init)
            return init
        return lax.fori_loop(0, 5, lambda c, carry: body(pl.ds(c * 10, 10), c, carry), init)

    def add_stats(carry, a, b):
        return carry[0] + jnp.sum(a, axis=0), carry[1] + jnp.sum(b, axis=0)

    zero_stats = (jnp.zeros((8, BLK), F32), jnp.zeros((8, BLK), F32))

    def store_z(ref, first, z, slot_sum, slot_square):
        z3 = z.reshape(PP, 8, BLK) if z.ndim == 2 else z
        ref[pl.ds(first, PP)] = z3
        tx[slot_sum] = jnp.sum(z3, axis=0)
        tx[slot_square] = jnp.sum(z3 * z3, axis=0)

    def raw_copy(turn, element_of):
        slot = lax.rem(turn, RING)
        return pltpu.make_async_copy(
            wts.at[:, pl.ds(pl.multiple_of(element_of(turn) * SUB, SUB), SUB)], raw.at[slot], ls.at[8 + slot]
        )

    def open_weights(element_of, total):
        for turn in range(min(RING - 1, total)):
            raw_copy(turn, element_of).start()

    def load_weights(element_of, total, first, count, put):
        def body(k, carry):
            turn = first + k

            @pl.when(turn + RING - 1 < total)
            def _():
                raw_copy(turn + RING - 1, element_of).start()

            raw_copy(turn, element_of).wait()
            st[0:512] = raw[lax.rem(turn, RING)].astype(F32).reshape(512, 128)
            put(turn)
            return carry

        lax.fori_loop(0, count, body, 0)

    def put_narrow(ref, row_of):
        def put(i):
            for j in range(4):
                ref[rows(row_of(i), 128), j * 128 : (j + 1) * 128] = st[
                    pl.ds(j, 128, stride=4), :
                ].astype(BF16)

        return put

    def put_wide(ref, base, block_rows, first):
        def put(i):
            for n in range(4):
                for j in range(4):
                    ref[rows(base + n * block_rows + (i - first) * 32, 32), j * 128 : (j + 1) * 128] = st[
                        pl.ds(4 * n + j, 32, stride=16), :
                    ].astype(BF16)

        return put

    def put_chunk(row, n, block):
        size = SUB_ROWS // 4
        for part in range(2 * SUBS):
            wh[rows(row + part * SUB_ROWS + n * size, size), :] = block[part * size : (part + 1) * size].astype(BF16)

    def plain(turn):
        return turn

    def own_parts(turn):
        late = turn - HALF
        return jnp.where(late < 0, 4 * turn + quarter, 4 * HALF + (late // 2) * 4 + 2 * d + lax.rem(late, 2))

    def half_rows(turn):
        return 8 * d + turn

    def piece_copy(kind, i, q, device):
        part = wx.at[rows(i * 512 + q * 128, 128)]
        return pltpu.make_async_remote_copy(
            src_ref=part, dst_ref=part, send_sem=wss.at[kind], recv_sem=ars.at[W_BASE[kind] + i],
            device_id=device, device_id_type=MESH,
        )

    def half_copy(kind, i, which, device):
        part = wx.at[rows(i * 512 + which * 256, 256)]
        order = min(i, 13) if kind == W_VIA else i
        return pltpu.make_async_remote_copy(
            src_ref=part, dst_ref=part, send_sem=wss.at[kind], recv_sem=ars.at[W_BASE[kind] + order],
            device_id=device, device_id_type=MESH,
        )

    def all_sent(semaphore, ref):
        pltpu.make_async_remote_copy(
            src_ref=ref, dst_ref=ref, send_sem=semaphore, recv_sem=rs.at[0], device_id=peer, device_id_type=MESH
        ).wait_send()

    def all_here(semaphore, ref):
        pltpu.make_async_remote_copy(
            src_ref=ref, dst_ref=ref, send_sem=ss.at[0], recv_sem=semaphore, device_id=peer, device_id_type=MESH
        ).wait_recv()

    def o1_copy(n, chip):
        part = u0.at[n * RW : (n + 1) * RW]
        return remote(part, part, C_O1 + n, C_O1 + n, (chip, d, r))

    def each(work, first, last):
        def body(i, carry):
            work(i)
            return carry

        lax.fori_loop(first, last, body, 0)

    def img_copy(q, slot):
        return pltpu.make_async_copy(img.at[pl.ds(q * 28, 28)], imgb.at[slot], ls.at[slot])

    def open_images():
        for q in range(3):
            img_copy(q, q).start()

    def over_images(body, init):
        def step(q, carry):
            slot = lax.rem(q, 4)

            @pl.when(q + 3 < 7)
            def _():
                img_copy(q + 3, lax.rem(q + 3, 4)).start()

            img_copy(q, slot).wait()
            return body(q, slot, carry)

        return lax.fori_loop(0, 7, step, init)

    outer = (r == 0) | (r == 3)
    inner = jnp.logical_not(outer)
    z_dev, across = (p, d, z_pair), (p, d, 3 - r)

    def grad_copy(send, recv, src, dst, device):
        return pltpu.make_async_remote_copy(
            src_ref=src, dst_ref=dst, send_sem=ass.at[send], recv_sem=ars.at[recv],
            device_id=device, device_id_type=MESH,
        )

    def in_turn(ring, u):
        return ring[0] + lax.rem(u, ring[1])

    def zero_rest(first, source):
        source[...] = jnp.zeros(source.shape, BF16)

        def body(i, carry):
            copy = pltpu.make_async_copy(source, dw.at[pl.ds((first + i) * 4, 4)], ls.at[18])
            copy.start()
            copy.wait()
            return carry

        lax.fori_loop(0, 13 - first, body, 0)

    def bn_sums():
        for k in range(NSETS):
            hot = (set_of == k).astype(F32)
            for n in range(8):
                cols = slice(n * BLK, (n + 1) * BLK)
                dgs[k : k + 1, cols] = jnp.sum(dg[n] * hot, axis=0, keepdims=True)
                dgs[4 + k : 5 + k, cols] = jnp.sum(dg[8 + n] * hot, axis=0, keepdims=True)

    def norm_half(channels):
        return pl.ds(pl.multiple_of(d * (channels // 2), 512), channels // 2)

    def bn_in(cols):
        return remote(dgs.at[:, cols], bz.at[0, :, cols], C_BN1, C_BN1, z_dev)

    def bn_across(cols):
        return remote(dgs.at[:, cols], bz.at[1, :, cols], C_BN2, C_BN2, across)

    def bn_out(cols):
        return remote(dgb.at[:, cols], bz.at[0, :, cols], C_BN3, C_BN3, z_dev)

    def bn_core(cols):
        return remote(dgb.at[:, cols], dgb.at[:, cols], C_BN4, C_BN4, peer)

    def say_ready():
        pl.semaphore_signal(ready.at[0], inc=1, device_id=z_dev, device_id_type=MESH)

        @pl.when(inner)
        def _():
            pl.semaphore_signal(ready.at[1], inc=1, device_id=across, device_id_type=MESH)

    def sum_gradients(
        count, compute, at_row, chunk_of, wide, z1, extra,
        lend=(), passed=(), helper=None, helper_turn=None, helper_row=None, handed_in=None, lent_by=None, computed=None, packed_here=None,
        norms_at=0, norms=4096, after=None, back=R_BACK, late_back=0,
    ):
        turns = SUBS * count
        last_lent = SUBS * (count + len(lend))
        last_given = last_lent + SUBS * len(passed)
        computed = (0, count) if computed is None else computed
        packed_here = (0, count) if packed_here is None else packed_here
        cols = norm_half(norms)
        first_own, own_turns = packed_here[0] * SUBS, packed_here[1] * SUBS
        z2 = z1 + last_given * SUB_ROWS

        def when_own(u, work):
            if handed_in is None:
                work()
            else:
                pl.when(jnp.logical_not(handed_in(u // SUBS)))(work)

        def when_handed(u, work):
            if handed_in is not None:
                pl.when(handed_in(u // SUBS))(work)

        def when_kept(u, work):
            if lent_by is None:
                work()
            else:
                pl.when(jnp.logical_not(lent_by[0](u // SUBS)))(work)

        def when_lent(u, work):
            if lent_by is not None:
                pl.when(lent_by[0](u // SUBS))(work)

        def half(u, which):
            return wh.at[rows(at_row(u // SUBS) + which * 256 + lax.rem(u, SUBS) * SUB_ROWS, SUB_ROWS)]

        def half_part(u, k):
            first = at_row(u // SUBS) + d * 256 + lax.rem(u, SUBS) * SUB_ROWS + k * HOP_ROWS
            return wh.at[rows(first, HOP_ROWS)]

        def from_z(u):
            return wx.at[rows(z1 + u * SUB_ROWS, SUB_ROWS)]

        def from_z_part(u, k):
            return wx.at[rows(z1 + u * SUB_ROWS + k * HOP_ROWS, HOP_ROWS)]

        def from_across(u, k):
            return wx.at[rows(z2 + u * SUB_ROWS + k * HOP_ROWS, HOP_ROWS)]

        def from_core(u):
            return rd.at[rows(u * SUB_ROWS, SUB_ROWS)]

        def to_core(u):
            recv = jnp.where(u < turns, in_turn(R_CORE, u), in_turn(R_GIVE, u))
            return grad_copy(S_CORE, recv, half(u, 1 - d), from_core(u), peer)

        def inwards(u, k):
            return grad_copy(S_IN, in_turn(R_Z, u * HOPS + k), half_part(u, k), from_z_part(u, k), z_dev)

        def exchange(u, k):
            turn = u * HOPS + k
            return grad_copy(
                S_ACROSS + lax.rem(turn, 16), in_turn(R_ACROSS, turn), half_part(u, k), from_across(u, k), across
            )

        def outwards(u, k):
            return grad_copy(S_OUT, in_turn(R_Z, u * HOPS + k), half_part(u, k), from_z_part(u, k), z_dev)

        def packed(u, which):
            return dw.at[chunk_of(u // SUBS) * 4 + which * 2 + lax.rem(u, SUBS)]

        def done_core(u, turn):
            slot = lax.rem(turn, 4)
            return grad_copy(S_DONE + slot, R_DONE, sb.at[slot], packed(u, d), peer)

        def done_here(u, turn):
            slot = lax.rem(turn, 4)
            return pltpu.make_async_copy(sb.at[slot], packed(u, d), ls.at[4 + slot])

        def add(mine, other):
            sums = mine[...].astype(F32) + other[...].astype(F32)
            mine[...] = sums.astype(BF16)

        def pack(u, turn, ref):
            @pl.when(turn >= 4)
            def _():
                done_here(u, turn).wait()
                done_core(u, turn).wait_send()

            value = ref[...].astype(F32)
            for j in range(4):
                cols = slice(j * 128, (j + 1) * 128)
                if wide:
                    for n in range(4):
                        part = SUB_ROWS // 4
                        st[pl.ds(4 * n + j, part, stride=16), :] = value[n * part : (n + 1) * part, cols]
                else:
                    st[pl.ds(j, SUB_ROWS, stride=4), :] = value[:, cols]
            sb[lax.rem(turn, 4)] = st[...].astype(BF16)
            done_here(u, turn).start()
            done_core(u, turn).start()

        def hand(u):
            t, part = u // SUBS, lax.rem(u, SUBS)
            theirs = helper_turn(t) * SUBS + part
            row = helper_turn(t) * 512 if helper_row is None else helper_row(t)
            place = wh.at[rows(row + d * 256 + part * SUB_ROWS, SUB_ROWS)]
            return grad_copy(S_HAND, R_HAND + theirs, half(u, d), place, (helper(t), d, r))

        def handed(u):
            return grad_copy(S_HAND, R_HAND + u, half(u, d), half(u, d), (p, d, r))

        def give_back(u, ref):
            t = u // SUBS
            theirs = lent_by[2](t) * SUBS + lax.rem(u, SUBS)
            place = wx.at[rows(jnp.where(lent_by[1](t) == 0, Z1_ZERO, 0) + theirs * SUB_ROWS, SUB_ROWS)]
            return grad_copy(S_BACK, back, ref, place, (lent_by[1](t), d, r))

        def finish(u, ref):
            when_kept(u, lambda: pack(u, u - first_own, ref))
            when_lent(u, lambda: give_back(u, ref).start())

        def give(t):
            compute(t)
            for k in range(SUBS):
                to_core(t * SUBS + k).start()
            for k in range(SUBS):
                u = t * SUBS + k
                to_core(u).wait_recv()
                add(half(u, d), from_core(u))
                hand(u).start()

        def unit_rows(units):
            return wh.at[0 : units * SUB_ROWS]

        take_at = turns + OUT_LAG - (last_lent - turns)

        def step(it, carry):
            for when, work in extra.items():
                pl.when(it == when)(work)
            for k, when in enumerate(lend + passed):
                pl.when(it == when)(lambda k=k: give(jnp.int32(count + k)))

            def start():
                @pl.when(lax.rem(it, SUBS) == 0)
                def _():
                    compute(it // SUBS)

                to_core(it).start()

            @pl.when(it < turns)
            def _():
                when_own(it, start)

            u1 = it - 1

            @pl.when((u1 >= 0) & (u1 < turns))
            def _():
                def join_cores():
                    to_core(u1).wait_recv()
                    add(half(u1, d), from_core(u1))

                when_own(u1, join_cores)
                when_handed(u1, lambda: handed(u1).wait_recv())

                @pl.when(outer & (u1 == 0))
                def _():
                    pl.semaphore_wait(ready.at[0], 1)

                @pl.when(outer)
                def _():
                    for k in range(HOPS):
                        inwards(u1, k).start()

            u2 = it - 2

            @pl.when(inner & (u2 >= 0) & (u2 < turns))
            def _():
                @pl.when(u2 == 0)
                def _():
                    pl.semaphore_wait(ready.at[1], 1)

                for k in range(HOPS):
                    inwards(u2, k).wait_recv()
                    add(half_part(u2, k), from_z_part(u2, k))
                    exchange(u2, k).start()

            u4 = it - ACROSS_LAG

            @pl.when(inner & (u4 >= 0) & (u4 < turns))
            def _():
                @pl.when(u4 == 0)
                def _():
                    pl.semaphore_wait(ready.at[0], 1)

                for k in range(HOPS):
                    exchange(u4, k).wait()
                    add(half_part(u4, k), from_across(u4, k))
                    outwards(u4, k).start()

                finish(u4, half(u4, d))

            u8 = it - OUT_LAG

            @pl.when(outer & (u8 >= 0) & (u8 < turns))
            def _():
                for k in range(HOPS):
                    outwards(u8, k).wait_recv()

                finish(u8, from_z(u8))

            @pl.when(it == norms_at)
            def _():
                bn_sums()

                @pl.when(outer)
                def _():
                    bn_in(cols).start()

            @pl.when(inner & (it == norms_at + 4))
            def _():
                bn_in(cols).wait_recv()
                dgs[:, cols] += bz[0, :, cols]
                bn_across(cols).start()

            @pl.when(inner & (it == norms_at + 8))
            def _():
                bn_across(cols).wait()
                dgb[:, cols] = dgs[:, cols] + bz[1, :, cols]
                bn_out(cols).start()
                bn_core(cols).start()

            @pl.when(outer & (it == norms_at + 14))
            def _():
                bn_out(cols).wait_recv()
                dgb[:, cols] = bz[0, :, cols]
                bn_core(cols).start()

            for when, work in (after or {}).items():
                pl.when(it == when)(work)

            if lend:
                u_back = turns + it - take_at

                late_units = late_back * SUBS

                @pl.when(it == take_at)
                def _():
                    all_here(ars.at[R_BACK], unit_rows(last_lent - turns - late_units))

                if late_units:

                    @pl.when(u_back == last_lent - late_units)
                    def _():
                        all_here(ars.at[R_BACK_HUB], unit_rows(late_units))

                @pl.when((u_back >= turns) & (u_back < last_lent))
                def _():
                    pack(u_back, own_turns + u_back - turns, from_z(u_back))

            return carry

        lax.fori_loop(0, turns + OUT_LAG, step, 0)

        bn_core(cols).wait()

        @pl.when(outer)
        def _():
            bn_in(cols).wait_send()

        @pl.when(inner)
        def _():
            bn_out(cols).wait_send()

        @pl.when(outer)
        def _():
            all_sent(ass.at[S_IN], unit_rows(turns))

        @pl.when(inner)
        def _():
            all_sent(ass.at[S_OUT], unit_rows(turns))

        made = computed[1] * SUBS + last_given - turns
        if made:
            all_sent(ass.at[S_CORE], unit_rows(made))
        if last_given > turns:
            all_sent(ass.at[S_HAND], unit_rows(last_given - turns))
        if lent_by is not None:
            all_sent(ass.at[S_BACK], unit_rows(lent_by[3] * SUBS))
        all_here(ars.at[R_DONE], dw.at[pl.ds(0, own_turns + last_lent - turns)])
        for slot in range(4):
            done_here(first_own, jnp.int32(slot)).wait()
            done_core(first_own, jnp.int32(slot)).wait_send()

    tables = [
        pltpu.make_async_copy(gain_in, gain, ls.at[17]),
        pltpu.make_async_copy(bias_in, bias, ls.at[18]),
    ]
    for copy in tables:
        copy.start()

    @pl.when(p == 0)
    def _():
        open_weights(plain, 44)
        open_images()

    @pl.when(p == 1)
    def _():
        open_weights(plain, 48)
        open_images()
        pltpu.make_async_copy(cot, cotb.at[0:PIX_OUT], ls.at[16]).start()

    @pl.when(p == 2)
    def _():
        open_weights(own_parts, 15)

    @pl.when(p == 3)
    def _():
        open_weights(half_rows, 8)

    barrier = pltpu.get_barrier_semaphore()
    for device in (peer, (p, d, z_pair), (p, d, 3 - r)) + tuple((lax.rem(p + k, 4), d, r) for k in (1, 2, 3)):
        pl.semaphore_signal(barrier, inc=1, device_id=device, device_id_type=MESH)

    for copy in tables:
        copy.wait()
    block_two = p >= 2
    set_of = per_row(lambda m: jnp.where(block_two, sets[1, m], sets[0, m]))
    for k in range(NSETS):
        hot = (set_of == k).astype(F32)
        for n in range(8):
            g = hot * gain[k : k + 1, n * BLK : (n + 1) * BLK]
            b = hot * bias[k : k + 1, n * BLK : (n + 1) * BLK]
            if k == 0:
                par[n] = g
                par[8 + n] = b
            else:
                par[n] += g
                par[8 + n] += b
    dg[...] = jnp.zeros_like(dg)
    dgb[...] = jnp.zeros_like(dgb)
    pl.semaphore_wait(barrier, 6)

    total_in, total_out = 2.0 * PIX_IN, 2.0 * PIX_OUT

    def build_patches(base):
        def body(tap, carry):
            row, col = base(tap)
            window = pb[pl.ds(row, 7), pl.ds(col, 7)].reshape(RV, BLK)
            pt[tap, 0:RV, :] = window.astype(BF16)
            return carry

        lax.fori_loop(0, 9, body, 0)

    def clear_patch_pad():
        def body(tap, carry):
            pt[tap, RW - 16 : RW, :] = jnp.zeros((16, BLK), BF16)
            return carry

        lax.fori_loop(0, 9, body, 0)

    def strided_base(tap):
        di, dj = tap // 3, lax.rem(tap, 3)
        return lax.rem(di, 2) * 8 + di // 2, lax.rem(dj, 2) * 8 + dj // 2

    def plain_base(tap):
        return tap // 3, lax.rem(tap, 3)

    def conv(ref, first, target):
        target[...] = jnp.zeros_like(target)

        def body(tap, carry):
            z = nn(pt[tap], ref[rows(first + tap * BLK, BLK), :])
            target[...] += z.reshape(PP, 8, BLK)
            return carry

        lax.fori_loop(0, 9, body, 0)

    def conv_back(dz, ref, first, base, side):
        pb[0:side, 0:side] = jnp.zeros((side, side, 8, BLK), F32)

        def body(tap, carry):
            row, col = base(tap)
            part = nt(dz[0:RV, :], ref[rows(first + tap * BLK, BLK), :])
            pb[pl.ds(row, 7), pl.ds(col, 7)] += part.reshape(7, 7, 8, BLK)
            return carry

        lax.fori_loop(0, 9, body, 0)

    def stats_of_map(ref, slot_sum, slot_square):
        def body(c, _, carry):
            z = ref[c]
            return add_stats(carry, z, z * z)

        tx[slot_sum], tx[slot_square] = five(body, zero_stats)

    def act_to(ref, target, center, scale, g, b, mask):
        def body(c, i, carry):
            zhat = (ref[c] - center) * scale
            ref[c] = zhat
            h = silu(zhat * g + b) * mask
            target[rows(i * 80, 80), :] = h.reshape(80, BLK).astype(BF16)
            return carry

        five(body)
        clear_pad(target, 0)

    def upstream(target, grad, zhat_ref, g, b, mask, slot_sum, slot_gain):
        def body(c, i, carry):
            zhat = zhat_ref[c]
            du = grad[rows(i * 80, 80), :].astype(F32).reshape(10, 8, BLK) * mask * slope(zhat * g + b)
            target[c] = du
            return add_stats(carry, du, du * zhat)

        tx[slot_sum], tx[slot_gain] = five(body, zero_stats)

    def norm_back(target, first, du_ref, du_first, zhat_ref, zhat_first, gscale, mean_du, mean_dg, unrolled=False):
        def body(c, i, carry):
            du = du_ref[pl.ds(du_first + i * 10, 10)]
            zhat = zhat_ref[pl.ds(zhat_first + i * 10, 10)]
            dz = gscale * (du - mean_du - zhat * mean_dg)
            target[rows(first + i * 80, 80), :] = dz.reshape(80, BLK).astype(BF16)
            return carry

        five(body, unrolled=unrolled)
        clear_pad(target, first)

    def gi_copy():
        return pltpu.make_async_copy(f3.at[0:PIX_IN, :, 0:256], gi, ls.at[17])

    def out_copy():
        return pltpu.make_async_copy(v_out, out, ls.at[0])

    def dgb_copy():
        return pltpu.make_async_copy(dgb, dgb_out, ls.at[1])

    def final_part():
        @pl.when(p != 1)
        def _():
            remote(ob, ob, C_SHARE, C_SHARE, (p, d, r)).wait_recv()
            remote(r1, r1, C_GP, C_GP, (p, d, r)).wait_recv()

        @pl.when(p != 0)
        def _():
            remote(r0, r0, C_GI, C_GI, (p, d, r)).wait_recv()

        v_out[...] = ob[0:RV, :].astype(F32).reshape(PIX_OUT, 8, BLK).astype(BF16)
        out_copy().start()
        f0[0:PP, :, 0:256] = r1[...].astype(F32).reshape(PP, 8, 256)

        def place(a, carry):
            m = r0[rows(a * 224, 224), :].astype(F32).reshape(28, 8, 256)
            first = m[0:14].reshape(7, 2, 8, 256)
            even = first[:, 0] + f0[pl.ds(a * 7, 7), :, 0:256]
            f3[pl.ds(a * 28, 14), :, 0:256] = jnp.stack([even, first[:, 1]], axis=1).reshape(14, 8, 256)
            f3[pl.ds(a * 28 + 14, 14), :, 0:256] = m[14:28]
            return carry

        lax.fori_loop(0, 7, place, 0)
        gi_copy().start()

    @pl.when(p == 0)
    def _():
        mask = mask_of(0)

        def relay(i):
            piece_copy(W_VIA, i, quarter, (0, d, r)).wait_recv()
            piece_copy(W_OWN, i, quarter, (1, d, r)).start()

        def relay_half(i):
            half_copy(W_VIA, i, d, (0, d, r)).wait_recv()
            half_copy(W_OWN, i, d, (1, d, r)).start()

        put_w = put_narrow(wh, lambda i: i * 128)
        load_weights(plain, 44, 0, 8, put_w)

        def first_conv(q, slot, carry):
            rows_q = imgb[slot].astype(F32).reshape(224, 1024).astype(BF16)
            wx[rows(q * 224, 224), :] = rows_q[:, 0:512]
            wx[rows(1568 + q * 224, 224), :] = rows_q[:, 512:1024]
            z = nn(rows_q, wh[0:1024, :]).reshape(28, 8, BLK)
            f0[pl.ds(q * 28, 28)] = z
            load_weights(plain, 44, 8 + 5 * q, 5, put_w)
            return add_stats(carry, z, z * z)

        tx[0], tx[1] = over_images(first_conv, zero_stats)
        relay(VIA)
        exchange = remote(tx.at[pl.ds(0, 2)], rx.at[pl.ds(0, 2)], 0, 0, peer)
        exchange.start()
        pb[...] = jnp.zeros_like(pb)
        clear_patch_pad()
        load_weights(plain, 44, 43, 1, put_w)
        exchange.wait()

        center, scale = moments(0, 1, total_in, 0)
        g1, b1, g2, b2 = par[0], par[8], par[1], par[9]

        def hidden(i, carry):
            zhat = (f0[pl.ds(i * 14, 14)] - center) * scale
            f0[pl.ds(i * 14, 14)] = zhat
            h = (silu(zhat * g1 + b1) * mask).astype(BF16).astype(F32).reshape(7, 2, 8, BLK)
            u = i + 1
            row = lax.rem(u, 2) * 8 + u // 2
            pb[row, 8:15] = h[:, 0]
            pb[row, 1:8] = h[:, 1]
            return carry

        lax.fori_loop(0, 14, hidden, 0)
        relay(VIA + 1)
        build_patches(strided_base)
        conv(wh, 1024, fs.at[0])
        relay(VIA + 2)
        stats_of_map(fs.at[0], 2, 3)
        sync(1, 2, 2)
        center, scale = moments(2, 3, total_out, 1)
        act_to(fs.at[0], h2, center, scale, g2, b2, mask)
        send = remote(h2, h2, C_H2, C_H2, (1, d, r))
        send.start()
        for i in (HALF, HALF + 1, 16):
            relay_half(i)
        zero_rest(11, sb)
        send.wait_send()
        all_sent(wss.at[W_OWN], wx.at[0 : 3 * 128 + 3 * 256])
        say_ready()

        remote(dh, dh, C_DH, C_DH, (0, d, r)).wait_recv()
        upstream(fs.at[1], dh, fs.at[0], g2, b2, mask, 4, 5)
        sync(0, 4, 2)
        s_du, s_dg = both(4), both(5)
        dg[1], dg[9] = s_dg, s_du
        norm_back(d5, 0, fs.at[1], 0, fs.at[0], 0, g2 * inv[1], s_du * (1.0 / total_out), s_dg * (1.0 / total_out))
        def back_conv():
            conv_back(d5, wh, 1024, strided_base, 16)

        def slopes(i, carry):
            u = i + 1
            row = lax.rem(u, 2) * 8 + u // 2
            grad = jnp.stack([pb[row, 8:15], pb[row, 1:8]], axis=1).reshape(14, 8, BLK)
            zhat = f0[pl.ds(i * 14, 14)]
            du = grad * mask * slope(zhat * g1 + b1)
            f1[pl.ds(i * 14, 14)] = du
            return add_stats(carry, du, du * zhat)

        def first_slopes():
            tx[6], tx[7] = lax.fori_loop(0, 14, slopes, zero_stats)
            sync(1, 6, 2)
            dg[0], dg[8] = both(7), both(6)

        def first_back():
            s_du, s_dg = both(6), both(7)
            gscale, m_du, m_dg = g1 * inv[0], s_du * (1.0 / total_in), s_dg * (1.0 / total_in)

            def body(q, carry):
                part = pl.ds(q * 28, 28)
                dz = gscale * (f1[part] - m_du - f0[part] * m_dg)
                u1[rows(q * 224, 224), :] = dz.reshape(224, BLK).astype(BF16)
                return carry

            lax.fori_loop(0, 7, body, 0)

        def share(target, column, k):
            def body(q, carry):
                g = nt(u1[rows(q * 224, 224), :], wh[k * 256 : (k + 1) * 256, :])
                target[rows(q * 224, 224), column : column + 256] = g.astype(BF16)
                return carry

            lax.fori_loop(0, 7, body, 0)

        places = {1: (u0, 0), 2: (u0, 256), 3: (u2, 0)}

        def share_copy(k):
            target, column = places[k]
            return remote(target.at[0:1568, column : column + 256], r0, C_GI + k - 1, C_GI, (k, d, r))

        def share_out(k):
            share(*places[k], k)
            share_copy(k).start()

        def back_and_share():
            first_back()
            share_out(1)

        def compute(t):
            taps = (t < 6) | (t >= 8)

            @pl.when(taps)
            def _():
                tap = jnp.where(t < 6, t, t - 2)
                wh[rows(at_row(t), 512), :] = tn(pt[tap], d5[...]).astype(BF16)

            @pl.when(jnp.logical_not(taps))
            def _():
                block = tn(wx[rows((t - 6) * 1568, 1568), :], u1[0:1568, :])
                wh[rows(at_row(t), 512), :] = block.astype(BF16)

        def at_row(t):
            return jnp.where(t < 2, 5632 + t * 512, jnp.where(t < 8, t * 512, 2560 + t * 512))

        def chunk_of(t):
            return jnp.where(t < 6, t + 2, jnp.where(t < 8, t - 6, t))

        sum_gradients(
            8, compute, at_row, chunk_of, False, Z1_ZERO,
            {LAST_TURN + 8 * SUBS: final_part},
            lend=(5, 6, 7), helper=lambda t: jnp.where(t < 10, 2, 1), helper_turn=lambda t: jnp.where(t < 10, t - 1, 8),
            helper_row=lambda t: jnp.where(t < 10, (t - 1) * 512, HUB_GUEST), norms_at=4 * SUBS, norms=1024, late_back=1,
            after={
                1: back_conv,
                2: first_slopes,
                3: back_and_share,
                4: lambda: share(r0, 0, 0),
                8: lambda: share_out(3),
                10: lambda: share_out(2),
            },
        )
        for k in (1, 2, 3):
            share_copy(k).wait_send()

    @pl.when(p == 1)
    def _():
        mask = mask_of(1)
        gate_v = per_row(lambda m: gates[m]).astype(F32)
        cotb[PIX_OUT] = jnp.zeros((8, C_OUT), BF16)
        clear_patch_pad()
        load_weights(plain, 48, 0, 16, put_wide(wh, 0, 512, 0))
        load_weights(plain, 48, 16, 32, put_wide(wh, 2048, 1024, 16))

        def shorten(a, slot, carry):
            v = imgb[slot, 0:14].astype(F32).reshape(7, 2, 8, 1024)[:, 0]
            f0[pl.ds(a * 7, 7)] = v[:, :, 0:512]
            f0[pl.ds(PP + a * 7, 7)] = v[:, :, 512:1024]
            return carry

        other_z = 2 * (1 - lax.rem(r, 2))
        this_z = 2 * lax.rem(r, 2)

        def pass_own(i):
            piece_copy(W_OWN, i, quarter, (1, d, r)).wait_recv()
            piece_copy(W_PEER, i, quarter, peer).start()
            piece_copy(W_Z, i, quarter, z_dev).start()

        def pass_on(i):
            piece_copy(W_Z, i, other_z + d, peer).wait_recv()
            piece_copy(W_ON, i, other_z + d, peer).start()

        def have(i):
            piece_copy(W_PEER, i, this_z + 1 - d, peer).wait_recv()
            piece_copy(W_ON, i, other_z + 1 - d, peer).wait_recv()

        def pass_half(i):
            half_copy(W_OWN, i, d, (1, d, r)).wait_recv()
            half_copy(W_PEER, i, d, peer).start()

        def have_half(i):
            half_copy(W_PEER, i, 1 - d, peer).wait_recv()

        pass_own(0)
        over_images(shorten, 0)
        f0[PIX_OUT] = jnp.zeros((8, BLK), F32)
        f0[PP + PIX_OUT] = jnp.zeros((8, BLK), F32)
        sx[...] = f0[0 : 2 * PP].reshape(2 * RW, BLK).astype(BF16)

        def shortcut(n, carry):
            z = nn(sx[0:RW, :], wh[rows(2048 + n * 1024, 512), :]) + nn(
                sx[RW : 2 * RW, :], wh[rows(2560 + n * 1024, 512), :]
            )
            store_z(f1, n * PP, z, 4 * n + 2, 4 * n + 3)
            return carry

        pass_own(1)
        lax.fori_loop(0, 4, shortcut, 0)

        pass_own(2)
        pass_own(VIA)
        pass_on(0)
        pass_own(3)
        pass_on(1)
        pass_own(VIA + 1)
        pass_own(4)
        pl.semaphore_signal(go, inc=1, device_id=(3, d, r), device_id_type=MESH)
        pass_on(2)
        pass_own(VIA + 2)
        pass_own(5)
        pass_on(VIA)
        pass_own(6)
        pass_on(3)
        pass_own(7)
        pass_on(VIA + 1)
        remote(h2, h2, C_H2, C_H2, (1, d, r)).wait_recv()

        def third_conv(n, carry):
            store_z(f0, n * PP, nn(h2[...], wh[rows(n * 512, 512), :]), 4 * n, 4 * n + 1)
            exchange_of(E_WIDE + n, 4 * n, 4).start()
            return carry

        lax.fori_loop(0, 4, third_conv, 0)
        pass_on(4)

        def join(n, carry):
            exchange_of(E_WIDE + n, 4 * n, 4).wait()
            c3, s3 = moments(4 * n, 4 * n + 1, total_out, 2 + n)
            cp, sp = moments(4 * n + 2, 4 * n + 3, total_out, 6 + n)
            g3, gp, b = par[n], par[4 + n], par[8 + n] + par[12 + n]

            def body(_, i, carry):
                part = pl.ds(n * PP + i * 10, 10)
                a = (f0[part] - c3) * s3
                b_ = (f1[part] - cp) * sp
                f0[part] = a
                f1[part] = b_
                o = silu(a * g3 + b_ * gp + b)
                u0[rows(n * RW + i * 80, 80), :] = o.reshape(80, BLK).astype(BF16)
                return carry

            five(body)
            clear_pad(u0, n * RW)
            return carry

        lax.fori_loop(0, 4, join, 0)
        for n in (1, 2, 3):
            o1_copy(n, 3).start()
        pass_half(13)
        pass_on(VIA + 2)
        pass_half(HALF)
        each(have, 0, 4)
        zhat4, zhat5 = fs.at[0], fs.at[1]
        z = nn(u0[0:RW, :], wx[0:512, :])
        for n in range(1, 4):
            z += nn(u0[n * RW : (n + 1) * RW, :], wx[n * 512 : (n + 1) * 512, :])
        store_z(zhat4, 0, z, 16, 17)
        sync(0, 16, 2)
        remote(parx.at[0:4], parx.at[0:4], C_PAR2, C_PAR2, (1, d, r)).wait_recv()
        center, scale = moments(16, 17, total_out, 10)
        g4, g5, b4, b5 = parx[0], parx[1], parx[2], parx[3]
        pb[0:9, 0:9] = jnp.zeros((9, 9, 8, BLK), F32)

        def hidden(a, carry):
            part = pl.ds(a * 7, 7)
            zhat = (zhat4[part] - center) * scale
            zhat4[part] = zhat
            h = silu(zhat * g4 + b4) * mask
            pb[a + 1, 1:8] = h.astype(BF16).astype(F32)
            return carry

        lax.fori_loop(0, 7, hidden, 0)
        h4[0:RV, :] = pb[1:8, 1:8].reshape(RV, BLK).astype(BF16)
        h4_send = remote(h4, h4, C_H4, C_H4, (2, d, r))
        h4_send.start()

        o1_copy(0, 2).start()
        pass_on(5)
        build_patches(plain_base)
        pass_on(6)

        def fifth_conv(taps):
            left = jnp.concatenate([pt[t] for t in taps], axis=1)
            right = jnp.concatenate([wx[2048 + t * 512 : 2560 + t * 512, :] for t in taps], axis=0)
            return nn(left, right).reshape(PP, 8, BLK)

        for i in (4, 5, VIA):
            have(i)
        zhat5[...] = fifth_conv((0, 1, 4))
        pass_half(HALF + 1)
        pass_on(7)
        for i in (6, VIA + 1, VIA + 2):
            have(i)
        zhat5[...] += fifth_conv((2, 5, 6))
        have(7)
        have_half(HALF)
        have_half(HALF + 1)
        store_z(zhat5, 0, zhat5[...] + fifth_conv((3, 7, 8)), 18, 19)
        exchange_z5 = exchange_of(1, 18, 2)
        exchange_z5.start()
        pass_half(14)
        exchange_z5.wait()
        center, scale = moments(18, 19, total_out, 11)
        act_to(zhat5, h5, center, scale, g5, b5, mask)


        def sixth_conv(n):
            have_half(13 + n)
            store_z(f2, n * PP, nn(h5[...], wx[6656 + n * 512 : 7168 + n * 512, :]), 20 + 2 * n, 21 + 2 * n)

        def exchange_z6(n):
            return exchange_of(E_WIDE_NEXT + n, 20 + 2 * n, 2)

        def exchange_d6(n):
            return exchange_of(E_WIDE + n, 28 + 2 * n, 2)

        def finish(n):
            center, scale = moments(20 + 2 * n, 21 + 2 * n, total_out, 12 + n)
            g6, b6 = parx[4 + n], parx[8 + n]

            def body(c, i, carry):
                part = pl.ds(n * PP + i * 10, 10)
                part_rows = rows(n * RW + i * 80, 80)
                zhat = (f2[part] - center) * scale
                f2[part] = zhat
                o = u0[part_rows, :].astype(F32).reshape(10, 8, BLK)
                q = o + zhat * g6 + b6
                s = sigmoid(q)
                act = q * s
                pt[n, rows(i * 80, 80), :] = (o + gate_v * (act - o)).reshape(80, BLK).astype(BF16)
                ct = cotb[c, :, n * BLK : (n + 1) * BLK].astype(F32)
                through = ct * gate_v
                dq = through * (s + act * (1.0 - s))
                f3[part] = dq
                u2[part_rows, :] = (dq + (ct - through)).reshape(80, BLK).astype(BF16)
                return add_stats(carry, dq, dq * zhat)

            tx[28 + 2 * n], tx[29 + 2 * n] = five(body, zero_stats, unrolled=True)

        for n in (0, 1):
            sixth_conv(n)
            exchange_z6(n).start()
        remote(parx.at[4:12], parx.at[4:12], C_PAR3, C_PAR3, (1, d, r)).wait_recv()
        pltpu.make_async_copy(cot, cotb.at[0:PIX_OUT], ls.at[16]).wait()
        pass_half(15)
        exchange_z6(0).wait()
        finish(0)
        exchange_d6(0).start()
        pass_half(16)
        exchange_z6(1).wait()
        finish(1)
        exchange_d6(1).start()
        have_half(15)
        store_z(f2, 2 * PP, nn(h5[...], wx[7680:8192, :]), 24, 25)
        exchange_z6(2).start()
        have_half(16)
        store_z(f2, 3 * PP, nn(h5[...], wx[8192:8704, :]), 26, 27)
        exchange_z6(3).start()
        exchange_z6(2).wait()
        finish(2)
        exchange_d6(2).start()
        exchange_z6(3).wait()
        finish(3)
        exchange_d6(3).start()
        ob[...] = pt[1]

        def output_copy(k):
            return remote(pt.at[k], ob, C_SHARE + k % 3, C_SHARE, (k, d, r))

        output_copy(3).start()


        def sixth_back(n):
            s_du, s_dg = both(28 + 2 * n), both(29 + 2 * n)
            dgx[4 + n] = s_dg
            dgx[8 + n] = s_du
            norm_back(
                u1, n * RW, f3, n * PP, f2, n * PP, parx[4 + n] * inv[12 + n],
                s_du * (1.0 / total_out), s_dg * (1.0 / total_out), unrolled=True,
            )

        grad = jnp.zeros((RW, BLK), F32)
        for n in range(5):
            if n < 4:
                exchange_d6(n).wait()
                sixth_back(n)
            if n > 0:
                grad += nt(u1[(n - 1) * RW : n * RW, :], wx[6144 + n * 512 : 6656 + n * 512, :])
        dh[...] = grad.astype(BF16)

        upstream(f2, dh, zhat5, g5, b5, mask, 36, 37)
        sync(0, 36, 2)
        s_du, s_dg = both(36), both(37)
        dgx[1] = s_dg
        dgx[3] = s_du
        norm_back(d5, 0, f2, 0, zhat5, 0, g5 * inv[11], s_du * (1.0 / total_out), s_dg * (1.0 / total_out))
        d5_send = remote(d5, d5, C_D5, C_D5, (2, d, r))
        d5_send.start()
        pb[0:9, 0:9] = jnp.zeros((9, 9, 8, BLK), F32)
        for tap in range(9):
            row, col = tap // 3, tap % 3
            part = nt(d5[0:RV, :], wx[2048 + tap * 512 : 2560 + tap * 512, :])
            pb[row : row + 7, col : col + 7] += part.reshape(7, 7, 8, BLK)

        def fourth_slopes(a, carry):
            part = pl.ds(a * 7, 7)
            zhat = zhat4[part]
            du = pb[a + 1, 1:8] * mask * slope(zhat * g4 + b4)
            f2[part] = du
            return add_stats(carry, du, du * zhat)

        tx[38], tx[39] = lax.fori_loop(0, 7, fourth_slopes, zero_stats)
        sync(1, 38, 2)
        s_du, s_dg = both(38), both(39)
        dgx[0] = s_dg
        dgx[2] = s_du
        norm_back(d4, 0, f2, 0, zhat4, 0, g4 * inv[10], s_du * (1.0 / total_out), s_dg * (1.0 / total_out))

        def carried_back(n):
            z = nt(d4[...], wx[n * 512 : (n + 1) * 512, :])
            f2[(n % 2) * PP : (n % 2 + 1) * PP] = z.reshape(PP, 8, BLK)

        def exchange_d1(n):
            return exchange_of(E_WIDE_NEXT + n, 40 + 3 * n, 3)

        def first_block_slopes(n):
            g3, gp, b = par[n], par[4 + n], par[8 + n] + par[12 + n]

            def body(_, i, carry):
                part = pl.ds(n * PP + i * 10, 10)
                do = u2[n * RW + i * 80 : n * RW + (i + 1) * 80, :].astype(F32).reshape(10, 8, BLK)
                do += f2[pl.ds((n % 2) * PP + i * 10, 10)]
                a, b_ = f0[part], f1[part]
                dp = do * slope(a * g3 + b_ * gp + b)
                f3[part] = dp
                s0, s1, s2 = carry
                return s0 + jnp.sum(dp, axis=0), s1 + jnp.sum(dp * a, axis=0), s2 + jnp.sum(dp * b_, axis=0)

            first = 40 + 3 * n
            tx[first], tx[first + 1], tx[first + 2] = five(body, zero_stats + zero_stats[:1], unrolled=True)

        carried_back(0)
        for n in range(4):
            if n < 3:
                carried_back(n + 1)
            first_block_slopes(n)
            exchange_d1(n).start()

        def third_back(n):
            first = 40 + 3 * n
            m_du, m_dg = both(first) * (1.0 / total_out), both(first + 1) * (1.0 / total_out)
            norm_back(
                pt.at[4 + n], 0, f3, n * PP, f0, n * PP, par[n] * inv[2 + n], m_du, m_dg, unrolled=True
            )

        grad = jnp.zeros((RW, BLK), F32)
        for n in range(5):
            if n < 4:
                exchange_d1(n).wait()
                third_back(n)
            if n > 0:
                grad += nt(pt[3 + n], wh[(n - 1) * 512 : n * 512, :])
        dh[...] = grad.astype(BF16)
        dh_send = remote(dh, dh, C_DH, C_DH, (0, d, r))
        dh_send.start()

        def shortcut_back(n, carry):
            first = 40 + 3 * n
            s_du, s_d3, s_dp = both(first), both(first + 1), both(first + 2)
            dg[n] = s_d3
            dg[4 + n] = s_dp
            dg[8 + n] = s_du
            dg[12 + n] = s_du
            m_du, m_dg = s_du * (1.0 / total_out), s_dp * (1.0 / total_out)
            norm_back(u2, n * RW, f3, n * PP, f1, n * PP, par[4 + n] * inv[6 + n], m_du, m_dg)
            return carry

        def all_shortcut_back():
            lax.fori_loop(0, 4, shortcut_back, 0)

        all_sent(wss.at[W_PEER], wx.at[0 : HALF * 128 + 6 * 256])
        all_sent(wss.at[W_Z], wx.at[0 : HALF * 128])
        all_sent(wss.at[W_ON], wx.at[0 : HALF * 128])
        say_ready()

        late = [remote(d4, d4, C_D4, C_D4, (2, d, r))]
        for first, last, sem, chip in ((0, 4, C_DG2, 2), (4, 12, C_DG3, 3)):
            late.append(remote(dgx.at[first:last], dgx.at[first:last], sem, sem, (chip, d, r)))

        def late_sends():
            dh_send.wait_send()
            for copy in late:
                copy.start()

        def shortcut_share(k):
            g = nt(u2[0:RW, :], wh[2048 + k * 256 : 2304 + k * 256, :])
            for n in range(1, 4):
                g += nt(u2[n * RW : (n + 1) * RW, :], wh[2048 + n * 1024 + k * 256 : 2304 + n * 1024 + k * 256, :])
            return g.astype(BF16)

        places = ((h4.at[:, 0:256], 0), (h4.at[:, 256:512], 2), (pt.at[8, :, 0:256], 3))

        def share_copy(slot):
            place, k = places[slot]
            return remote(place, r1, C_GP + slot, C_GP, (k, d, r))

        def shortcut_shares(slot):
            place, k = places[slot]
            if slot == 0:
                h4_send.wait_send()
            place[...] = shortcut_share(k)

        def shortcut_own():
            r1[...] = shortcut_share(1)


        def own_and_output():
            shortcut_own()
            output_copy(2).start()

        def late_shares():
            for slot in range(3):
                share_copy(slot).start()

        def at_row(t):
            early = jnp.where(t == 8, HUB_GUEST, t * 512)
            return jnp.where(t < 11, early, jnp.where(t < 16, t * 512 + 512, 5632))

        def compute(t):
            @pl.when(t < 4)
            def _():
                left = h2[:, pl.ds(pl.multiple_of(t * 128, 128), 128)]
                for n in range(4):
                    put_chunk(at_row(t), n, tn(left, pt[4 + n]))

            @pl.when((t >= 4) & (t < 13))
            def _():
                m = jnp.where(t < 8, t - 4, t - 5)
                left = sx[rows((m // 4) * RW, RW), pl.ds(pl.multiple_of(lax.rem(m, 4) * 128, 128), 128)]
                for n in range(4):
                    put_chunk(at_row(t), n, tn(left, u2[n * RW : (n + 1) * RW, :]))

            @pl.when(t >= 13)
            def _():
                left = h5[:, pl.ds(pl.multiple_of((t - 13) * 128, 128), 128)]
                for n in range(4):
                    put_chunk(at_row(t), n, tn(left, u1[n * RW : (n + 1) * RW, :]))

        zero_rest(12, sb)
        sum_gradients(
            11, compute, at_row, lambda t: jnp.where(t < 8, t, t - 1), True, 0,
            {LAST_TURN + 11 * SUBS: final_part},
            after={
                1: all_shortcut_back,
                2: lambda: shortcut_shares(0),
                4: lambda: shortcut_shares(1),
                5: late_sends,
                6: lambda: shortcut_shares(2),
                7: own_and_output,
                11: lambda: output_copy(0).start(),
                15: late_shares,
            },
            lend=(3, 5), passed=(7, 9, 11, 13), helper=lambda t: 3, helper_turn=lambda t: t - 7, norms_at=2,
            handed_in=lambda t: t == 8, lent_by=(lambda t: t == 8, lambda t: 0, lambda t: t + 2, 1), back=R_BACK_HUB,
            computed=(0, 10), packed_here=(0, 10),
        )
        for copy in [d5_send, o1_copy(0, 2)] + [o1_copy(n, 3) for n in (1, 2, 3)] + late:
            copy.wait_send()
        for slot in range(3):
            share_copy(slot).wait_send()
        for k in (0, 2, 3):
            output_copy(k).wait_send()


    @pl.when(p == 2)
    def _():
        for k, slot in ((0, 0), (1, 1), (2, 8), (3, 9)):
            parx[k] = par[slot]
        par_send = remote(parx.at[0:4], parx.at[0:4], C_PAR2, C_PAR2, (1, d, r))
        par_send.start()

        put_w = put_narrow(wx, lambda i: own_parts(i) * 128)

        def put(i):
            put_w(i)

            @pl.when(i < VIA)
            def _():
                piece_copy(W_OWN, i, quarter, (1, d, r)).start()

            @pl.when((i >= VIA) & (i < HALF))
            def _():
                piece_copy(W_VIA, i, quarter, (0, d, r)).start()

            for k in range(HALF, 13):
                @pl.when(i == HALF + 2 * (k - HALF) + 1)
                def _(k=k):
                    half_copy(W_VIA, k, d, (0, d, r)).start()

        load_weights(own_parts, 15, 0, 15, put)
        pb[...] = jnp.zeros_like(pb)
        clear_patch_pad()

        all_sent(wss.at[W_OWN], wx.at[0 : VIA * 128])
        all_sent(wss.at[W_VIA], wx.at[0 : 3 * 128 + 2 * 256])
        say_ready()
        remote(h4, h4, C_H4, C_H4, (2, d, r)).wait_recv()
        pb[1:8, 1:8] = h4[0:RV, :].astype(F32).reshape(7, 7, 8, BLK)
        build_patches(plain_base)
        remote(d5, d5, C_D5, C_D5, (2, d, r)).wait_recv()

        def compute(t):
            taps = (t < 5) | (t >= 11)

            @pl.when(taps)
            def _():
                tap = jnp.where(t < 5, t + 4, t - 11)
                wh[rows(t * 512, 512), :] = tn(pt[tap], d5[...]).astype(BF16)

            @pl.when(t == 5)
            def _():
                remote(d4, d4, C_D4, C_D4, (2, d, r)).wait_recv()
                for n in range(4):
                    o1_copy(n, 2).wait_recv()

            @pl.when(jnp.logical_not(taps))
            def _():
                n = jnp.where(t < 7, t - 5, t - 7)
                wh[rows(t * 512, 512), :] = tn(u0[rows(n * RW, RW), :], d4[...]).astype(BF16)

        def chunk_of(t):
            return jnp.where(t < 5, t + 8, jnp.where(t < 7, t - 5, t - 7))

        def norm_grads():
            remote(dgx.at[0:4], dgx.at[0:4], C_DG2, C_DG2, (2, d, r)).wait_recv()
            dg[0], dg[1], dg[8], dg[9] = dgx[0], dgx[1], dgx[2], dgx[3]

        sum_gradients(
            11, compute, lambda t: t * 512, chunk_of, False, 0,
            {6 * SUBS: norm_grads, LAST_TURN + 11 * SUBS: final_part},
            lend=(2, 3, 4, 6), helper=lambda t: 3, helper_turn=lambda t: t - 11,
            handed_in=lambda t: (t >= 7) & (t < 9),
            lent_by=(lambda t: (t >= 7) & (t < 9), lambda t: 0, lambda t: t + 1, 2),
            computed=(0, 9), packed_here=(0, 9), norms_at=6 * SUBS, norms=1024,
        )
        par_send.wait_send()

    @pl.when(p == 3)
    def _():
        for k in range(4):
            parx[4 + k] = par[k]
            parx[8 + k] = par[8 + k]
        par_send = remote(parx.at[4:12], parx.at[4:12], C_PAR3, C_PAR3, (1, d, r))
        par_send.start()
        say_ready()

        def put(i):
            for n in range(4):
                for j in range(4):
                    wx[rows(6656 + n * 512 + d * 256 + i * 32, 32), j * 128 : (j + 1) * 128] = st[
                        pl.ds(4 * n + j, 32, stride=16), :
                    ].astype(BF16)

        load_weights(half_rows, 8, 0, 8, put)
        zero_rest(4, sb)
        pl.semaphore_wait(go, 1)

        half_copy(W_VIA, 16, d, (0, d, r)).start()
        for i in (13, 14, 15):
            half_copy(W_OWN, i, d, (1, d, r)).start()
        for n in (1, 2, 3):
            o1_copy(n, 3).wait_recv()
            o1_copy(n, 2).start()
        def norm_grads():
            remote(dgx.at[4:12], dgx.at[4:12], C_DG3, C_DG3, (3, d, r)).wait_recv()
            for k in range(4):
                dg[k] = dgx[4 + k]
                dg[8 + k] = dgx[8 + k]

        sum_gradients(
            10, lambda t: None, lambda t: t * 512, lambda t: t - 6, True, 0,
            {5 * SUBS: norm_grads, LAST_TURN + 10 * SUBS: final_part},
            handed_in=lambda t: t >= 0,
            lent_by=(lambda t: t < 6, lambda t: jnp.where(t < 4, 2, 1), lambda t: jnp.where(t < 4, t + 11, t + 7), 6),
            computed=(0, 0), packed_here=(6, 4), norms_at=5 * SUBS, norms=2048,
        )
        for n in (1, 2, 3):
            o1_copy(n, 2).wait_send()
        all_sent(wss.at[W_VIA], wx.at[0:256])
        all_sent(wss.at[W_OWN], wx.at[0 : 3 * 256])
        par_send.wait_send()

    dgb_copy().start()
    gi_copy().wait()
    out_copy().wait()
    dgb_copy().wait()


def widen_kernel(out_in, gi_in, dw_in, dgb_in, out, gi, dw, gain, bias, v_out, v_gi, v_dw, v_wide, v_dgb, sin, sout):
    count = v_dw.shape[0] // 3328

    def part(i):
        return pl.ds(i * 3328, 3328)

    loads = [pltpu.make_async_copy(dw_in.at[part(i)], v_dw.at[part(i)], sin.at[i]) for i in range(count)]
    others = (
        (dgb_in, v_dgb, ((v_dgb.at[0:4], gain), (v_dgb.at[4:8], bias))),
        (out_in, v_out, ((v_out, out),)),
        (gi_in, v_gi, ((v_gi, gi),)),
    )
    more = [pltpu.make_async_copy(a, b, sin.at[count + k]) for k, (a, b, _) in enumerate(others)]
    for copy in more + loads:
        copy.start()
    stores = []
    for i in range(count):
        loads[i].wait()
        v_wide[part(i)] = v_dw[part(i)].astype(F32)
        stores.append(pltpu.make_async_copy(v_wide.at[part(i)], dw.at[part(i)], sout.at[i]))
        stores[-1].start()
    for k, (_, _, ends) in enumerate(others):
        more[k].wait()
        for a, b in ends:
            stores.append(pltpu.make_async_copy(a, b, sout.at[len(stores)]))
            stores[-1].start()
    for copy in stores:
        copy.wait()


def widen(out, gi, dw, dgb):
    count = P_SIZE // 128 // 3328
    any_space = pl.BlockSpec(memory_space=pl.ANY)
    return pl.pallas_call(
        widen_kernel,
        out_shape=(
            jax.ShapeDtypeStruct(out.shape, out.dtype),
            jax.ShapeDtypeStruct(gi.shape, gi.dtype),
            jax.ShapeDtypeStruct(dw.shape, F32),
            jax.ShapeDtypeStruct((4, 4096), F32),
            jax.ShapeDtypeStruct((4, 4096), F32),
        ),
        in_specs=[any_space] * 4,
        out_specs=(any_space,) * 5,
        scratch_shapes=[
            pltpu.VMEM(out.shape, out.dtype),
            pltpu.VMEM(gi.shape, gi.dtype),
            pltpu.VMEM(dw.shape, BF16),
            pltpu.VMEM(dw.shape, F32),
            pltpu.VMEM(dgb.shape, F32),
            pltpu.SemaphoreType.DMA((count + 3,)),
            pltpu.SemaphoreType.DMA((count + 4,)),
        ],
        compiler_params=pltpu.CompilerParams(vmem_limit_bytes=64 * 1024 * 1024),
    )(out, gi, dw, dgb)


def one_kernel(images, section_weights, bn_gain, bn_bias, width, bn_set, gate, cotangent):
    any_space = pl.BlockSpec(memory_space=pl.ANY)
    smem = pl.BlockSpec(memory_space=pltpu.SMEM)
    out, gi, dw, dgb = pl.pallas_call(
        whole_kernel,
        out_shape=(
            jax.ShapeDtypeStruct((PIX_OUT, 8, BLK), BF16),
            jax.ShapeDtypeStruct((PIX_IN, 8, 256), F32),
            jax.ShapeDtypeStruct((P_SIZE // SUB, 512, 128), BF16),
            jax.ShapeDtypeStruct((8, 4096), F32),
        ),
        in_specs=[any_space, any_space, any_space, any_space, smem, smem, smem, any_space],
        out_specs=(any_space,) * 4,
        scratch_shapes=[
            pltpu.VMEM((4, 28, 8, 1024), BF16),
            pltpu.VMEM((RING, 1, SUB), BF16),
            pltpu.VMEM((512, 128), F32),
            pltpu.VMEM((9216, BLK), BF16),
            pltpu.VMEM((8768, BLK), BF16),
            pltpu.VMEM((4 * PP, 8, BLK), F32),
            pltpu.VMEM((4 * PP, 8, BLK), F32),
            pltpu.VMEM((4 * PP, 8, BLK), F32),
            pltpu.VMEM((4 * PP, 8, BLK), F32),
            pltpu.VMEM((2, PP, 8, BLK), F32),
            pltpu.VMEM((16, 16, 8, BLK), F32),
            pltpu.VMEM((9, RW, BLK), BF16),
            pltpu.VMEM((4 * RW, BLK), BF16),
            pltpu.VMEM((4 * RW, BLK), BF16),
            pltpu.VMEM((4 * RW, BLK), BF16),
            pltpu.VMEM((2 * RW, BLK), BF16),
            pltpu.VMEM((PP, 8, C_OUT), BF16),
            pltpu.VMEM((RW, BLK), BF16),
            pltpu.VMEM((RW, BLK), BF16),
            pltpu.VMEM((RW, BLK), BF16),
            pltpu.VMEM((RW, BLK), BF16),
            pltpu.VMEM((RW, BLK), BF16),
            pltpu.VMEM((RW, BLK), BF16),
            pltpu.VMEM((8 * PIX_IN, 256), BF16),
            pltpu.VMEM((RW, 256), BF16),
            pltpu.VMEM((RW, BLK), BF16),
            pltpu.VMEM((52, 8, BLK), F32),
            pltpu.VMEM((52, 8, BLK), F32),
            pltpu.VMEM((16, 8, BLK), F32),
            pltpu.VMEM((16, 8, BLK), F32),
            pltpu.VMEM((12, 8, BLK), F32),
            pltpu.VMEM((16, 8, BLK), F32),
            pltpu.VMEM((12, 8, BLK), F32),
            pltpu.VMEM((4, 512, 128), BF16),
            pltpu.VMEM((4352, BLK), BF16),
            pltpu.VMEM((2, 8, 4096), F32),
            pltpu.VMEM((8, 4096), F32),
            pltpu.VMEM((8, 4096), F32),
            pltpu.VMEM((PIX_OUT, 8, BLK), BF16),
            pltpu.VMEM((NSETS, 4096), F32),
            pltpu.VMEM((NSETS, 4096), F32),
            pltpu.SemaphoreType.DMA((19,)),
            pltpu.SemaphoreType.DMA((N_SEM,)),
            pltpu.SemaphoreType.DMA((N_SEM,)),
            pltpu.SemaphoreType.DMA((5,)),
            pltpu.SemaphoreType.DMA((N_SUM_SEND,)),
            pltpu.SemaphoreType.DMA((N_SUM_RECV,)),
            pltpu.SemaphoreType.REGULAR((2,)),
            pltpu.SemaphoreType.REGULAR,
        ],
        compiler_params=pltpu.CompilerParams(
            collective_id=0, has_side_effects=True, vmem_limit_bytes=64 * 1024 * 1024
        ),
    )(
        jnp.transpose(images, (1, 0, 2)),
        section_weights,
        bn_gain[0],
        bn_bias[0],
        width.T,
        bn_set.T,
        gate,
        jnp.transpose(cotangent, (1, 0, 2)),
    )
    out, gi, dw, gain_sum, bias_sum = widen(out, gi, dw.reshape(P_SIZE // 128, 128), dgb)
    return (
        jnp.transpose(out, (1, 0, 2)),
        jnp.transpose(gi, (1, 0, 2)),
        dw.reshape(1, P_SIZE),
        gain_sum[None],
        bias_sum[None],
    )


def solution(mesh):
    sizes = dict(mesh.shape)
    fits = sizes["pipe"] == 4 and sizes["dp"] == 2 and sizes["rep"] == 4
    placed = (
        P(("dp", "rep"), None, None),
        P("pipe", None),
        P("pipe", None, None),
        P("pipe", None, None),
        P(),
        P(),
        P(),
        P(("dp", "rep"), None, None),
    )
    return jax.shard_map(
        one_kernel if fits else on_device,
        mesh=mesh,
        in_specs=placed,
        out_specs=(
            P(("dp", "rep"), None, "pipe"),
            P(("dp", "rep"), None, "pipe"),
            P("pipe", None),
            P("pipe", None, None),
            P("pipe", None, None),
        ),
        check_vma=False,
    )
```
